32 devices in a mesh: section: 2 (over x), context: 4 (over z), tensor: 4 (over y, core).
Axes of the slice: x: 2, y: 2, z: 4, core: 2. Of those that a mesh axis runs over, the one named last changes fastest.
Arguments:
- image_tokens: bfloat16 [2, 896, 1536], P(None, ('context', 'tensor')), may hold values from -6 to 6
- text_tokens: bfloat16 [2, 128, 1536], P(None, ('context', 'tensor')), may hold values from -6 to 6
- conditioning: bfloat16 [2, 3, 1536], P(None, None, ('context', 'tensor')), may hold values from -6 to 6
- image_seq_ids: int32 [2, 896], replicated, may hold values from 0 to 2, as said below
- text_seq_ids: int32 [2, 128], replicated, may hold values from 0 to 2, as said below
- ada_weight: bfloat16 [2, 2, 1536, 9216], P('section', None, ('context', 'tensor')), may hold values from -0.15625 to 0.15625
- qkv_weight: bfloat16 [2, 2, 1536, 4608], P('section', None, 'context', 'tensor'), may hold values from -0.15625 to 0.15625
- out_weight: bfloat16 [2, 2, 1536, 1536], P('section', None, 'tensor', 'context'), may hold values from -0.625 to 0.625
- up_weight: bfloat16 [2, 2, 1536, 6144], P('section', None, 'context', 'tensor'), may hold values from -0.15625 to 0.15625
- down_weight: bfloat16 [2, 2, 6144, 1536], P('section', None, 'tensor', 'context'), may hold values from -0.078125 to 0.078125
- biases: bfloat16 [2, 2, 21504], P('section', None, ('context', 'tensor')), may hold values from -2 to 2
- image_cotangent: bfloat16 [2, 896, 1536], P(None, ('context', 'tensor')), may hold values from -6 to 6
- text_cotangent: bfloat16 [2, 128, 1536], P(None, ('context', 'tensor')), may hold values from -6 to 6
Outputs:
- image_out: float32 [2, 2, 896, 1536], P('section', None, ('context', 'tensor'))
- text_out: float32 [2, 2, 128, 1536], P('section', None, ('context', 'tensor'))
- image_grad: float32 [2, 2, 896, 1536], P('section', None, ('context', 'tensor'))
- text_grad: float32 [2, 2, 128, 1536], P('section', None, ('context', 'tensor'))
- cond_grad: float32 [2, 3, 1536], P(None, None, ('context', 'tensor'))
- ada_grad: float32 [2, 2, 1536, 9216], P('section', None, ('context', 'tensor'))
- qkv_grad: float32 [2, 2, 1536, 4608], P('section', None, 'context', 'tensor')
- out_grad: float32 [2, 2, 1536, 1536], P('section', None, 'tensor', 'context')
- up_grad: float32 [2, 2, 1536, 6144], P('section', None, 'context', 'tensor')
- down_grad: float32 [2, 2, 6144, 1536], P('section', None, 'tensor', 'context')
- bias_grad: float32 [2, 2, 21504], P('section', None, ('context', 'tensor'))
The draws below stay inside these ranges and needn't reach their ends.
Inputs may be any that keep to these rules, and one draw needn't show every extreme that they name: `image_seq_ids`: in each micro-batch the ids never fall and take every value; id 0 ends and id 2 begins inside the first and the last 224 rows, so that sequence 1 runs through the rows of every index of context. `text_seq_ids`: likewise with 32 rows; a sequence's text and image tokens carry the same id.
All inputs are finite; a program needn't handle non-finite values.
Results may differ from the reference program's by a relative error of at most 0.03.
Values may be sent and summed in bfloat16 or wider, within the bound.
No kernel may reach another device: no remote copies, remote signals or barrier semaphores. Data moves between devices by JAX's collectives and lax.ppermute only.
A program may use at most 320 MiB of HBM per device.

```python
import jax
import jax.numpy as jnp
from jax import lax

D = 1536
HEADS = 24
HEAD = 64
FF = 6144
IMG_DEV = 224
TXT_DEV = 32
MICRO = 2
SEQS = 3
SECTIONS = 2
IMG = 896
TXT = 128
NB = 21504


def segment_ids(key, rows_all, rows_device):
    first_cut = jax.random.randint(jax.random.fold_in(key, 1), (MICRO, 1), 1, rows_device)
    last_cut = jax.random.randint(jax.random.fold_in(key, 2), (MICRO, 1), rows_all - rows_device + 1, rows_all)
    position = jnp.arange(rows_all, dtype=jnp.int32)[None, :]
    return (position >= first_cut).astype(jnp.int32) + (position >= last_cut).astype(jnp.int32)


def draw_image_seq_ids(key, part):
    key = jax.random.fold_in(key, 11)
    return segment_ids(key, IMG, IMG_DEV)


def draw_text_seq_ids(key, part):
    key = jax.random.fold_in(key, 12)
    return segment_ids(key, TXT, TXT_DEV)


def block_levels(own_key, dims, split, low, largest):
    def one(axis_at, shards_of):
        heights = jax.random.uniform(jax.random.fold_in(jax.random.fold_in(own_key, 6), axis_at), (shards_of,), jnp.float32, low / len(split), largest / len(split))
        return jnp.repeat(jnp.exp(heights), dims[axis_at] // shards_of).reshape((-1,) + (1,) * (len(dims) - axis_at - 1))

    loudness = one(*split[0])
    for cut in split[1:]:
        loudness = loudness * one(*cut)
    return loudness


def scatter_about(own_key, extent, spread, limit, cuts=(), kind=jnp.bfloat16):
    loudness = block_levels(own_key, extent, cuts, -0.22, 0.18) if cuts else 1.0
    entries = jax.random.normal(own_key, extent, jnp.float32) * spread * loudness
    return jnp.minimum(jnp.maximum(entries, -limit), limit).astype(kind)


def setup_inputs(seed: int = 0) -> dict:
    key_of = jax.random.split(jax.random.key(seed), 14)
    return {
        "image_tokens": scatter_about(key_of[0], (MICRO, IMG, D), 1.0, 6.0, ((1, 16),)),
        "text_tokens": scatter_about(key_of[1], (MICRO, TXT, D), 1.0, 6.0, ((1, 16),)),
        "conditioning": scatter_about(key_of[2], (MICRO, SEQS, D), 1.0, 6.0, ((2, 16),)),
        "image_seq_ids": draw_image_seq_ids(jax.random.fold_in(key_of[13], 71), 0),
        "text_seq_ids": draw_text_seq_ids(jax.random.fold_in(key_of[13], 71), 0),
        "ada_weight": scatter_about(key_of[5], (SECTIONS, 2, D, 6 * D), D ** -0.5, 0.15625, ((0, 2), (2, 16))),
        "qkv_weight": scatter_about(key_of[6], (SECTIONS, 2, D, 3 * D), D ** -0.5, 0.15625, ((0, 2), (2, 4), (3, 4))),
        "out_weight": scatter_about(key_of[7], (SECTIONS, 2, D, D), (D // 16) ** -0.5, 0.625, ((0, 2), (2, 4), (3, 4))),
        "up_weight": scatter_about(key_of[8], (SECTIONS, 2, D, FF), D ** -0.5, 0.15625, ((0, 2), (2, 4), (3, 4))),
        "down_weight": scatter_about(key_of[9], (SECTIONS, 2, FF, D), FF ** -0.5, 0.078125, ((0, 2), (2, 4), (3, 4))),
        "biases": scatter_about(key_of[10], (SECTIONS, 2, NB), 0.3, 2.0, ((0, 2), (2, 16))),
        "image_cotangent": scatter_about(key_of[11], (MICRO, IMG, D), 1.0, 6.0, ((1, 16),)),
        "text_cotangent": scatter_about(key_of[12], (MICRO, TXT, D), 1.0, 6.0, ((1, 16),)),
    }


@jax.custom_vjp
def low(v):
    return lax.optimization_barrier(v.astype(jnp.bfloat16)).astype(jnp.float32)

@jax.custom_vjp
def low_back(v):
    return v

def low_keep(v):
    return (low(v), None)

def low_pass(kept, grad):
    return (grad,)

def back_keep(v):
    return (v, None)

def back_low(kept, grad):
    return (low(grad),)
low.defvjp(low_keep, low_pass)
low_back.defvjp(back_keep, back_low)
NORM_EPS = 1e-06
HIGHEST = lax.Precision.HIGHEST
MASKED = -1e+30

def layer_norm(values):
    centre = lax.optimization_barrier(jnp.mean(values, axis=-1, keepdims=True))
    centred = values - centre
    variance = lax.optimization_barrier(jnp.mean(centred * centred, axis=-1, keepdims=True))
    return centred * lax.rsqrt(variance + NORM_EPS)

def modulated(values, shift_rows, scale_rows):
    return layer_norm(values) * (1.0 + scale_rows) + shift_rows

def attention(queries, key_rows, value_rows, seq_ids):
    row_total = queries.shape[0]
    block_rows = min(512, row_total)
    block_count = row_total // block_rows
    score_scale = HEAD ** (-0.5)

    def one_block(block_args):
        query_block, id_block = block_args
        scores = low_back(jnp.einsum('qhd,khd->hqk', query_block, key_rows, precision=HIGHEST) * score_scale)
        same_seq = (id_block[:, None] == seq_ids[None, :])[None]
        masked = jnp.where(same_seq, scores, MASKED)
        row_max = lax.optimization_barrier(jnp.max(masked, axis=2, keepdims=True))
        weights = jnp.where(same_seq, jnp.exp(masked - row_max), 0.0)
        probabilities = weights / lax.optimization_barrier(jnp.sum(weights, axis=2, keepdims=True))
        return jnp.einsum('hqk,khd->qhd', low(probabilities), value_rows, precision=HIGHEST)
    attended = lax.map(jax.checkpoint(one_block), (queries.reshape(block_count, block_rows, HEADS, HEAD), seq_ids.reshape(block_count, block_rows)))
    return attended.reshape(row_total, HEADS * HEAD)

def joint_block(entry_pair, mod_tables, id_pair, qkv_w, out_w, up_w, down_w, bias_rows):
    mod_list, query_list, key_list, value_list = ([], [], [], [])
    for modality in range(2):
        mod_rows = mod_tables[modality][id_pair[modality]]
        mod_list.append(mod_rows)
        first_in = low(modulated(entry_pair[modality], mod_rows[:, :D], mod_rows[:, D:2 * D]))
        mixture = jnp.dot(first_in, qkv_w[modality], precision=HIGHEST).reshape(-1, HEADS, 3, HEAD)
        query_list.append(mixture[:, :, 0] + bias_rows[modality, 6 * D:7 * D].reshape(HEADS, HEAD))
        key_list.append(mixture[:, :, 1])
        value_list.append(mixture[:, :, 2] + bias_rows[modality, 7 * D:8 * D].reshape(HEADS, HEAD))
    queries = low(low_back(jnp.concatenate(query_list, 0)))
    key_rows = low(low_back(jnp.concatenate(key_list, 0)))
    value_rows = low(low_back(jnp.concatenate(value_list, 0)))
    attended = low(low_back(attention(queries, key_rows, value_rows, jnp.concatenate(id_pair, 0))))
    split_at = entry_pair[0].shape[0]
    attn_halves = (attended[:split_at], attended[split_at:])
    outputs = []
    for modality in range(2):
        mod_rows = mod_list[modality]
        branch = low_back(jnp.dot(attn_halves[modality], out_w[modality], precision=HIGHEST) + bias_rows[modality, 8 * D:9 * D])
        middle = entry_pair[modality] + mod_rows[:, 2 * D:3 * D] * branch
        second = low(modulated(middle, mod_rows[:, 3 * D:4 * D], mod_rows[:, 4 * D:5 * D]))
        up_proj = low_back(jnp.dot(second, up_w[modality], precision=HIGHEST) + bias_rows[modality, 9 * D:9 * D + FF])
        activated = low(jax.nn.gelu(up_proj, approximate=True))
        down_proj = low_back(jnp.dot(activated, down_w[modality], precision=HIGHEST) + bias_rows[modality, 9 * D + FF:])
        outputs.append(middle + mod_rows[:, 5 * D:] * down_proj)
    return tuple(outputs)

def reference(image_tokens, text_tokens, conditioning, image_seq_ids, text_seq_ids, ada_weight, qkv_weight, out_weight, up_weight, down_weight, biases, image_cotangent, text_cotangent):

    def forward(image_in, text_in, cond_in, ada_w, qkv_w, out_w, up_w, down_w, bias_all, probe_image, probe_text):
        silu_cond = low(jax.nn.silu(cond_in))
        modulation = [jnp.einsum('msd,jdk->mjsk', silu_cond, ada_w[section_number], precision=HIGHEST) + bias_all[section_number][None, :, None, :6 * D] for section_number in range(SECTIONS)]
        image_sections = [[] for section_number in range(SECTIONS)]
        text_sections = [[] for section_number in range(SECTIONS)]
        for micro_number in range(MICRO):
            entry_pair = (image_in[micro_number], text_in[micro_number])
            for section_number in range(SECTIONS):
                mod_tables = (modulation[section_number][micro_number, 0], modulation[section_number][micro_number, 1])
                entry_pair = joint_block(entry_pair, mod_tables, (image_seq_ids[micro_number], text_seq_ids[micro_number]), qkv_w[section_number], out_w[section_number], up_w[section_number], down_w[section_number], bias_all[section_number])
                image_sections[section_number].append(entry_pair[0])
                text_sections[section_number].append(entry_pair[1])
                if section_number + 1 < SECTIONS:
                    entry_pair = (entry_pair[0] + probe_image[micro_number], entry_pair[1] + probe_text[micro_number])
        return (jnp.stack([jnp.stack(rows_list) for rows_list in image_sections]), jnp.stack([jnp.stack(rows_list) for rows_list in text_sections]))
    floats = tuple((array.astype(jnp.float32) for array in (image_tokens, text_tokens, conditioning, ada_weight, qkv_weight, out_weight, up_weight, down_weight, biases)))
    probes = (jnp.zeros((MICRO, IMG, D), jnp.float32), jnp.zeros((MICRO, TXT, D), jnp.float32))
    (image_all, text_all), pullback = jax.vjp(forward, *floats, *probes)
    cotangent_image = jnp.concatenate((jnp.zeros((SECTIONS - 1, MICRO, IMG, D), jnp.float32), image_cotangent.astype(jnp.float32)[None]), 0)
    cotangent_text = jnp.concatenate((jnp.zeros((SECTIONS - 1, MICRO, TXT, D), jnp.float32), text_cotangent.astype(jnp.float32)[None]), 0)
    gradients = pullback((cotangent_image, cotangent_text))
    image_grad = jnp.stack((gradients[0], gradients[9]))
    text_grad = jnp.stack((gradients[1], gradients[10]))
    return (image_all, text_all, image_grad, text_grad, gradients[2], gradients[3], gradients[4], gradients[5], gradients[6], gradients[7], gradients[8])
```

```python
from functools import partial

import jax
import jax.numpy as jnp
from jax import lax
from jax.experimental import pallas as pl
from jax.experimental.pallas import tpu as pltpu
from jax.sharding import PartitionSpec as P

HEADS = 24
HEAD = 64
NORM_EPS = 1e-06
MASKED = -1e30
BF = jnp.bfloat16
F32 = jnp.float32
BOTH = ("context", "tensor")


def dot_nn(a, b):
    return lax.dot_general(a, b, (((1,), (0,)), ((), ())), preferred_element_type=F32)


def dot_nt(a, b):
    return lax.dot_general(a, b, (((1,), (1,)), ((), ())), preferred_element_type=F32)


def dot_tn(a, b):
    return lax.dot_general(a, b, (((0,), (0,)), ((), ())), preferred_element_type=F32)


def attend_kernel(heads, chunk, q_ref, k_ref, v_ref, idq_ref, idk_ref, out_ref, lse_ref):
    queries = q_ref.shape[0]

    def one_chunk(step, carry):
        start = pl.multiple_of(step * chunk, chunk)
        rows = pl.ds(start, chunk)
        bias = jnp.where(idk_ref[...] == idq_ref[:, rows], 0.0, MASKED)
        outs = []
        for head in range(heads):
            cols = slice(head * HEAD, (head + 1) * HEAD)
            q = q_ref[rows, cols] * jnp.asarray(HEAD**-0.5, BF)
            scores = dot_nt(k_ref[:, cols], q) + bias
            top = jnp.max(scores, axis=0, keepdims=True)
            weights = jnp.exp(scores - top)
            total = jnp.sum(weights, axis=0, keepdims=True)
            summed = dot_tn(v_ref[:, cols], weights.astype(BF))
            outs.append((summed / total).T)
            lse_ref[head : head + 1, rows] = top + jnp.log(total)
        out_ref[rows, :] = jnp.concatenate(outs, axis=1).astype(out_ref.dtype)
        return carry

    lax.fori_loop(0, queries // chunk, one_chunk, 0)


def attend(q, k, v, ids_q, ids_k, heads):
    queries, keys = q.shape[0], k.shape[0]
    chunk = 256 if keys <= 1024 else 128
    return pl.pallas_call(
        partial(attend_kernel, heads, chunk),
        out_shape=(
            jax.ShapeDtypeStruct((queries, heads * HEAD), BF),
            jax.ShapeDtypeStruct((heads, queries), F32),
        ),
        compiler_params=pltpu.CompilerParams(vmem_limit_bytes=48 * 2**20),
        cost_estimate=pl.CostEstimate(
            flops=4 * queries * keys * heads * HEAD,
            bytes_accessed=2 * (queries + 2 * keys) * heads * HEAD,
            transcendentals=queries * keys * heads,
        ),
    )(q, k, v, ids_q.reshape(1, queries), ids_k.reshape(keys, 1))


def attend_back_kernel(
    heads, chunk, q_ref, k_ref, v_ref, g_ref, lse_ref, idq_ref, idk_ref, dq_ref, dk_ref, dv_ref, dk_acc, dv_acc
):
    queries = q_ref.shape[0]
    dk_acc[...] = jnp.zeros_like(dk_acc)
    dv_acc[...] = jnp.zeros_like(dv_acc)

    def one_chunk(step, carry):
        start = pl.multiple_of(step * chunk, chunk)
        rows = pl.ds(start, chunk)
        bias = jnp.where(idk_ref[...] == idq_ref[:, rows], 0.0, MASKED)
        grads = []
        for head in range(heads):
            cols = slice(head * HEAD, (head + 1) * HEAD)
            q = q_ref[rows, cols] * jnp.asarray(HEAD**-0.5, BF)
            g = g_ref[rows, cols]
            k = k_ref[:, cols]
            scores = dot_nt(k, q) + bias
            probs = jnp.exp(scores - lse_ref[head : head + 1, rows])
            dv_acc[head] += dot_nn(probs.astype(BF), g)
            dprobs = dot_nt(v_ref[:, cols], g)
            both = probs * dprobs
            delta = jnp.sum(both, axis=0, keepdims=True)
            dscores = (both - probs * delta).astype(BF)
            dk_acc[head] += dot_nn(dscores, q)
            grads.append((dot_tn(k, dscores) * HEAD**-0.5).T)
        dq_ref[rows, :] = jnp.concatenate(grads, axis=1).astype(dq_ref.dtype)
        return carry

    lax.fori_loop(0, queries // chunk, one_chunk, 0)
    dk_ref[...] = jnp.concatenate([dk_acc[head] for head in range(heads)], axis=1).astype(dk_ref.dtype)
    dv_ref[...] = jnp.concatenate([dv_acc[head] for head in range(heads)], axis=1).astype(dv_ref.dtype)


def attend_back(q, k, v, g, lse, ids_q, ids_k, heads):
    queries, keys = q.shape[0], k.shape[0]
    chunk = 256 if keys <= 1024 else 128
    return pl.pallas_call(
        partial(attend_back_kernel, heads, chunk),
        out_shape=(
            jax.ShapeDtypeStruct((queries, heads * HEAD), BF),
            jax.ShapeDtypeStruct((keys, heads * HEAD), BF),
            jax.ShapeDtypeStruct((keys, heads * HEAD), BF),
        ),
        scratch_shapes=[
            pltpu.VMEM((heads, keys, HEAD), F32),
            pltpu.VMEM((heads, keys, HEAD), F32),
        ],
        compiler_params=pltpu.CompilerParams(vmem_limit_bytes=56 * 2**20),
        cost_estimate=pl.CostEstimate(
            flops=10 * queries * keys * heads * HEAD,
            bytes_accessed=4 * (queries + 2 * keys) * heads * HEAD,
            transcendentals=queries * keys * heads,
        ),
    )(q, k, v, g, lse, ids_q.reshape(1, queries), ids_k.reshape(keys, 1))


def normalized(x):
    centred = x - jnp.mean(x, axis=-1, keepdims=True)
    inverse = lax.rsqrt(jnp.mean(centred * centred, axis=-1, keepdims=True) + NORM_EPS)
    return centred * inverse, inverse


def norm_back(n, inverse, w):
    return (w - jnp.mean(w, axis=-1, keepdims=True) - n * jnp.mean(w * n, axis=-1, keepdims=True)) * inverse


def gelu_pair(u):
    c = 0.7978845608028654
    inner = jnp.tanh(c * (u + 0.044715 * u * u * u))
    value = 0.5 * u * (1.0 + inner)
    slope = 0.5 * (1.0 + inner) + 0.5 * u * (1.0 - inner * inner) * c * (1.0 + 3 * 0.044715 * u * u)
    return value.astype(BF), slope.astype(BF)


def shards(
    image_tokens,
    text_tokens,
    conditioning,
    image_seq_ids,
    text_seq_ids,
    ada_weight,
    qkv_weight,
    out_weight,
    up_weight,
    down_weight,
    biases,
    image_cotangent,
    text_cotangent,
):
    section = lax.axis_index("section")
    context = lax.axis_index("context")
    tensor = lax.axis_index("tensor")
    ncontext = lax.axis_size("context")
    ntensor = lax.axis_size("tensor")
    ndev = ncontext * ntensor
    device = context * ntensor + tensor
    first = section == 0
    micros, own_image, width = image_tokens.shape
    own_text = text_tokens.shape[1]
    seqs = conditioning.shape[1]
    rows_image, rows_text = micros * own_image, micros * own_text
    own_rows = rows_image + rows_text
    heads_here = HEADS // ntensor
    local = heads_here * HEAD
    hidden = up_weight.shape[3]
    bias_here = biases.shape[2]
    depth = qkv_weight.shape[2]
    mods = 6 * width
    groups_rows = 2 * micros * seqs
    by_heads = (micros * heads_here) % ncontext == 0 and ncontext % micros == 0
    groups = ncontext // micros if by_heads else 1
    group_heads = heads_here // groups
    group = group_heads * HEAD
    ctx_image, ctx_text = ntensor * own_image, ntensor * own_text
    ctx_rows = ctx_image + ctx_text

    qkv_cols = (
        qkv_weight[0]
        .reshape(2, depth, groups, group_heads, 3, HEAD)
        .transpose(0, 2, 1, 4, 3, 5)
        .reshape(2, groups, depth, 3 * group)
    )
    qkv_full = lax.all_gather(qkv_cols, "context", axis=2, tiled=True)
    out_full = lax.all_gather(out_weight[0], "context", axis=2, tiled=True)
    up_full = lax.all_gather(up_weight[0], "context", axis=1, tiled=True)
    down_full = lax.all_gather(down_weight[0], "context", axis=2, tiled=True)

    cond_float = conditioning.astype(F32)
    silu_cond = jax.nn.silu(cond_float).astype(BF).reshape(micros * seqs, -1)
    ada_part = jnp.einsum("rc,jck->jrk", silu_cond, ada_weight[0], preferred_element_type=F32)
    mod_piece = mods // ndev
    ada_sent = ada_part.reshape(groups_rows, ndev, mod_piece).transpose(1, 0, 2).astype(BF)
    ada_got = lax.all_to_all(ada_sent, BOTH, 0, 0)
    ada_sum = jnp.sum(ada_got.astype(F32), axis=0)
    ada_all = lax.all_gather(ada_sum, BOTH).transpose(1, 0, 2).reshape(2, micros * seqs, mods)
    bias_full = lax.all_gather(biases[0], BOTH).transpose(1, 0, 2).reshape(2, -1).astype(F32)
    table = (ada_all + bias_full[:, None, :mods]).astype(BF).reshape(groups_rows, mods)
    query_bias = lax.dynamic_slice_in_dim(bias_full, mods + tensor * local, local, 1)
    value_bias = lax.dynamic_slice_in_dim(bias_full, mods + width + tensor * local, local, 1)
    qkv_bias = jnp.concatenate(
        (
            query_bias.reshape(2, groups, group),
            jnp.zeros((2, groups, group), F32),
            value_bias.reshape(2, groups, group),
        ),
        axis=2,
    )
    out_bias = bias_full[:, mods + 2 * width : mods + 3 * width]
    up_bias = lax.dynamic_slice_in_dim(bias_full, mods + 3 * width + tensor * hidden, hidden, 1)
    down_bias = bias_full[:, mods + 3 * width + hidden * ntensor :]

    def by_modality(pair):
        return jnp.concatenate(
            (
                jnp.broadcast_to(pair[0][None], (rows_image, width)),
                jnp.broadcast_to(pair[1][None], (rows_text, width)),
            ),
            0,
        )

    own_ids_image = lax.dynamic_slice_in_dim(image_seq_ids, device * own_image, own_image, 1)
    own_ids_text = lax.dynamic_slice_in_dim(text_seq_ids, device * own_text, own_text, 1)
    offsets = jnp.arange(micros, dtype=jnp.int32)[:, None] * seqs
    group_ids = jnp.concatenate(
        ((own_ids_image + offsets).reshape(-1), (own_ids_text + offsets + micros * seqs).reshape(-1))
    )
    onehot = (group_ids[:, None] == jnp.arange(groups_rows)[None, :]).astype(BF)
    row_mods = dot_nn(onehot, table).astype(BF)

    def row_mod(index):
        return row_mods[:, index * width : (index + 1) * width].astype(F32)

    joint_ids = jnp.concatenate(
        (
            image_seq_ids.reshape(micros, ncontext, ctx_image),
            text_seq_ids.reshape(micros, ncontext, ctx_text),
        ),
        axis=2,
    )
    if by_heads:
        attn_ids = lax.dynamic_index_in_dim(joint_ids, context // groups, 0, keepdims=False).reshape(-1)
    else:
        all_ids = joint_ids.reshape(micros, -1)
        local_ids = lax.dynamic_index_in_dim(joint_ids, context, 1, keepdims=False)

    def spread(rows):
        got = lax.all_gather(rows, "tensor")
        return (
            got[:, :rows_image].reshape(ntensor * rows_image, width),
            got[:, rows_image:].reshape(ntensor * rows_text, width),
        )

    def collect(image_rows, text_rows):
        sent = jnp.concatenate(
            (
                image_rows.astype(BF).reshape(ntensor, rows_image, width),
                text_rows.astype(BF).reshape(ntensor, rows_text, width),
            ),
            axis=1,
        )
        return jnp.sum(lax.all_to_all(sent, "tensor", 0, 0).astype(F32), axis=0)

    def to_joint(image_rows, text_rows):
        cols = image_rows.shape[-1]
        return jnp.concatenate(
            (
                image_rows.reshape(ntensor, micros, own_image, cols)
                .transpose(1, 0, 2, 3)
                .reshape(micros, ctx_image, cols),
                text_rows.reshape(ntensor, micros, own_text, cols)
                .transpose(1, 0, 2, 3)
                .reshape(micros, ctx_text, cols),
            ),
            axis=1,
        )

    def from_joint(rows):
        cols = rows.shape[-1]
        image_rows = (
            rows[:, :ctx_image]
            .reshape(micros, ntensor, own_image, cols)
            .transpose(1, 0, 2, 3)
            .reshape(ntensor * rows_image, cols)
        )
        text_rows = (
            rows[:, ctx_image:]
            .reshape(micros, ntensor, own_text, cols)
            .transpose(1, 0, 2, 3)
            .reshape(ntensor * rows_text, cols)
        )
        return image_rows, text_rows

    def to_heads(parts):
        sent = jnp.stack(parts, axis=1).reshape(ncontext, ctx_rows, -1)
        return lax.all_to_all(sent, "context", 0, 0).reshape(ncontext * ctx_rows, -1)

    def from_heads(rows):
        got = lax.all_to_all(rows.reshape(ncontext, ctx_rows, -1), "context", 0, 0)
        got = got.reshape(micros, groups, ctx_rows, -1)
        return [from_joint(got[:, index]) for index in range(groups)]

    def attention(joint):
        if by_heads:
            rows = to_heads(joint)
            q, k, v = rows[:, :group], rows[:, group : 2 * group], rows[:, 2 * group :]
            attended, lse = attend(q, k, v, attn_ids, attn_ids, group_heads)
            return from_heads(attended), (q, k, v, lse)
        q, k, v = (joint[0][:, :, i * group : (i + 1) * group] for i in range(3))
        k_all = lax.all_gather(k, "context", axis=1, tiled=True)
        v_all = lax.all_gather(v, "context", axis=1, tiled=True)
        results = [
            attend(q[m], k_all[m], v_all[m], local_ids[m], all_ids[m], group_heads) for m in range(micros)
        ]
        attended = jnp.stack([r[0] for r in results])
        return [from_joint(attended)], (q, k_all, v_all, [r[1] for r in results])

    def attention_back(grad_joint, kept):
        q, k, v, lse = kept
        if by_heads:
            grads = attend_back(q, k, v, to_heads(grad_joint), lse, attn_ids, attn_ids, group_heads)
            return from_heads(jnp.concatenate(grads, axis=1))
        results = [
            attend_back(q[m], k[m], v[m], grad_joint[0][m], lse[m], local_ids[m], all_ids[m], group_heads)
            for m in range(micros)
        ]
        dq = jnp.stack([r[0] for r in results])
        dk, dv = (
            lax.psum_scatter(
                jnp.stack([r[i] for r in results]), "context", scatter_dimension=1, tiled=True
            )
            for i in (1, 2)
        )
        return [from_joint(jnp.concatenate((dq, dk, dv), axis=2))]

    def forward(x):
        n1, inv1 = normalized(x)
        h1 = (n1 * (1.0 + row_mod(1)) + row_mod(0)).astype(BF)
        h1_all = spread(h1)
        joint = []
        for g in range(groups):
            pair = [
                (dot_nn(h1_all[j], qkv_full[j, g]) + qkv_bias[j, g]).astype(BF) for j in range(2)
            ]
            joint.append(to_joint(*pair))
        attended, kept = attention(joint)
        attn = [jnp.concatenate([attended[g][j] for g in range(groups)], axis=1) for j in range(2)]
        branch = collect(*(dot_nn(attn[j], out_full[j]) for j in range(2))) + by_modality(out_bias)
        middle = x + row_mod(2) * branch
        n2, inv2 = normalized(middle)
        h2 = (n2 * (1.0 + row_mod(4)) + row_mod(3)).astype(BF)
        h2_all = spread(h2)
        pairs = [gelu_pair(dot_nn(h2_all[j], up_full[j]) + up_bias[j]) for j in range(2)]
        acts = [p[0] for p in pairs]
        slopes = [p[1] for p in pairs]
        down = collect(*(dot_nn(acts[j], down_full[j]) for j in range(2))) + by_modality(down_bias)
        out = middle + row_mod(5) * down
        saved = dict(
            x=x, h1=h1_all, kept=kept, attn=attn, branch=branch, middle=middle, h2=h2_all,
            acts=acts, slopes=slopes, down=down,
        )
        return out, saved

    def backward(saved, g_out):
        g_down = (row_mod(5) * g_out).astype(BF)
        gd_all = spread(g_down)
        g_up = [
            (dot_nt(gd_all[j], down_full[j]) * saved["slopes"][j].astype(F32)).astype(BF) for j in range(2)
        ]
        g_h2 = collect(*(dot_nt(g_up[j], up_full[j]) for j in range(2)))
        n2, inv2 = normalized(saved["middle"])
        g_middle = g_out + norm_back(n2, inv2, g_h2 * (1.0 + row_mod(4)))
        g_branch = (row_mod(2) * g_middle).astype(BF)
        gb_all = spread(g_branch)
        g_attn = [dot_nt(gb_all[j], out_full[j]).astype(BF) for j in range(2)]
        grad_joint = [
            to_joint(*(g_attn[j][:, g * group : (g + 1) * group] for j in range(2))) for g in range(groups)
        ]
        g_qkv = attention_back(grad_joint, saved["kept"])
        g_h1 = collect(
            *(sum(dot_nt(g_qkv[g][j], qkv_full[j, g]) for g in range(groups)) for j in range(2))
        )
        n1, inv1 = normalized(saved["x"])
        g_x = g_middle + norm_back(n1, inv1, g_h1 * (1.0 + row_mod(1)))
        row_grads = jnp.concatenate(
            [
                part.astype(BF)
                for part in (
                    g_h1, g_h1 * n1, g_middle * saved["branch"], g_h2, g_h2 * n2, g_out * saved["down"]
                )
            ],
            axis=1,
        )
        mod_grad = dot_tn(onehot, row_grads)
        tensors = dict(
            h1=saved["h1"], g_qkv=g_qkv, attn=saved["attn"], gb=gb_all, h2=saved["h2"], g_up=g_up,
            acts=saved["acts"], gd=gd_all, g_down=g_down, g_branch=g_branch, mod=mod_grad,
        )
        return g_x, tensors

    def rows_of(image, text):
        return jnp.concatenate(
            (image.reshape(rows_image, width), text.reshape(rows_text, width)), 0
        ).astype(F32)

    def handed(rows, by):
        return lax.ppermute(rows.astype(BF), "section", [(0, 1)] if by > 0 else [(1, 0)]).astype(F32)

    out_first, saved_first = forward(rows_of(image_tokens, text_tokens))
    out_last, saved_last = forward(handed(out_first, 1))
    grad_last, tensors_last = backward(saved_last, rows_of(image_cotangent, text_cotangent))
    grad_first, tensors_first = backward(saved_first, handed(grad_last, -1))
    out = jnp.where(first, out_first, out_last)
    grad = jnp.where(first, grad_first, grad_last)
    use = jax.tree.map(lambda a, b: jnp.where(first, a, b), tensors_first, tensors_last)

    def scattered(parts, dim):
        return lax.psum_scatter(
            jnp.stack(parts).astype(BF), "context", scatter_dimension=dim, tiled=True
        ).astype(F32)

    down_grad = scattered([dot_tn(use["acts"][j], use["gd"][j]) for j in range(2)], 2)
    up_grad = scattered([dot_tn(use["h2"][j], use["g_up"][j]) for j in range(2)], 1)
    out_grad = scattered([dot_tn(use["attn"][j], use["gb"][j]) for j in range(2)], 2)
    qkv_grad = scattered(
        [jnp.stack([dot_tn(use["h1"][j], use["g_qkv"][g][j]) for g in range(groups)]) for j in range(2)], 2
    )
    qkv_grad = (
        qkv_grad.reshape(2, groups, depth, 3, group_heads, HEAD)
        .transpose(0, 2, 1, 4, 3, 5)
        .reshape(2, depth, 3 * local)
    )

    def column_sums(parts):
        return jnp.stack([jnp.sum(p.astype(F32), axis=0) for p in parts])

    def own_sums(rows):
        return column_sums((rows[:rows_image], rows[rows_image:]))

    qkv_sums = jnp.stack([column_sums(use["g_qkv"][g]) for g in range(groups)], axis=1)
    qkv_sums = qkv_sums.reshape(2, groups, 3, group)
    bias_part = jnp.zeros((2, bias_here * ndev), F32)
    for at, value in (
        (0, jnp.sum(use["mod"].reshape(2, micros * seqs, mods), axis=1)),
        (mods + tensor * local, qkv_sums[:, :, 0].reshape(2, local)),
        (mods + width + tensor * local, qkv_sums[:, :, 2].reshape(2, local)),
        (mods + 2 * width, own_sums(use["g_branch"])),
        (mods + 3 * width + tensor * hidden, column_sums(use["g_up"])),
        (mods + 3 * width + ntensor * hidden, own_sums(use["g_down"])),
    ):
        bias_part = lax.dynamic_update_slice_in_dim(bias_part, value, at, 1)
    sent = jnp.concatenate(
        (
            use["mod"].reshape(groups_rows, ndev, mod_piece).transpose(1, 0, 2).reshape(ndev, -1),
            bias_part.reshape(2, ndev, bias_here).transpose(1, 0, 2).reshape(ndev, -1),
        ),
        axis=1,
    ).astype(BF)
    summed = jnp.sum(lax.all_to_all(sent, BOTH, 0, 0).astype(F32), axis=0)
    bias_grad = summed[groups_rows * mod_piece :].reshape(2, bias_here)
    mod_all = lax.all_gather(summed[: groups_rows * mod_piece].astype(BF), BOTH)
    mod_all = mod_all.reshape(ndev, groups_rows, mod_piece).transpose(1, 0, 2).reshape(2, micros * seqs, mods)
    ada_grad = jnp.einsum("rc,jrk->jck", silu_cond, mod_all, preferred_element_type=F32)
    cond_inner = jnp.einsum("jrk,jck->rc", mod_all, ada_weight[0], preferred_element_type=F32)
    unused, silu_back = jax.vjp(jax.nn.silu, cond_float)
    cond_grad = silu_back(lax.psum(cond_inner, "section").reshape(cond_float.shape))[0]

    def halves(rows):
        return (
            rows[:rows_image].reshape(1, micros, own_image, width),
            rows[rows_image:].reshape(1, micros, own_text, width),
        )

    return (
        *halves(out),
        *halves(grad),
        cond_grad,
        ada_grad[None],
        qkv_grad[None],
        out_grad[None],
        up_grad[None],
        down_grad[None],
        bias_grad[None],
    )


def solution(mesh):
    tokens = P(None, BOTH, None)
    block_rows = P("section", None, BOTH, None)
    by_rows = P("section", None, "context", "tensor")
    by_cols = P("section", None, "tensor", "context")
    block_biases = P("section", None, BOTH)
    in_specs = (
        tokens,
        tokens,
        P(None, None, BOTH),
        P(),
        P(),
        block_rows,
        by_rows,
        by_cols,
        by_rows,
        by_cols,
        block_biases,
        tokens,
        tokens,
    )
    out_specs = (
        block_rows,
        block_rows,
        block_rows,
        block_rows,
        P(None, None, BOTH),
        block_rows,
        by_rows,
        by_cols,
        by_rows,
        by_cols,
        block_biases,
    )
    return jax.shard_map(shards, mesh=mesh, in_specs=in_specs, out_specs=out_specs, check_vma=False)
```

```python
from functools import partial

import jax
import jax.numpy as jnp
from jax import lax
from jax.experimental import pallas as pl
from jax.experimental.pallas import tpu as pltpu
from jax.sharding import PartitionSpec as P

HEADS = 24
HEAD = 64
NORM_EPS = 1e-06
MASKED = -1e30
BF = jnp.bfloat16
F32 = jnp.float32
BOTH = ("context", "tensor")


def dot_nn(a, b):
    return lax.dot_general(a, b, (((1,), (0,)), ((), ())), preferred_element_type=F32)


def dot_nt(a, b):
    return lax.dot_general(a, b, (((1,), (1,)), ((), ())), preferred_element_type=F32)


def dot_tn(a, b):
    return lax.dot_general(a, b, (((0,), (0,)), ((), ())), preferred_element_type=F32)


def scaled(q):
    return q * jnp.asarray(HEAD**-0.5, BF)


def attend_body(heads, chunk, places, q_ref, k_ref, v_ref, idq_ref, idk_ref, store, lse_ref):
    at_q, at_k, at_v = places

    def one_chunk(step, carry):
        rows = pl.ds(pl.multiple_of(step * chunk, chunk), chunk)
        bias = jnp.where(idk_ref[...] == idq_ref[:, rows], 0.0, MASKED)
        outs = []
        for head in range(heads):
            at = head * HEAD
            q = scaled(q_ref[rows, at_q + at : at_q + at + HEAD])
            scores = dot_nt(k_ref[:, at_k + at : at_k + at + HEAD], q) + bias
            top = jnp.max(scores, axis=0, keepdims=True)
            weights = jnp.exp(scores - top)
            total = jnp.sum(weights, axis=0, keepdims=True)
            summed = dot_tn(v_ref[:, at_v + at : at_v + at + HEAD], weights.astype(BF))
            outs.append((summed / total).T)
            lse_ref[head : head + 1, rows] = top + jnp.log(total)
        store(rows, jnp.concatenate(outs, axis=1).astype(BF))
        return carry

    lax.fori_loop(0, idq_ref.shape[1] // chunk, one_chunk, 0)


def attend_back_body(
    heads, chunk, places, q_ref, k_ref, v_ref, g_ref, lse_ref, idq_ref, idk_ref, store_dq, dk_acc, dv_acc
):
    at_q, at_k, at_v = places
    dk_acc[...] = jnp.zeros_like(dk_acc)
    dv_acc[...] = jnp.zeros_like(dv_acc)

    def one_chunk(step, carry):
        rows = pl.ds(pl.multiple_of(step * chunk, chunk), chunk)
        bias = jnp.where(idk_ref[...] == idq_ref[:, rows], 0.0, MASKED)
        grads = []
        for head in range(heads):
            at = head * HEAD
            q = scaled(q_ref[rows, at_q + at : at_q + at + HEAD])
            g = g_ref[rows, at : at + HEAD]
            k = k_ref[:, at_k + at : at_k + at + HEAD]
            probs = jnp.exp(dot_nt(k, q) + bias - lse_ref[head : head + 1, rows])
            dv_acc[head] += dot_nn(probs.astype(BF), g)
            both = probs * dot_nt(v_ref[:, at_v + at : at_v + at + HEAD], g)
            delta = jnp.sum(both, axis=0, keepdims=True)
            dscores = (both - probs * delta).astype(BF)
            dk_acc[head] += dot_nn(dscores, q)
            grads.append((dot_tn(k, dscores) * HEAD**-0.5).T)
        store_dq(rows, jnp.concatenate(grads, axis=1).astype(BF))
        return carry

    lax.fori_loop(0, idq_ref.shape[1] // chunk, one_chunk, 0)


def heads_of(acc):
    return jnp.concatenate([acc[head] for head in range(acc.shape[0])], axis=1).astype(BF)


def attend_costs(queries, keys, heads, factor):
    return pl.CostEstimate(
        flops=factor * queries * keys * heads * HEAD,
        bytes_accessed=2 * (queries + 2 * keys) * heads * HEAD * factor // 4,
        transcendentals=queries * keys * heads,
    )


def chunk_for(keys):
    return 256 if keys <= 1024 else 128


VMEM_LIMIT = pltpu.CompilerParams(vmem_limit_bytes=56 * 2**20)


def attend(q, k, v, ids_q, ids_k, heads):
    queries, keys = q.shape[0], k.shape[0]

    def kernel(q_ref, k_ref, v_ref, idq_ref, idk_ref, out_ref, lse_ref):
        def store(rows, value):
            out_ref[rows, :] = value

        attend_body(
            heads, chunk_for(keys), (0, 0, 0), q_ref, k_ref, v_ref, idq_ref, idk_ref, store, lse_ref
        )

    return pl.pallas_call(
        kernel,
        out_shape=(
            jax.ShapeDtypeStruct((queries, heads * HEAD), BF),
            jax.ShapeDtypeStruct((heads, queries), F32),
        ),
        compiler_params=VMEM_LIMIT,
        cost_estimate=attend_costs(queries, keys, heads, 4),
    )(q, k, v, ids_q.reshape(1, queries), ids_k.reshape(keys, 1))


def attend_back(q, k, v, g, lse, ids_q, ids_k, heads):
    queries, keys = q.shape[0], k.shape[0]

    def kernel(
        q_ref, k_ref, v_ref, g_ref, lse_ref, idq_ref, idk_ref, dq_ref, dk_ref, dv_ref, dk_acc, dv_acc
    ):
        def store(rows, value):
            dq_ref[rows, :] = value

        attend_back_body(
            heads, chunk_for(keys), (0, 0, 0), q_ref, k_ref, v_ref, g_ref, lse_ref, idq_ref, idk_ref,
            store, dk_acc, dv_acc,
        )
        dk_ref[...] = heads_of(dk_acc)
        dv_ref[...] = heads_of(dv_acc)

    return pl.pallas_call(
        kernel,
        out_shape=(
            jax.ShapeDtypeStruct((queries, heads * HEAD), BF),
            jax.ShapeDtypeStruct((keys, heads * HEAD), BF),
            jax.ShapeDtypeStruct((keys, heads * HEAD), BF),
        ),
        scratch_shapes=[pltpu.VMEM((heads, keys, HEAD), F32), pltpu.VMEM((heads, keys, HEAD), F32)],
        compiler_params=VMEM_LIMIT,
        cost_estimate=attend_costs(queries, keys, heads, 10),
    )(q, k, v, g, lse, ids_q.reshape(1, queries), ids_k.reshape(keys, 1))


def attend_pair(mine, theirs, ids, heads):
    half, wide = mine.shape
    rows_all, group = 2 * half, heads * HEAD

    def kernel(mine_ref, theirs_ref, idq_ref, idk_ref, out_ref, lse_ref, x_ref):
        x_ref[:half] = mine_ref[...]
        x_ref[half:] = theirs_ref[...]

        def store(rows, value):
            out_ref[rows, :] = value

        attend_body(
            heads, 256, (0, group, 2 * group), x_ref, x_ref, x_ref, idq_ref, idk_ref, store, lse_ref
        )

    return pl.pallas_call(
        kernel,
        out_shape=(
            jax.ShapeDtypeStruct((rows_all, group), BF),
            jax.ShapeDtypeStruct((heads, rows_all), F32),
        ),
        scratch_shapes=[pltpu.VMEM((rows_all, wide), BF)],
        compiler_params=VMEM_LIMIT,
        cost_estimate=attend_costs(rows_all, rows_all, heads, 4),
    )(mine, theirs, ids.reshape(1, rows_all), ids.reshape(rows_all, 1))


def attend_pair_back(mine, theirs, g_mine, g_theirs, lse, ids, heads):
    half, wide = mine.shape
    rows_all, group = 2 * half, heads * HEAD

    def kernel(
        mine_ref, theirs_ref, gm_ref, gt_ref, lse_ref, idq_ref, idk_ref, dmine_ref, dtheirs_ref,
        x_ref, g_ref, dq_acc, dk_acc, dv_acc,
    ):
        x_ref[:half] = mine_ref[...]
        x_ref[half:] = theirs_ref[...]
        g_ref[:half] = gm_ref[...]
        g_ref[half:] = gt_ref[...]

        def store(rows, value):
            dq_acc[rows, :] = value

        attend_back_body(
            heads, 256, (0, group, 2 * group), x_ref, x_ref, x_ref, g_ref, lse_ref, idq_ref, idk_ref,
            store, dk_acc, dv_acc,
        )
        grads = jnp.concatenate((dq_acc[...], heads_of(dk_acc), heads_of(dv_acc)), axis=1)
        dmine_ref[...] = grads[:half]
        dtheirs_ref[...] = grads[half:]

    return pl.pallas_call(
        kernel,
        out_shape=(jax.ShapeDtypeStruct((half, wide), BF), jax.ShapeDtypeStruct((half, wide), BF)),
        scratch_shapes=[
            pltpu.VMEM((rows_all, wide), BF),
            pltpu.VMEM((rows_all, group), BF),
            pltpu.VMEM((rows_all, group), BF),
            pltpu.VMEM((heads, rows_all, HEAD), F32),
            pltpu.VMEM((heads, rows_all, HEAD), F32),
        ],
        compiler_params=VMEM_LIMIT,
        cost_estimate=attend_costs(rows_all, rows_all, heads, 10),
    )(mine, theirs, g_mine, g_theirs, lse, ids.reshape(1, rows_all), ids.reshape(rows_all, 1))


def normalized(x):
    centred = x - jnp.mean(x, axis=-1, keepdims=True)
    inverse = lax.rsqrt(jnp.mean(centred * centred, axis=-1, keepdims=True) + NORM_EPS)
    return centred * inverse, inverse


def norm_back(n, inverse, w):
    return (w - jnp.mean(w, axis=-1, keepdims=True) - n * jnp.mean(w * n, axis=-1, keepdims=True)) * inverse


def gelu_pair(u):
    c = 0.7978845608028654
    inner = jnp.tanh(c * (u + 0.044715 * u * u * u))
    value = 0.5 * u * (1.0 + inner)
    slope = 0.5 * (1.0 + inner) + 0.5 * u * (1.0 - inner * inner) * c * (1.0 + 3 * 0.044715 * u * u)
    return value.astype(BF), slope.astype(BF)


def shards(
    image_tokens,
    text_tokens,
    conditioning,
    image_seq_ids,
    text_seq_ids,
    ada_weight,
    qkv_weight,
    out_weight,
    up_weight,
    down_weight,
    biases,
    image_cotangent,
    text_cotangent,
):
    section = lax.axis_index("section")
    context = lax.axis_index("context")
    tensor = lax.axis_index("tensor")
    ncontext = lax.axis_size("context")
    ntensor = lax.axis_size("tensor")
    ndev = ncontext * ntensor
    first = section == 0
    micros, own_image, width = image_tokens.shape
    own_text = text_tokens.shape[1]
    seqs = conditioning.shape[1]
    rows_image, rows_text = micros * own_image, micros * own_text
    heads_here = HEADS // ntensor
    local = heads_here * HEAD
    hidden = up_weight.shape[3]
    bias_here = biases.shape[2]
    depth = qkv_weight.shape[2]
    mods = 6 * width
    table_rows = 2 * seqs
    per = ncontext // micros
    micro = context // per
    paired = per == 2 and heads_here % 2 == 0
    groups = 2 if paired else 1
    group_heads = heads_here // groups
    group = group_heads * HEAD
    side = context % per
    ctx_image, ctx_text = ntensor * rows_image, ntensor * rows_text
    ctx_rows = ctx_image + ctx_text
    text_all = ncontext * ctx_text

    order = (0, 2, 1, 3)

    def swapped(x, axis, bit):
        return lax.ppermute(x, axis, [(i, i ^ bit) for i in range(lax.axis_size(axis))])

    def near(x):
        return swapped(x, "tensor", 1)

    def far(x):
        return swapped(x, "tensor", 2)

    def gather_tensor(x):
        beside = near(x)
        across = far(x)
        return x, across, beside, near(across)

    def reduce_tensor(x):
        n = x.shape[0] // 4
        got = near(x[2 * n :])
        mine = x[: 2 * n].astype(F32) + got.astype(F32)
        return mine[:n] + far(mine[n:].astype(BF)).astype(F32)

    def spread(rows):
        parts = gather_tensor(rows)
        return [
            jnp.concatenate([p[:rows_image] for p in parts], 0),
            jnp.concatenate([p[rows_image:] for p in parts], 0),
        ]

    def collect(image_rows, text_rows):
        return jnp.concatenate(
            (reduce_tensor(image_rows.astype(BF)), reduce_tensor(text_rows.astype(BF))), 0
        )

    def text_columns(rows):
        sent = rows.reshape(rows_text, ncontext, depth).transpose(1, 0, 2)
        got = lax.all_to_all(sent, "context", 0, 0).reshape(ncontext * rows_text, depth)
        parts = jnp.stack([p.reshape(ncontext, rows_text, depth) for p in gather_tensor(got)], axis=1)
        return parts.reshape(text_all, depth)

    def text_rows_of(partial_sums):
        turned = (
            partial_sums.astype(BF)
            .reshape(ncontext, ntensor, rows_text, depth)
            .transpose(1, 0, 2, 3)
            .reshape(ntensor * ncontext * rows_text, depth)
        )
        mine = reduce_tensor(turned).astype(BF).reshape(ncontext, rows_text, depth)
        got = lax.all_to_all(mine, "context", 0, 0)
        return got.transpose(1, 0, 2).reshape(rows_text, width).astype(F32)

    def context_sum(partial_sums):
        sent = partial_sums.astype(BF).reshape(ncontext, ctx_text, -1)
        return jnp.sum(lax.all_to_all(sent, "context", 0, 0).astype(F32), axis=0)

    def context_gather(rows):
        return lax.all_gather(rows, "context", axis=0, tiled=True)

    def gather_both(x):
        got = lax.all_gather(lax.all_gather(x, "tensor"), "context")
        return got.reshape((ndev,) + x.shape)

    def rounds(step, back):
        pairs = []
        for h in range(ncontext):
            m = (h + step) % micros
            pairs.append((h, m * per + h // micros))
        return [(b, a) for a, b in pairs] if back else pairs

    def to_work(image, text):
        pieces = []
        for step in range(micros):
            m = (context + step) % micros
            pieces.append(
                [
                    lax.ppermute(
                        lax.dynamic_index_in_dim(x, m, 0, keepdims=False), "context", rounds(step, False)
                    )
                    for x in (image, text)
                ]
            )
        return jnp.concatenate([p[0] for p in pieces] + [p[1] for p in pieces], 0).astype(F32)

    def to_home(rows):
        image, text = [], []
        for step in range(micros):
            image.append(
                lax.ppermute(
                    rows[step * own_image : (step + 1) * own_image], "context", rounds(step, True)
                )
            )
            at = rows_image + step * own_text
            text.append(lax.ppermute(rows[at : at + own_text], "context", rounds(step, True)))
        image, text = jnp.stack(image), jnp.stack(text)
        turns = [(m - context) % micros for m in range(micros)]
        return tuple(
            jnp.stack([lax.dynamic_index_in_dim(x, turn, 0, keepdims=False) for turn in turns])[None]
            for x in (image, text)
        )

    def gathered(w):
        return lax.all_gather(w, "context", axis=0, tiled=True)

    def qkv_order(w):
        return (
            w.reshape(depth, groups, group_heads, 3, HEAD).transpose(0, 1, 3, 2, 4).reshape(depth, 3 * local)
        )

    qkv_full = [gathered(qkv_order(qkv_weight[0, j])) for j in range(2)]
    out_full = [gathered(out_weight[0, j].T) for j in range(2)]
    up_full = gathered(up_weight[0, 0])
    down_full = gathered(down_weight[0, 0].T)
    up_text, down_text = up_weight[0, 1], down_weight[0, 1]

    cond_float = conditioning.astype(F32)
    silu_cond = jax.nn.silu(cond_float).astype(BF).reshape(micros * seqs, -1)
    ada_part = jnp.einsum("rc,jck->jrk", silu_cond, ada_weight[0], preferred_element_type=F32)
    mod_piece = mods // ndev
    ada_sent = ada_part.reshape(2 * micros * seqs, ndev, mod_piece).transpose(1, 0, 2).astype(BF)
    ada_got = lax.all_to_all(ada_sent, BOTH, 0, 0)
    ada_sum = jnp.sum(ada_got.astype(F32), axis=0)
    pieces = gather_both(jnp.concatenate((ada_sum.reshape(-1), biases[0].astype(F32).reshape(-1))))
    split_at = 2 * micros * seqs * mod_piece
    ada_all = (
        pieces[:, :split_at]
        .reshape(ndev, 2, micros, seqs, mod_piece)
        .transpose(2, 1, 3, 0, 4)
        .reshape(micros, 2, seqs, mods)
    )
    bias_full = pieces[:, split_at:].reshape(ndev, 2, bias_here).transpose(1, 0, 2).reshape(2, -1)
    table = lax.dynamic_index_in_dim(ada_all, micro, 0, keepdims=False) + bias_full[:, None, :mods]
    table = table.astype(BF).reshape(table_rows, mods)
    query_bias = lax.dynamic_slice_in_dim(bias_full, mods + tensor * local, local, 1)
    value_bias = lax.dynamic_slice_in_dim(bias_full, mods + width + tensor * local, local, 1)
    qkv_bias = jnp.concatenate(
        (
            query_bias.reshape(2, groups, group),
            jnp.zeros((2, groups, group), F32),
            value_bias.reshape(2, groups, group),
        ),
        axis=2,
    ).reshape(2, 3 * local)
    out_bias = bias_full[:, mods + 2 * width : mods + 3 * width]
    up_bias = lax.dynamic_slice_in_dim(bias_full, mods + 3 * width + tensor * hidden, hidden, 1)
    down_bias = bias_full[:, mods + 3 * width + hidden * ntensor :]

    def by_modality(pair):
        return jnp.concatenate(
            (
                jnp.broadcast_to(pair[0][None], (rows_image, width)),
                jnp.broadcast_to(pair[1][None], (rows_text, width)),
            ),
            0,
        )

    def ids_of(work_context):
        m, u = work_context // per, work_context % per
        found = []
        for ids, own in ((image_seq_ids, own_image), (text_seq_ids, own_text)):
            table_ids = lax.dynamic_index_in_dim(ids, m, 0, keepdims=False).reshape(ndev, own)
            homes = jnp.stack([u * micros + (m - step) % micros for step in range(micros)])
            places = homes[None, :] * ntensor + (tensor ^ jnp.array(order))[:, None]
            found.append(jnp.take(table_ids, places.reshape(-1), axis=0).reshape(-1))
        return found

    own_found = ids_of(context)
    own_ids = jnp.concatenate((own_found[0][:rows_image], own_found[1][:rows_text] + seqs))
    onehot = (own_ids[:, None] == jnp.arange(table_rows)[None, :]).astype(BF)
    row_mods = dot_nn(onehot, table).astype(BF)
    joint_ids = jnp.concatenate(own_found)
    if paired:
        attn_ids = jnp.concatenate([joint_ids] + ids_of(context ^ 1))
    else:
        sharing = [[m * per + u for u in range(per)] for m in range(micros)]
        attn_ids = jnp.concatenate([x for u in range(per) for x in ids_of(micro * per + u)])

    def row_mod(index):
        return row_mods[:, index * width : (index + 1) * width].astype(F32)

    def sided(a, b):
        return jnp.where(side == 0, a, b), jnp.where(side == 0, b, a)

    def attention(joint):
        if paired:
            mine, theirs = sided(joint[:, : 3 * group], joint[:, 3 * group :])
            theirs = swapped(theirs, "context", 1)
            attended, lse = attend_pair(mine, theirs, attn_ids, group_heads)
            here, there = attended[:ctx_rows], swapped(attended[ctx_rows:], "context", 1)
            return jnp.concatenate(sided(here, there), axis=1), (mine, theirs, lse)
        q, k, v = (joint[:, i * group : (i + 1) * group] for i in range(3))
        k, v = (
            lax.all_gather(x, "context", axis=0, tiled=True, axis_index_groups=sharing) for x in (k, v)
        )
        attended, lse = attend(q, k, v, joint_ids, attn_ids, group_heads)
        return attended, (q, k, v, lse)

    def attention_back(grad, kept):
        if paired:
            mine, theirs, lse = kept
            g_mine, g_theirs = sided(grad[:, :group], grad[:, group:])
            g_theirs = swapped(g_theirs, "context", 1)
            d_mine, d_theirs = attend_pair_back(mine, theirs, g_mine, g_theirs, lse, attn_ids, group_heads)
            return jnp.concatenate(sided(d_mine, swapped(d_theirs, "context", 1)), axis=1)
        q, k, v, lse = kept
        dq, dk, dv = attend_back(q, k, v, grad, lse, joint_ids, attn_ids, group_heads)
        dk, dv = (
            lax.psum_scatter(x, "context", scatter_dimension=0, tiled=True, axis_index_groups=sharing)
            for x in (dk, dv)
        )
        return jnp.concatenate((dq, dk, dv), axis=1)

    def forward(x):
        n1, inv1 = normalized(x)
        h1 = spread((n1 * (1.0 + row_mod(1)) + row_mod(0)).astype(BF))
        joint = jnp.concatenate(
            [(dot_nn(h1[j], qkv_full[j]) + qkv_bias[j]).astype(BF) for j in range(2)], 0
        )
        attended, kept = attention(joint)
        attn = [attended[:ctx_image], attended[ctx_image:]]
        branch = collect(*(dot_nt(attn[j], out_full[j]) for j in range(2))) + by_modality(out_bias)
        middle = x + row_mod(2) * branch
        n2, inv2 = normalized(middle)
        h2_rows = (n2 * (1.0 + row_mod(4)) + row_mod(3)).astype(BF)
        h2 = [jnp.concatenate(gather_tensor(h2_rows[:rows_image]), 0), text_columns(h2_rows[rows_image:])]
        act_image, slope_image = gelu_pair(dot_nn(h2[0], up_full) + up_bias[0])
        act_text, slope_text = gelu_pair(context_sum(dot_nn(h2[1], up_text)) + up_bias[1])
        acts = [act_image, context_gather(act_text)]
        down_image = reduce_tensor(dot_nt(act_image, down_full).astype(BF))
        down_text_rows = text_rows_of(dot_nn(acts[1], down_text))
        down = jnp.concatenate((down_image, down_text_rows), 0) + by_modality(down_bias)
        out = middle + row_mod(5) * down
        saved = dict(
            x=x, h1=h1, kept=kept, attn=attn, branch=branch, middle=middle, h2=h2, acts=acts,
            slopes=[slope_image, slope_text], down=down,
        )
        return out, saved

    def backward(saved, g_out):
        g_down = (row_mod(5) * g_out).astype(BF)
        gd = [jnp.concatenate(gather_tensor(g_down[:rows_image]), 0), text_columns(g_down[rows_image:])]
        g_up_image = (dot_nn(gd[0], down_full) * saved["slopes"][0].astype(F32)).astype(BF)
        g_up_text = (context_sum(dot_nt(gd[1], down_text)) * saved["slopes"][1].astype(F32)).astype(BF)
        g_up = [g_up_image, context_gather(g_up_text)]
        g_h2_image = reduce_tensor(dot_nt(g_up[0], up_full).astype(BF))
        g_h2_text = text_rows_of(dot_nt(g_up[1], up_text))
        g_h2 = jnp.concatenate((g_h2_image, g_h2_text), 0)
        n2, inv2 = normalized(saved["middle"])
        g_middle = g_out + norm_back(n2, inv2, g_h2 * (1.0 + row_mod(4)))
        g_branch = (row_mod(2) * g_middle).astype(BF)
        gb = spread(g_branch)
        g_attn = jnp.concatenate([dot_nn(gb[j], out_full[j]).astype(BF) for j in range(2)], 0)
        g_joint = attention_back(g_attn, saved["kept"])
        g_qkv = [g_joint[:ctx_image], g_joint[ctx_image:]]
        g_h1 = collect(*(dot_nt(g_qkv[j], qkv_full[j]) for j in range(2)))
        n1, inv1 = normalized(saved["x"])
        g_x = g_middle + norm_back(n1, inv1, g_h1 * (1.0 + row_mod(1)))
        row_grads = jnp.concatenate(
            [
                part.astype(BF)
                for part in (
                    g_h1, g_h1 * n1, g_middle * saved["branch"], g_h2, g_h2 * n2, g_out * saved["down"]
                )
            ],
            axis=1,
        )
        mod_grad = dot_tn(onehot, row_grads)
        tensors = dict(
            h1=saved["h1"], g_qkv=g_qkv, attn=saved["attn"], gb=gb, h2=saved["h2"], g_up=g_up,
            acts=saved["acts"], gd=gd, g_down=g_down, g_branch=g_branch, g_up_text=g_up_text, mod=mod_grad,
        )
        return g_x, tensors

    def handed(rows, by):
        return lax.ppermute(rows.astype(BF), "section", [(0, 1)] if by > 0 else [(1, 0)]).astype(F32)

    out_first, saved_first = forward(to_work(image_tokens, text_tokens))
    out_last, saved_last = forward(handed(out_first, 1))
    grad_last, tensors_last = backward(saved_last, to_work(image_cotangent, text_cotangent))
    grad_first, tensors_first = backward(saved_first, handed(grad_last, -1))
    out = to_home(jnp.where(first, out_first, out_last))
    grad = to_home(jnp.where(first, grad_first, grad_last))
    use = jax.tree.map(lambda a, b: jnp.where(first, a, b), tensors_first, tensors_last)

    def scattered(full):
        return lax.psum_scatter(full.astype(BF), "context", scatter_dimension=0, tiled=True).astype(F32)

    def qkv_order_back(w):
        return (
            w.reshape(depth, groups, 3, group_heads, HEAD).transpose(0, 1, 3, 2, 4).reshape(depth, 3 * local)
        )

    down_image_grad = scattered(dot_tn(use["gd"][0], use["acts"][0])).T
    up_image_grad = scattered(dot_tn(use["h2"][0], use["g_up"][0]))
    down_grad = jnp.stack((down_image_grad, dot_tn(use["acts"][1], use["gd"][1])))
    up_grad = jnp.stack((up_image_grad, dot_tn(use["h2"][1], use["g_up"][1])))
    out_grad = jnp.stack([scattered(dot_tn(use["gb"][j], use["attn"][j])).T for j in range(2)])
    qkv_grad = jnp.stack(
        [qkv_order_back(scattered(dot_tn(use["h1"][j], use["g_qkv"][j]))) for j in range(2)]
    )

    def column_sums(parts):
        return jnp.stack([jnp.sum(p.astype(F32), axis=0) for p in parts])

    def own_sums(rows):
        return column_sums((rows[:rows_image], rows[rows_image:]))

    qkv_sums = column_sums(use["g_qkv"]).reshape(2, groups, 3, group)
    bias_part = jnp.zeros((2, bias_here * ndev), F32)
    for at, value in (
        (0, jnp.sum(use["mod"].reshape(2, seqs, mods), axis=1)),
        (mods + tensor * local, qkv_sums[:, :, 0].reshape(2, local)),
        (mods + width + tensor * local, qkv_sums[:, :, 2].reshape(2, local)),
        (mods + 2 * width, own_sums(use["g_branch"])),
        (mods + 3 * width + tensor * hidden, column_sums((use["g_up"][0], use["g_up_text"]))),
        (mods + 3 * width + ntensor * hidden, own_sums(use["g_down"])),
    ):
        bias_part = lax.dynamic_update_slice_in_dim(bias_part, value, at, 1)
    sent = jnp.concatenate(
        (
            use["mod"].reshape(table_rows, ndev, mod_piece).transpose(1, 0, 2).reshape(ndev, -1),
            bias_part.reshape(2, ndev, bias_here).transpose(1, 0, 2).reshape(ndev, -1),
        ),
        axis=1,
    ).astype(BF)
    got = lax.all_to_all(sent, BOTH, 0, 0).astype(F32)
    bias_grad = jnp.sum(got[:, table_rows * mod_piece :], axis=0).reshape(2, bias_here)
    mod_sum = jnp.sum(got[:, : table_rows * mod_piece].reshape(micros, ndev // micros, -1), axis=1)
    mod_all = (
        gather_both(mod_sum.astype(BF))
        .reshape(ndev, micros, 2, seqs, mod_piece)
        .transpose(2, 1, 3, 0, 4)
        .reshape(2, micros * seqs, mods)
    )
    ada_grad = jnp.einsum("rc,jrk->jck", silu_cond, mod_all, preferred_element_type=F32)
    cond_inner = jnp.einsum("jrk,jck->rc", mod_all, ada_weight[0], preferred_element_type=F32)
    unused, silu_back = jax.vjp(jax.nn.silu, cond_float)
    cond_grad = silu_back(lax.psum(cond_inner, "section").reshape(cond_float.shape))[0]
    return (
        *out,
        *grad,
        cond_grad,
        ada_grad[None],
        qkv_grad[None],
        out_grad[None],
        up_grad[None],
        down_grad[None],
        bias_grad[None],
    )


def solution(mesh):
    tokens = P(None, BOTH, None)
    block_rows = P("section", None, BOTH, None)
    by_rows = P("section", None, "context", "tensor")
    by_cols = P("section", None, "tensor", "context")
    block_biases = P("section", None, BOTH)
    in_specs = (
        tokens,
        tokens,
        P(None, None, BOTH),
        P(),
        P(),
        block_rows,
        by_rows,
        by_cols,
        by_rows,
        by_cols,
        block_biases,
        tokens,
        tokens,
    )
    out_specs = (
        block_rows,
        block_rows,
        block_rows,
        block_rows,
        P(None, None, BOTH),
        block_rows,
        by_rows,
        by_cols,
        by_rows,
        by_cols,
        block_biases,
    )
    return jax.shard_map(shards, mesh=mesh, in_specs=in_specs, out_specs=out_specs, check_vma=False)
```

```python
from functools import partial

import jax
import jax.numpy as jnp
from jax import lax
from jax.experimental import pallas as pl
from jax.experimental.pallas import tpu as pltpu
from jax.sharding import PartitionSpec as P

HEADS = 24
HEAD = 64
NORM_EPS = 1e-06
MASKED = -1e30
BF = jnp.bfloat16
F32 = jnp.float32
BOTH = ("context", "tensor")


def dot_nn(a, b):
    return lax.dot_general(a, b, (((1,), (0,)), ((), ())), preferred_element_type=F32)


def dot_nt(a, b):
    return lax.dot_general(a, b, (((1,), (1,)), ((), ())), preferred_element_type=F32)


def dot_tn(a, b):
    return lax.dot_general(a, b, (((0,), (0,)), ((), ())), preferred_element_type=F32)


def scaled(q):
    return q * jnp.asarray(HEAD**-0.5, BF)


def attend_body(heads, chunk, places, q_ref, k_ref, v_ref, idq_ref, idk_ref, store, lse_ref):
    at_q, at_k, at_v = places

    def one_chunk(step, carry):
        rows = pl.ds(pl.multiple_of(step * chunk, chunk), chunk)
        bias = jnp.where(idk_ref[...] == idq_ref[:, rows], 0.0, MASKED)
        outs = []
        for head in range(heads):
            at = head * HEAD
            q = scaled(q_ref[rows, at_q + at : at_q + at + HEAD])
            scores = dot_nt(k_ref[:, at_k + at : at_k + at + HEAD], q) + bias
            top = jnp.max(scores, axis=0, keepdims=True)
            weights = jnp.exp(scores - top)
            total = jnp.sum(weights, axis=0, keepdims=True)
            summed = dot_tn(v_ref[:, at_v + at : at_v + at + HEAD], weights.astype(BF))
            outs.append((summed / total).T)
            lse_ref[head : head + 1, rows] = top + jnp.log(total)
        store(rows, jnp.concatenate(outs, axis=1).astype(BF))
        return carry

    lax.fori_loop(0, idq_ref.shape[1] // chunk, one_chunk, 0)


def attend_back_body(
    heads, chunk, places, q_ref, k_ref, v_ref, g_ref, lse_ref, idq_ref, idk_ref, store_dq, dk_acc, dv_acc
):
    at_q, at_k, at_v = places
    dk_acc[...] = jnp.zeros_like(dk_acc)
    dv_acc[...] = jnp.zeros_like(dv_acc)

    def one_chunk(step, carry):
        rows = pl.ds(pl.multiple_of(step * chunk, chunk), chunk)
        bias = jnp.where(idk_ref[...] == idq_ref[:, rows], 0.0, MASKED)
        grads = []
        for head in range(heads):
            at = head * HEAD
            q = scaled(q_ref[rows, at_q + at : at_q + at + HEAD])
            g = g_ref[rows, at : at + HEAD]
            k = k_ref[:, at_k + at : at_k + at + HEAD]
            probs = jnp.exp(dot_nt(k, q) + bias - lse_ref[head : head + 1, rows])
            dv_acc[head] += dot_nn(probs.astype(BF), g)
            both = probs * dot_nt(v_ref[:, at_v + at : at_v + at + HEAD], g)
            delta = jnp.sum(both, axis=0, keepdims=True)
            dscores = (both - probs * delta).astype(BF)
            dk_acc[head] += dot_nn(dscores, q)
            grads.append((dot_tn(k, dscores) * HEAD**-0.5).T)
        store_dq(rows, jnp.concatenate(grads, axis=1).astype(BF))
        return carry

    lax.fori_loop(0, idq_ref.shape[1] // chunk, one_chunk, 0)


def heads_of(acc):
    return jnp.concatenate([acc[head] for head in range(acc.shape[0])], axis=1).astype(BF)


def attend_costs(queries, keys, heads, factor):
    return pl.CostEstimate(
        flops=factor * queries * keys * heads * HEAD,
        bytes_accessed=2 * (queries + 2 * keys) * heads * HEAD * factor // 4,
        transcendentals=queries * keys * heads,
    )


def chunk_for(keys):
    return 256 if keys <= 1024 else 128


VMEM_LIMIT = pltpu.CompilerParams(vmem_limit_bytes=56 * 2**20)


def attend(q, k, v, ids_q, ids_k, heads):
    queries, keys = q.shape[0], k.shape[0]

    def kernel(q_ref, k_ref, v_ref, idq_ref, idk_ref, out_ref, lse_ref):
        def store(rows, value):
            out_ref[rows, :] = value

        attend_body(
            heads, chunk_for(keys), (0, 0, 0), q_ref, k_ref, v_ref, idq_ref, idk_ref, store, lse_ref
        )

    return pl.pallas_call(
        kernel,
        out_shape=(
            jax.ShapeDtypeStruct((queries, heads * HEAD), BF),
            jax.ShapeDtypeStruct((heads, queries), F32),
        ),
        compiler_params=VMEM_LIMIT,
        cost_estimate=attend_costs(queries, keys, heads, 4),
    )(q, k, v, ids_q.reshape(1, queries), ids_k.reshape(keys, 1))


def attend_back(q, k, v, g, lse, ids_q, ids_k, heads):
    queries, keys = q.shape[0], k.shape[0]

    def kernel(
        q_ref, k_ref, v_ref, g_ref, lse_ref, idq_ref, idk_ref, dq_ref, dk_ref, dv_ref, dk_acc, dv_acc
    ):
        def store(rows, value):
            dq_ref[rows, :] = value

        attend_back_body(
            heads, chunk_for(keys), (0, 0, 0), q_ref, k_ref, v_ref, g_ref, lse_ref, idq_ref, idk_ref,
            store, dk_acc, dv_acc,
        )
        dk_ref[...] = heads_of(dk_acc)
        dv_ref[...] = heads_of(dv_acc)

    return pl.pallas_call(
        kernel,
        out_shape=(
            jax.ShapeDtypeStruct((queries, heads * HEAD), BF),
            jax.ShapeDtypeStruct((keys, heads * HEAD), BF),
            jax.ShapeDtypeStruct((keys, heads * HEAD), BF),
        ),
        scratch_shapes=[pltpu.VMEM((heads, keys, HEAD), F32), pltpu.VMEM((heads, keys, HEAD), F32)],
        compiler_params=VMEM_LIMIT,
        cost_estimate=attend_costs(queries, keys, heads, 10),
    )(q, k, v, g, lse, ids_q.reshape(1, queries), ids_k.reshape(keys, 1))


def attend_pair(mine, theirs, ids, heads):
    half, wide = mine.shape
    rows_all, group = 2 * half, heads * HEAD

    def kernel(mine_ref, theirs_ref, idq_ref, idk_ref, out_ref, lse_ref, x_ref):
        x_ref[:half] = mine_ref[...]
        x_ref[half:] = theirs_ref[...]

        def store(rows, value):
            out_ref[rows, :] = value

        attend_body(
            heads, 256, (0, group, 2 * group), x_ref, x_ref, x_ref, idq_ref, idk_ref, store, lse_ref
        )

    return pl.pallas_call(
        kernel,
        out_shape=(
            jax.ShapeDtypeStruct((rows_all, group), BF),
            jax.ShapeDtypeStruct((heads, rows_all), F32),
        ),
        scratch_shapes=[pltpu.VMEM((rows_all, wide), BF)],
        compiler_params=VMEM_LIMIT,
        cost_estimate=attend_costs(rows_all, rows_all, heads, 4),
    )(mine, theirs, ids.reshape(1, rows_all), ids.reshape(rows_all, 1))


def attend_pair_back(mine, theirs, g_mine, g_theirs, lse, ids, heads):
    half, wide = mine.shape
    rows_all, group = 2 * half, heads * HEAD

    def kernel(
        mine_ref, theirs_ref, gm_ref, gt_ref, lse_ref, idq_ref, idk_ref, dmine_ref, dtheirs_ref,
        x_ref, g_ref, dq_acc, dk_acc, dv_acc,
    ):
        x_ref[:half] = mine_ref[...]
        x_ref[half:] = theirs_ref[...]
        g_ref[:half] = gm_ref[...]
        g_ref[half:] = gt_ref[...]

        def store(rows, value):
            dq_acc[rows, :] = value

        attend_back_body(
            heads, 256, (0, group, 2 * group), x_ref, x_ref, x_ref, g_ref, lse_ref, idq_ref, idk_ref,
            store, dk_acc, dv_acc,
        )
        grads = jnp.concatenate((dq_acc[...], heads_of(dk_acc), heads_of(dv_acc)), axis=1)
        dmine_ref[...] = grads[:half]
        dtheirs_ref[...] = grads[half:]

    return pl.pallas_call(
        kernel,
        out_shape=(jax.ShapeDtypeStruct((half, wide), BF), jax.ShapeDtypeStruct((half, wide), BF)),
        scratch_shapes=[
            pltpu.VMEM((rows_all, wide), BF),
            pltpu.VMEM((rows_all, group), BF),
            pltpu.VMEM((rows_all, group), BF),
            pltpu.VMEM((heads, rows_all, HEAD), F32),
            pltpu.VMEM((heads, rows_all, HEAD), F32),
        ],
        compiler_params=VMEM_LIMIT,
        cost_estimate=attend_costs(rows_all, rows_all, heads, 10),
    )(mine, theirs, g_mine, g_theirs, lse, ids.reshape(1, rows_all), ids.reshape(rows_all, 1))


def normalized(x):
    centred = x - jnp.mean(x, axis=-1, keepdims=True)
    inverse = lax.rsqrt(jnp.mean(centred * centred, axis=-1, keepdims=True) + NORM_EPS)
    return centred * inverse, inverse


def norm_back(n, inverse, w):
    return (w - jnp.mean(w, axis=-1, keepdims=True) - n * jnp.mean(w * n, axis=-1, keepdims=True)) * inverse


def gelu_pair(u):
    c = 0.7978845608028654
    inner = jnp.tanh(c * (u + 0.044715 * u * u * u))
    value = 0.5 * u * (1.0 + inner)
    slope = 0.5 * (1.0 + inner) + 0.5 * u * (1.0 - inner * inner) * c * (1.0 + 3 * 0.044715 * u * u)
    return value.astype(BF), slope.astype(BF)


def shards(
    image_tokens,
    text_tokens,
    conditioning,
    image_seq_ids,
    text_seq_ids,
    ada_weight,
    qkv_weight,
    out_weight,
    up_weight,
    down_weight,
    biases,
    image_cotangent,
    text_cotangent,
):
    section = lax.axis_index("section")
    context = lax.axis_index("context")
    tensor = lax.axis_index("tensor")
    ncontext = lax.axis_size("context")
    ntensor = lax.axis_size("tensor")
    ndev = ncontext * ntensor
    first = section == 0
    micros, own_image, width = image_tokens.shape
    own_text = text_tokens.shape[1]
    seqs = conditioning.shape[1]
    rows_image, rows_text = micros * own_image, micros * own_text
    heads_here = HEADS // ntensor
    local = heads_here * HEAD
    hidden = up_weight.shape[3]
    bias_here = biases.shape[2]
    depth = qkv_weight.shape[2]
    mods = 6 * width
    table_rows = 2 * seqs
    per = ncontext // micros
    micro = context // per
    paired = per == 2 and heads_here % 2 == 0
    groups = 2 if paired else 1
    group_heads = heads_here // groups
    group = group_heads * HEAD
    side = context % per
    ctx_image, ctx_text = ntensor * rows_image, ntensor * rows_text
    ctx_rows = ctx_image + ctx_text
    text_all = ncontext * ctx_text

    order = (0, 2, 1, 3)

    def swapped(x, axis, bit):
        return lax.ppermute(x, axis, [(i, i ^ bit) for i in range(lax.axis_size(axis))])

    def near(x):
        return swapped(x, "tensor", 1)

    def far(x):
        return swapped(x, "tensor", 2)

    def gather_tensor(x):
        beside = near(x)
        across = far(x)
        return x, across, beside, near(across)

    def reduce_tensor(x):
        n = x.shape[0] // 4
        got = near(x[2 * n :])
        mine = x[: 2 * n].astype(F32) + got.astype(F32)
        return mine[:n] + far(mine[n:].astype(BF)).astype(F32)

    def spread(rows):
        parts = gather_tensor(rows)
        return [
            jnp.concatenate([p[:rows_image] for p in parts], 0),
            jnp.concatenate([p[rows_image:] for p in parts], 0),
        ]

    def collect(image_rows, text_rows):
        return jnp.concatenate(
            (reduce_tensor(image_rows.astype(BF)), reduce_tensor(text_rows.astype(BF))), 0
        )

    def text_columns(rows):
        sent = rows.reshape(ctx_text, ncontext, depth).transpose(1, 0, 2)
        return lax.all_to_all(sent, "context", 0, 0).reshape(text_all, depth)

    def text_rows_of(partial_sums):
        turned = (
            partial_sums.astype(BF)
            .reshape(ncontext, ntensor, rows_text, depth)
            .transpose(1, 0, 2, 3)
            .reshape(ntensor * ncontext * rows_text, depth)
        )
        mine = reduce_tensor(turned).astype(BF).reshape(ncontext, rows_text, depth)
        got = lax.all_to_all(mine, "context", 0, 0)
        return got.transpose(1, 0, 2).reshape(rows_text, width).astype(F32)

    def context_sum(partial_sums):
        sent = partial_sums.astype(BF).reshape(ncontext, ctx_text, -1)
        return jnp.sum(lax.all_to_all(sent, "context", 0, 0).astype(F32), axis=0)

    def context_gather(rows):
        sent = jnp.broadcast_to(rows[None], (ncontext,) + rows.shape)
        return lax.all_to_all(sent, "context", 0, 0).reshape(text_all, rows.shape[1])

    def gather_both(x):
        got = lax.all_gather(lax.all_gather(x, "tensor"), "context")
        return got.reshape((ndev,) + x.shape)

    def rounds(step, back):
        pairs = []
        for h in range(ncontext):
            m = (h + step) % micros
            pairs.append((h, m * per + h // micros))
        return [(b, a) for a, b in pairs] if back else pairs

    def to_work(image, text):
        pieces = []
        for step in range(micros):
            m = (context + step) % micros
            pieces.append(
                [
                    lax.ppermute(
                        lax.dynamic_index_in_dim(x, m, 0, keepdims=False), "context", rounds(step, False)
                    )
                    for x in (image, text)
                ]
            )
        return jnp.concatenate([p[0] for p in pieces] + [p[1] for p in pieces], 0).astype(F32)

    def to_home(rows):
        image, text = [], []
        for step in range(micros):
            image.append(
                lax.ppermute(
                    rows[step * own_image : (step + 1) * own_image], "context", rounds(step, True)
                )
            )
            at = rows_image + step * own_text
            text.append(lax.ppermute(rows[at : at + own_text], "context", rounds(step, True)))
        image, text = jnp.stack(image), jnp.stack(text)
        turns = [(m - context) % micros for m in range(micros)]
        return tuple(
            jnp.stack([lax.dynamic_index_in_dim(x, turn, 0, keepdims=False) for turn in turns])[None]
            for x in (image, text)
        )

    def gathered(w):
        return lax.all_gather(w, "context", axis=0, tiled=True)

    def qkv_order(w):
        return (
            w.reshape(depth, groups, group_heads, 3, HEAD).transpose(0, 1, 3, 2, 4).reshape(depth, 3 * local)
        )

    def both(parts):
        full = gathered(jnp.concatenate(parts, axis=1))
        wide = full.shape[1] // 2
        return [full[:, :wide], full[:, wide:]]

    qkv_full = both([qkv_order(qkv_weight[0, j]) for j in range(2)])
    out_full = both([out_weight[0, j].T for j in range(2)])
    up_full = [gathered(up_weight[0, j]) for j in range(2)]
    down_full = [gathered(down_weight[0, j].T) for j in range(2)]
    up_text, down_text = up_weight[0, 1], down_weight[0, 1]

    cond_float = conditioning.astype(F32)
    silu_cond = jax.nn.silu(cond_float).astype(BF).reshape(micros * seqs, -1)
    ada_part = jnp.einsum("rc,jck->jrk", silu_cond, ada_weight[0], preferred_element_type=F32)
    mod_piece = mods // ndev
    ada_sent = ada_part.reshape(2 * micros * seqs, ndev, mod_piece).transpose(1, 0, 2).astype(BF)
    ada_got = lax.all_to_all(ada_sent, BOTH, 0, 0)
    ada_sum = jnp.sum(ada_got.astype(F32), axis=0)
    pieces = gather_both(jnp.concatenate((ada_sum.reshape(-1), biases[0].astype(F32).reshape(-1))))
    split_at = 2 * micros * seqs * mod_piece
    ada_all = (
        pieces[:, :split_at]
        .reshape(ndev, 2, micros, seqs, mod_piece)
        .transpose(2, 1, 3, 0, 4)
        .reshape(micros, 2, seqs, mods)
    )
    bias_full = pieces[:, split_at:].reshape(ndev, 2, bias_here).transpose(1, 0, 2).reshape(2, -1)
    table = lax.dynamic_index_in_dim(ada_all, micro, 0, keepdims=False) + bias_full[:, None, :mods]
    table = table.astype(BF).reshape(table_rows, mods)
    query_bias = lax.dynamic_slice_in_dim(bias_full, mods + tensor * local, local, 1)
    value_bias = lax.dynamic_slice_in_dim(bias_full, mods + width + tensor * local, local, 1)
    qkv_bias = jnp.concatenate(
        (
            query_bias.reshape(2, groups, group),
            jnp.zeros((2, groups, group), F32),
            value_bias.reshape(2, groups, group),
        ),
        axis=2,
    ).reshape(2, 3 * local)
    out_bias = bias_full[:, mods + 2 * width : mods + 3 * width]
    up_bias = lax.dynamic_slice_in_dim(bias_full, mods + 3 * width + tensor * hidden, hidden, 1)
    down_bias = bias_full[:, mods + 3 * width + hidden * ntensor :]

    def by_modality(pair):
        return jnp.concatenate(
            (
                jnp.broadcast_to(pair[0][None], (rows_image, width)),
                jnp.broadcast_to(pair[1][None], (rows_text, width)),
            ),
            0,
        )

    def ids_of(work_context):
        m, u = work_context // per, work_context % per
        found = []
        for ids, own in ((image_seq_ids, own_image), (text_seq_ids, own_text)):
            table_ids = lax.dynamic_index_in_dim(ids, m, 0, keepdims=False).reshape(ndev, own)
            homes = jnp.stack([u * micros + (m - step) % micros for step in range(micros)])
            places = homes[None, :] * ntensor + (tensor ^ jnp.array(order))[:, None]
            found.append(jnp.take(table_ids, places.reshape(-1), axis=0).reshape(-1))
        return found

    own_found = ids_of(context)
    own_ids = jnp.concatenate((own_found[0][:rows_image], own_found[1][:rows_text] + seqs))
    onehot = (own_ids[:, None] == jnp.arange(table_rows)[None, :]).astype(BF)
    row_mods = dot_nn(onehot, table).astype(BF)
    joint_ids = jnp.concatenate(own_found)
    if paired:
        attn_ids = jnp.concatenate([joint_ids] + ids_of(context ^ 1))
    else:
        sharing = [[m * per + u for u in range(per)] for m in range(micros)]
        attn_ids = jnp.concatenate([x for u in range(per) for x in ids_of(micro * per + u)])

    def row_mod(index):
        return row_mods[:, index * width : (index + 1) * width].astype(F32)

    def sided(a, b):
        return jnp.where(side == 0, a, b), jnp.where(side == 0, b, a)

    def attention(joint):
        if paired:
            mine, theirs = sided(joint[:, : 3 * group], joint[:, 3 * group :])
            theirs = swapped(theirs, "context", 1)
            attended, lse = attend_pair(mine, theirs, attn_ids, group_heads)
            here, there = attended[:ctx_rows], swapped(attended[ctx_rows:], "context", 1)
            return jnp.concatenate(sided(here, there), axis=1), (mine, theirs, lse)
        q, k, v = (joint[:, i * group : (i + 1) * group] for i in range(3))
        k, v = (
            lax.all_gather(x, "context", axis=0, tiled=True, axis_index_groups=sharing) for x in (k, v)
        )
        attended, lse = attend(q, k, v, joint_ids, attn_ids, group_heads)
        return attended, (q, k, v, lse)

    def attention_back(grad, kept):
        if paired:
            mine, theirs, lse = kept
            g_mine, g_theirs = sided(grad[:, :group], grad[:, group:])
            g_theirs = swapped(g_theirs, "context", 1)
            d_mine, d_theirs = attend_pair_back(mine, theirs, g_mine, g_theirs, lse, attn_ids, group_heads)
            return jnp.concatenate(sided(d_mine, swapped(d_theirs, "context", 1)), axis=1)
        q, k, v, lse = kept
        dq, dk, dv = attend_back(q, k, v, grad, lse, joint_ids, attn_ids, group_heads)
        dk, dv = (
            lax.psum_scatter(x, "context", scatter_dimension=0, tiled=True, axis_index_groups=sharing)
            for x in (dk, dv)
        )
        return jnp.concatenate((dq, dk, dv), axis=1)

    def forward(x):
        n1, inv1 = normalized(x)
        h1 = spread((n1 * (1.0 + row_mod(1)) + row_mod(0)).astype(BF))
        joint = jnp.concatenate(
            [(dot_nn(h1[j], qkv_full[j]) + qkv_bias[j]).astype(BF) for j in range(2)], 0
        )
        attended, kept = attention(joint)
        attn = [attended[:ctx_image], attended[ctx_image:]]
        branch = collect(*(dot_nt(attn[j], out_full[j]) for j in range(2))) + by_modality(out_bias)
        middle = x + row_mod(2) * branch
        n2, inv2 = normalized(middle)
        h2_image, h2_text = spread((n2 * (1.0 + row_mod(4)) + row_mod(3)).astype(BF))
        h2 = [h2_image, text_columns(h2_text)]
        act_image, slope_image = gelu_pair(dot_nn(h2[0], up_full[0]) + up_bias[0])
        act_text, slope_text = gelu_pair(context_sum(dot_nn(h2[1], up_text)) + up_bias[1])
        acts = [act_image, context_gather(act_text)]
        down_image = reduce_tensor(dot_nt(act_image, down_full[0]).astype(BF))
        down_text_rows = text_rows_of(dot_nn(acts[1], down_text))
        down = jnp.concatenate((down_image, down_text_rows), 0) + by_modality(down_bias)
        out = middle + row_mod(5) * down
        saved = dict(
            x=x, h1=h1, kept=kept, attn=attn, branch=branch, middle=middle, h2=h2, acts=acts,
            slopes=[slope_image, slope_text], down=down,
        )
        return out, saved

    def chosen(a, b):
        return jax.tree.map(lambda x, y: jnp.where(first, x, y), a, b)

    def backward(saved, g_out, last=None):
        g_down = (row_mod(5) * g_out).astype(BF)
        gd = spread(g_down)
        g_up = [
            (dot_nn(gd[j], down_full[j]) * saved["slopes"][j].astype(F32)).astype(BF) for j in range(2)
        ]
        g_h2 = collect(*(dot_nt(g_up[j], up_full[j]) for j in range(2)))
        if last:
            use = chosen(
                dict(h2=saved["h2"], acts=saved["acts"], gd=gd, g_up=g_up),
                {k: last[k] for k in ("h2", "acts", "gd", "g_up")},
            )
            parts = (dot_tn(use["gd"][0], use["acts"][0]).astype(BF), dot_tn(use["h2"][0], use["g_up"][0]).astype(BF))
            g_h2, early = lax.optimization_barrier((g_h2, parts))
        n2, inv2 = normalized(saved["middle"])
        g_middle = g_out + norm_back(n2, inv2, g_h2 * (1.0 + row_mod(4)))
        g_branch = (row_mod(2) * g_middle).astype(BF)
        gb = spread(g_branch)
        g_attn = jnp.concatenate([dot_nn(gb[j], out_full[j]).astype(BF) for j in range(2)], 0)
        g_joint = attention_back(g_attn, saved["kept"])
        g_qkv = [g_joint[:ctx_image], g_joint[ctx_image:]]
        g_h1 = collect(*(dot_nt(g_qkv[j], qkv_full[j]) for j in range(2)))
        n1, inv1 = normalized(saved["x"])
        g_x = g_middle + norm_back(n1, inv1, g_h1 * (1.0 + row_mod(1)))
        row_grads = jnp.concatenate(
            [
                part.astype(BF)
                for part in (
                    g_h1, g_h1 * n1, g_middle * saved["branch"], g_h2, g_h2 * n2, g_out * saved["down"]
                )
            ],
            axis=1,
        )
        mod_grad = dot_tn(onehot, row_grads)
        tensors = dict(
            h1=saved["h1"], g_qkv=g_qkv, attn=saved["attn"], gb=gb, h2=saved["h2"], g_up=g_up,
            acts=saved["acts"], gd=gd, g_down=g_down, g_branch=g_branch, mod=mod_grad,
        )
        return g_x, tensors, early if last else None

    def handed(rows, by):
        return lax.ppermute(rows.astype(BF), "section", [(0, 1)] if by > 0 else [(1, 0)]).astype(F32)

    out_first, saved_first = forward(to_work(image_tokens, text_tokens))
    out_last, saved_last = forward(handed(out_first, 1))
    grad_last, tensors_last, unused = backward(saved_last, to_work(image_cotangent, text_cotangent))
    grad_first, tensors_first, early = backward(saved_first, handed(grad_last, -1), tensors_last)
    out = to_home(jnp.where(first, out_first, out_last))
    grad = to_home(jnp.where(first, grad_first, grad_last))
    use = chosen(tensors_first, tensors_last)

    def scattered(full):
        return lax.psum_scatter(full.astype(BF), "context", scatter_dimension=0, tiled=True).astype(F32)

    def qkv_order_back(w):
        return (
            w.reshape(depth, groups, 3, group_heads, HEAD).transpose(0, 1, 3, 2, 4).reshape(depth, 3 * local)
        )

    down_image_grad = scattered(early[0]).T
    up_image_grad = scattered(early[1])
    down_grad = jnp.stack((down_image_grad, dot_tn(use["acts"][1], text_columns(use["gd"][1]))))
    up_grad = jnp.stack((up_image_grad, dot_tn(use["h2"][1], context_gather(use["g_up"][1]))))
    out_grad = jnp.stack(
        (
            scattered(dot_tn(use["gb"][0], use["attn"][0])).T,
            dot_tn(context_gather(use["attn"][1]), text_columns(use["gb"][1])),
        )
    )
    qkv_grad = jnp.stack(
        (
            qkv_order_back(scattered(dot_tn(use["h1"][0], use["g_qkv"][0]))),
            qkv_order_back(dot_tn(text_columns(use["h1"][1]), context_gather(use["g_qkv"][1]))),
        )
    )

    def column_sums(parts):
        return jnp.stack([jnp.sum(p.astype(F32), axis=0) for p in parts])

    def own_sums(rows):
        return column_sums((rows[:rows_image], rows[rows_image:]))

    qkv_sums = column_sums(use["g_qkv"]).reshape(2, groups, 3, group)
    bias_part = jnp.zeros((2, bias_here * ndev), F32)
    for at, value in (
        (0, jnp.sum(use["mod"].reshape(2, seqs, mods), axis=1)),
        (mods + tensor * local, qkv_sums[:, :, 0].reshape(2, local)),
        (mods + width + tensor * local, qkv_sums[:, :, 2].reshape(2, local)),
        (mods + 2 * width, own_sums(use["g_branch"])),
        (mods + 3 * width + tensor * hidden, column_sums(use["g_up"])),
        (mods + 3 * width + ntensor * hidden, own_sums(use["g_down"])),
    ):
        bias_part = lax.dynamic_update_slice_in_dim(bias_part, value, at, 1)
    sent = jnp.concatenate(
        (
            use["mod"].reshape(table_rows, ndev, mod_piece).transpose(1, 0, 2).reshape(ndev, -1),
            bias_part.reshape(2, ndev, bias_here).transpose(1, 0, 2).reshape(ndev, -1),
        ),
        axis=1,
    ).astype(BF)
    got = lax.all_to_all(sent, BOTH, 0, 0).astype(F32)
    bias_grad = jnp.sum(got[:, table_rows * mod_piece :], axis=0).reshape(2, bias_here)
    mod_sum = jnp.sum(got[:, : table_rows * mod_piece].reshape(micros, ndev // micros, -1), axis=1)
    mod_all = (
        gather_both(mod_sum.astype(BF))
        .reshape(ndev, micros, 2, seqs, mod_piece)
        .transpose(2, 1, 3, 0, 4)
        .reshape(2, micros * seqs, mods)
    )
    ada_grad = jnp.einsum("rc,jrk->jck", silu_cond, mod_all, preferred_element_type=F32)
    cond_inner = jnp.einsum("jrk,jck->rc", mod_all, ada_weight[0], preferred_element_type=F32)
    unused, silu_back = jax.vjp(jax.nn.silu, cond_float)
    cond_grad = silu_back(lax.psum(cond_inner, "section").reshape(cond_float.shape))[0]
    return (
        *out,
        *grad,
        cond_grad,
        ada_grad[None],
        qkv_grad[None],
        out_grad[None],
        up_grad[None],
        down_grad[None],
        bias_grad[None],
    )


def solution(mesh):
    tokens = P(None, BOTH, None)
    block_rows = P("section", None, BOTH, None)
    by_rows = P("section", None, "context", "tensor")
    by_cols = P("section", None, "tensor", "context")
    block_biases = P("section", None, BOTH)
    in_specs = (
        tokens,
        tokens,
        P(None, None, BOTH),
        P(),
        P(),
        block_rows,
        by_rows,
        by_cols,
        by_rows,
        by_cols,
        block_biases,
        tokens,
        tokens,
    )
    out_specs = (
        block_rows,
        block_rows,
        block_rows,
        block_rows,
        P(None, None, BOTH),
        block_rows,
        by_rows,
        by_cols,
        by_rows,
        by_cols,
        block_biases,
    )
    return jax.shard_map(shards, mesh=mesh, in_specs=in_specs, out_specs=out_specs, check_vma=False)
```

```python
from functools import partial

import jax
import jax.numpy as jnp
from jax import lax
from jax.experimental import pallas as pl
from jax.experimental.pallas import tpu as pltpu
from jax.sharding import PartitionSpec as P

HEADS = 24
HEAD = 64
NORM_EPS = 1e-06
MASKED = -1e30
BF = jnp.bfloat16
F32 = jnp.float32
BOTH = ("context", "tensor")


def dot_nn(a, b):
    return lax.dot_general(a, b, (((1,), (0,)), ((), ())), preferred_element_type=F32)


def dot_nt(a, b):
    return lax.dot_general(a, b, (((1,), (1,)), ((), ())), preferred_element_type=F32)


def dot_tn(a, b):
    return lax.dot_general(a, b, (((0,), (0,)), ((), ())), preferred_element_type=F32)


def scaled(q):
    return q * jnp.asarray(HEAD**-0.5, BF)


def attend_body(heads, chunk, places, q_ref, k_ref, v_ref, idq_ref, idk_ref, store, lse_ref):
    at_q, at_k, at_v = places

    def one_chunk(step, carry):
        rows = pl.ds(pl.multiple_of(step * chunk, chunk), chunk)
        bias = jnp.where(idk_ref[...] == idq_ref[:, rows], 0.0, MASKED)
        outs = []
        for head in range(heads):
            at = head * HEAD
            q = scaled(q_ref[rows, at_q + at : at_q + at + HEAD])
            scores = dot_nt(k_ref[:, at_k + at : at_k + at + HEAD], q) + bias
            top = jnp.max(scores, axis=0, keepdims=True)
            weights = jnp.exp(scores - top)
            total = jnp.sum(weights, axis=0, keepdims=True)
            summed = dot_tn(v_ref[:, at_v + at : at_v + at + HEAD], weights.astype(BF))
            outs.append((summed / total).T)
            lse_ref[head : head + 1, rows] = top + jnp.log(total)
        store(rows, jnp.concatenate(outs, axis=1).astype(BF))
        return carry

    lax.fori_loop(0, idq_ref.shape[1] // chunk, one_chunk, 0)


def attend_back_body(
    heads, chunk, places, q_ref, k_ref, v_ref, g_ref, lse_ref, idq_ref, idk_ref, store_dq, dk_acc, dv_acc
):
    at_q, at_k, at_v = places
    dk_acc[...] = jnp.zeros_like(dk_acc)
    dv_acc[...] = jnp.zeros_like(dv_acc)

    def one_chunk(step, carry):
        rows = pl.ds(pl.multiple_of(step * chunk, chunk), chunk)
        bias = jnp.where(idk_ref[...] == idq_ref[:, rows], 0.0, MASKED)
        grads = []
        for head in range(heads):
            at = head * HEAD
            q = scaled(q_ref[rows, at_q + at : at_q + at + HEAD])
            g = g_ref[rows, at : at + HEAD]
            k = k_ref[:, at_k + at : at_k + at + HEAD]
            probs = jnp.exp(dot_nt(k, q) + bias - lse_ref[head : head + 1, rows])
            dv_acc[head] += dot_nn(probs.astype(BF), g)
            both = probs * dot_nt(v_ref[:, at_v + at : at_v + at + HEAD], g)
            delta = jnp.sum(both, axis=0, keepdims=True)
            dscores = (both - probs * delta).astype(BF)
            dk_acc[head] += dot_nn(dscores, q)
            grads.append((dot_tn(k, dscores) * HEAD**-0.5).T)
        store_dq(rows, jnp.concatenate(grads, axis=1).astype(BF))
        return carry

    lax.fori_loop(0, idq_ref.shape[1] // chunk, one_chunk, 0)


def heads_of(acc):
    return jnp.concatenate([acc[head] for head in range(acc.shape[0])], axis=1).astype(BF)


def attend_costs(queries, keys, heads, factor):
    return pl.CostEstimate(
        flops=factor * queries * keys * heads * HEAD,
        bytes_accessed=2 * (queries + 2 * keys) * heads * HEAD * factor // 4,
        transcendentals=queries * keys * heads,
    )


def chunk_for(keys):
    return 256 if keys <= 1024 else 128


VMEM_LIMIT = pltpu.CompilerParams(vmem_limit_bytes=56 * 2**20)


def attend(q, k, v, ids_q, ids_k, heads):
    queries, keys = q.shape[0], k.shape[0]

    def kernel(q_ref, k_ref, v_ref, idq_ref, idk_ref, out_ref, lse_ref):
        def store(rows, value):
            out_ref[rows, :] = value

        attend_body(
            heads, chunk_for(keys), (0, 0, 0), q_ref, k_ref, v_ref, idq_ref, idk_ref, store, lse_ref
        )

    return pl.pallas_call(
        kernel,
        out_shape=(
            jax.ShapeDtypeStruct((queries, heads * HEAD), BF),
            jax.ShapeDtypeStruct((heads, queries), F32),
        ),
        compiler_params=VMEM_LIMIT,
        cost_estimate=attend_costs(queries, keys, heads, 4),
    )(q, k, v, ids_q.reshape(1, queries), ids_k.reshape(keys, 1))


def attend_back(q, k, v, g, lse, ids_q, ids_k, heads):
    queries, keys = q.shape[0], k.shape[0]

    def kernel(
        q_ref, k_ref, v_ref, g_ref, lse_ref, idq_ref, idk_ref, dq_ref, dk_ref, dv_ref, dk_acc, dv_acc
    ):
        def store(rows, value):
            dq_ref[rows, :] = value

        attend_back_body(
            heads, chunk_for(keys), (0, 0, 0), q_ref, k_ref, v_ref, g_ref, lse_ref, idq_ref, idk_ref,
            store, dk_acc, dv_acc,
        )
        dk_ref[...] = heads_of(dk_acc)
        dv_ref[...] = heads_of(dv_acc)

    return pl.pallas_call(
        kernel,
        out_shape=(
            jax.ShapeDtypeStruct((queries, heads * HEAD), BF),
            jax.ShapeDtypeStruct((keys, heads * HEAD), BF),
            jax.ShapeDtypeStruct((keys, heads * HEAD), BF),
        ),
        scratch_shapes=[pltpu.VMEM((heads, keys, HEAD), F32), pltpu.VMEM((heads, keys, HEAD), F32)],
        compiler_params=VMEM_LIMIT,
        cost_estimate=attend_costs(queries, keys, heads, 10),
    )(q, k, v, g, lse, ids_q.reshape(1, queries), ids_k.reshape(keys, 1))


def attend_pair(mine, theirs, ids, heads):
    half, wide = mine.shape
    rows_all, group = 2 * half, heads * HEAD

    def kernel(mine_ref, theirs_ref, idq_ref, idk_ref, out_ref, lse_ref, x_ref):
        x_ref[:half] = mine_ref[...]
        x_ref[half:] = theirs_ref[...]

        def store(rows, value):
            out_ref[rows, :] = value

        attend_body(
            heads, 256, (0, group, 2 * group), x_ref, x_ref, x_ref, idq_ref, idk_ref, store, lse_ref
        )

    return pl.pallas_call(
        kernel,
        out_shape=(
            jax.ShapeDtypeStruct((rows_all, group), BF),
            jax.ShapeDtypeStruct((heads, rows_all), F32),
        ),
        scratch_shapes=[pltpu.VMEM((rows_all, wide), BF)],
        compiler_params=VMEM_LIMIT,
        cost_estimate=attend_costs(rows_all, rows_all, heads, 4),
    )(mine, theirs, ids.reshape(1, rows_all), ids.reshape(rows_all, 1))


def attend_pair_back(mine, theirs, g_mine, g_theirs, lse, ids, heads):
    half, wide = mine.shape
    rows_all, group = 2 * half, heads * HEAD

    def kernel(
        mine_ref, theirs_ref, gm_ref, gt_ref, lse_ref, idq_ref, idk_ref, dmine_ref, dtheirs_ref,
        x_ref, g_ref, dq_acc, dk_acc, dv_acc,
    ):
        x_ref[:half] = mine_ref[...]
        x_ref[half:] = theirs_ref[...]
        g_ref[:half] = gm_ref[...]
        g_ref[half:] = gt_ref[...]

        def store(rows, value):
            dq_acc[rows, :] = value

        attend_back_body(
            heads, 256, (0, group, 2 * group), x_ref, x_ref, x_ref, g_ref, lse_ref, idq_ref, idk_ref,
            store, dk_acc, dv_acc,
        )
        grads = jnp.concatenate((dq_acc[...], heads_of(dk_acc), heads_of(dv_acc)), axis=1)
        dmine_ref[...] = grads[:half]
        dtheirs_ref[...] = grads[half:]

    return pl.pallas_call(
        kernel,
        out_shape=(jax.ShapeDtypeStruct((half, wide), BF), jax.ShapeDtypeStruct((half, wide), BF)),
        scratch_shapes=[
            pltpu.VMEM((rows_all, wide), BF),
            pltpu.VMEM((rows_all, group), BF),
            pltpu.VMEM((rows_all, group), BF),
            pltpu.VMEM((heads, rows_all, HEAD), F32),
            pltpu.VMEM((heads, rows_all, HEAD), F32),
        ],
        compiler_params=VMEM_LIMIT,
        cost_estimate=attend_costs(rows_all, rows_all, heads, 10),
    )(mine, theirs, g_mine, g_theirs, lse, ids.reshape(1, rows_all), ids.reshape(rows_all, 1))


def after(x, *others):
    anywhere = pl.BlockSpec(memory_space=pl.ANY)

    def kernel(*refs):
        pass

    return pl.pallas_call(
        kernel,
        out_shape=jax.ShapeDtypeStruct(x.shape, x.dtype),
        in_specs=[anywhere] * (1 + len(others)),
        out_specs=anywhere,
        input_output_aliases={0: 0},
    )(x, *others)


def normalized(x):
    centred = x - jnp.mean(x, axis=-1, keepdims=True)
    inverse = lax.rsqrt(jnp.mean(centred * centred, axis=-1, keepdims=True) + NORM_EPS)
    return centred * inverse, inverse


def norm_back(n, inverse, w):
    return (w - jnp.mean(w, axis=-1, keepdims=True) - n * jnp.mean(w * n, axis=-1, keepdims=True)) * inverse


def gelu_pair(u):
    c = 0.7978845608028654
    inner = jnp.tanh(c * (u + 0.044715 * u * u * u))
    value = 0.5 * u * (1.0 + inner)
    slope = 0.5 * (1.0 + inner) + 0.5 * u * (1.0 - inner * inner) * c * (1.0 + 3 * 0.044715 * u * u)
    return value.astype(BF), slope.astype(BF)


def shards(
    image_tokens,
    text_tokens,
    conditioning,
    image_seq_ids,
    text_seq_ids,
    ada_weight,
    qkv_weight,
    out_weight,
    up_weight,
    down_weight,
    biases,
    image_cotangent,
    text_cotangent,
):
    section = lax.axis_index("section")
    context = lax.axis_index("context")
    tensor = lax.axis_index("tensor")
    ncontext = lax.axis_size("context")
    ntensor = lax.axis_size("tensor")
    ndev = ncontext * ntensor
    first = section == 0
    micros, own_image, width = image_tokens.shape
    own_text = text_tokens.shape[1]
    seqs = conditioning.shape[1]
    rows_image, rows_text = micros * own_image, micros * own_text
    heads_here = HEADS // ntensor
    local = heads_here * HEAD
    hidden = up_weight.shape[3]
    bias_here = biases.shape[2]
    depth = qkv_weight.shape[2]
    mods = 6 * width
    table_rows = 2 * seqs
    per = ncontext // micros
    micro = context // per
    paired = per == 2 and heads_here % 2 == 0
    groups = 2 if paired else 1
    group_heads = heads_here // groups
    group = group_heads * HEAD
    side = context % per
    ctx_image, ctx_text = ntensor * rows_image, ntensor * rows_text
    ctx_rows = ctx_image + ctx_text
    text_all = ncontext * ctx_text

    order = (0, 2, 1, 3)

    def swapped(x, axis, bit):
        return lax.ppermute(x, axis, [(i, i ^ bit) for i in range(lax.axis_size(axis))])

    def near(x):
        return swapped(x, "tensor", 1)

    def far(x):
        return swapped(x, "tensor", 2)

    def gather_tensor(x):
        beside = near(x)
        across = far(x)
        return x, across, beside, near(across)

    def reduce_tensor(x):
        n = x.shape[0] // 4
        got = near(x[2 * n :])
        mine = x[: 2 * n].astype(F32) + got.astype(F32)
        return mine[:n] + far(mine[n:].astype(BF)).astype(F32)

    def spread(rows):
        parts = gather_tensor(rows)
        return [
            jnp.concatenate([p[:rows_image] for p in parts], 0),
            jnp.concatenate([p[rows_image:] for p in parts], 0),
        ]

    def collect(image_rows, text_rows):
        return jnp.concatenate(
            (reduce_tensor(image_rows.astype(BF)), reduce_tensor(text_rows.astype(BF))), 0
        )

    def text_columns(rows):
        sent = rows.reshape(ctx_text, ncontext, depth).transpose(1, 0, 2)
        return lax.all_to_all(sent, "context", 0, 0).reshape(text_all, depth)

    def text_rows_of(partial_sums):
        turned = (
            partial_sums.astype(BF)
            .reshape(ncontext, ntensor, rows_text, depth)
            .transpose(1, 0, 2, 3)
            .reshape(ntensor * ncontext * rows_text, depth)
        )
        mine = reduce_tensor(turned).astype(BF).reshape(ncontext, rows_text, depth)
        got = lax.all_to_all(mine, "context", 0, 0)
        return got.transpose(1, 0, 2).reshape(rows_text, width).astype(F32)

    def context_sum(partial_sums):
        sent = partial_sums.astype(BF).reshape(ncontext, ctx_text, -1)
        return jnp.sum(lax.all_to_all(sent, "context", 0, 0).astype(F32), axis=0)

    def context_gather(rows):
        sent = jnp.broadcast_to(rows[None], (ncontext,) + rows.shape)
        return lax.all_to_all(sent, "context", 0, 0).reshape(text_all, rows.shape[1])

    def gather_both(x):
        got = lax.all_gather(lax.all_gather(x, "tensor"), "context")
        return got.reshape((ndev,) + x.shape)

    def rounds(step, back):
        pairs = []
        for h in range(ncontext):
            m = (h + step) % micros
            pairs.append((h, m * per + h // micros))
        return [(b, a) for a, b in pairs] if back else pairs

    def to_work(image, text):
        pieces = []
        for step in range(micros):
            m = (context + step) % micros
            pieces.append(
                [
                    lax.ppermute(
                        lax.dynamic_index_in_dim(x, m, 0, keepdims=False), "context", rounds(step, False)
                    )
                    for x in (image, text)
                ]
            )
        return jnp.concatenate([p[0] for p in pieces] + [p[1] for p in pieces], 0).astype(F32)

    def to_home(rows):
        image, text = [], []
        for step in range(micros):
            image.append(
                lax.ppermute(
                    rows[step * own_image : (step + 1) * own_image], "context", rounds(step, True)
                )
            )
            at = rows_image + step * own_text
            text.append(lax.ppermute(rows[at : at + own_text], "context", rounds(step, True)))
        image, text = jnp.stack(image), jnp.stack(text)
        turns = [(m - context) % micros for m in range(micros)]
        return tuple(
            jnp.stack([lax.dynamic_index_in_dim(x, turn, 0, keepdims=False) for turn in turns])[None]
            for x in (image, text)
        )

    def gathered(w):
        return lax.all_gather(w, "context", axis=0, tiled=True)

    def qkv_order(w):
        return (
            w.reshape(depth, groups, group_heads, 3, HEAD).transpose(0, 1, 3, 2, 4).reshape(depth, 3 * local)
        )

    qkv_here = [qkv_order(qkv_weight[0, j]) for j in range(2)]
    qkv_full = [gathered(w) for w in qkv_here]
    out_full = [gathered(out_weight[0, j].T) for j in range(2)]
    up_full = [gathered(up_weight[0, j]) for j in range(2)]
    down_full = [gathered(down_weight[0, j].T) for j in range(2)]
    qkv_text, out_text = qkv_here[1], out_weight[0, 1]
    up_text, down_text = up_weight[0, 1], down_weight[0, 1]

    cond_float = conditioning.astype(F32)
    silu_cond = jax.nn.silu(cond_float).astype(BF).reshape(micros * seqs, -1)
    ada_part = jnp.einsum("rc,jck->jrk", silu_cond, ada_weight[0], preferred_element_type=F32)
    mod_piece = mods // ndev
    sharing = [[m * per + u for u in range(per)] for m in range(micros)]
    shares = per * ntensor
    share = mods // shares
    bias_full = gather_both(biases[0]).transpose(1, 0, 2).reshape(2, -1).astype(F32)
    ada_sent = (
        ada_part.astype(BF)
        .reshape(2, micros, seqs, shares, share)
        .transpose(1, 3, 0, 2, 4)
        .reshape(ndev, table_rows, share)
    )
    ada_sum = jnp.sum(lax.all_to_all(ada_sent, BOTH, 0, 0).astype(F32), axis=0)
    share_bias = lax.dynamic_slice_in_dim(bias_full[:, :mods], (side * ntensor + tensor) * share, share, 1)
    table_part = (ada_sum.reshape(2, seqs, share) + share_bias[:, None]).astype(BF)
    table = lax.all_gather(
        lax.all_gather(table_part.reshape(table_rows, share), "tensor"),
        "context",
        axis_index_groups=sharing,
    )
    table = table.reshape(shares, table_rows, share).transpose(1, 0, 2).reshape(table_rows, mods)
    query_bias = lax.dynamic_slice_in_dim(bias_full, mods + tensor * local, local, 1)
    value_bias = lax.dynamic_slice_in_dim(bias_full, mods + width + tensor * local, local, 1)
    qkv_bias = jnp.concatenate(
        (
            query_bias.reshape(2, groups, group),
            jnp.zeros((2, groups, group), F32),
            value_bias.reshape(2, groups, group),
        ),
        axis=2,
    ).reshape(2, 3 * local)
    out_bias = bias_full[:, mods + 2 * width : mods + 3 * width]
    up_bias = lax.dynamic_slice_in_dim(bias_full, mods + 3 * width + tensor * hidden, hidden, 1)
    down_bias = bias_full[:, mods + 3 * width + hidden * ntensor :]

    def by_modality(pair):
        return jnp.concatenate(
            (
                jnp.broadcast_to(pair[0][None], (rows_image, width)),
                jnp.broadcast_to(pair[1][None], (rows_text, width)),
            ),
            0,
        )

    def ids_of(work_context):
        m, u = work_context // per, work_context % per
        found = []
        for ids, own in ((image_seq_ids, own_image), (text_seq_ids, own_text)):
            table_ids = lax.dynamic_index_in_dim(ids, m, 0, keepdims=False).reshape(ndev, own)
            homes = jnp.stack([u * micros + (m - step) % micros for step in range(micros)])
            places = homes[None, :] * ntensor + (tensor ^ jnp.array(order))[:, None]
            found.append(jnp.take(table_ids, places.reshape(-1), axis=0).reshape(-1))
        return found

    own_found = ids_of(context)
    own_ids = jnp.concatenate((own_found[0][:rows_image], own_found[1][:rows_text] + seqs))
    onehot = (own_ids[:, None] == jnp.arange(table_rows)[None, :]).astype(BF)
    row_mods = dot_nn(onehot, table).astype(BF)
    joint_ids = jnp.concatenate(own_found)
    if paired:
        attn_ids = jnp.concatenate([joint_ids] + ids_of(context ^ 1))
    else:
        attn_ids = jnp.concatenate([x for u in range(per) for x in ids_of(micro * per + u)])

    def row_mod(index):
        return row_mods[:, index * width : (index + 1) * width].astype(F32)

    def sided(a, b):
        return jnp.where(side == 0, a, b), jnp.where(side == 0, b, a)

    def attention(joint):
        if paired:
            mine, theirs = sided(joint[:, : 3 * group], joint[:, 3 * group :])
            theirs = swapped(theirs, "context", 1)
            attended, lse = attend_pair(mine, theirs, attn_ids, group_heads)
            here, there = attended[:ctx_rows], swapped(attended[ctx_rows:], "context", 1)
            return jnp.concatenate(sided(here, there), axis=1), (mine, theirs, lse)
        q, k, v = (joint[:, i * group : (i + 1) * group] for i in range(3))
        k, v = (
            lax.all_gather(x, "context", axis=0, tiled=True, axis_index_groups=sharing) for x in (k, v)
        )
        attended, lse = attend(q, k, v, joint_ids, attn_ids, group_heads)
        return attended, (q, k, v, lse)

    def attention_back(grad, kept):
        if paired:
            mine, theirs, lse = kept
            g_mine, g_theirs = sided(grad[:, :group], grad[:, group:])
            g_theirs = swapped(g_theirs, "context", 1)
            d_mine, d_theirs = attend_pair_back(mine, theirs, g_mine, g_theirs, lse, attn_ids, group_heads)
            return jnp.concatenate(sided(d_mine, swapped(d_theirs, "context", 1)), axis=1)
        q, k, v, lse = kept
        dq, dk, dv = attend_back(q, k, v, grad, lse, joint_ids, attn_ids, group_heads)
        dk, dv = (
            lax.psum_scatter(x, "context", scatter_dimension=0, tiled=True, axis_index_groups=sharing)
            for x in (dk, dv)
        )
        return jnp.concatenate((dq, dk, dv), axis=1)

    def forward(x):
        n1, inv1 = normalized(x)
        h1_image, h1_text = spread((n1 * (1.0 + row_mod(1)) + row_mod(0)).astype(BF))
        h1 = [h1_image, text_columns(h1_text)]
        joint = jnp.concatenate(
            (
                (dot_nn(h1_image, qkv_full[0]) + qkv_bias[0]).astype(BF),
                (context_sum(dot_nn(h1[1], qkv_text)) + qkv_bias[1]).astype(BF),
            ),
            0,
        )
        attended, kept = attention(joint)
        attn = [attended[:ctx_image], context_gather(attended[ctx_image:])]
        branch = jnp.concatenate(
            (
                reduce_tensor(dot_nt(attn[0], out_full[0]).astype(BF)),
                text_rows_of(dot_nn(attn[1], out_text)),
            ),
            0,
        ) + by_modality(out_bias)
        middle = x + row_mod(2) * branch
        n2, inv2 = normalized(middle)
        h2_image, h2_text = spread((n2 * (1.0 + row_mod(4)) + row_mod(3)).astype(BF))
        h2 = [h2_image, text_columns(h2_text)]
        act_image, slope_image = gelu_pair(dot_nn(h2[0], up_full[0]) + up_bias[0])
        act_text, slope_text = gelu_pair(context_sum(dot_nn(h2[1], up_text)) + up_bias[1])
        acts = [act_image, context_gather(act_text)]
        down_image = reduce_tensor(dot_nt(act_image, down_full[0]).astype(BF))
        down_text_rows = text_rows_of(dot_nn(acts[1], down_text))
        down = jnp.concatenate((down_image, down_text_rows), 0) + by_modality(down_bias)
        out = middle + row_mod(5) * down
        saved = dict(
            x=x, h1=h1, kept=kept, attn=attn, branch=branch, middle=middle, h2=h2, acts=acts,
            slopes=[slope_image, slope_text], down=down,
        )
        return out, saved

    def chosen(a, b):
        return jax.tree.map(lambda x, y: jnp.where(first, x, y), a, b)

    def backward(saved, g_out, last=None):
        g_down = (row_mod(5) * g_out).astype(BF)
        gd = spread(g_down)
        g_up = [
            (dot_nn(gd[j], down_full[j]) * saved["slopes"][j].astype(F32)).astype(BF) for j in range(2)
        ]
        g_h2 = collect(*(dot_nt(g_up[j], up_full[j]) for j in range(2)))
        early = None
        if last:
            use = chosen(
                dict(h2=saved["h2"][0], acts=saved["acts"][0], gd=gd[0], g_up=g_up[0]),
                {k: last[k][0] for k in ("h2", "acts", "gd", "g_up")},
            )
            early = (dot_tn(use["gd"], use["acts"]), dot_tn(use["h2"], use["g_up"]))
        n2, inv2 = normalized(saved["middle"])
        g_middle = g_out + norm_back(n2, inv2, g_h2 * (1.0 + row_mod(4)))
        g_branch = (row_mod(2) * g_middle).astype(BF)
        gb = spread(g_branch)
        g_attn = jnp.concatenate([dot_nn(gb[j], out_full[j]).astype(BF) for j in range(2)], 0)
        g_joint = attention_back(g_attn, saved["kept"])
        g_qkv = [g_joint[:ctx_image], g_joint[ctx_image:]]
        g_h1 = collect(*(dot_nt(g_qkv[j], qkv_full[j]) for j in range(2)))
        n1, inv1 = normalized(saved["x"])
        g_x = g_middle + norm_back(n1, inv1, g_h1 * (1.0 + row_mod(1)))
        row_grads = jnp.concatenate(
            [
                part.astype(BF)
                for part in (
                    g_h1, g_h1 * n1, g_middle * saved["branch"], g_h2, g_h2 * n2, g_out * saved["down"]
                )
            ],
            axis=1,
        )
        mod_grad = dot_tn(onehot, row_grads)
        tensors = dict(
            h1=saved["h1"], g_qkv=g_qkv, attn=saved["attn"], gb=gb, h2=saved["h2"], g_up=g_up,
            acts=saved["acts"], gd=gd, g_down=g_down, g_branch=g_branch, mod=mod_grad,
        )
        return g_x, tensors, early

    def handed(rows, by):
        return lax.ppermute(rows.astype(BF), "section", [(0, 1)] if by > 0 else [(1, 0)]).astype(F32)

    out_first, saved_first = forward(to_work(image_tokens, text_tokens))
    out_last, saved_last = forward(handed(out_first, 1))
    grad_last, tensors_last, unused = backward(saved_last, to_work(image_cotangent, text_cotangent))
    grad_first, tensors_first, early = backward(saved_first, handed(grad_last, -1), tensors_last)
    out = to_home(jnp.where(first, out_first, out_last))
    grad = to_home(jnp.where(first, grad_first, grad_last))
    use = chosen(tensors_first, tensors_last)

    def scattered(full):
        return lax.psum_scatter(full.astype(BF), "context", scatter_dimension=0, tiled=True)

    def qkv_order_back(w):
        return (
            w.reshape(depth, groups, 3, group_heads, HEAD).transpose(0, 1, 3, 2, 4).reshape(depth, 3 * local)
        )

    down_shard, up_shard = scattered(early[0]), scattered(early[1])
    down_image_grad = down_shard.astype(F32).T
    up_image_grad = up_shard.astype(F32)
    out_image_grad = scattered(dot_tn(use["gb"][0], use["attn"][0])).astype(F32).T
    qkv_image_grad = qkv_order_back(scattered(dot_tn(use["h1"][0], use["g_qkv"][0])).astype(F32))

    def blocks(rows):
        return rows.reshape(ctx_text, ncontext, depth).transpose(1, 0, 2)

    def copies(rows):
        return jnp.broadcast_to(rows[None], (ncontext,) + rows.shape)

    text_sent = jnp.concatenate(
        (blocks(use["gd"][1]), blocks(use["gb"][1]), copies(use["g_up"][1]), copies(use["g_qkv"][1])), axis=2
    )
    text_got = lax.all_to_all(after(text_sent, grad_first), "context", 0, 0).reshape(text_all, -1)
    at_up, at_qkv = 2 * depth, 2 * depth + hidden
    down_text_grad = dot_tn(use["acts"][1], text_got[:, :depth])
    out_text_grad = dot_tn(use["attn"][1], text_got[:, depth:at_up])
    up_text_grad = dot_tn(use["h2"][1], text_got[:, at_up:at_qkv])
    qkv_text_grad = qkv_order_back(dot_tn(use["h1"][1], text_got[:, at_qkv:]))
    down_grad = jnp.stack((down_image_grad, down_text_grad))
    up_grad = jnp.stack((up_image_grad, up_text_grad))
    out_grad = jnp.stack((out_image_grad, out_text_grad))
    qkv_grad = jnp.stack((qkv_image_grad, qkv_text_grad))

    def column_sums(parts):
        return jnp.stack([jnp.sum(p.astype(F32), axis=0) for p in parts])

    def own_sums(rows):
        return column_sums((rows[:rows_image], rows[rows_image:]))

    qkv_sums = column_sums(use["g_qkv"]).reshape(2, groups, 3, group)
    bias_part = jnp.zeros((2, bias_here * ndev), F32)
    for at, value in (
        (0, jnp.sum(use["mod"].reshape(2, seqs, mods), axis=1)),
        (mods + tensor * local, qkv_sums[:, :, 0].reshape(2, local)),
        (mods + width + tensor * local, qkv_sums[:, :, 2].reshape(2, local)),
        (mods + 2 * width, own_sums(use["g_branch"])),
        (mods + 3 * width + tensor * hidden, column_sums(use["g_up"])),
        (mods + 3 * width + ntensor * hidden, own_sums(use["g_down"])),
    ):
        bias_part = lax.dynamic_update_slice_in_dim(bias_part, value, at, 1)
    sent = jnp.concatenate(
        (
            use["mod"].reshape(table_rows, ndev, mod_piece).transpose(1, 0, 2).reshape(ndev, -1),
            bias_part.reshape(2, ndev, bias_here).transpose(1, 0, 2).reshape(ndev, -1),
        ),
        axis=1,
    ).astype(BF)
    sent = after(sent, down_shard, up_shard)
    got = lax.all_to_all(sent, BOTH, 0, 0).astype(F32)
    bias_grad = jnp.sum(got[:, table_rows * mod_piece :], axis=0).reshape(2, bias_here)
    mod_sum = jnp.sum(got[:, : table_rows * mod_piece].reshape(micros, ndev // micros, -1), axis=1)
    mod_all = (
        gather_both(mod_sum.astype(BF))
        .reshape(ndev, micros, 2, seqs, mod_piece)
        .transpose(2, 1, 3, 0, 4)
        .reshape(2, micros * seqs, mods)
    )
    ada_grad = jnp.einsum("rc,jrk->jck", silu_cond, mod_all, preferred_element_type=F32)
    cond_inner = jnp.einsum("jrk,jck->rc", mod_all, ada_weight[0], preferred_element_type=F32)
    unused, silu_back = jax.vjp(jax.nn.silu, cond_float)
    cond_grad = silu_back(lax.psum(cond_inner, "section").reshape(cond_float.shape))[0]
    return (
        *out,
        *grad,
        cond_grad,
        ada_grad[None],
        qkv_grad[None],
        out_grad[None],
        up_grad[None],
        down_grad[None],
        bias_grad[None],
    )


def solution(mesh):
    tokens = P(None, BOTH, None)
    block_rows = P("section", None, BOTH, None)
    by_rows = P("section", None, "context", "tensor")
    by_cols = P("section", None, "tensor", "context")
    block_biases = P("section", None, BOTH)
    in_specs = (
        tokens,
        tokens,
        P(None, None, BOTH),
        P(),
        P(),
        block_rows,
        by_rows,
        by_cols,
        by_rows,
        by_cols,
        block_biases,
        tokens,
        tokens,
    )
    out_specs = (
        block_rows,
        block_rows,
        block_rows,
        block_rows,
        P(None, None, BOTH),
        block_rows,
        by_rows,
        by_cols,
        by_rows,
        by_cols,
        block_biases,
    )
    return jax.shard_map(shards, mesh=mesh, in_specs=in_specs, out_specs=out_specs, check_vma=False)
```

```python
from functools import partial

import jax
import jax.numpy as jnp
from jax import lax
from jax.experimental import pallas as pl
from jax.experimental.pallas import tpu as pltpu
from jax.sharding import PartitionSpec as P

HEADS = 24
HEAD = 64
NORM_EPS = 1e-06
MASKED = -1e30
BF = jnp.bfloat16
F32 = jnp.float32
BOTH = ("context", "tensor")


def dot_nn(a, b):
    return lax.dot_general(a, b, (((1,), (0,)), ((), ())), preferred_element_type=F32)


def dot_nt(a, b):
    return lax.dot_general(a, b, (((1,), (1,)), ((), ())), preferred_element_type=F32)


def dot_tn(a, b):
    return lax.dot_general(a, b, (((0,), (0,)), ((), ())), preferred_element_type=F32)


def scaled(q):
    return q * jnp.asarray(HEAD**-0.5, BF)


def attend_body(heads, chunk, places, q_ref, k_ref, v_ref, idq_ref, idk_ref, store, lse_ref):
    at_q, at_k, at_v = places

    def one_chunk(step, carry):
        rows = pl.ds(pl.multiple_of(step * chunk, chunk), chunk)
        bias = jnp.where(idk_ref[...] == idq_ref[:, rows], 0.0, MASKED)
        outs = []
        for head in range(heads):
            at = head * HEAD
            q = scaled(q_ref[rows, at_q + at : at_q + at + HEAD])
            scores = dot_nt(k_ref[:, at_k + at : at_k + at + HEAD], q) + bias
            top = jnp.max(scores, axis=0, keepdims=True)
            weights = jnp.exp(scores - top)
            total = jnp.sum(weights, axis=0, keepdims=True)
            summed = dot_tn(v_ref[:, at_v + at : at_v + at + HEAD], weights.astype(BF))
            outs.append((summed / total).T)
            lse_ref[head : head + 1, rows] = top + jnp.log(total)
        store(rows, jnp.concatenate(outs, axis=1).astype(BF))
        return carry

    lax.fori_loop(0, idq_ref.shape[1] // chunk, one_chunk, 0)


def attend_back_body(
    heads, chunk, places, q_ref, k_ref, v_ref, g_ref, lse_ref, idq_ref, idk_ref, store_dq, dk_acc, dv_acc
):
    at_q, at_k, at_v = places
    dk_acc[...] = jnp.zeros_like(dk_acc)
    dv_acc[...] = jnp.zeros_like(dv_acc)

    def one_chunk(step, carry):
        rows = pl.ds(pl.multiple_of(step * chunk, chunk), chunk)
        bias = jnp.where(idk_ref[...] == idq_ref[:, rows], 0.0, MASKED)
        grads = []
        for head in range(heads):
            at = head * HEAD
            q = scaled(q_ref[rows, at_q + at : at_q + at + HEAD])
            g = g_ref[rows, at : at + HEAD]
            k = k_ref[:, at_k + at : at_k + at + HEAD]
            probs = jnp.exp(dot_nt(k, q) + bias - lse_ref[head : head + 1, rows])
            dv_acc[head] += dot_nn(probs.astype(BF), g)
            both = probs * dot_nt(v_ref[:, at_v + at : at_v + at + HEAD], g)
            delta = jnp.sum(both, axis=0, keepdims=True)
            dscores = (both - probs * delta).astype(BF)
            dk_acc[head] += dot_nn(dscores, q)
            grads.append((dot_tn(k, dscores) * HEAD**-0.5).T)
        store_dq(rows, jnp.concatenate(grads, axis=1).astype(BF))
        return carry

    lax.fori_loop(0, idq_ref.shape[1] // chunk, one_chunk, 0)


def heads_of(acc):
    return jnp.concatenate([acc[head] for head in range(acc.shape[0])], axis=1).astype(BF)


def attend_costs(queries, keys, heads, factor):
    return pl.CostEstimate(
        flops=factor * queries * keys * heads * HEAD,
        bytes_accessed=2 * (queries + 2 * keys) * heads * HEAD * factor // 4,
        transcendentals=queries * keys * heads,
    )


def chunk_for(keys):
    return 256 if keys <= 1024 else 128


VMEM_LIMIT = pltpu.CompilerParams(vmem_limit_bytes=56 * 2**20)


def attend(q, k, v, ids_q, ids_k, heads):
    queries, keys = q.shape[0], k.shape[0]

    def kernel(q_ref, k_ref, v_ref, idq_ref, idk_ref, out_ref, lse_ref):
        def store(rows, value):
            out_ref[rows, :] = value

        attend_body(
            heads, chunk_for(keys), (0, 0, 0), q_ref, k_ref, v_ref, idq_ref, idk_ref, store, lse_ref
        )

    return pl.pallas_call(
        kernel,
        out_shape=(
            jax.ShapeDtypeStruct((queries, heads * HEAD), BF),
            jax.ShapeDtypeStruct((heads, queries), F32),
        ),
        compiler_params=VMEM_LIMIT,
        cost_estimate=attend_costs(queries, keys, heads, 4),
    )(q, k, v, ids_q.reshape(1, queries), ids_k.reshape(keys, 1))


def attend_back(q, k, v, g, lse, ids_q, ids_k, heads):
    queries, keys = q.shape[0], k.shape[0]

    def kernel(
        q_ref, k_ref, v_ref, g_ref, lse_ref, idq_ref, idk_ref, dq_ref, dk_ref, dv_ref, dk_acc, dv_acc
    ):
        def store(rows, value):
            dq_ref[rows, :] = value

        attend_back_body(
            heads, chunk_for(keys), (0, 0, 0), q_ref, k_ref, v_ref, g_ref, lse_ref, idq_ref, idk_ref,
            store, dk_acc, dv_acc,
        )
        dk_ref[...] = heads_of(dk_acc)
        dv_ref[...] = heads_of(dv_acc)

    return pl.pallas_call(
        kernel,
        out_shape=(
            jax.ShapeDtypeStruct((queries, heads * HEAD), BF),
            jax.ShapeDtypeStruct((keys, heads * HEAD), BF),
            jax.ShapeDtypeStruct((keys, heads * HEAD), BF),
        ),
        scratch_shapes=[pltpu.VMEM((heads, keys, HEAD), F32), pltpu.VMEM((heads, keys, HEAD), F32)],
        compiler_params=VMEM_LIMIT,
        cost_estimate=attend_costs(queries, keys, heads, 10),
    )(q, k, v, g, lse, ids_q.reshape(1, queries), ids_k.reshape(keys, 1))


def attend_pair(mine, theirs, ids, heads):
    half, wide = mine.shape
    rows_all, group = 2 * half, heads * HEAD

    def kernel(mine_ref, theirs_ref, idq_ref, idk_ref, out_ref, lse_ref, x_ref):
        x_ref[:half] = mine_ref[...]
        x_ref[half:] = theirs_ref[...]

        def store(rows, value):
            out_ref[rows, :] = value

        attend_body(
            heads, 256, (0, group, 2 * group), x_ref, x_ref, x_ref, idq_ref, idk_ref, store, lse_ref
        )

    return pl.pallas_call(
        kernel,
        out_shape=(
            jax.ShapeDtypeStruct((rows_all, group), BF),
            jax.ShapeDtypeStruct((heads, rows_all), F32),
        ),
        scratch_shapes=[pltpu.VMEM((rows_all, wide), BF)],
        compiler_params=VMEM_LIMIT,
        cost_estimate=attend_costs(rows_all, rows_all, heads, 4),
    )(mine, theirs, ids.reshape(1, rows_all), ids.reshape(rows_all, 1))


def attend_pair_back(mine, theirs, g_mine, g_theirs, lse, ids, heads):
    half, wide = mine.shape
    rows_all, group = 2 * half, heads * HEAD

    def kernel(
        mine_ref, theirs_ref, gm_ref, gt_ref, lse_ref, idq_ref, idk_ref, dmine_ref, dtheirs_ref,
        x_ref, g_ref, dq_acc, dk_acc, dv_acc,
    ):
        x_ref[:half] = mine_ref[...]
        x_ref[half:] = theirs_ref[...]
        g_ref[:half] = gm_ref[...]
        g_ref[half:] = gt_ref[...]

        def store(rows, value):
            dq_acc[rows, :] = value

        attend_back_body(
            heads, 256, (0, group, 2 * group), x_ref, x_ref, x_ref, g_ref, lse_ref, idq_ref, idk_ref,
            store, dk_acc, dv_acc,
        )
        grads = jnp.concatenate((dq_acc[...], heads_of(dk_acc), heads_of(dv_acc)), axis=1)
        dmine_ref[...] = grads[:half]
        dtheirs_ref[...] = grads[half:]

    return pl.pallas_call(
        kernel,
        out_shape=(jax.ShapeDtypeStruct((half, wide), BF), jax.ShapeDtypeStruct((half, wide), BF)),
        scratch_shapes=[
            pltpu.VMEM((rows_all, wide), BF),
            pltpu.VMEM((rows_all, group), BF),
            pltpu.VMEM((rows_all, group), BF),
            pltpu.VMEM((heads, rows_all, HEAD), F32),
            pltpu.VMEM((heads, rows_all, HEAD), F32),
        ],
        compiler_params=VMEM_LIMIT,
        cost_estimate=attend_costs(rows_all, rows_all, heads, 10),
    )(mine, theirs, g_mine, g_theirs, lse, ids.reshape(1, rows_all), ids.reshape(rows_all, 1))


def after(x, *others):
    anywhere = pl.BlockSpec(memory_space=pl.ANY)

    def kernel(*refs):
        pass

    return pl.pallas_call(
        kernel,
        out_shape=jax.ShapeDtypeStruct(x.shape, x.dtype),
        in_specs=[anywhere] * (1 + len(others)),
        out_specs=anywhere,
        input_output_aliases={0: 0},
    )(x, *others)


def normalized(x):
    centred = x - jnp.mean(x, axis=-1, keepdims=True)
    inverse = lax.rsqrt(jnp.mean(centred * centred, axis=-1, keepdims=True) + NORM_EPS)
    return centred * inverse, inverse


def norm_back(n, inverse, w):
    return (w - jnp.mean(w, axis=-1, keepdims=True) - n * jnp.mean(w * n, axis=-1, keepdims=True)) * inverse


def gelu_pair(u):
    c = 0.7978845608028654
    inner = jnp.tanh(c * (u + 0.044715 * u * u * u))
    value = 0.5 * u * (1.0 + inner)
    slope = 0.5 * (1.0 + inner) + 0.5 * u * (1.0 - inner * inner) * c * (1.0 + 3 * 0.044715 * u * u)
    return value.astype(BF), slope.astype(BF)


def shards(
    image_tokens,
    text_tokens,
    conditioning,
    image_seq_ids,
    text_seq_ids,
    ada_weight,
    qkv_weight,
    out_weight,
    up_weight,
    down_weight,
    biases,
    image_cotangent,
    text_cotangent,
):
    section = lax.axis_index("section")
    context = lax.axis_index("context")
    tensor = lax.axis_index("tensor")
    ncontext = lax.axis_size("context")
    ntensor = lax.axis_size("tensor")
    ndev = ncontext * ntensor
    first = section == 0
    micros, own_image, width = image_tokens.shape
    own_text = text_tokens.shape[1]
    seqs = conditioning.shape[1]
    rows_image, rows_text = micros * own_image, micros * own_text
    heads_here = HEADS // ntensor
    local = heads_here * HEAD
    hidden = up_weight.shape[3]
    bias_here = biases.shape[2]
    depth = qkv_weight.shape[2]
    mods = 6 * width
    table_rows = 2 * seqs
    per = ncontext // micros
    micro = context // per
    paired = per == 2 and heads_here % 2 == 0
    groups = 2 if paired else 1
    group_heads = heads_here // groups
    group = group_heads * HEAD
    side = context % per
    ctx_image, ctx_text = ntensor * rows_image, ntensor * rows_text
    ctx_rows = ctx_image + ctx_text
    text_all = ncontext * ctx_text

    order = (0, 2, 1, 3)

    def swapped(x, axis, bit):
        return lax.ppermute(x, axis, [(i, i ^ bit) for i in range(lax.axis_size(axis))])

    def near(x):
        return swapped(x, "tensor", 1)

    def far(x):
        return swapped(x, "tensor", 2)

    def gather_tensor(x):
        beside = near(x)
        across = far(x)
        return x, across, beside, near(across)

    def reduce_tensor(x):
        n = x.shape[0] // 4
        got = near(x[2 * n :])
        mine = x[: 2 * n].astype(F32) + got.astype(F32)
        return mine[:n] + far(mine[n:].astype(BF)).astype(F32)

    def spread(rows):
        parts = gather_tensor(rows)
        return [
            jnp.concatenate([p[:rows_image] for p in parts], 0),
            jnp.concatenate([p[rows_image:] for p in parts], 0),
        ]

    def collect(image_rows, text_rows):
        return jnp.concatenate(
            (reduce_tensor(image_rows.astype(BF)), reduce_tensor(text_rows.astype(BF))), 0
        )

    def text_columns(rows):
        sent = rows.reshape(ctx_text, ncontext, depth).transpose(1, 0, 2)
        return lax.all_to_all(sent, "context", 0, 0).reshape(text_all, depth)

    def text_rows_of(partial_sums):
        turned = (
            partial_sums.astype(BF)
            .reshape(ncontext, ntensor, rows_text, depth)
            .transpose(1, 0, 2, 3)
            .reshape(ntensor * ncontext * rows_text, depth)
        )
        mine = reduce_tensor(turned).astype(BF).reshape(ncontext, rows_text, depth)
        got = lax.all_to_all(mine, "context", 0, 0)
        return got.transpose(1, 0, 2).reshape(rows_text, width).astype(F32)

    def context_sum(partial_sums):
        sent = partial_sums.astype(BF).reshape(ncontext, ctx_text, -1)
        return jnp.sum(lax.all_to_all(sent, "context", 0, 0).astype(F32), axis=0)

    def context_gather(rows):
        sent = jnp.broadcast_to(rows[None], (ncontext,) + rows.shape)
        return lax.all_to_all(sent, "context", 0, 0).reshape(text_all, rows.shape[1])

    def gather_both(x):
        got = lax.all_gather(lax.all_gather(x, "tensor"), "context")
        return got.reshape((ndev,) + x.shape)

    def rounds(step, back):
        pairs = []
        for h in range(ncontext):
            m = (h + step) % micros
            pairs.append((h, m * per + h // micros))
        return [(b, a) for a, b in pairs] if back else pairs

    def to_work(image, text):
        pieces = []
        for step in range(micros):
            m = (context + step) % micros
            pieces.append(
                [
                    lax.ppermute(
                        lax.dynamic_index_in_dim(x, m, 0, keepdims=False), "context", rounds(step, False)
                    )
                    for x in (image, text)
                ]
            )
        return jnp.concatenate([p[0] for p in pieces] + [p[1] for p in pieces], 0).astype(F32)

    def to_home(rows):
        image, text = [], []
        for step in range(micros):
            image.append(
                lax.ppermute(
                    rows[step * own_image : (step + 1) * own_image], "context", rounds(step, True)
                )
            )
            at = rows_image + step * own_text
            text.append(lax.ppermute(rows[at : at + own_text], "context", rounds(step, True)))
        image, text = jnp.stack(image), jnp.stack(text)
        turns = [(m - context) % micros for m in range(micros)]
        return tuple(
            jnp.stack([lax.dynamic_index_in_dim(x, turn, 0, keepdims=False) for turn in turns])[None]
            for x in (image, text)
        )

    def gathered(w):
        return lax.all_gather(w, "context", axis=0, tiled=True)

    def qkv_order(w):
        return (
            w.reshape(depth, groups, group_heads, 3, HEAD).transpose(0, 1, 3, 2, 4).reshape(depth, 3 * local)
        )

    qkv_here = [qkv_order(qkv_weight[0, j]) for j in range(2)]
    qkv_full = gathered(qkv_here[0])
    out_full = gathered(out_weight[0, 0].T)
    up_full = gathered(up_weight[0, 0])
    down_full = gathered(down_weight[0, 0].T)
    qkv_text, out_text = qkv_here[1], out_weight[0, 1]
    up_text, down_text = up_weight[0, 1], down_weight[0, 1]

    cond_float = conditioning.astype(F32)
    silu_cond = jax.nn.silu(cond_float).astype(BF).reshape(micros * seqs, -1)
    ada_part = jnp.einsum("rc,jck->jrk", silu_cond, ada_weight[0], preferred_element_type=F32)
    mod_piece = mods // ndev
    sharing = [[m * per + u for u in range(per)] for m in range(micros)]
    shares = per * ntensor
    share = mods // shares
    bias_full = gather_both(biases[0]).transpose(1, 0, 2).reshape(2, -1).astype(F32)
    bias_placed = lax.dynamic_update_slice_in_dim(
        jnp.zeros((2, bias_here * ndev), F32),
        biases[0].astype(F32),
        (context * ntensor + tensor) * bias_here,
        1,
    )
    ada_sent = (
        (ada_part + bias_placed[:, None, :mods])
        .astype(BF)
        .reshape(2, micros, seqs, shares, share)
        .transpose(1, 3, 0, 2, 4)
        .reshape(ndev, table_rows, share)
    )
    ada_sum = jnp.sum(lax.all_to_all(ada_sent, BOTH, 0, 0).astype(F32), axis=0)
    table = lax.all_gather(
        lax.all_gather(ada_sum.astype(BF), "tensor"),
        "context",
        axis_index_groups=sharing,
    )
    table = table.reshape(shares, table_rows, share).transpose(1, 0, 2).reshape(table_rows, mods)
    query_bias = lax.dynamic_slice_in_dim(bias_full, mods + tensor * local, local, 1)
    value_bias = lax.dynamic_slice_in_dim(bias_full, mods + width + tensor * local, local, 1)
    qkv_bias = jnp.concatenate(
        (
            query_bias.reshape(2, groups, group),
            jnp.zeros((2, groups, group), F32),
            value_bias.reshape(2, groups, group),
        ),
        axis=2,
    ).reshape(2, 3 * local)
    out_bias = bias_full[:, mods + 2 * width : mods + 3 * width]
    up_bias = lax.dynamic_slice_in_dim(bias_full, mods + 3 * width + tensor * hidden, hidden, 1)
    down_bias = bias_full[:, mods + 3 * width + hidden * ntensor :]

    def by_modality(pair):
        return jnp.concatenate(
            (
                jnp.broadcast_to(pair[0][None], (rows_image, width)),
                jnp.broadcast_to(pair[1][None], (rows_text, width)),
            ),
            0,
        )

    def ids_of(work_context):
        m, u = work_context // per, work_context % per
        found = []
        for ids, own in ((image_seq_ids, own_image), (text_seq_ids, own_text)):
            table_ids = lax.dynamic_index_in_dim(ids, m, 0, keepdims=False).reshape(ndev, own)
            homes = jnp.stack([u * micros + (m - step) % micros for step in range(micros)])
            places = homes[None, :] * ntensor + (tensor ^ jnp.array(order))[:, None]
            found.append(jnp.take(table_ids, places.reshape(-1), axis=0).reshape(-1))
        return found

    own_found = ids_of(context)
    own_ids = jnp.concatenate((own_found[0][:rows_image], own_found[1][:rows_text] + seqs))
    onehot = (own_ids[:, None] == jnp.arange(table_rows)[None, :]).astype(BF)
    row_mods = dot_nn(onehot, table).astype(BF)
    joint_ids = jnp.concatenate(own_found)
    if paired:
        attn_ids = jnp.concatenate([joint_ids] + ids_of(context ^ 1))
    else:
        attn_ids = jnp.concatenate([x for u in range(per) for x in ids_of(micro * per + u)])

    def row_mod(index):
        return row_mods[:, index * width : (index + 1) * width].astype(F32)

    def sided(a, b):
        return jnp.where(side == 0, a, b), jnp.where(side == 0, b, a)

    def attention(joint):
        if paired:
            mine, theirs = sided(joint[:, : 3 * group], joint[:, 3 * group :])
            theirs = swapped(theirs, "context", 1)
            attended, lse = attend_pair(mine, theirs, attn_ids, group_heads)
            here, there = attended[:ctx_rows], swapped(attended[ctx_rows:], "context", 1)
            return jnp.concatenate(sided(here, there), axis=1), (mine, theirs, lse)
        q, k, v = (joint[:, i * group : (i + 1) * group] for i in range(3))
        k, v = (
            lax.all_gather(x, "context", axis=0, tiled=True, axis_index_groups=sharing) for x in (k, v)
        )
        attended, lse = attend(q, k, v, joint_ids, attn_ids, group_heads)
        return attended, (q, k, v, lse)

    def attention_back(grad, kept):
        if paired:
            mine, theirs, lse = kept
            g_mine, g_theirs = sided(grad[:, :group], grad[:, group:])
            g_theirs = swapped(g_theirs, "context", 1)
            d_mine, d_theirs = attend_pair_back(mine, theirs, g_mine, g_theirs, lse, attn_ids, group_heads)
            return jnp.concatenate(sided(d_mine, swapped(d_theirs, "context", 1)), axis=1)
        q, k, v, lse = kept
        dq, dk, dv = attend_back(q, k, v, grad, lse, joint_ids, attn_ids, group_heads)
        dk, dv = (
            lax.psum_scatter(x, "context", scatter_dimension=0, tiled=True, axis_index_groups=sharing)
            for x in (dk, dv)
        )
        return jnp.concatenate((dq, dk, dv), axis=1)

    def forward(x):
        n1, inv1 = normalized(x)
        h1_image, h1_text = spread((n1 * (1.0 + row_mod(1)) + row_mod(0)).astype(BF))
        h1 = [h1_image, text_columns(h1_text)]
        joint = jnp.concatenate(
            (
                (dot_nn(h1_image, qkv_full) + qkv_bias[0]).astype(BF),
                (context_sum(dot_nn(h1[1], qkv_text)) + qkv_bias[1]).astype(BF),
            ),
            0,
        )
        attended, kept = attention(joint)
        attn = [attended[:ctx_image], context_gather(attended[ctx_image:])]
        branch = jnp.concatenate(
            (
                reduce_tensor(dot_nt(attn[0], out_full).astype(BF)),
                text_rows_of(dot_nn(attn[1], out_text)),
            ),
            0,
        ) + by_modality(out_bias)
        middle = x + row_mod(2) * branch
        n2, inv2 = normalized(middle)
        h2_image, h2_text = spread((n2 * (1.0 + row_mod(4)) + row_mod(3)).astype(BF))
        h2 = [h2_image, text_columns(h2_text)]
        act_image, slope_image = gelu_pair(dot_nn(h2[0], up_full) + up_bias[0])
        act_text, slope_text = gelu_pair(context_sum(dot_nn(h2[1], up_text)) + up_bias[1])
        acts = [act_image, context_gather(act_text)]
        down_image = reduce_tensor(dot_nt(act_image, down_full).astype(BF))
        down_text_rows = text_rows_of(dot_nn(acts[1], down_text))
        down = jnp.concatenate((down_image, down_text_rows), 0) + by_modality(down_bias)
        out = middle + row_mod(5) * down
        saved = dict(
            x=x, h1=h1, kept=kept, attn=attn, branch=branch, middle=middle, h2=h2, acts=acts,
            slopes=[slope_image, slope_text], down=down,
        )
        return out, saved

    def chosen(a, b):
        return jax.tree.map(lambda x, y: jnp.where(first, x, y), a, b)

    def backward(saved, g_out, last=None):
        g_down = (row_mod(5) * g_out).astype(BF)
        gd_image, gd_text = spread(g_down)
        gd = [gd_image, text_columns(gd_text)]
        g_up_image = (dot_nn(gd_image, down_full) * saved["slopes"][0].astype(F32)).astype(BF)
        g_up_text = (context_sum(dot_nt(gd[1], down_text)) * saved["slopes"][1].astype(F32)).astype(BF)
        g_up = [g_up_image, context_gather(g_up_text)]
        g_h2_image = reduce_tensor(dot_nt(g_up_image, up_full).astype(BF))
        up_part = None
        if last:
            mine = chosen(dict(h2=saved["h2"][0], g_up=g_up_image), dict(h2=last["h2"][0], g_up=last["g_up"][0]))
            up_part = dot_tn(mine["h2"], mine["g_up"]).astype(BF)
            g_h2_image = after(g_h2_image, up_part)
        g_h2 = jnp.concatenate((g_h2_image, text_rows_of(dot_nt(g_up[1], up_text))), 0)
        n2, inv2 = normalized(saved["middle"])
        g_middle = g_out + norm_back(n2, inv2, g_h2 * (1.0 + row_mod(4)))
        g_branch = (row_mod(2) * g_middle).astype(BF)
        gb_image, gb_text = spread(g_branch)
        gb = [gb_image, text_columns(gb_text)]
        g_attn = jnp.concatenate(
            (
                dot_nn(gb_image, out_full).astype(BF),
                context_sum(dot_nt(gb[1], out_text)).astype(BF),
            ),
            0,
        )
        g_joint = attention_back(g_attn, saved["kept"])
        g_qkv = [g_joint[:ctx_image], context_gather(g_joint[ctx_image:])]
        g_h1 = jnp.concatenate(
            (
                reduce_tensor(dot_nt(g_qkv[0], qkv_full).astype(BF)),
                text_rows_of(dot_nt(g_qkv[1], qkv_text)),
            ),
            0,
        )
        n1, inv1 = normalized(saved["x"])
        g_x = g_middle + norm_back(n1, inv1, g_h1 * (1.0 + row_mod(1)))
        row_grads = jnp.concatenate(
            [
                part.astype(BF)
                for part in (
                    g_h1, g_h1 * n1, g_middle * saved["branch"], g_h2, g_h2 * n2, g_out * saved["down"]
                )
            ],
            axis=1,
        )
        mod_grad = dot_tn(onehot, row_grads)
        tensors = dict(
            h1=saved["h1"], g_qkv=g_qkv, attn=saved["attn"], gb=gb, h2=saved["h2"], g_up=g_up,
            acts=saved["acts"], gd=gd, g_down=g_down, g_branch=g_branch, mod=mod_grad,
            g_up_text=g_up_text, g_qkv_text=g_joint[ctx_image:],
        )
        return g_x, tensors, up_part

    def handed(rows, by):
        return lax.ppermute(rows.astype(BF), "section", [(0, 1)] if by > 0 else [(1, 0)]).astype(F32)

    out_first, saved_first = forward(to_work(image_tokens, text_tokens))
    out_last, saved_last = forward(handed(out_first, 1))
    grad_last, tensors_last, unused = backward(saved_last, to_work(image_cotangent, text_cotangent))
    grad_first, tensors_first, up_part = backward(saved_first, handed(grad_last, -1), tensors_last)
    out = to_home(jnp.where(first, out_first, out_last))
    grad = to_home(jnp.where(first, grad_first, grad_last))
    use = chosen(tensors_first, tensors_last)

    def scattered(full):
        return lax.psum_scatter(full.astype(BF), "context", scatter_dimension=0, tiled=True)

    def qkv_order_back(w):
        return (
            w.reshape(depth, groups, 3, group_heads, HEAD).transpose(0, 1, 3, 2, 4).reshape(depth, 3 * local)
        )

    def columns(rows):
        sent = rows.reshape(rows.shape[0], ncontext, depth).transpose(1, 0, 2)
        return lax.all_to_all(sent, "context", 0, 0).reshape(ncontext * rows.shape[0], depth)

    up_shard = scattered(up_part)
    out_shard = scattered(dot_tn(use["gb"][0], use["attn"][0]))
    qkv_shard = scattered(dot_tn(use["h1"][0], use["g_qkv"][0]))
    acts_all = gathered(jnp.where(first, saved_first["acts"][0], saved_last["acts"][0]))
    down_grad = jnp.stack(
        (dot_tn(acts_all, columns(use["gd"][0])), dot_tn(use["acts"][1], use["gd"][1]))
    )
    up_grad = jnp.stack((up_shard.astype(F32), dot_tn(use["h2"][1], use["g_up"][1])))
    out_grad = jnp.stack((out_shard.astype(F32).T, dot_tn(use["attn"][1], use["gb"][1])))
    qkv_grad = jnp.stack(
        [qkv_order_back(w) for w in (qkv_shard.astype(F32), dot_tn(use["h1"][1], use["g_qkv"][1]))]
    )

    def column_sums(parts):
        return jnp.stack([jnp.sum(p.astype(F32), axis=0) for p in parts])

    def own_sums(rows):
        return column_sums((rows[:rows_image], rows[rows_image:]))

    qkv_sums = column_sums((use["g_qkv"][0], use["g_qkv_text"])).reshape(2, groups, 3, group)
    bias_part = jnp.zeros((2, bias_here * ndev), F32)
    for at, value in (
        (0, jnp.sum(use["mod"].reshape(2, seqs, mods), axis=1)),
        (mods + tensor * local, qkv_sums[:, :, 0].reshape(2, local)),
        (mods + width + tensor * local, qkv_sums[:, :, 2].reshape(2, local)),
        (mods + 2 * width, own_sums(use["g_branch"])),
        (mods + 3 * width + tensor * hidden, column_sums((use["g_up"][0], use["g_up_text"]))),
        (mods + 3 * width + ntensor * hidden, own_sums(use["g_down"])),
    ):
        bias_part = lax.dynamic_update_slice_in_dim(bias_part, value, at, 1)
    sent = jnp.concatenate(
        (
            use["mod"].reshape(table_rows, ndev, mod_piece).transpose(1, 0, 2).reshape(ndev, -1),
            bias_part.reshape(2, ndev, bias_here).transpose(1, 0, 2).reshape(ndev, -1),
        ),
        axis=1,
    ).astype(BF)
    sent = after(sent, up_shard)
    got = lax.all_to_all(sent, BOTH, 0, 0).astype(F32)
    bias_grad = jnp.sum(got[:, table_rows * mod_piece :], axis=0).reshape(2, bias_here)
    mod_sum = jnp.sum(got[:, : table_rows * mod_piece].reshape(micros, ndev // micros, -1), axis=1)
    mod_all = (
        gather_both(mod_sum.astype(BF))
        .reshape(ndev, micros, 2, seqs, mod_piece)
        .transpose(2, 1, 3, 0, 4)
        .reshape(2, micros * seqs, mods)
    )
    ada_grad = jnp.einsum("rc,jrk->jck", silu_cond, mod_all, preferred_element_type=F32)
    cond_inner = jnp.einsum("jrk,jck->rc", mod_all, ada_weight[0], preferred_element_type=F32)
    unused, silu_back = jax.vjp(jax.nn.silu, cond_float)
    cond_grad = silu_back(lax.psum(cond_inner, "section").reshape(cond_float.shape))[0]
    return (
        *out,
        *grad,
        cond_grad,
        ada_grad[None],
        qkv_grad[None],
        out_grad[None],
        up_grad[None],
        down_grad[None],
        bias_grad[None],
    )


def solution(mesh):
    tokens = P(None, BOTH, None)
    block_rows = P("section", None, BOTH, None)
    by_rows = P("section", None, "context", "tensor")
    by_cols = P("section", None, "tensor", "context")
    block_biases = P("section", None, BOTH)
    in_specs = (
        tokens,
        tokens,
        P(None, None, BOTH),
        P(),
        P(),
        block_rows,
        by_rows,
        by_cols,
        by_rows,
        by_cols,
        block_biases,
        tokens,
        tokens,
    )
    out_specs = (
        block_rows,
        block_rows,
        block_rows,
        block_rows,
        P(None, None, BOTH),
        block_rows,
        by_rows,
        by_cols,
        by_rows,
        by_cols,
        block_biases,
    )
    return jax.shard_map(shards, mesh=mesh, in_specs=in_specs, out_specs=out_specs, check_vma=False)
```

```python
from functools import partial

import jax
import jax.numpy as jnp
from jax import lax
from jax.experimental import pallas as pl
from jax.experimental.pallas import tpu as pltpu
from jax.sharding import PartitionSpec as P

HEADS = 24
HEAD = 64
NORM_EPS = 1e-06
MASKED = -1e30
BF = jnp.bfloat16
F32 = jnp.float32
BOTH = ("context", "tensor")


def dot_nn(a, b):
    return lax.dot_general(a, b, (((1,), (0,)), ((), ())), preferred_element_type=F32)


def dot_nt(a, b):
    return lax.dot_general(a, b, (((1,), (1,)), ((), ())), preferred_element_type=F32)


def dot_tn(a, b):
    return lax.dot_general(a, b, (((0,), (0,)), ((), ())), preferred_element_type=F32)


def dot_tt(a, b):
    return lax.dot_general(a, b, (((0,), (1,)), ((), ())), preferred_element_type=F32)


def scaled(q):
    return q * jnp.asarray(HEAD**-0.5, BF)


def attend_body(heads, chunk, places, q_ref, k_ref, v_ref, idq_ref, idk_ref, store, lse_ref):
    at_q, at_k, at_v = places

    def one_chunk(step, carry):
        rows = pl.ds(pl.multiple_of(step * chunk, chunk), chunk)
        bias = jnp.where(idk_ref[...] == idq_ref[:, rows], 0.0, MASKED)
        outs = []
        for head in range(heads):
            at = head * HEAD
            q = scaled(q_ref[rows, at_q + at : at_q + at + HEAD])
            scores = dot_nt(k_ref[:, at_k + at : at_k + at + HEAD], q) + bias
            top = jnp.max(scores, axis=0, keepdims=True)
            weights = jnp.exp(scores - top)
            total = jnp.sum(weights, axis=0, keepdims=True)
            summed = dot_tn(v_ref[:, at_v + at : at_v + at + HEAD], weights.astype(BF))
            outs.append((summed / total).T)
            lse_ref[head : head + 1, rows] = top + jnp.log(total)
        store(rows, jnp.concatenate(outs, axis=1).astype(BF))
        return carry

    lax.fori_loop(0, idq_ref.shape[1] // chunk, one_chunk, 0)


def attend_back_body(
    heads, chunk, places, q_ref, k_ref, v_ref, g_ref, lse_ref, idq_ref, idk_ref, store_dq, dk_acc, dv_acc
):
    at_q, at_k, at_v = places
    dk_acc[...] = jnp.zeros_like(dk_acc)
    dv_acc[...] = jnp.zeros_like(dv_acc)

    def one_chunk(step, carry):
        rows = pl.ds(pl.multiple_of(step * chunk, chunk), chunk)
        bias = jnp.where(idk_ref[...] == idq_ref[:, rows], 0.0, MASKED)
        grads = []
        for head in range(heads):
            at = head * HEAD
            q = scaled(q_ref[rows, at_q + at : at_q + at + HEAD])
            g = g_ref[rows, at : at + HEAD]
            k = k_ref[:, at_k + at : at_k + at + HEAD]
            probs = jnp.exp(dot_nt(k, q) + bias - lse_ref[head : head + 1, rows])
            dv_acc[head] += dot_nn(probs.astype(BF), g)
            both = probs * dot_nt(v_ref[:, at_v + at : at_v + at + HEAD], g)
            delta = jnp.sum(both, axis=0, keepdims=True)
            dscores = (both - probs * delta).astype(BF)
            dk_acc[head] += dot_nn(dscores, q)
            grads.append((dot_tn(k, dscores) * HEAD**-0.5).T)
        store_dq(rows, jnp.concatenate(grads, axis=1).astype(BF))
        return carry

    lax.fori_loop(0, idq_ref.shape[1] // chunk, one_chunk, 0)


def heads_of(acc):
    return jnp.concatenate([acc[head] for head in range(acc.shape[0])], axis=1).astype(BF)


def attend_costs(queries, keys, heads, factor):
    return pl.CostEstimate(
        flops=factor * queries * keys * heads * HEAD,
        bytes_accessed=2 * (queries + 2 * keys) * heads * HEAD * factor // 4,
        transcendentals=queries * keys * heads,
    )


def chunk_for(keys):
    return 256 if keys <= 1024 else 128


VMEM_LIMIT = pltpu.CompilerParams(vmem_limit_bytes=56 * 2**20)


def attend(q, k, v, ids_q, ids_k, heads):
    queries, keys = q.shape[0], k.shape[0]

    def kernel(q_ref, k_ref, v_ref, idq_ref, idk_ref, out_ref, lse_ref):
        def store(rows, value):
            out_ref[rows, :] = value

        attend_body(
            heads, chunk_for(keys), (0, 0, 0), q_ref, k_ref, v_ref, idq_ref, idk_ref, store, lse_ref
        )

    return pl.pallas_call(
        kernel,
        out_shape=(
            jax.ShapeDtypeStruct((queries, heads * HEAD), BF),
            jax.ShapeDtypeStruct((heads, queries), F32),
        ),
        compiler_params=VMEM_LIMIT,
        cost_estimate=attend_costs(queries, keys, heads, 4),
    )(q, k, v, ids_q.reshape(1, queries), ids_k.reshape(keys, 1))


def attend_back(q, k, v, g, lse, ids_q, ids_k, heads):
    queries, keys = q.shape[0], k.shape[0]

    def kernel(
        q_ref, k_ref, v_ref, g_ref, lse_ref, idq_ref, idk_ref, dq_ref, dk_ref, dv_ref, dk_acc, dv_acc
    ):
        def store(rows, value):
            dq_ref[rows, :] = value

        attend_back_body(
            heads, chunk_for(keys), (0, 0, 0), q_ref, k_ref, v_ref, g_ref, lse_ref, idq_ref, idk_ref,
            store, dk_acc, dv_acc,
        )
        dk_ref[...] = heads_of(dk_acc)
        dv_ref[...] = heads_of(dv_acc)

    return pl.pallas_call(
        kernel,
        out_shape=(
            jax.ShapeDtypeStruct((queries, heads * HEAD), BF),
            jax.ShapeDtypeStruct((keys, heads * HEAD), BF),
            jax.ShapeDtypeStruct((keys, heads * HEAD), BF),
        ),
        scratch_shapes=[pltpu.VMEM((heads, keys, HEAD), F32), pltpu.VMEM((heads, keys, HEAD), F32)],
        compiler_params=VMEM_LIMIT,
        cost_estimate=attend_costs(queries, keys, heads, 10),
    )(q, k, v, g, lse, ids_q.reshape(1, queries), ids_k.reshape(keys, 1))


def attend_pair(mine, theirs, ids, heads):
    wide, half = mine.shape
    rows_all, group = 2 * half, heads * HEAD
    chunk = 256

    def kernel(mine_ref, theirs_ref, idq_ref, idk_ref, here_ref, there_ref, lse_ref, x_ref, out_ref):
        x_ref[:, :half] = mine_ref[...]
        x_ref[:, half:] = theirs_ref[...]

        def one_chunk(step, carry):
            rows = pl.ds(pl.multiple_of(step * chunk, chunk), chunk)
            bias = jnp.where(idk_ref[...] == idq_ref[:, rows], 0.0, MASKED)
            for head in range(heads):
                at = slice(head * HEAD, (head + 1) * HEAD)
                q = scaled(x_ref[at, rows])
                k = x_ref[group + head * HEAD : group + (head + 1) * HEAD, :]
                v = x_ref[2 * group + head * HEAD : 2 * group + (head + 1) * HEAD, :]
                scores = dot_tn(k, q) + bias
                top = jnp.max(scores, axis=0, keepdims=True)
                weights = jnp.exp(scores - top)
                total = jnp.sum(weights, axis=0, keepdims=True)
                out_ref[at, rows] = (dot_nn(v, weights.astype(BF)) / total).astype(BF)
                lse_ref[head : head + 1, rows] = top + jnp.log(total)
            return carry

        lax.fori_loop(0, rows_all // chunk, one_chunk, 0)
        here_ref[...] = out_ref[:, :half]
        there_ref[...] = out_ref[:, half:]

    return pl.pallas_call(
        kernel,
        out_shape=(
            jax.ShapeDtypeStruct((group, half), BF),
            jax.ShapeDtypeStruct((group, half), BF),
            jax.ShapeDtypeStruct((heads, rows_all), F32),
        ),
        scratch_shapes=[pltpu.VMEM((wide, rows_all), BF), pltpu.VMEM((group, rows_all), BF)],
        compiler_params=VMEM_LIMIT,
        cost_estimate=attend_costs(rows_all, rows_all, heads, 4),
    )(mine, theirs, ids.reshape(1, rows_all), ids.reshape(rows_all, 1))


def attend_pair_back(mine, theirs, g_mine, g_theirs, lse, ids, heads):
    wide, half = mine.shape
    rows_all, group = 2 * half, heads * HEAD
    chunk = 256

    def kernel(
        mine_ref, theirs_ref, gm_ref, gt_ref, lse_ref, idq_ref, idk_ref, dmine_ref, dtheirs_ref,
        x_ref, g_ref, dq_ref, dk_ref, dv_ref,
    ):
        x_ref[:, :half] = mine_ref[...]
        x_ref[:, half:] = theirs_ref[...]
        g_ref[:, :half] = gm_ref[...]
        g_ref[:, half:] = gt_ref[...]
        dk_ref[...] = jnp.zeros_like(dk_ref)
        dv_ref[...] = jnp.zeros_like(dv_ref)

        def one_chunk(step, carry):
            rows = pl.ds(pl.multiple_of(step * chunk, chunk), chunk)
            bias = jnp.where(idk_ref[...] == idq_ref[:, rows], 0.0, MASKED)
            for head in range(heads):
                at = slice(head * HEAD, (head + 1) * HEAD)
                q = scaled(x_ref[at, rows])
                g = g_ref[at, rows]
                k = x_ref[group + head * HEAD : group + (head + 1) * HEAD, :]
                v = x_ref[2 * group + head * HEAD : 2 * group + (head + 1) * HEAD, :]
                probs = jnp.exp(dot_tn(k, q) + bias - lse_ref[head : head + 1, rows])
                dv_ref[at, :] += dot_nt(g, probs.astype(BF))
                both = probs * dot_tn(v, g)
                delta = jnp.sum(both, axis=0, keepdims=True)
                dscores = (both - probs * delta).astype(BF)
                dk_ref[at, :] += dot_nt(q, dscores)
                dq_ref[at, rows] = (dot_nn(k, dscores) * HEAD**-0.5).astype(BF)
            return carry

        lax.fori_loop(0, rows_all // chunk, one_chunk, 0)
        for out_ref, cols in ((dmine_ref, slice(0, half)), (dtheirs_ref, slice(half, rows_all))):
            out_ref[:group, :] = dq_ref[:, cols]
            out_ref[group : 2 * group, :] = dk_ref[:, cols].astype(BF)
            out_ref[2 * group :, :] = dv_ref[:, cols].astype(BF)

    return pl.pallas_call(
        kernel,
        out_shape=(jax.ShapeDtypeStruct((wide, half), BF), jax.ShapeDtypeStruct((wide, half), BF)),
        scratch_shapes=[
            pltpu.VMEM((wide, rows_all), BF),
            pltpu.VMEM((group, rows_all), BF),
            pltpu.VMEM((group, rows_all), BF),
            pltpu.VMEM((group, rows_all), F32),
            pltpu.VMEM((group, rows_all), F32),
        ],
        compiler_params=VMEM_LIMIT,
        cost_estimate=attend_costs(rows_all, rows_all, heads, 10),
    )(mine, theirs, g_mine, g_theirs, lse, ids.reshape(1, rows_all), ids.reshape(rows_all, 1))


def after(x, *others):
    anywhere = pl.BlockSpec(memory_space=pl.ANY)

    def kernel(*refs):
        pass

    return pl.pallas_call(
        kernel,
        out_shape=jax.ShapeDtypeStruct(x.shape, x.dtype),
        in_specs=[anywhere] * (1 + len(others)),
        out_specs=anywhere,
        input_output_aliases={0: 0},
    )(x, *others)


def normalized(x):
    centred = x - jnp.mean(x, axis=-1, keepdims=True)
    inverse = lax.rsqrt(jnp.mean(centred * centred, axis=-1, keepdims=True) + NORM_EPS)
    return centred * inverse, inverse


def norm_back(n, inverse, w):
    return (w - jnp.mean(w, axis=-1, keepdims=True) - n * jnp.mean(w * n, axis=-1, keepdims=True)) * inverse


def gelu_pair(u):
    c = 0.7978845608028654
    inner = jnp.tanh(c * (u + 0.044715 * u * u * u))
    value = 0.5 * u * (1.0 + inner)
    slope = 0.5 * (1.0 + inner) + 0.5 * u * (1.0 - inner * inner) * c * (1.0 + 3 * 0.044715 * u * u)
    return value.astype(BF), slope.astype(BF)


def shards(
    image_tokens,
    text_tokens,
    conditioning,
    image_seq_ids,
    text_seq_ids,
    ada_weight,
    qkv_weight,
    out_weight,
    up_weight,
    down_weight,
    biases,
    image_cotangent,
    text_cotangent,
):
    section = lax.axis_index("section")
    context = lax.axis_index("context")
    tensor = lax.axis_index("tensor")
    ncontext = lax.axis_size("context")
    ntensor = lax.axis_size("tensor")
    ndev = ncontext * ntensor
    first = section == 0
    micros, own_image, width = image_tokens.shape
    own_text = text_tokens.shape[1]
    seqs = conditioning.shape[1]
    rows_image, rows_text = micros * own_image, micros * own_text
    heads_here = HEADS // ntensor
    local = heads_here * HEAD
    hidden = up_weight.shape[3]
    bias_here = biases.shape[2]
    depth = qkv_weight.shape[2]
    mods = 6 * width
    table_rows = 2 * seqs
    per = ncontext // micros
    micro = context // per
    paired = per == 2 and heads_here % 2 == 0
    groups = 2 if paired else 1
    group_heads = heads_here // groups
    group = group_heads * HEAD
    side = context % per
    ctx_image, ctx_text = ntensor * rows_image, ntensor * rows_text
    ctx_rows = ctx_image + ctx_text

    order = (0, 2, 1, 3)

    def swapped(x, axis, bit):
        return lax.ppermute(x, axis, [(i, i ^ bit) for i in range(lax.axis_size(axis))])

    def near(x):
        return swapped(x, "tensor", 1)

    def far(x):
        return swapped(x, "tensor", 2)

    def gather_tensor(x):
        beside = near(x)
        across = far(x)
        return x, across, beside, near(across)

    def reduce_tensor(x):
        n = x.shape[0] // 4
        got = near(x[2 * n :])
        mine = x[: 2 * n].astype(F32) + got.astype(F32)
        return mine[:n] + far(mine[n:].astype(BF)).astype(F32)

    def spread(rows):
        return jnp.concatenate(gather_tensor(rows), 0)

    def text_gather(rows):
        return lax.all_gather(rows, "context", axis=0, tiled=True)

    def text_scatter(partial_sums):
        sent = partial_sums.astype(BF).reshape(ncontext, rows_text, width)
        return jnp.sum(lax.all_to_all(sent, "context", 0, 0).astype(F32), axis=0)

    def to_joint(rows):
        sent = rows.astype(BF).reshape(ncontext, rows_text, ntensor, -1).transpose(0, 2, 1, 3)
        part = sent.shape[-1]
        got = lax.all_to_all(sent.reshape(ndev, rows_text, part), BOTH, 0, 0)
        got = got.reshape(ncontext, ntensor, rows_text, part)
        return got.transpose(0, 3, 1, 2).reshape(ncontext * part, ctx_text)

    def from_joint(rows):
        part = rows.shape[0] // ncontext
        sent = rows.reshape(ncontext, part, ntensor, rows_text).transpose(0, 2, 3, 1)
        got = lax.all_to_all(sent.reshape(ndev, rows_text, part), BOTH, 0, 0)
        got = got.reshape(ncontext, ntensor, rows_text, part)
        return got.transpose(0, 2, 1, 3).reshape(ncontext * rows_text, ntensor * part)

    def gather_both(x):
        got = lax.all_gather(lax.all_gather(x, "tensor"), "context")
        return got.reshape((ndev,) + x.shape)

    def rounds(step, back):
        pairs = []
        for h in range(ncontext):
            m = (h + step) % micros
            pairs.append((h, m * per + h // micros))
        return [(b, a) for a, b in pairs] if back else pairs

    def to_work(image, text):
        pieces = []
        for step in range(micros):
            m = (context + step) % micros
            pieces.append(
                [
                    lax.ppermute(
                        lax.dynamic_index_in_dim(x, m, 0, keepdims=False), "context", rounds(step, False)
                    )
                    for x in (image, text)
                ]
            )
        return jnp.concatenate([p[0] for p in pieces] + [p[1] for p in pieces], 0).astype(F32)

    def to_home(rows):
        image, text = [], []
        for step in range(micros):
            image.append(
                lax.ppermute(
                    rows[step * own_image : (step + 1) * own_image], "context", rounds(step, True)
                )
            )
            at = rows_image + step * own_text
            text.append(lax.ppermute(rows[at : at + own_text], "context", rounds(step, True)))
        image, text = jnp.stack(image), jnp.stack(text)
        turns = [(m - context) % micros for m in range(micros)]
        return tuple(
            jnp.stack([lax.dynamic_index_in_dim(x, turn, 0, keepdims=False) for turn in turns])[None]
            for x in (image, text)
        )

    def gathered(w):
        return lax.all_gather(w, "context", axis=0, tiled=True)

    def qkv_order(w):
        return (
            w.reshape(depth, groups, group_heads, 3, HEAD).transpose(0, 1, 3, 2, 4).reshape(depth, 3 * local)
        )

    qkv_full = gathered(qkv_order(qkv_weight[0, 0]))
    out_full = gathered(out_weight[0, 0].T)
    up_full = gathered(up_weight[0, 0])
    down_full = gathered(down_weight[0, 0].T)

    def text_weights(shards_here):
        sent = jnp.concatenate([w.reshape(ncontext, -1, depth) for w in shards_here], axis=1)
        got = lax.all_to_all(sent, "context", 0, 0).transpose(1, 0, 2).reshape(-1, width)
        blocks = gather_tensor(got)
        full, at = [], 0
        for w in shards_here:
            part = w.shape[0] // ncontext
            whole = jnp.zeros((ntensor * part, width), BF)
            for block, bit in zip(blocks, order):
                whole = lax.dynamic_update_slice_in_dim(
                    whole, block[at : at + part], (tensor ^ bit) * part, 0
                )
            full.append(whole)
            at += part
        return full

    qkv_text, out_text = text_weights((qkv_order(qkv_weight[0, 1]).T, out_weight[0, 1]))
    up_text, down_text = text_weights((up_weight[0, 1].T, down_weight[0, 1]))

    cond_float = conditioning.astype(F32)
    silu_cond = jax.nn.silu(cond_float).astype(BF).reshape(micros * seqs, -1)
    ada_part = jnp.einsum("rc,jck->jrk", silu_cond, ada_weight[0], preferred_element_type=F32)
    mod_piece = mods // ndev
    sharing = [[m * per + u for u in range(per)] for m in range(micros)]
    shares = per * ntensor
    share = mods // shares
    bias_full = gather_both(biases[0]).transpose(1, 0, 2).reshape(2, -1).astype(F32)
    bias_placed = lax.dynamic_update_slice_in_dim(
        jnp.zeros((2, bias_here * ndev), F32),
        biases[0].astype(F32),
        (context * ntensor + tensor) * bias_here,
        1,
    )
    ada_sent = (
        (ada_part + bias_placed[:, None, :mods])
        .astype(BF)
        .reshape(2, micros, seqs, shares, share)
        .transpose(1, 3, 0, 2, 4)
        .reshape(ndev, table_rows, share)
    )
    ada_sum = jnp.sum(lax.all_to_all(ada_sent, BOTH, 0, 0).astype(F32), axis=0)
    table = lax.all_gather(
        lax.all_gather(ada_sum.astype(BF), "tensor"),
        "context",
        axis_index_groups=sharing,
    )
    table = table.reshape(shares, table_rows, share).transpose(1, 0, 2).reshape(table_rows, mods)
    query_bias = lax.dynamic_slice_in_dim(bias_full, mods + tensor * local, local, 1)
    value_bias = lax.dynamic_slice_in_dim(bias_full, mods + width + tensor * local, local, 1)
    qkv_bias = jnp.concatenate(
        (
            query_bias.reshape(2, groups, group),
            jnp.zeros((2, groups, group), F32),
            value_bias.reshape(2, groups, group),
        ),
        axis=2,
    ).reshape(2, 3 * local)
    out_bias = bias_full[:, mods + 2 * width : mods + 3 * width]
    at_up = mods + 3 * width
    up_bias = lax.dynamic_slice_in_dim(bias_full[0], at_up + tensor * hidden, hidden, 0)
    up_bias_text = bias_full[1, at_up : at_up + ntensor * hidden].reshape(ntensor, ncontext, -1)
    up_bias_text = lax.dynamic_index_in_dim(up_bias_text, context, 1, keepdims=False).reshape(-1)
    down_bias = bias_full[:, mods + 3 * width + hidden * ntensor :]

    def by_modality(pair):
        return jnp.concatenate(
            (
                jnp.broadcast_to(pair[0][None], (rows_image, width)),
                jnp.broadcast_to(pair[1][None], (rows_text, width)),
            ),
            0,
        )

    def ids_of(work_context):
        m, u = work_context // per, work_context % per
        homes = jnp.stack([u * micros + (m - step) % micros for step in range(micros)])
        found = []
        for ids, own, members in (
            (image_seq_ids, own_image, tensor ^ jnp.array(order)),
            (text_seq_ids, own_text, jnp.arange(ntensor)),
        ):
            table_ids = lax.dynamic_index_in_dim(ids, m, 0, keepdims=False).reshape(ndev, own)
            places = homes[None, :] * ntensor + members[:, None]
            found.append(jnp.take(table_ids, places.reshape(-1), axis=0).reshape(-1))
        return found

    own_found = ids_of(context)
    own_text_ids = lax.dynamic_slice_in_dim(own_found[1], tensor * rows_text, rows_text, 0)
    own_ids = jnp.concatenate((own_found[0][:rows_image], own_text_ids + seqs))
    onehot = (own_ids[:, None] == jnp.arange(table_rows)[None, :]).astype(BF)
    row_mods = dot_nn(onehot, table).astype(BF)
    joint_ids = jnp.concatenate(own_found)
    if paired:
        attn_ids = jnp.concatenate([joint_ids] + ids_of(context ^ 1))
    else:
        attn_ids = jnp.concatenate([x for u in range(per) for x in ids_of(micro * per + u)])

    def row_mod(index):
        return row_mods[:, index * width : (index + 1) * width].astype(F32)

    def sided(a, b):
        return jnp.where(side == 0, a, b), jnp.where(side == 0, b, a)

    def attention(joint):
        if paired:
            mine, theirs = sided(joint[: 3 * group], joint[3 * group :])
            theirs = swapped(theirs, "context", 1)
            here, there, lse = attend_pair(mine, theirs, attn_ids, group_heads)
            return jnp.concatenate(sided(here, swapped(there, "context", 1)), axis=0), (mine, theirs, lse)
        q, k, v = (joint[i * group : (i + 1) * group].T for i in range(3))
        k, v = (
            lax.all_gather(x, "context", axis=0, tiled=True, axis_index_groups=sharing) for x in (k, v)
        )
        attended, lse = attend(q, k, v, joint_ids, attn_ids, group_heads)
        return attended.T, (q, k, v, lse)

    def attention_back(grad, kept):
        if paired:
            mine, theirs, lse = kept
            g_mine, g_theirs = sided(grad[:group], grad[group:])
            g_theirs = swapped(g_theirs, "context", 1)
            d_mine, d_theirs = attend_pair_back(mine, theirs, g_mine, g_theirs, lse, attn_ids, group_heads)
            return jnp.concatenate(sided(d_mine, swapped(d_theirs, "context", 1)), axis=0)
        q, k, v, lse = kept
        dq, dk, dv = attend_back(q, k, v, grad.T, lse, joint_ids, attn_ids, group_heads)
        dk, dv = (
            lax.psum_scatter(x, "context", scatter_dimension=0, tiled=True, axis_index_groups=sharing)
            for x in (dk, dv)
        )
        return jnp.concatenate((dq.T, dk.T, dv.T), axis=0)

    def forward(x):
        n1, inv1 = normalized(x)
        h1_rows = (n1 * (1.0 + row_mod(1)) + row_mod(0)).astype(BF)
        h1 = [spread(h1_rows[:rows_image]), text_gather(h1_rows[rows_image:])]
        joint = jnp.concatenate(
            (
                (dot_tt(qkv_full, h1[0]) + qkv_bias[0][:, None]).astype(BF),
                (to_joint(dot_nt(h1[1], qkv_text)).astype(F32) + qkv_bias[1][:, None]).astype(BF),
            ),
            axis=1,
        )
        attended, kept = attention(joint)
        attn_text = from_joint(attended[:, ctx_image:])
        branch = jnp.concatenate(
            (
                reduce_tensor(dot_tt(attended, out_full)[:ctx_image].astype(BF)),
                text_scatter(dot_nn(attn_text, out_text)),
            ),
            0,
        ) + by_modality(out_bias)
        middle = x + row_mod(2) * branch
        n2, inv2 = normalized(middle)
        h2_rows = (n2 * (1.0 + row_mod(4)) + row_mod(3)).astype(BF)
        h2 = [spread(h2_rows[:rows_image]), text_gather(h2_rows[rows_image:])]
        act_image, slope_image = gelu_pair(dot_nn(h2[0], up_full) + up_bias)
        act_text, slope_text = gelu_pair(dot_nt(h2[1], up_text) + up_bias_text)
        down = jnp.concatenate(
            (
                reduce_tensor(dot_nt(act_image, down_full).astype(BF)),
                text_scatter(dot_nn(act_text, down_text)),
            ),
            0,
        ) + by_modality(down_bias)
        out = middle + row_mod(5) * down
        saved = dict(
            x=x, h1=h1, kept=kept, attn=[attended, attn_text], branch=branch, middle=middle, h2=h2,
            acts=[act_image, act_text], slopes=[slope_image, slope_text], down=down,
        )
        return out, saved

    def chosen(a, b):
        return jax.tree.map(lambda x, y: jnp.where(first, x, y), a, b)

    def backward(saved, g_out, last=None):
        g_down = (row_mod(5) * g_out).astype(BF)
        gd = [spread(g_down[:rows_image]), text_gather(g_down[rows_image:])]
        g_up = [
            (dot_nn(gd[0], down_full) * saved["slopes"][0].astype(F32)).astype(BF),
            (dot_nt(gd[1], down_text) * saved["slopes"][1].astype(F32)).astype(BF),
        ]
        g_h2_image = reduce_tensor(dot_nt(g_up[0], up_full).astype(BF))
        early = None
        if last:
            use = chosen(
                dict(h2=saved["h2"][0], acts=saved["acts"][0], gd=gd[0], g_up=g_up[0]),
                {k: last[k][0] for k in ("h2", "acts", "gd", "g_up")},
            )
            early = (
                dot_tn(use["gd"], use["acts"]).astype(BF),
                dot_tn(use["h2"], use["g_up"]).astype(BF),
            )
            g_h2_image = after(g_h2_image, *early)
        g_h2 = jnp.concatenate((g_h2_image, text_scatter(dot_nn(g_up[1], up_text))), 0)
        n2, inv2 = normalized(saved["middle"])
        g_middle = g_out + norm_back(n2, inv2, g_h2 * (1.0 + row_mod(4)))
        g_branch = (row_mod(2) * g_middle).astype(BF)
        gb = [spread(g_branch[:rows_image]), text_gather(g_branch[rows_image:])]
        g_attn = jnp.concatenate(
            (dot_tt(out_full, gb[0]).astype(BF), to_joint(dot_nt(gb[1], out_text))), axis=1
        )
        g_joint = attention_back(g_attn, saved["kept"])
        g_qkv_text = from_joint(g_joint[:, ctx_image:])
        g_h1 = jnp.concatenate(
            (
                reduce_tensor(dot_tt(g_joint, qkv_full)[:ctx_image].astype(BF)),
                text_scatter(dot_nn(g_qkv_text, qkv_text)),
            ),
            0,
        )
        n1, inv1 = normalized(saved["x"])
        g_x = g_middle + norm_back(n1, inv1, g_h1 * (1.0 + row_mod(1)))
        row_grads = jnp.concatenate(
            [
                part.astype(BF)
                for part in (
                    g_h1, g_h1 * n1, g_middle * saved["branch"], g_h2, g_h2 * n2, g_out * saved["down"]
                )
            ],
            axis=1,
        )
        mod_grad = dot_tn(onehot, row_grads)
        tensors = dict(
            h1=saved["h1"], attn=saved["attn"], h2=saved["h2"], acts=saved["acts"], g_joint=g_joint,
            g_qkv_text=g_qkv_text, gb=gb, g_up=g_up, gd=gd, g_down=g_down, g_branch=g_branch, mod=mod_grad,
        )
        return g_x, tensors, early

    def handed(rows, by):
        return lax.ppermute(rows.astype(BF), "section", [(0, 1)] if by > 0 else [(1, 0)]).astype(F32)

    out_first, saved_first = forward(to_work(image_tokens, text_tokens))
    out_last, saved_last = forward(handed(out_first, 1))
    grad_last, tensors_last, unused = backward(saved_last, to_work(image_cotangent, text_cotangent))
    grad_first, tensors_first, early = backward(saved_first, handed(grad_last, -1), tensors_last)
    out = to_home(jnp.where(first, out_first, out_last))
    grad = to_home(jnp.where(first, grad_first, grad_last))
    use = chosen(tensors_first, tensors_last)

    def scattered(full):
        return lax.psum_scatter(full.astype(BF), "context", scatter_dimension=0, tiled=True)

    def qkv_order_back(w):
        return (
            w.reshape(depth, groups, 3, group_heads, HEAD).transpose(0, 1, 3, 2, 4).reshape(depth, 3 * local)
        )

    down_shard, up_shard = scattered(early[0]), scattered(early[1])
    out_shard = scattered(dot_tt(use["gb"][0], use["attn"][0][:, :ctx_image]))
    qkv_shard = scattered(dot_tt(use["h1"][0], use["g_joint"][:, :ctx_image]))

    def text_columns(rows):
        part = lax.dynamic_slice_in_dim(rows, context * depth, depth, 1)
        return lax.all_gather(part, "tensor", axis=0, tiled=True)

    def text_whole(parts):
        sent = jnp.concatenate(
            [p.reshape(p.shape[0], ntensor, -1).transpose(1, 0, 2) for p in parts], axis=2
        )
        got = lax.all_to_all(sent, "tensor", 0, 0)
        got = lax.all_gather(got.reshape(-1, got.shape[2]), "context")
        whole, at = [], 0
        for p in parts:
            part = p.shape[1] // ntensor
            whole.append(got[:, :, at : at + part].transpose(1, 0, 2).reshape(got.shape[1], -1))
            at += part
        return whole

    acts_all, attn_all, g_up_all, g_qkv_all = text_whole(
        (use["acts"][1], use["attn"][1], use["g_up"][1], after(use["g_qkv_text"], grad_first))
    )
    gd_cols, gb_cols, h2_cols, h1_cols = (
        text_columns(use[name][1]) for name in ("gd", "gb", "h2", "h1")
    )
    down_grad = jnp.stack((down_shard.astype(F32).T, dot_tn(acts_all, gd_cols)))
    up_grad = jnp.stack((up_shard.astype(F32), dot_tn(h2_cols, g_up_all)))
    out_grad = jnp.stack((out_shard.astype(F32).T, dot_tn(attn_all, gb_cols)))
    qkv_grad = jnp.stack([qkv_order_back(w) for w in (qkv_shard.astype(F32), dot_tn(h1_cols, g_qkv_all))])

    def column_sums(parts):
        return jnp.stack([jnp.sum(p.astype(F32), axis=0) for p in parts])

    def own_sums(rows):
        return column_sums((rows[:rows_image], rows[rows_image:]))

    qkv_sums = jnp.stack(
        [
            jnp.sum(part.astype(F32), axis=1)
            for part in (use["g_joint"][:, :ctx_image], use["g_joint"][:, ctx_image:])
        ]
    ).reshape(2, groups, 3, group)
    up_sums_text = jnp.zeros((ntensor, ncontext, hidden // ncontext), F32)
    up_sums_text = lax.dynamic_update_slice_in_dim(
        up_sums_text,
        jnp.sum(use["g_up"][1].astype(F32), axis=0).reshape(ntensor, 1, -1),
        context,
        1,
    ).reshape(1, -1)
    up_sums_image = lax.dynamic_update_slice_in_dim(
        jnp.zeros((1, ntensor * hidden), F32), column_sums((use["g_up"][0],)), tensor * hidden, 1
    )
    bias_part = jnp.zeros((2, bias_here * ndev), F32)
    for at, value in (
        (0, jnp.sum(use["mod"].reshape(2, seqs, mods), axis=1)),
        (mods + tensor * local, qkv_sums[:, :, 0].reshape(2, local)),
        (mods + width + tensor * local, qkv_sums[:, :, 2].reshape(2, local)),
        (mods + 2 * width, own_sums(use["g_branch"])),
        (mods + 3 * width, jnp.concatenate((up_sums_image, up_sums_text), 0)),
        (mods + 3 * width + ntensor * hidden, own_sums(use["g_down"])),
    ):
        bias_part = lax.dynamic_update_slice_in_dim(bias_part, value, at, 1)
    sent = jnp.concatenate(
        (
            use["mod"].reshape(table_rows, ndev, mod_piece).transpose(1, 0, 2).reshape(ndev, -1),
            bias_part.reshape(2, ndev, bias_here).transpose(1, 0, 2).reshape(ndev, -1),
        ),
        axis=1,
    ).astype(BF)
    sent = after(sent, down_shard, up_shard)
    got = lax.all_to_all(sent, BOTH, 0, 0).astype(F32)
    bias_grad = jnp.sum(got[:, table_rows * mod_piece :], axis=0).reshape(2, bias_here)
    mod_sum = jnp.sum(got[:, : table_rows * mod_piece].reshape(micros, ndev // micros, -1), axis=1)
    mod_all = (
        gather_both(mod_sum.astype(BF))
        .reshape(ndev, micros, 2, seqs, mod_piece)
        .transpose(2, 1, 3, 0, 4)
        .reshape(2, micros * seqs, mods)
    )
    ada_grad = jnp.einsum("rc,jrk->jck", silu_cond, mod_all, preferred_element_type=F32)
    cond_inner = jnp.einsum("jrk,jck->rc", mod_all, ada_weight[0], preferred_element_type=F32)
    unused, silu_back = jax.vjp(jax.nn.silu, cond_float)
    cond_grad = silu_back(lax.psum(cond_inner, "section").reshape(cond_float.shape))[0]
    return (
        *out,
        *grad,
        cond_grad,
        ada_grad[None],
        qkv_grad[None],
        out_grad[None],
        up_grad[None],
        down_grad[None],
        bias_grad[None],
    )


def solution(mesh):
    tokens = P(None, BOTH, None)
    block_rows = P("section", None, BOTH, None)
    by_rows = P("section", None, "context", "tensor")
    by_cols = P("section", None, "tensor", "context")
    block_biases = P("section", None, BOTH)
    in_specs = (
        tokens,
        tokens,
        P(None, None, BOTH),
        P(),
        P(),
        block_rows,
        by_rows,
        by_cols,
        by_rows,
        by_cols,
        block_biases,
        tokens,
        tokens,
    )
    out_specs = (
        block_rows,
        block_rows,
        block_rows,
        block_rows,
        P(None, None, BOTH),
        block_rows,
        by_rows,
        by_cols,
        by_rows,
        by_cols,
        block_biases,
    )
    return jax.shard_map(shards, mesh=mesh, in_specs=in_specs, out_specs=out_specs, check_vma=False)
```

```python
from functools import partial

import jax
import jax.numpy as jnp
from jax import lax
from jax.experimental import pallas as pl
from jax.experimental.pallas import tpu as pltpu
from jax.sharding import PartitionSpec as P

HEADS = 24
HEAD = 64
NORM_EPS = 1e-06
MASKED = -1e30
BF = jnp.bfloat16
F32 = jnp.float32
BOTH = ("context", "tensor")


def dot_nn(a, b):
    return lax.dot_general(a, b, (((1,), (0,)), ((), ())), preferred_element_type=F32)


def dot_nt(a, b):
    return lax.dot_general(a, b, (((1,), (1,)), ((), ())), preferred_element_type=F32)


def dot_tn(a, b):
    return lax.dot_general(a, b, (((0,), (0,)), ((), ())), preferred_element_type=F32)


def dot_tt(a, b):
    return lax.dot_general(a, b, (((0,), (1,)), ((), ())), preferred_element_type=F32)


def scaled(q):
    return q * jnp.asarray(HEAD**-0.5, BF)


def attend_body(heads, chunk, places, q_ref, k_ref, v_ref, idq_ref, idk_ref, store, lse_ref):
    at_q, at_k, at_v = places

    def one_chunk(step, carry):
        rows = pl.ds(pl.multiple_of(step * chunk, chunk), chunk)
        bias = jnp.where(idk_ref[...] == idq_ref[:, rows], 0.0, MASKED)
        outs = []
        for head in range(heads):
            at = head * HEAD
            q = scaled(q_ref[rows, at_q + at : at_q + at + HEAD])
            scores = dot_nt(k_ref[:, at_k + at : at_k + at + HEAD], q) + bias
            top = jnp.max(scores, axis=0, keepdims=True)
            weights = jnp.exp(scores - top)
            total = jnp.sum(weights, axis=0, keepdims=True)
            summed = dot_tn(v_ref[:, at_v + at : at_v + at + HEAD], weights.astype(BF))
            outs.append((summed / total).T)
            lse_ref[head : head + 1, rows] = top + jnp.log(total)
        store(rows, jnp.concatenate(outs, axis=1).astype(BF))
        return carry

    lax.fori_loop(0, idq_ref.shape[1] // chunk, one_chunk, 0)


def attend_back_body(
    heads, chunk, places, q_ref, k_ref, v_ref, g_ref, lse_ref, idq_ref, idk_ref, store_dq, dk_acc, dv_acc
):
    at_q, at_k, at_v = places
    dk_acc[...] = jnp.zeros_like(dk_acc)
    dv_acc[...] = jnp.zeros_like(dv_acc)

    def one_chunk(step, carry):
        rows = pl.ds(pl.multiple_of(step * chunk, chunk), chunk)
        bias = jnp.where(idk_ref[...] == idq_ref[:, rows], 0.0, MASKED)
        grads = []
        for head in range(heads):
            at = head * HEAD
            q = scaled(q_ref[rows, at_q + at : at_q + at + HEAD])
            g = g_ref[rows, at : at + HEAD]
            k = k_ref[:, at_k + at : at_k + at + HEAD]
            probs = jnp.exp(dot_nt(k, q) + bias - lse_ref[head : head + 1, rows])
            dv_acc[head] += dot_nn(probs.astype(BF), g)
            both = probs * dot_nt(v_ref[:, at_v + at : at_v + at + HEAD], g)
            delta = jnp.sum(both, axis=0, keepdims=True)
            dscores = (both - probs * delta).astype(BF)
            dk_acc[head] += dot_nn(dscores, q)
            grads.append((dot_tn(k, dscores) * HEAD**-0.5).T)
        store_dq(rows, jnp.concatenate(grads, axis=1).astype(BF))
        return carry

    lax.fori_loop(0, idq_ref.shape[1] // chunk, one_chunk, 0)


def heads_of(acc):
    return jnp.concatenate([acc[head] for head in range(acc.shape[0])], axis=1).astype(BF)


def attend_costs(queries, keys, heads, factor):
    return pl.CostEstimate(
        flops=factor * queries * keys * heads * HEAD,
        bytes_accessed=2 * (queries + 2 * keys) * heads * HEAD * factor // 4,
        transcendentals=queries * keys * heads,
    )


def chunk_for(keys):
    return 256 if keys <= 1024 else 128


VMEM_LIMIT = pltpu.CompilerParams(vmem_limit_bytes=56 * 2**20)


def attend(q, k, v, ids_q, ids_k, heads):
    queries, keys = q.shape[0], k.shape[0]

    def kernel(q_ref, k_ref, v_ref, idq_ref, idk_ref, out_ref, lse_ref):
        def store(rows, value):
            out_ref[rows, :] = value

        attend_body(
            heads, chunk_for(keys), (0, 0, 0), q_ref, k_ref, v_ref, idq_ref, idk_ref, store, lse_ref
        )

    return pl.pallas_call(
        kernel,
        out_shape=(
            jax.ShapeDtypeStruct((queries, heads * HEAD), BF),
            jax.ShapeDtypeStruct((heads, queries), F32),
        ),
        compiler_params=VMEM_LIMIT,
        cost_estimate=attend_costs(queries, keys, heads, 4),
    )(q, k, v, ids_q.reshape(1, queries), ids_k.reshape(keys, 1))


def attend_back(q, k, v, g, lse, ids_q, ids_k, heads):
    queries, keys = q.shape[0], k.shape[0]

    def kernel(
        q_ref, k_ref, v_ref, g_ref, lse_ref, idq_ref, idk_ref, dq_ref, dk_ref, dv_ref, dk_acc, dv_acc
    ):
        def store(rows, value):
            dq_ref[rows, :] = value

        attend_back_body(
            heads, chunk_for(keys), (0, 0, 0), q_ref, k_ref, v_ref, g_ref, lse_ref, idq_ref, idk_ref,
            store, dk_acc, dv_acc,
        )
        dk_ref[...] = heads_of(dk_acc)
        dv_ref[...] = heads_of(dv_acc)

    return pl.pallas_call(
        kernel,
        out_shape=(
            jax.ShapeDtypeStruct((queries, heads * HEAD), BF),
            jax.ShapeDtypeStruct((keys, heads * HEAD), BF),
            jax.ShapeDtypeStruct((keys, heads * HEAD), BF),
        ),
        scratch_shapes=[pltpu.VMEM((heads, keys, HEAD), F32), pltpu.VMEM((heads, keys, HEAD), F32)],
        compiler_params=VMEM_LIMIT,
        cost_estimate=attend_costs(queries, keys, heads, 10),
    )(q, k, v, g, lse, ids_q.reshape(1, queries), ids_k.reshape(keys, 1))


def attend_pair(mine, theirs, ids, heads):
    wide, half = mine.shape
    rows_all, group = 2 * half, heads * HEAD
    chunk = 256

    def kernel(mine_ref, theirs_ref, idq_ref, idk_ref, here_ref, there_ref, lse_ref, x_ref, out_ref):
        x_ref[:, :half] = mine_ref[...]
        x_ref[:, half:] = theirs_ref[...]

        def one_chunk(step, carry):
            rows = pl.ds(pl.multiple_of(step * chunk, chunk), chunk)
            bias = jnp.where(idk_ref[...] == idq_ref[:, rows], 0.0, MASKED)
            for head in range(heads):
                at = slice(head * HEAD, (head + 1) * HEAD)
                base = 3 * head * HEAD
                q = scaled(x_ref[base : base + HEAD, rows])
                k = x_ref[base + HEAD : base + 2 * HEAD, :]
                v = x_ref[base + 2 * HEAD : base + 3 * HEAD, :]
                scores = dot_tn(k, q) + bias
                top = jnp.max(scores, axis=0, keepdims=True)
                weights = jnp.exp(scores - top)
                total = jnp.sum(weights, axis=0, keepdims=True)
                out_ref[at, rows] = (dot_nn(v, weights.astype(BF)) / total).astype(BF)
                lse_ref[head : head + 1, rows] = top + jnp.log(total)
            return carry

        lax.fori_loop(0, rows_all // chunk, one_chunk, 0)
        here_ref[...] = out_ref[:, :half]
        there_ref[...] = out_ref[:, half:]

    return pl.pallas_call(
        kernel,
        out_shape=(
            jax.ShapeDtypeStruct((group, half), BF),
            jax.ShapeDtypeStruct((group, half), BF),
            jax.ShapeDtypeStruct((heads, rows_all), F32),
        ),
        scratch_shapes=[pltpu.VMEM((wide, rows_all), BF), pltpu.VMEM((group, rows_all), BF)],
        compiler_params=VMEM_LIMIT,
        cost_estimate=attend_costs(rows_all, rows_all, heads, 4),
    )(mine, theirs, ids.reshape(1, rows_all), ids.reshape(rows_all, 1))


def attend_pair_back(mine, theirs, g_mine, g_theirs, lse, ids, heads):
    wide, half = mine.shape
    rows_all, group = 2 * half, heads * HEAD
    chunk = 256

    def kernel(
        mine_ref, theirs_ref, gm_ref, gt_ref, lse_ref, idq_ref, idk_ref, dmine_ref, dtheirs_ref,
        x_ref, g_ref, dq_ref, dk_ref, dv_ref,
    ):
        x_ref[:, :half] = mine_ref[...]
        x_ref[:, half:] = theirs_ref[...]
        g_ref[:, :half] = gm_ref[...]
        g_ref[:, half:] = gt_ref[...]
        dk_ref[...] = jnp.zeros_like(dk_ref)
        dv_ref[...] = jnp.zeros_like(dv_ref)

        def one_chunk(step, carry):
            rows = pl.ds(pl.multiple_of(step * chunk, chunk), chunk)
            bias = jnp.where(idk_ref[...] == idq_ref[:, rows], 0.0, MASKED)
            for head in range(heads):
                at = slice(head * HEAD, (head + 1) * HEAD)
                base = 3 * head * HEAD
                q = scaled(x_ref[base : base + HEAD, rows])
                g = g_ref[at, rows]
                k = x_ref[base + HEAD : base + 2 * HEAD, :]
                v = x_ref[base + 2 * HEAD : base + 3 * HEAD, :]
                probs = jnp.exp(dot_tn(k, q) + bias - lse_ref[head : head + 1, rows])
                dv_ref[at, :] += dot_nt(g, probs.astype(BF))
                both = probs * dot_tn(v, g)
                delta = jnp.sum(both, axis=0, keepdims=True)
                dscores = (both - probs * delta).astype(BF)
                dk_ref[at, :] += dot_nt(q, dscores)
                dq_ref[at, rows] = (dot_nn(k, dscores) * HEAD**-0.5).astype(BF)
            return carry

        lax.fori_loop(0, rows_all // chunk, one_chunk, 0)
        for out_ref, cols in ((dmine_ref, slice(0, half)), (dtheirs_ref, slice(half, rows_all))):
            for head in range(heads):
                at = slice(head * HEAD, (head + 1) * HEAD)
                base = 3 * head * HEAD
                out_ref[base : base + HEAD, :] = dq_ref[at, cols]
                out_ref[base + HEAD : base + 2 * HEAD, :] = dk_ref[at, cols].astype(BF)
                out_ref[base + 2 * HEAD : base + 3 * HEAD, :] = dv_ref[at, cols].astype(BF)

    return pl.pallas_call(
        kernel,
        out_shape=(jax.ShapeDtypeStruct((wide, half), BF), jax.ShapeDtypeStruct((wide, half), BF)),
        scratch_shapes=[
            pltpu.VMEM((wide, rows_all), BF),
            pltpu.VMEM((group, rows_all), BF),
            pltpu.VMEM((group, rows_all), BF),
            pltpu.VMEM((group, rows_all), F32),
            pltpu.VMEM((group, rows_all), F32),
        ],
        compiler_params=VMEM_LIMIT,
        cost_estimate=attend_costs(rows_all, rows_all, heads, 10),
    )(mine, theirs, g_mine, g_theirs, lse, ids.reshape(1, rows_all), ids.reshape(rows_all, 1))


def after(x, *others):
    anywhere = pl.BlockSpec(memory_space=pl.ANY)

    def kernel(*refs):
        pass

    return pl.pallas_call(
        kernel,
        out_shape=jax.ShapeDtypeStruct(x.shape, x.dtype),
        in_specs=[anywhere] * (1 + len(others)),
        out_specs=anywhere,
        input_output_aliases={0: 0},
    )(x, *others)


def lanes(n):
    return -(-n // 128) * 128


def packed(sums, rest, groups_of, shares):
    rows, columns = sums.shape[1], sums.shape[2]
    seqs, share, extra = rows // groups_of, columns // shares, rest.shape[2]
    wide = lanes(max(share, extra))

    def kernel(sums_ref, rest_ref, out_ref):
        for group in range(groups_of):
            for j in range(2):
                out_ref[group, 0, j * seqs : (j + 1) * seqs, :share] = sums_ref[
                    j, group * seqs : (group + 1) * seqs, :
                ]
            out_ref[group, 0, 2 * seqs : 2 * seqs + 2, :extra] = rest_ref[group, 0]

    if share % 128 == 0:
        sums_in, sums_spec = sums, pl.BlockSpec((2, rows, share), lambda k: (0, 0, k))
    else:
        sums_in = sums.reshape(2, rows, shares, share).transpose(2, 0, 1, 3)
        sums_spec = pl.BlockSpec((None, 2, rows, share), lambda k: (k, 0, 0, 0))
    out = pl.pallas_call(
        kernel,
        grid=(shares,),
        in_specs=[sums_spec, pl.BlockSpec((groups_of, 1, 2, extra), lambda k: (0, k, 0, 0))],
        out_specs=pl.BlockSpec((groups_of, 1, 8, wide), lambda k: (0, k, 0, 0)),
        out_shape=jax.ShapeDtypeStruct((groups_of, shares, 8, wide), F32),
    )(sums_in, rest.reshape(groups_of, shares, 2, extra))
    return out.reshape(groups_of * shares, 8, wide)


def normalized(x):
    centred = x - jnp.mean(x, axis=-1, keepdims=True)
    inverse = lax.rsqrt(jnp.mean(centred * centred, axis=-1, keepdims=True) + NORM_EPS)
    return centred * inverse, inverse


def norm_back(n, inverse, w):
    return (w - jnp.mean(w, axis=-1, keepdims=True) - n * jnp.mean(w * n, axis=-1, keepdims=True)) * inverse


def gelu_pair(u):
    c = 0.7978845608028654
    inner = jnp.tanh(c * (u + 0.044715 * u * u * u))
    value = 0.5 * u * (1.0 + inner)
    slope = 0.5 * (1.0 + inner) + 0.5 * u * (1.0 - inner * inner) * c * (1.0 + 3 * 0.044715 * u * u)
    return value.astype(BF), slope.astype(BF)


def shards(
    image_tokens,
    text_tokens,
    conditioning,
    image_seq_ids,
    text_seq_ids,
    ada_weight,
    qkv_weight,
    out_weight,
    up_weight,
    down_weight,
    biases,
    image_cotangent,
    text_cotangent,
):
    section = lax.axis_index("section")
    context = lax.axis_index("context")
    tensor = lax.axis_index("tensor")
    ncontext = lax.axis_size("context")
    ntensor = lax.axis_size("tensor")
    ndev = ncontext * ntensor
    first = section == 0
    micros, own_image, width = image_tokens.shape
    own_text = text_tokens.shape[1]
    seqs = conditioning.shape[1]
    rows_image, rows_text = micros * own_image, micros * own_text
    heads_here = HEADS // ntensor
    local = heads_here * HEAD
    hidden = up_weight.shape[3]
    bias_here = biases.shape[2]
    depth = qkv_weight.shape[2]
    mods = 6 * width
    table_rows = 2 * seqs
    per = ncontext // micros
    micro = context // per
    paired = per == 2 and heads_here % 2 == 0
    groups = 2 if paired else 1
    group_heads = heads_here // groups
    group = group_heads * HEAD
    side = context % per
    ctx_image, ctx_text = ntensor * rows_image, ntensor * rows_text
    ctx_rows = ctx_image + ctx_text

    order = (0, 2, 1, 3)

    def swapped(x, axis, bit):
        return lax.ppermute(x, axis, [(i, i ^ bit) for i in range(lax.axis_size(axis))])

    def sided(a, b):
        return jnp.where(side == 0, a, b), jnp.where(side == 0, b, a)

    def near(x):
        return swapped(x, "tensor", 1)

    def far(x):
        return swapped(x, "tensor", 2)

    def gather_tensor(x):
        beside = near(x)
        across = far(x)
        return x, across, beside, near(across)

    def reduce_tensor(x):
        n = x.shape[0] // 4
        got = near(x[2 * n :])
        mine = x[: 2 * n].astype(F32) + got.astype(F32)
        return mine[:n] + far(mine[n:].astype(BF)).astype(F32)

    def spread(rows):
        return jnp.concatenate(gather_tensor(rows), 0)

    def text_gather(rows):
        sent = jnp.broadcast_to(rows[None], (ncontext,) + rows.shape)
        return lax.all_to_all(sent, "context", 0, 0).reshape(ncontext * rows_text, width)

    def by_tensor(x, axis):
        places = [jnp.array(order)[tensor ^ k] for k in range(ntensor)]
        return jnp.stack([lax.dynamic_index_in_dim(x, at, axis, keepdims=False) for at in places], axis)

    def in_group(x, axis):
        places = [tensor ^ bit for bit in order]
        return jnp.stack([lax.dynamic_index_in_dim(x, at, axis, keepdims=False) for at in places], axis)

    def text_scatter(partial_sums):
        sent = partial_sums.astype(BF).reshape(ncontext, rows_text, width)
        return jnp.sum(lax.all_to_all(sent, "context", 0, 0).astype(F32), axis=0)

    def to_joint(rows):
        sent = by_tensor(rows.astype(BF).reshape(ncontext, rows_text, ntensor, -1), 2).transpose(0, 2, 1, 3)
        part = sent.shape[-1]
        got = lax.all_to_all(sent.reshape(ndev, rows_text, part), BOTH, 0, 0)
        got = got.reshape(ncontext, ntensor, rows_text, part)
        return got.transpose(0, 3, 1, 2).reshape(ncontext * part, ctx_text)

    def from_joint(rows):
        part = rows.shape[0] // ncontext
        sent = rows.reshape(ncontext, part, ntensor, rows_text).transpose(0, 2, 3, 1)
        got = lax.all_to_all(sent.reshape(ndev, rows_text, part), BOTH, 0, 0)
        got = in_group(got.reshape(ncontext, ntensor, rows_text, part), 1)
        return got.transpose(0, 2, 1, 3).reshape(ncontext * rows_text, ntensor * part)

    def gather_both(x):
        got = lax.all_gather(x, "tensor")
        got = lax.all_to_all(jnp.broadcast_to(got[None], (ncontext,) + got.shape), "context", 0, 0)
        return got.reshape((ndev,) + x.shape)

    def rounds(step, back):
        pairs = []
        for h in range(ncontext):
            m = (h + step) % micros
            pairs.append((h, m * per + h // micros))
        return [(b, a) for a, b in pairs] if back else pairs

    def to_work(image, text):
        pieces = []
        for step in range(micros):
            m = (context + step) % micros
            pieces.append(
                [
                    lax.ppermute(
                        lax.dynamic_index_in_dim(x, m, 0, keepdims=False), "context", rounds(step, False)
                    )
                    for x in (image, text)
                ]
            )
        return jnp.concatenate([p[0] for p in pieces] + [p[1] for p in pieces], 0).astype(F32)

    def to_home(rows):
        image, text = [], []
        for step in range(micros):
            image.append(
                lax.ppermute(
                    rows[step * own_image : (step + 1) * own_image], "context", rounds(step, True)
                )
            )
            at = rows_image + step * own_text
            text.append(lax.ppermute(rows[at : at + own_text], "context", rounds(step, True)))
        image, text = jnp.stack(image), jnp.stack(text)
        turns = [(m - context) % micros for m in range(micros)]
        return tuple(
            jnp.stack([lax.dynamic_index_in_dim(x, turn, 0, keepdims=False) for turn in turns])[None]
            for x in (image, text)
        )

    def gathered(w):
        return lax.all_gather(w, "context", axis=0, tiled=True)

    qkv_full = gathered(qkv_weight[0, 0])
    out_full = gathered(out_weight[0, 0].T)
    up_full = gathered(up_weight[0, 0])
    down_full = gathered(down_weight[0, 0].T)

    text_full = []
    text_shards = (qkv_weight[0, 1].T, out_weight[0, 1], up_weight[0, 1].T, down_weight[0, 1])
    text_parts = [w.shape[0] // ncontext for w in text_shards]
    def text_moved(first_of, send_after):
        sent = [w.reshape(ncontext, -1, depth) for w in text_shards[first_of : first_of + 2]]
        return lax.all_to_all(after(jnp.concatenate(sent, axis=1), send_after), "context", 0, 0)

    text_moves = []

    def text_weights():
        if not text_full:
            for first_of, got in zip((0, 2), text_moves):
                parts = text_parts[first_of : first_of + 2]
                rows = got.transpose(1, 0, 2).reshape(-1, width)
                blocks = gather_tensor(rows)
                text_full.append(jnp.concatenate([b[: parts[0]] for b in blocks], 0))
                text_full.append(jnp.concatenate([b[parts[0] :] for b in blocks], 0))
        return text_full

    cond_float = conditioning.astype(F32)
    silu_cond = jax.nn.silu(cond_float).astype(BF).reshape(micros * seqs, -1)
    ada_part = jnp.einsum("rc,jck->jrk", silu_cond, ada_weight[0], preferred_element_type=F32)
    sharing = [[m * per + u for u in range(per)] for m in range(micros)]
    shares = per * ntensor
    share = mods // shares
    bias_placed = lax.dynamic_update_slice_in_dim(
        jnp.zeros((2, bias_here * ndev), F32),
        biases[0].astype(F32),
        (context * ntensor + tensor) * bias_here,
        1,
    )
    ada_sent = packed(
        ada_part + bias_placed[:, None, :mods],
        jnp.broadcast_to(biases[0].astype(F32)[None], (ndev, 2, bias_here)),
        micros,
        shares,
    )
    ada_got = lax.all_to_all(ada_sent.astype(BF), BOTH, 0, 0)
    bias_full = ada_got[:, table_rows : table_rows + 2, :bias_here].transpose(1, 0, 2).reshape(2, -1).astype(F32)
    ada_sum = jnp.sum(ada_got[:, :table_rows, :share].astype(F32), axis=0).astype(BF)
    table = lax.all_gather(ada_sum, "tensor")
    if paired:
        table = jnp.stack(sided(table, swapped(table, "context", 1)))
    else:
        table = lax.all_gather(table, "context", axis_index_groups=sharing)
    table = table.reshape(shares, table_rows, share).transpose(1, 0, 2).reshape(table_rows, mods)
    text_moves += [text_moved(0, ada_got), text_moved(2, table)]
    query_bias = lax.dynamic_slice_in_dim(bias_full, mods + tensor * local, local, 1)
    value_bias = lax.dynamic_slice_in_dim(bias_full, mods + width + tensor * local, local, 1)
    qkv_bias = jnp.stack(
        (
            query_bias.reshape(2, heads_here, HEAD),
            jnp.zeros((2, heads_here, HEAD), F32),
            value_bias.reshape(2, heads_here, HEAD),
        ),
        axis=2,
    ).reshape(2, 3 * local)
    out_bias = bias_full[:, mods + 2 * width : mods + 3 * width]
    at_up = mods + 3 * width
    up_bias = lax.dynamic_slice_in_dim(bias_full[0], at_up + tensor * hidden, hidden, 0)
    up_bias_text = bias_full[1, at_up : at_up + ntensor * hidden].reshape(ntensor, ncontext, -1)
    up_bias_text = in_group(lax.dynamic_index_in_dim(up_bias_text, context, 1, keepdims=False), 0).reshape(-1)
    down_bias = bias_full[:, mods + 3 * width + hidden * ntensor :]

    def by_modality(pair):
        return jnp.concatenate(
            (
                jnp.broadcast_to(pair[0][None], (rows_image, width)),
                jnp.broadcast_to(pair[1][None], (rows_text, width)),
            ),
            0,
        )

    def ids_of(work_context):
        m, u = work_context // per, work_context % per
        homes = jnp.stack([u * micros + (m - step) % micros for step in range(micros)])
        found = []
        for ids, own, members in (
            (image_seq_ids, own_image, tensor ^ jnp.array(order)),
            (text_seq_ids, own_text, jnp.arange(ntensor)),
        ):
            table_ids = lax.dynamic_index_in_dim(ids, m, 0, keepdims=False).reshape(ndev, own)
            places = homes[None, :] * ntensor + members[:, None]
            found.append(jnp.take(table_ids, places.reshape(-1), axis=0).reshape(-1))
        return found

    own_found = ids_of(context)
    own_text_ids = lax.dynamic_slice_in_dim(own_found[1], tensor * rows_text, rows_text, 0)
    own_ids = jnp.concatenate((own_found[0][:rows_image], own_text_ids + seqs))
    onehot = (own_ids[:, None] == jnp.arange(table_rows)[None, :]).astype(BF)
    row_mods = dot_nn(onehot, table).astype(BF)
    joint_ids = jnp.concatenate(own_found)
    if paired:
        attn_ids = jnp.concatenate([joint_ids] + ids_of(context ^ 1))
    else:
        attn_ids = jnp.concatenate([x for u in range(per) for x in ids_of(micro * per + u)])

    def row_mod(index):
        return row_mods[:, index * width : (index + 1) * width].astype(F32)

    def attention(joint):
        if paired:
            mine, theirs = sided(joint[: 3 * group], joint[3 * group :])
            theirs = swapped(theirs, "context", 1)
            here, there, lse = attend_pair(mine, theirs, attn_ids, group_heads)
            return jnp.concatenate(sided(here, swapped(there, "context", 1)), axis=0), (mine, theirs, lse)
        by_kind = joint.reshape(heads_here, 3, HEAD, ctx_rows)
        q, k, v = (by_kind[:, i].reshape(local, ctx_rows).T for i in range(3))
        k, v = (
            lax.all_gather(x, "context", axis=0, tiled=True, axis_index_groups=sharing) for x in (k, v)
        )
        attended, lse = attend(q, k, v, joint_ids, attn_ids, group_heads)
        return attended.T, (q, k, v, lse)

    def attention_back(grad, kept):
        if paired:
            mine, theirs, lse = kept
            g_mine, g_theirs = sided(grad[:group], grad[group:])
            g_theirs = swapped(g_theirs, "context", 1)
            d_mine, d_theirs = attend_pair_back(mine, theirs, g_mine, g_theirs, lse, attn_ids, group_heads)
            return jnp.concatenate(sided(d_mine, swapped(d_theirs, "context", 1)), axis=0)
        q, k, v, lse = kept
        dq, dk, dv = attend_back(q, k, v, grad.T, lse, joint_ids, attn_ids, group_heads)
        dk, dv = (
            lax.psum_scatter(x, "context", scatter_dimension=0, tiled=True, axis_index_groups=sharing)
            for x in (dk, dv)
        )
        kinds = [x.T.reshape(heads_here, HEAD, ctx_rows) for x in (dq, dk, dv)]
        return jnp.stack(kinds, axis=1).reshape(3 * local, ctx_rows)

    def forward(x):
        n1, inv1 = normalized(x)
        h1_rows = (n1 * (1.0 + row_mod(1)) + row_mod(0)).astype(BF)
        fresh = not text_full
        qkv_text, out_text, up_text, down_text = text_weights()
        h1 = [spread(h1_rows[:rows_image]), text_gather(h1_rows[rows_image:])]
        joint = jnp.concatenate(
            (
                (dot_tt(qkv_full, h1[0]) + qkv_bias[0][:, None]).astype(BF),
                (to_joint(dot_nt(h1[1], qkv_text)).astype(F32) + qkv_bias[1][:, None]).astype(BF),
            ),
            axis=1,
        )
        attended, kept = attention(joint)
        if fresh:
            attended = after(attended, text_moves[1])
        attn_text = from_joint(attended[:, ctx_image:])
        branch = jnp.concatenate(
            (
                reduce_tensor(dot_tt(attended, out_full)[:ctx_image].astype(BF)),
                text_scatter(dot_nn(attn_text, out_text)),
            ),
            0,
        ) + by_modality(out_bias)
        middle = x + row_mod(2) * branch
        n2, inv2 = normalized(middle)
        h2_rows = (n2 * (1.0 + row_mod(4)) + row_mod(3)).astype(BF)
        h2 = [spread(h2_rows[:rows_image]), text_gather(h2_rows[rows_image:])]
        act_image, slope_image = gelu_pair(dot_nn(h2[0], up_full) + up_bias)
        act_text, slope_text = gelu_pair(dot_nt(h2[1], up_text) + up_bias_text)
        down = jnp.concatenate(
            (
                reduce_tensor(dot_nt(act_image, down_full).astype(BF)),
                text_scatter(dot_nn(act_text, down_text)),
            ),
            0,
        ) + by_modality(down_bias)
        out = middle + row_mod(5) * down
        saved = dict(
            x=x, h1=h1, kept=kept, attn=[attended, attn_text], branch=branch, middle=middle, h2=h2,
            acts=[act_image, act_text], slopes=[slope_image, slope_text], down=down,
        )
        return out, saved

    def chosen(a, b):
        return jax.tree.map(lambda x, y: jnp.where(first, x, y), a, b)

    def scattered(full):
        return lax.psum_scatter(full.astype(BF), "context", scatter_dimension=0, tiled=True)

    def backward(saved, g_out, last=None):
        qkv_text, out_text, up_text, down_text = text_full
        g_down = (row_mod(5) * g_out).astype(BF)
        gd = [spread(g_down[:rows_image]), text_gather(g_down[rows_image:])]
        g_up = [
            (dot_nn(gd[0], down_full) * saved["slopes"][0].astype(F32)).astype(BF),
            (dot_nt(gd[1], down_text) * saved["slopes"][1].astype(F32)).astype(BF),
        ]
        g_h2_image = reduce_tensor(dot_nt(g_up[0], up_full).astype(BF))
        early = []
        if last:
            use = chosen(
                dict(h2=saved["h2"][0], acts=saved["acts"][0], gd=gd[0], g_up=g_up[0]),
                {k: last[k][0] for k in ("h2", "acts", "gd", "g_up")},
            )
            early = (
                dot_tn(use["gd"], use["acts"]).astype(BF),
                dot_tn(use["h2"], use["g_up"]).astype(BF),
            )
            g_h2_image = after(g_h2_image, *early)
            early = [scattered(part) for part in early]
        g_h2 = jnp.concatenate((g_h2_image, text_scatter(dot_nn(g_up[1], up_text))), 0)
        n2, inv2 = normalized(saved["middle"])
        g_middle = g_out + norm_back(n2, inv2, g_h2 * (1.0 + row_mod(4)))
        g_branch = (row_mod(2) * g_middle).astype(BF)
        gb = [spread(g_branch[:rows_image]), text_gather(g_branch[rows_image:])]
        g_attn = jnp.concatenate(
            (dot_tt(out_full, gb[0]).astype(BF), to_joint(dot_nt(gb[1], out_text))), axis=1
        )
        if last:
            use = chosen(
                dict(gb=gb[0], attn=saved["attn"][0]), dict(gb=last["gb"][0], attn=last["attn"][0])
            )
            early.append(dot_tt(use["gb"], use["attn"][:, :ctx_image]).astype(BF))
            g_attn = after(g_attn, early[2])
        g_joint = attention_back(g_attn, saved["kept"])
        g_qkv_text = from_joint(g_joint[:, ctx_image:])
        g_h1 = jnp.concatenate(
            (
                reduce_tensor(dot_tt(g_joint, qkv_full)[:ctx_image].astype(BF)),
                text_scatter(dot_nn(g_qkv_text, qkv_text)),
            ),
            0,
        )
        n1, inv1 = normalized(saved["x"])
        g_x = g_middle + norm_back(n1, inv1, g_h1 * (1.0 + row_mod(1)))
        if last:
            g_x = after(g_x, *early)
        row_grads = jnp.concatenate(
            [
                part.astype(BF)
                for part in (
                    g_h1, g_h1 * n1, g_middle * saved["branch"], g_h2, g_h2 * n2, g_out * saved["down"]
                )
            ],
            axis=1,
        )
        mod_grad = dot_tn(onehot, row_grads)
        tensors = dict(
            h1=saved["h1"], attn=saved["attn"], h2=saved["h2"], acts=saved["acts"], g_joint=g_joint,
            g_qkv_text=g_qkv_text, gb=gb, g_up=g_up, gd=gd, g_down=g_down, g_branch=g_branch, mod=mod_grad,
        )
        return g_x, tensors, early

    def text_whole(parts):
        sent = by_tensor(
            jnp.concatenate(
                [p.reshape(p.shape[0], ntensor, -1).transpose(1, 0, 2) for p in parts], axis=2
            ),
            0,
        )
        ours = lax.all_to_all(sent, "tensor", 0, 0)
        got = ours.reshape(1, -1, sent.shape[2])
        got = lax.all_to_all(jnp.broadcast_to(got, (ncontext,) + got.shape[1:]), "context", 0, 0)
        whole, at = [], 0
        for p in parts:
            part = p.shape[1] // ntensor
            whole.append(got[:, :, at : at + part].transpose(1, 0, 2).reshape(got.shape[1], -1))
            at += part
        return whole, ours, got

    def handed(rows, by):
        return lax.ppermute(rows.astype(BF), "section", [(0, 1)] if by > 0 else [(1, 0)]).astype(F32)

    out_first, saved_first = forward(to_work(image_tokens, text_tokens))
    out_last, saved_last = forward(handed(out_first, 1))
    grad_last, tensors_last, unused = backward(saved_last, to_work(image_cotangent, text_cotangent))
    (acts_all, attn_all), unused, acts_got = text_whole(
        [jnp.where(first, saved_first[name][1], saved_last[name][1]) for name in ("acts", "attn")]
    )
    out = to_home(jnp.where(first, out_first, out_last))
    returned = after(handed(grad_last, -1), acts_got, *out)
    grad_first, tensors_first, early = backward(saved_first, returned, tensors_last)
    grad = to_home(jnp.where(first, grad_first, grad_last))
    use = chosen(tensors_first, tensors_last)

    down_shard, up_shard, out_part = early
    out_shard = after(scattered(out_part), grad_first)
    qkv_shard = after(scattered(dot_tt(use["h1"][0], use["g_joint"][:, :ctx_image])), grad_first)

    text_cols = jnp.concatenate(
        [
            lax.dynamic_slice_in_dim(use[name][1], context * depth, depth, 1)
            for name in ("gd", "gb", "h2", "h1")
        ],
        axis=1,
    )
    text_cols = lax.all_gather(after(text_cols, grad_first), "tensor", axis=0, tiled=True)
    gd_cols, gb_cols, h2_cols, h1_cols = (
        text_cols[:, i * depth : (i + 1) * depth] for i in range(4)
    )
    (g_up_all, g_qkv_all), text_ours, text_got = text_whole((use["g_up"][1], after(use["g_qkv_text"], grad_first)))
    down_grad = jnp.stack((down_shard.astype(F32).T, dot_tn(acts_all, gd_cols)))
    up_grad = jnp.stack((up_shard.astype(F32), dot_tn(h2_cols, g_up_all)))
    out_grad = jnp.stack((out_shard.astype(F32).T, dot_tn(attn_all, gb_cols)))
    qkv_grad = jnp.stack((qkv_shard.astype(F32), dot_tn(h1_cols, g_qkv_all)))

    def column_sums(parts):
        return jnp.stack([dot_nn(jnp.ones((8, p.shape[0]), BF), p)[0] for p in parts])

    def own_sums(rows):
        return column_sums((rows[:rows_image], rows[rows_image:]))

    qkv_sums = jnp.stack(
        [
            dot_nt(jnp.ones((8, part.shape[1]), BF), part)[0]
            for part in (use["g_joint"][:, :ctx_image], use["g_joint"][:, ctx_image:])
        ]
    ).reshape(2, heads_here, 3, HEAD)
    up_sums_text = jnp.zeros((ntensor, ncontext, hidden // ncontext), F32)
    up_sums_text = lax.dynamic_update_slice_in_dim(
        up_sums_text,
        by_tensor(column_sums((use["g_up"][1],)).reshape(ntensor, 1, -1), 0),
        context,
        1,
    ).reshape(1, -1)
    up_sums_image = lax.dynamic_update_slice_in_dim(
        jnp.zeros((1, ntensor * hidden), F32), column_sums((use["g_up"][0],)), tensor * hidden, 1
    )
    bias_part = jnp.zeros((2, bias_here * ndev), F32)
    for at, value in (
        (0, jnp.sum(use["mod"].reshape(2, seqs, mods), axis=1)),
        (mods + tensor * local, qkv_sums[:, :, 0].reshape(2, local)),
        (mods + width + tensor * local, qkv_sums[:, :, 2].reshape(2, local)),
        (mods + 2 * width, own_sums(use["g_branch"])),
        (mods + 3 * width, jnp.concatenate((up_sums_image, up_sums_text), 0)),
        (mods + 3 * width + ntensor * hidden, own_sums(use["g_down"])),
    ):
        bias_part = lax.dynamic_update_slice_in_dim(bias_part, value, at, 1)
    mod_sent = use["mod"].reshape(2, 1, seqs, mods)
    mod_sent = jnp.where(jnp.arange(micros)[None, :, None, None] == micro, mod_sent, 0.0)
    bias_sent = bias_part.reshape(2, ndev, bias_here).transpose(1, 0, 2)
    sent = packed(mod_sent.reshape(2, micros * seqs, mods), bias_sent, micros, shares).astype(BF)
    sent = after(sent, text_ours)
    got = jnp.sum(lax.all_to_all(sent, BOTH, 0, 0).astype(F32), axis=0)
    bias_grad = got[table_rows:, :bias_here]
    mod_all = (
        gather_both(after(got[:table_rows, :share].astype(BF), text_got))
        .reshape(micros, shares, 2, seqs, share)
        .transpose(2, 0, 3, 1, 4)
        .reshape(2, micros * seqs, mods)
    )
    ada_grad = jnp.einsum("rc,jrk->jck", silu_cond, mod_all, preferred_element_type=F32)
    cond_inner = jnp.einsum("jrk,jck->rc", mod_all, ada_weight[0], preferred_element_type=F32)
    unused, silu_back = jax.vjp(jax.nn.silu, cond_float)
    cond_grad = silu_back(lax.psum(cond_inner, "section").reshape(cond_float.shape))[0]
    return (
        *out,
        *grad,
        cond_grad,
        ada_grad[None],
        qkv_grad[None],
        out_grad[None],
        up_grad[None],
        down_grad[None],
        bias_grad[None],
    )


def solution(mesh):
    tokens = P(None, BOTH, None)
    block_rows = P("section", None, BOTH, None)
    by_rows = P("section", None, "context", "tensor")
    by_cols = P("section", None, "tensor", "context")
    block_biases = P("section", None, BOTH)
    in_specs = (
        tokens,
        tokens,
        P(None, None, BOTH),
        P(),
        P(),
        block_rows,
        by_rows,
        by_cols,
        by_rows,
        by_cols,
        block_biases,
        tokens,
        tokens,
    )
    out_specs = (
        block_rows,
        block_rows,
        block_rows,
        block_rows,
        P(None, None, BOTH),
        block_rows,
        by_rows,
        by_cols,
        by_rows,
        by_cols,
        block_biases,
    )
    return jax.shard_map(shards, mesh=mesh, in_specs=in_specs, out_specs=out_specs, check_vma=False)
```

```python
from functools import partial

import jax
import jax.numpy as jnp
from jax import lax
from jax.experimental import pallas as pl
from jax.experimental.pallas import tpu as pltpu
from jax.sharding import PartitionSpec as P

HEADS = 24
HEAD = 64
NORM_EPS = 1e-06
MASKED = -1e30
BF = jnp.bfloat16
F32 = jnp.float32
BOTH = ("context", "tensor")


def dot_nn(a, b):
    return lax.dot_general(a, b, (((1,), (0,)), ((), ())), preferred_element_type=F32)


def dot_nt(a, b):
    return lax.dot_general(a, b, (((1,), (1,)), ((), ())), preferred_element_type=F32)


def dot_tn(a, b):
    return lax.dot_general(a, b, (((0,), (0,)), ((), ())), preferred_element_type=F32)


def dot_tt(a, b):
    return lax.dot_general(a, b, (((0,), (1,)), ((), ())), preferred_element_type=F32)


def scaled(q):
    return q * jnp.asarray(HEAD**-0.5, BF)


def attend_body(heads, chunk, places, q_ref, k_ref, v_ref, idq_ref, idk_ref, store, lse_ref):
    at_q, at_k, at_v = places

    def one_chunk(step, carry):
        rows = pl.ds(pl.multiple_of(step * chunk, chunk), chunk)
        bias = jnp.where(idk_ref[...] == idq_ref[:, rows], 0.0, MASKED)
        outs = []
        for head in range(heads):
            at = head * HEAD
            q = scaled(q_ref[rows, at_q + at : at_q + at + HEAD])
            scores = dot_nt(k_ref[:, at_k + at : at_k + at + HEAD], q) + bias
            top = jnp.max(scores, axis=0, keepdims=True)
            weights = jnp.exp(scores - top)
            total = jnp.sum(weights, axis=0, keepdims=True)
            summed = dot_tn(v_ref[:, at_v + at : at_v + at + HEAD], weights.astype(BF))
            outs.append((summed / total).T)
            lse_ref[head : head + 1, rows] = top + jnp.log(total)
        store(rows, jnp.concatenate(outs, axis=1).astype(BF))
        return carry

    lax.fori_loop(0, idq_ref.shape[1] // chunk, one_chunk, 0)


def attend_back_body(
    heads, chunk, places, q_ref, k_ref, v_ref, g_ref, lse_ref, idq_ref, idk_ref, store_dq, dk_acc, dv_acc
):
    at_q, at_k, at_v = places
    dk_acc[...] = jnp.zeros_like(dk_acc)
    dv_acc[...] = jnp.zeros_like(dv_acc)

    def one_chunk(step, carry):
        rows = pl.ds(pl.multiple_of(step * chunk, chunk), chunk)
        bias = jnp.where(idk_ref[...] == idq_ref[:, rows], 0.0, MASKED)
        grads = []
        for head in range(heads):
            at = head * HEAD
            q = scaled(q_ref[rows, at_q + at : at_q + at + HEAD])
            g = g_ref[rows, at : at + HEAD]
            k = k_ref[:, at_k + at : at_k + at + HEAD]
            probs = jnp.exp(dot_nt(k, q) + bias - lse_ref[head : head + 1, rows])
            dv_acc[head] += dot_nn(probs.astype(BF), g)
            both = probs * dot_nt(v_ref[:, at_v + at : at_v + at + HEAD], g)
            delta = jnp.sum(both, axis=0, keepdims=True)
            dscores = (both - probs * delta).astype(BF)
            dk_acc[head] += dot_nn(dscores, q)
            grads.append((dot_tn(k, dscores) * HEAD**-0.5).T)
        store_dq(rows, jnp.concatenate(grads, axis=1).astype(BF))
        return carry

    lax.fori_loop(0, idq_ref.shape[1] // chunk, one_chunk, 0)


def heads_of(acc):
    return jnp.concatenate([acc[head] for head in range(acc.shape[0])], axis=1).astype(BF)


def attend_costs(queries, keys, heads, factor):
    return pl.CostEstimate(
        flops=factor * queries * keys * heads * HEAD,
        bytes_accessed=2 * (queries + 2 * keys) * heads * HEAD * factor // 4,
        transcendentals=queries * keys * heads,
    )


def chunk_for(keys):
    return 256 if keys <= 1024 else 128


VMEM_LIMIT = pltpu.CompilerParams(vmem_limit_bytes=56 * 2**20)


def attend(q, k, v, ids_q, ids_k, heads):
    queries, keys = q.shape[0], k.shape[0]

    def kernel(q_ref, k_ref, v_ref, idq_ref, idk_ref, out_ref, lse_ref):
        def store(rows, value):
            out_ref[rows, :] = value

        attend_body(
            heads, chunk_for(keys), (0, 0, 0), q_ref, k_ref, v_ref, idq_ref, idk_ref, store, lse_ref
        )

    return pl.pallas_call(
        kernel,
        out_shape=(
            jax.ShapeDtypeStruct((queries, heads * HEAD), BF),
            jax.ShapeDtypeStruct((heads, queries), F32),
        ),
        compiler_params=VMEM_LIMIT,
        cost_estimate=attend_costs(queries, keys, heads, 4),
    )(q, k, v, ids_q.reshape(1, queries), ids_k.reshape(keys, 1))


def attend_back(q, k, v, g, lse, ids_q, ids_k, heads):
    queries, keys = q.shape[0], k.shape[0]

    def kernel(
        q_ref, k_ref, v_ref, g_ref, lse_ref, idq_ref, idk_ref, dq_ref, dk_ref, dv_ref, dk_acc, dv_acc
    ):
        def store(rows, value):
            dq_ref[rows, :] = value

        attend_back_body(
            heads, chunk_for(keys), (0, 0, 0), q_ref, k_ref, v_ref, g_ref, lse_ref, idq_ref, idk_ref,
            store, dk_acc, dv_acc,
        )
        dk_ref[...] = heads_of(dk_acc)
        dv_ref[...] = heads_of(dv_acc)

    return pl.pallas_call(
        kernel,
        out_shape=(
            jax.ShapeDtypeStruct((queries, heads * HEAD), BF),
            jax.ShapeDtypeStruct((keys, heads * HEAD), BF),
            jax.ShapeDtypeStruct((keys, heads * HEAD), BF),
        ),
        scratch_shapes=[pltpu.VMEM((heads, keys, HEAD), F32), pltpu.VMEM((heads, keys, HEAD), F32)],
        compiler_params=VMEM_LIMIT,
        cost_estimate=attend_costs(queries, keys, heads, 10),
    )(q, k, v, g, lse, ids_q.reshape(1, queries), ids_k.reshape(keys, 1))


def attend_pair(mine, theirs, ids, heads):
    wide, half = mine.shape
    rows_all, group = 2 * half, heads * HEAD
    chunk = 256

    def kernel(mine_ref, theirs_ref, idq_ref, idk_ref, here_ref, there_ref, lse_ref, x_ref, out_ref):
        x_ref[:, :half] = mine_ref[...]
        x_ref[:, half:] = theirs_ref[...]

        def one_chunk(step, carry):
            rows = pl.ds(pl.multiple_of(step * chunk, chunk), chunk)
            bias = jnp.where(idk_ref[...] == idq_ref[:, rows], 0.0, MASKED)
            for head in range(heads):
                at = slice(head * HEAD, (head + 1) * HEAD)
                base = 3 * head * HEAD
                q = scaled(x_ref[base : base + HEAD, rows])
                k = x_ref[base + HEAD : base + 2 * HEAD, :]
                v = x_ref[base + 2 * HEAD : base + 3 * HEAD, :]
                scores = dot_tn(k, q) + bias
                top = jnp.max(scores, axis=0, keepdims=True)
                weights = jnp.exp(scores - top)
                total = jnp.sum(weights, axis=0, keepdims=True)
                out_ref[at, rows] = (dot_nn(v, weights.astype(BF)) / total).astype(BF)
                lse_ref[head : head + 1, rows] = top + jnp.log(total)
            return carry

        lax.fori_loop(0, rows_all // chunk, one_chunk, 0)
        here_ref[...] = out_ref[:, :half]
        there_ref[...] = out_ref[:, half:]

    return pl.pallas_call(
        kernel,
        out_shape=(
            jax.ShapeDtypeStruct((group, half), BF),
            jax.ShapeDtypeStruct((group, half), BF),
            jax.ShapeDtypeStruct((heads, rows_all), F32),
        ),
        scratch_shapes=[pltpu.VMEM((wide, rows_all), BF), pltpu.VMEM((group, rows_all), BF)],
        compiler_params=VMEM_LIMIT,
        cost_estimate=attend_costs(rows_all, rows_all, heads, 4),
    )(mine, theirs, ids.reshape(1, rows_all), ids.reshape(rows_all, 1))


def attend_pair_back(mine, theirs, g_mine, g_theirs, lse, ids, heads):
    wide, half = mine.shape
    rows_all, group = 2 * half, heads * HEAD
    chunk = 256

    def kernel(
        mine_ref, theirs_ref, gm_ref, gt_ref, lse_ref, idq_ref, idk_ref, dmine_ref, dtheirs_ref,
        x_ref, g_ref, dq_ref, dk_ref, dv_ref,
    ):
        x_ref[:, :half] = mine_ref[...]
        x_ref[:, half:] = theirs_ref[...]
        g_ref[:, :half] = gm_ref[...]
        g_ref[:, half:] = gt_ref[...]
        dk_ref[...] = jnp.zeros_like(dk_ref)
        dv_ref[...] = jnp.zeros_like(dv_ref)

        def one_chunk(step, carry):
            rows = pl.ds(pl.multiple_of(step * chunk, chunk), chunk)
            bias = jnp.where(idk_ref[...] == idq_ref[:, rows], 0.0, MASKED)
            for head in range(heads):
                at = slice(head * HEAD, (head + 1) * HEAD)
                base = 3 * head * HEAD
                q = scaled(x_ref[base : base + HEAD, rows])
                g = g_ref[at, rows]
                k = x_ref[base + HEAD : base + 2 * HEAD, :]
                v = x_ref[base + 2 * HEAD : base + 3 * HEAD, :]
                probs = jnp.exp(dot_tn(k, q) + bias - lse_ref[head : head + 1, rows])
                dv_ref[at, :] += dot_nt(g, probs.astype(BF))
                both = probs * dot_tn(v, g)
                delta = jnp.sum(both, axis=0, keepdims=True)
                dscores = (both - probs * delta).astype(BF)
                dk_ref[at, :] += dot_nt(q, dscores)
                dq_ref[at, rows] = (dot_nn(k, dscores) * HEAD**-0.5).astype(BF)
            return carry

        lax.fori_loop(0, rows_all // chunk, one_chunk, 0)
        for out_ref, cols in ((dmine_ref, slice(0, half)), (dtheirs_ref, slice(half, rows_all))):
            for head in range(heads):
                at = slice(head * HEAD, (head + 1) * HEAD)
                base = 3 * head * HEAD
                out_ref[base : base + HEAD, :] = dq_ref[at, cols]
                out_ref[base + HEAD : base + 2 * HEAD, :] = dk_ref[at, cols].astype(BF)
                out_ref[base + 2 * HEAD : base + 3 * HEAD, :] = dv_ref[at, cols].astype(BF)

    return pl.pallas_call(
        kernel,
        out_shape=(jax.ShapeDtypeStruct((wide, half), BF), jax.ShapeDtypeStruct((wide, half), BF)),
        scratch_shapes=[
            pltpu.VMEM((wide, rows_all), BF),
            pltpu.VMEM((group, rows_all), BF),
            pltpu.VMEM((group, rows_all), BF),
            pltpu.VMEM((group, rows_all), F32),
            pltpu.VMEM((group, rows_all), F32),
        ],
        compiler_params=VMEM_LIMIT,
        cost_estimate=attend_costs(rows_all, rows_all, heads, 10),
    )(mine, theirs, g_mine, g_theirs, lse, ids.reshape(1, rows_all), ids.reshape(rows_all, 1))


def after(x, *others):
    anywhere = pl.BlockSpec(memory_space=pl.ANY)

    def kernel(*refs):
        pass

    return pl.pallas_call(
        kernel,
        out_shape=jax.ShapeDtypeStruct(x.shape, x.dtype),
        in_specs=[anywhere] * (1 + len(others)),
        out_specs=anywhere,
        input_output_aliases={0: 0},
    )(x, *others)


def lanes(n):
    return -(-n // 128) * 128


def packed(sums, rest, groups_of, shares):
    rows, columns = sums.shape[1], sums.shape[2]
    seqs, share, extra = rows // groups_of, columns // shares, rest.shape[2]
    wide = lanes(max(share, extra))

    def kernel(sums_ref, rest_ref, out_ref):
        for group in range(groups_of):
            for j in range(2):
                out_ref[group, 0, j * seqs : (j + 1) * seqs, :share] = sums_ref[
                    j, group * seqs : (group + 1) * seqs, :
                ]
            out_ref[group, 0, 2 * seqs : 2 * seqs + 2, :extra] = rest_ref[group, 0]

    if share % 128 == 0:
        sums_in, sums_spec = sums, pl.BlockSpec((2, rows, share), lambda k: (0, 0, k))
    else:
        sums_in = sums.reshape(2, rows, shares, share).transpose(2, 0, 1, 3)
        sums_spec = pl.BlockSpec((None, 2, rows, share), lambda k: (k, 0, 0, 0))
    out = pl.pallas_call(
        kernel,
        grid=(shares,),
        in_specs=[sums_spec, pl.BlockSpec((groups_of, 1, 2, extra), lambda k: (0, k, 0, 0))],
        out_specs=pl.BlockSpec((groups_of, 1, 8, wide), lambda k: (0, k, 0, 0)),
        out_shape=jax.ShapeDtypeStruct((groups_of, shares, 8, wide), F32),
    )(sums_in, rest.reshape(groups_of, shares, 2, extra))
    return out.reshape(groups_of * shares, 8, wide)


def normalized(x):
    centred = x - jnp.mean(x, axis=-1, keepdims=True)
    inverse = lax.rsqrt(jnp.mean(centred * centred, axis=-1, keepdims=True) + NORM_EPS)
    return centred * inverse, inverse


def norm_back(n, inverse, w):
    return (w - jnp.mean(w, axis=-1, keepdims=True) - n * jnp.mean(w * n, axis=-1, keepdims=True)) * inverse


def gelu_pair(u):
    c = 0.7978845608028654
    inner = jnp.tanh(c * (u + 0.044715 * u * u * u))
    value = 0.5 * u * (1.0 + inner)
    slope = 0.5 * (1.0 + inner) + 0.5 * u * (1.0 - inner * inner) * c * (1.0 + 3 * 0.044715 * u * u)
    return value.astype(BF), slope.astype(BF)


def shards(
    image_tokens,
    text_tokens,
    conditioning,
    image_seq_ids,
    text_seq_ids,
    ada_weight,
    qkv_weight,
    out_weight,
    up_weight,
    down_weight,
    biases,
    image_cotangent,
    text_cotangent,
):
    section = lax.axis_index("section")
    context = lax.axis_index("context")
    tensor = lax.axis_index("tensor")
    ncontext = lax.axis_size("context")
    ntensor = lax.axis_size("tensor")
    ndev = ncontext * ntensor
    first = section == 0
    micros, own_image, width = image_tokens.shape
    own_text = text_tokens.shape[1]
    seqs = conditioning.shape[1]
    rows_image, rows_text = micros * own_image, micros * own_text
    heads_here = HEADS // ntensor
    local = heads_here * HEAD
    hidden = up_weight.shape[3]
    bias_here = biases.shape[2]
    depth = qkv_weight.shape[2]
    mods = 6 * width
    table_rows = 2 * seqs
    per = ncontext // micros
    micro = context // per
    paired = per == 2 and heads_here % 2 == 0
    groups = 2 if paired else 1
    group_heads = heads_here // groups
    group = group_heads * HEAD
    side = context % per
    ctx_image, ctx_text = ntensor * rows_image, ntensor * rows_text
    ctx_rows = ctx_image + ctx_text

    order = (0, 2, 1, 3)

    def swapped(x, axis, bit):
        return lax.ppermute(x, axis, [(i, i ^ bit) for i in range(lax.axis_size(axis))])

    def sided(a, b):
        return jnp.where(side == 0, a, b), jnp.where(side == 0, b, a)

    def near(x):
        return swapped(x, "tensor", 1)

    def far(x):
        return swapped(x, "tensor", 2)

    def gather_tensor(x):
        beside = near(x)
        across = far(x)
        return x, across, beside, near(across)

    def reduce_tensor(x):
        n = x.shape[0] // 4
        got = near(x[2 * n :])
        mine = x[: 2 * n].astype(F32) + got.astype(F32)
        return mine[:n] + far(mine[n:].astype(BF)).astype(F32)

    def spread(rows):
        return jnp.concatenate(gather_tensor(rows), 0)

    def spread_both(rows):
        return [spread(rows[:rows_image]), spread(rows[rows_image:])]

    def collect(image_rows, text_rows):
        return jnp.concatenate(
            (reduce_tensor(image_rows.astype(BF)), reduce_tensor(text_rows.astype(BF))), 0
        )

    def gather_both(x):
        got = lax.all_gather(x, "tensor")
        got = lax.all_to_all(jnp.broadcast_to(got[None], (ncontext,) + got.shape), "context", 0, 0)
        return got.reshape((ndev,) + x.shape)

    def rounds(step, back):
        pairs = []
        for h in range(ncontext):
            m = (h + step) % micros
            pairs.append((h, m * per + h // micros))
        return [(b, a) for a, b in pairs] if back else pairs

    def to_work(image, text):
        pieces = []
        for step in range(micros):
            m = (context + step) % micros
            pieces.append(
                [
                    lax.ppermute(
                        lax.dynamic_index_in_dim(x, m, 0, keepdims=False), "context", rounds(step, False)
                    )
                    for x in (image, text)
                ]
            )
        return jnp.concatenate([p[0] for p in pieces] + [p[1] for p in pieces], 0).astype(F32)

    def to_home(rows):
        image, text = [], []
        for step in range(micros):
            image.append(
                lax.ppermute(
                    rows[step * own_image : (step + 1) * own_image], "context", rounds(step, True)
                )
            )
            at = rows_image + step * own_text
            text.append(lax.ppermute(rows[at : at + own_text], "context", rounds(step, True)))
        image, text = jnp.stack(image), jnp.stack(text)
        turns = [(m - context) % micros for m in range(micros)]
        return tuple(
            jnp.stack([lax.dynamic_index_in_dim(x, turn, 0, keepdims=False) for turn in turns])[None]
            for x in (image, text)
        )

    def gathered(w):
        return lax.all_gather(w, "context", axis=0, tiled=True)

    qkv_full = [gathered(qkv_weight[0, j]) for j in range(2)]
    out_both = gathered(jnp.concatenate([out_weight[0, j].T for j in range(2)], axis=1))
    out_full = [out_both[:, :local], out_both[:, local:]]
    up_full = [gathered(up_weight[0, j]) for j in range(2)]
    down_full = [gathered(down_weight[0, j].T) for j in range(2)]

    cond_float = conditioning.astype(F32)
    silu_cond = jax.nn.silu(cond_float).astype(BF).reshape(micros * seqs, -1)
    ada_part = jnp.einsum("rc,jck->jrk", silu_cond, ada_weight[0], preferred_element_type=F32)
    sharing = [[m * per + u for u in range(per)] for m in range(micros)]
    shares = per * ntensor
    share = mods // shares
    bias_placed = lax.dynamic_update_slice_in_dim(
        jnp.zeros((2, bias_here * ndev), F32),
        biases[0].astype(F32),
        (context * ntensor + tensor) * bias_here,
        1,
    )
    ada_sent = packed(
        ada_part + bias_placed[:, None, :mods],
        jnp.broadcast_to(biases[0].astype(F32)[None], (ndev, 2, bias_here)),
        micros,
        shares,
    )
    ada_got = lax.all_to_all(ada_sent.astype(BF), BOTH, 0, 0)
    bias_full = ada_got[:, table_rows : table_rows + 2, :bias_here].transpose(1, 0, 2).reshape(2, -1).astype(F32)
    ada_sum = jnp.sum(ada_got[:, :table_rows, :share].astype(F32), axis=0).astype(BF)
    table = lax.all_gather(ada_sum, "tensor")
    if paired:
        table = jnp.stack(sided(table, swapped(table, "context", 1)))
    else:
        table = lax.all_gather(table, "context", axis_index_groups=sharing)
    table = table.reshape(shares, table_rows, share).transpose(1, 0, 2).reshape(table_rows, mods)
    query_bias = lax.dynamic_slice_in_dim(bias_full, mods + tensor * local, local, 1)
    value_bias = lax.dynamic_slice_in_dim(bias_full, mods + width + tensor * local, local, 1)
    qkv_bias = jnp.stack(
        (
            query_bias.reshape(2, heads_here, HEAD),
            jnp.zeros((2, heads_here, HEAD), F32),
            value_bias.reshape(2, heads_here, HEAD),
        ),
        axis=2,
    ).reshape(2, 3 * local)
    out_bias = bias_full[:, mods + 2 * width : mods + 3 * width]
    at_up = mods + 3 * width
    up_bias = lax.dynamic_slice_in_dim(bias_full, at_up + tensor * hidden, hidden, 1)
    down_bias = bias_full[:, mods + 3 * width + hidden * ntensor :]

    def by_modality(pair):
        return jnp.concatenate(
            (
                jnp.broadcast_to(pair[0][None], (rows_image, width)),
                jnp.broadcast_to(pair[1][None], (rows_text, width)),
            ),
            0,
        )

    def ids_of(work_context):
        m, u = work_context // per, work_context % per
        homes = jnp.stack([u * micros + (m - step) % micros for step in range(micros)])
        places = homes[None, :] * ntensor + (tensor ^ jnp.array(order))[:, None]
        found = []
        for ids, own in ((image_seq_ids, own_image), (text_seq_ids, own_text)):
            table_ids = lax.dynamic_index_in_dim(ids, m, 0, keepdims=False).reshape(ndev, own)
            found.append(jnp.take(table_ids, places.reshape(-1), axis=0).reshape(-1))
        return found

    own_found = ids_of(context)
    own_ids = jnp.concatenate((own_found[0][:rows_image], own_found[1][:rows_text] + seqs))
    onehot = (own_ids[:, None] == jnp.arange(table_rows)[None, :]).astype(BF)
    row_mods = dot_nn(onehot, table).astype(BF)
    joint_ids = jnp.concatenate(own_found)
    if paired:
        attn_ids = jnp.concatenate([joint_ids] + ids_of(context ^ 1))
    else:
        attn_ids = jnp.concatenate([x for u in range(per) for x in ids_of(micro * per + u)])

    def row_mod(index):
        return row_mods[:, index * width : (index + 1) * width].astype(F32)

    def attention(joint):
        if paired:
            mine, theirs = sided(joint[: 3 * group], joint[3 * group :])
            theirs = swapped(theirs, "context", 1)
            here, there, lse = attend_pair(mine, theirs, attn_ids, group_heads)
            return jnp.concatenate(sided(here, swapped(there, "context", 1)), axis=0), (mine, theirs, lse)
        by_kind = joint.reshape(heads_here, 3, HEAD, ctx_rows)
        q, k, v = (by_kind[:, i].reshape(local, ctx_rows).T for i in range(3))
        k, v = (
            lax.all_gather(x, "context", axis=0, tiled=True, axis_index_groups=sharing) for x in (k, v)
        )
        attended, lse = attend(q, k, v, joint_ids, attn_ids, group_heads)
        return attended.T, (q, k, v, lse)

    def attention_back(grad, kept):
        if paired:
            mine, theirs, lse = kept
            g_mine, g_theirs = sided(grad[:group], grad[group:])
            g_theirs = swapped(g_theirs, "context", 1)
            d_mine, d_theirs = attend_pair_back(mine, theirs, g_mine, g_theirs, lse, attn_ids, group_heads)
            return jnp.concatenate(sided(d_mine, swapped(d_theirs, "context", 1)), axis=0)
        q, k, v, lse = kept
        dq, dk, dv = attend_back(q, k, v, grad.T, lse, joint_ids, attn_ids, group_heads)
        dk, dv = (
            lax.psum_scatter(x, "context", scatter_dimension=0, tiled=True, axis_index_groups=sharing)
            for x in (dk, dv)
        )
        kinds = [x.T.reshape(heads_here, HEAD, ctx_rows) for x in (dq, dk, dv)]
        return jnp.stack(kinds, axis=1).reshape(3 * local, ctx_rows)

    def forward(x):
        n1, inv1 = normalized(x)
        h1 = spread_both((n1 * (1.0 + row_mod(1)) + row_mod(0)).astype(BF))
        joint = jnp.concatenate(
            [(dot_tt(qkv_full[j], h1[j]) + qkv_bias[j][:, None]).astype(BF) for j in range(2)], axis=1
        )
        attended, kept = attention(joint)
        branch = collect(
            dot_tt(attended, out_full[0])[:ctx_image], dot_tt(attended[:, ctx_image:], out_full[1])
        ) + by_modality(out_bias)
        middle = x + row_mod(2) * branch
        n2, inv2 = normalized(middle)
        h2 = spread_both((n2 * (1.0 + row_mod(4)) + row_mod(3)).astype(BF))
        pairs = [gelu_pair(dot_nn(h2[j], up_full[j]) + up_bias[j]) for j in range(2)]
        acts, slopes = [p[0] for p in pairs], [p[1] for p in pairs]
        down = collect(*(dot_nt(acts[j], down_full[j]) for j in range(2))) + by_modality(down_bias)
        out = middle + row_mod(5) * down
        saved = dict(
            x=x, h1=h1, kept=kept, attn=attended, branch=branch, middle=middle, h2=h2, acts=acts,
            slopes=slopes, down=down,
        )
        return out, saved

    def chosen(a, b):
        return jax.tree.map(lambda x, y: jnp.where(first, x, y), a, b)

    def scattered(full):
        return lax.psum_scatter(full.astype(BF), "context", scatter_dimension=0, tiled=True)

    def backward(saved, g_out, last=None):
        g_down = (row_mod(5) * g_out).astype(BF)
        gd = spread_both(g_down)
        g_up = [
            (dot_nn(gd[j], down_full[j]) * saved["slopes"][j].astype(F32)).astype(BF) for j in range(2)
        ]
        g_h2 = collect(*(dot_nt(g_up[j], up_full[j]) for j in range(2)))
        early = []
        if last:
            use = chosen(
                dict(h2=saved["h2"][0], acts=saved["acts"][0], gd=gd[0], g_up=g_up[0]),
                {k: last[k][0] for k in ("h2", "acts", "gd", "g_up")},
            )
            early = [
                dot_tn(use["gd"], use["acts"]).astype(BF),
                dot_tn(use["h2"], use["g_up"]).astype(BF),
            ]
            g_h2 = after(g_h2, *early)
            early = [scattered(part) for part in early]
        n2, inv2 = normalized(saved["middle"])
        g_middle = g_out + norm_back(n2, inv2, g_h2 * (1.0 + row_mod(4)))
        g_branch = (row_mod(2) * g_middle).astype(BF)
        gb = spread_both(g_branch)
        g_attn = jnp.concatenate([dot_tt(out_full[j], gb[j]).astype(BF) for j in range(2)], axis=1)
        if last:
            use = chosen(dict(gb=gb[0], attn=saved["attn"]), dict(gb=last["gb"][0], attn=last["attn"]))
            early.append(dot_tt(use["gb"], use["attn"][:, :ctx_image]).astype(BF))
            g_attn = after(g_attn, early[2])
        g_joint = attention_back(g_attn, saved["kept"])
        g_h1 = collect(
            dot_tt(g_joint, qkv_full[0])[:ctx_image], dot_tt(g_joint[:, ctx_image:], qkv_full[1])
        )
        n1, inv1 = normalized(saved["x"])
        g_x = g_middle + norm_back(n1, inv1, g_h1 * (1.0 + row_mod(1)))
        if last:
            g_x = after(g_x, *early[:2])
        row_grads = jnp.concatenate(
            [
                part.astype(BF)
                for part in (
                    g_h1, g_h1 * n1, g_middle * saved["branch"], g_h2, g_h2 * n2, g_out * saved["down"]
                )
            ],
            axis=1,
        )
        mod_grad = dot_tn(onehot, row_grads)
        tensors = dict(
            h1=saved["h1"], attn=saved["attn"], h2=saved["h2"], acts=saved["acts"], g_joint=g_joint,
            gb=gb, g_up=g_up, gd=gd, g_down=g_down, g_branch=g_branch, mod=mod_grad,
        )
        return g_x, tensors, early

    def blocks(rows):
        return rows.reshape(ctx_text, ncontext, depth).transpose(1, 0, 2)

    def copies(rows):
        return jnp.broadcast_to(rows[None], (ncontext,) + rows.shape)

    def text_round(parts):
        sent = jnp.concatenate(parts, axis=2)
        got = lax.all_to_all(sent, "context", 0, 0).reshape(ncontext * ctx_text, -1)
        cuts, at = [], 0
        for p in parts:
            cuts.append(got[:, at : at + p.shape[2]])
            at += p.shape[2]
        return cuts, got

    def handed(rows, by):
        return lax.ppermute(rows.astype(BF), "section", [(0, 1)] if by > 0 else [(1, 0)]).astype(F32)

    out_first, saved_first = forward(to_work(image_tokens, text_tokens))
    out_last, saved_last = forward(handed(out_first, 1))
    grad_last, tensors_last, unused = backward(saved_last, to_work(image_cotangent, text_cotangent))
    kept = chosen(
        dict(acts=saved_first["acts"][1], attn=saved_first["attn"][:, ctx_image:], h1=saved_first["h1"][1], h2=saved_first["h2"][1]),
        dict(acts=saved_last["acts"][1], attn=saved_last["attn"][:, ctx_image:], h1=saved_last["h1"][1], h2=saved_last["h2"][1]),
    )
    (acts_all, attn_all, h1_cols, h2_cols), acts_got = text_round(
        (copies(kept["acts"]), copies(kept["attn"].T), blocks(kept["h1"]), blocks(kept["h2"]))
    )
    out = to_home(jnp.where(first, out_first, out_last))
    returned = after(handed(grad_last, -1), acts_got, *out)
    grad_first, tensors_first, early = backward(saved_first, returned, tensors_last)
    grad = to_home(jnp.where(first, grad_first, grad_last))
    use = chosen(tensors_first, tensors_last)

    down_shard, up_shard, out_part = early
    out_shard = after(scattered(out_part), grad_first)
    qkv_shard = after(scattered(dot_tt(use["h1"][0], use["g_joint"][:, :ctx_image])), grad_first)

    (gd_cols, gb_cols, g_up_all, g_qkv_all), text_got = text_round(
        (
            blocks(use["gd"][1]),
            blocks(use["gb"][1]),
            copies(use["g_up"][1]),
            copies(use["g_joint"][:, ctx_image:].T),
        )
    )
    down_grad = jnp.stack((down_shard.astype(F32).T, dot_tn(acts_all, gd_cols)))
    up_grad = jnp.stack((up_shard.astype(F32), dot_tn(h2_cols, g_up_all)))
    out_grad = jnp.stack((out_shard.astype(F32).T, dot_tn(attn_all, gb_cols)))
    qkv_grad = jnp.stack((qkv_shard.astype(F32), dot_tn(h1_cols, g_qkv_all)))

    def column_sums(parts):
        return jnp.stack([dot_nn(jnp.ones((8, p.shape[0]), BF), p)[0] for p in parts])

    def own_sums(rows):
        return column_sums((rows[:rows_image], rows[rows_image:]))

    qkv_sums = jnp.stack(
        [
            dot_nt(jnp.ones((8, part.shape[1]), BF), part)[0]
            for part in (use["g_joint"][:, :ctx_image], use["g_joint"][:, ctx_image:])
        ]
    ).reshape(2, heads_here, 3, HEAD)
    bias_part = jnp.zeros((2, bias_here * ndev), F32)
    for at, value in (
        (0, jnp.sum(use["mod"].reshape(2, seqs, mods), axis=1)),
        (mods + tensor * local, qkv_sums[:, :, 0].reshape(2, local)),
        (mods + width + tensor * local, qkv_sums[:, :, 2].reshape(2, local)),
        (mods + 2 * width, own_sums(use["g_branch"])),
        (mods + 3 * width + tensor * hidden, column_sums(use["g_up"])),
        (mods + 3 * width + ntensor * hidden, own_sums(use["g_down"])),
    ):
        bias_part = lax.dynamic_update_slice_in_dim(bias_part, value, at, 1)
    mod_sent = use["mod"].reshape(2, 1, seqs, mods)
    mod_sent = jnp.where(jnp.arange(micros)[None, :, None, None] == micro, mod_sent, 0.0)
    bias_sent = bias_part.reshape(2, ndev, bias_here).transpose(1, 0, 2)
    sent = packed(mod_sent.reshape(2, micros * seqs, mods), bias_sent, micros, shares).astype(BF)
    got = jnp.sum(lax.all_to_all(sent, BOTH, 0, 0).astype(F32), axis=0)
    bias_grad = got[table_rows:, :bias_here]
    mod_all = (
        gather_both(after(got[:table_rows, :share].astype(BF), text_got))
        .reshape(micros, shares, 2, seqs, share)
        .transpose(2, 0, 3, 1, 4)
        .reshape(2, micros * seqs, mods)
    )
    ada_grad = jnp.einsum("rc,jrk->jck", silu_cond, mod_all, preferred_element_type=F32)
    cond_inner = jnp.einsum("jrk,jck->rc", mod_all, ada_weight[0], preferred_element_type=F32)
    unused, silu_back = jax.vjp(jax.nn.silu, cond_float)
    cond_grad = silu_back(lax.psum(cond_inner, "section").reshape(cond_float.shape))[0]
    return (
        *out,
        *grad,
        cond_grad,
        ada_grad[None],
        qkv_grad[None],
        out_grad[None],
        up_grad[None],
        down_grad[None],
        bias_grad[None],
    )


def solution(mesh):
    tokens = P(None, BOTH, None)
    block_rows = P("section", None, BOTH, None)
    by_rows = P("section", None, "context", "tensor")
    by_cols = P("section", None, "tensor", "context")
    block_biases = P("section", None, BOTH)
    in_specs = (
        tokens,
        tokens,
        P(None, None, BOTH),
        P(),
        P(),
        block_rows,
        by_rows,
        by_cols,
        by_rows,
        by_cols,
        block_biases,
        tokens,
        tokens,
    )
    out_specs = (
        block_rows,
        block_rows,
        block_rows,
        block_rows,
        P(None, None, BOTH),
        block_rows,
        by_rows,
        by_cols,
        by_rows,
        by_cols,
        block_biases,
    )
    return jax.shard_map(shards, mesh=mesh, in_specs=in_specs, out_specs=out_specs, check_vma=False)
```

```python
from functools import partial

import jax
import jax.numpy as jnp
from jax import lax
from jax.experimental import pallas as pl
from jax.experimental.pallas import tpu as pltpu
from jax.sharding import PartitionSpec as P

HEADS = 24
HEAD = 64
NORM_EPS = 1e-06
MASKED = -1e30
BF = jnp.bfloat16
F32 = jnp.float32
BOTH = ("context", "tensor")


def dot_nn(a, b):
    return lax.dot_general(a, b, (((1,), (0,)), ((), ())), preferred_element_type=F32)


def dot_nt(a, b):
    return lax.dot_general(a, b, (((1,), (1,)), ((), ())), preferred_element_type=F32)


def dot_tn(a, b):
    return lax.dot_general(a, b, (((0,), (0,)), ((), ())), preferred_element_type=F32)


def dot_tt(a, b):
    return lax.dot_general(a, b, (((0,), (1,)), ((), ())), preferred_element_type=F32)


def scaled(q):
    return q * jnp.asarray(HEAD**-0.5, BF)


def attend_body(heads, chunk, places, q_ref, k_ref, v_ref, idq_ref, idk_ref, store, lse_ref):
    at_q, at_k, at_v = places

    def one_chunk(step, carry):
        rows = pl.ds(pl.multiple_of(step * chunk, chunk), chunk)
        bias = jnp.where(idk_ref[...] == idq_ref[:, rows], 0.0, MASKED)
        outs = []
        for head in range(heads):
            at = head * HEAD
            q = scaled(q_ref[rows, at_q + at : at_q + at + HEAD])
            scores = dot_nt(k_ref[:, at_k + at : at_k + at + HEAD], q) + bias
            top = jnp.max(scores, axis=0, keepdims=True)
            weights = jnp.exp(scores - top)
            total = jnp.sum(weights, axis=0, keepdims=True)
            summed = dot_tn(v_ref[:, at_v + at : at_v + at + HEAD], weights.astype(BF))
            outs.append((summed / total).T)
            lse_ref[head : head + 1, rows] = top + jnp.log(total)
        store(rows, jnp.concatenate(outs, axis=1).astype(BF))
        return carry

    lax.fori_loop(0, idq_ref.shape[1] // chunk, one_chunk, 0)


def attend_back_body(
    heads, chunk, places, q_ref, k_ref, v_ref, g_ref, lse_ref, idq_ref, idk_ref, store_dq, dk_acc, dv_acc
):
    at_q, at_k, at_v = places
    dk_acc[...] = jnp.zeros_like(dk_acc)
    dv_acc[...] = jnp.zeros_like(dv_acc)

    def one_chunk(step, carry):
        rows = pl.ds(pl.multiple_of(step * chunk, chunk), chunk)
        bias = jnp.where(idk_ref[...] == idq_ref[:, rows], 0.0, MASKED)
        grads = []
        for head in range(heads):
            at = head * HEAD
            q = scaled(q_ref[rows, at_q + at : at_q + at + HEAD])
            g = g_ref[rows, at : at + HEAD]
            k = k_ref[:, at_k + at : at_k + at + HEAD]
            probs = jnp.exp(dot_nt(k, q) + bias - lse_ref[head : head + 1, rows])
            dv_acc[head] += dot_nn(probs.astype(BF), g)
            both = probs * dot_nt(v_ref[:, at_v + at : at_v + at + HEAD], g)
            delta = jnp.sum(both, axis=0, keepdims=True)
            dscores = (both - probs * delta).astype(BF)
            dk_acc[head] += dot_nn(dscores, q)
            grads.append((dot_tn(k, dscores) * HEAD**-0.5).T)
        store_dq(rows, jnp.concatenate(grads, axis=1).astype(BF))
        return carry

    lax.fori_loop(0, idq_ref.shape[1] // chunk, one_chunk, 0)


def heads_of(acc):
    return jnp.concatenate([acc[head] for head in range(acc.shape[0])], axis=1).astype(BF)


def attend_costs(queries, keys, heads, factor):
    return pl.CostEstimate(
        flops=factor * queries * keys * heads * HEAD,
        bytes_accessed=2 * (queries + 2 * keys) * heads * HEAD * factor // 4,
        transcendentals=queries * keys * heads,
    )


def chunk_for(keys):
    return 256 if keys <= 1024 else 128


VMEM_LIMIT = pltpu.CompilerParams(vmem_limit_bytes=56 * 2**20)


def attend(q, k, v, ids_q, ids_k, heads):
    queries, keys = q.shape[0], k.shape[0]

    def kernel(q_ref, k_ref, v_ref, idq_ref, idk_ref, out_ref, lse_ref):
        def store(rows, value):
            out_ref[rows, :] = value

        attend_body(
            heads, chunk_for(keys), (0, 0, 0), q_ref, k_ref, v_ref, idq_ref, idk_ref, store, lse_ref
        )

    return pl.pallas_call(
        kernel,
        out_shape=(
            jax.ShapeDtypeStruct((queries, heads * HEAD), BF),
            jax.ShapeDtypeStruct((heads, queries), F32),
        ),
        compiler_params=VMEM_LIMIT,
        cost_estimate=attend_costs(queries, keys, heads, 4),
    )(q, k, v, ids_q.reshape(1, queries), ids_k.reshape(keys, 1))


def attend_back(q, k, v, g, lse, ids_q, ids_k, heads):
    queries, keys = q.shape[0], k.shape[0]

    def kernel(
        q_ref, k_ref, v_ref, g_ref, lse_ref, idq_ref, idk_ref, dq_ref, dk_ref, dv_ref, dk_acc, dv_acc
    ):
        def store(rows, value):
            dq_ref[rows, :] = value

        attend_back_body(
            heads, chunk_for(keys), (0, 0, 0), q_ref, k_ref, v_ref, g_ref, lse_ref, idq_ref, idk_ref,
            store, dk_acc, dv_acc,
        )
        dk_ref[...] = heads_of(dk_acc)
        dv_ref[...] = heads_of(dv_acc)

    return pl.pallas_call(
        kernel,
        out_shape=(
            jax.ShapeDtypeStruct((queries, heads * HEAD), BF),
            jax.ShapeDtypeStruct((keys, heads * HEAD), BF),
            jax.ShapeDtypeStruct((keys, heads * HEAD), BF),
        ),
        scratch_shapes=[pltpu.VMEM((heads, keys, HEAD), F32), pltpu.VMEM((heads, keys, HEAD), F32)],
        compiler_params=VMEM_LIMIT,
        cost_estimate=attend_costs(queries, keys, heads, 10),
    )(q, k, v, g, lse, ids_q.reshape(1, queries), ids_k.reshape(keys, 1))


def attend_pair(mine, theirs, ids, heads):
    wide, half = mine.shape
    rows_all, group = 2 * half, heads * HEAD
    chunk = 256

    def kernel(mine_ref, theirs_ref, idq_ref, idk_ref, here_ref, there_ref, lse_ref, x_ref, out_ref):
        x_ref[:, :half] = mine_ref[...]
        x_ref[:, half:] = theirs_ref[...]

        def one_chunk(step, carry):
            rows = pl.ds(pl.multiple_of(step * chunk, chunk), chunk)
            bias = jnp.where(idk_ref[...] == idq_ref[:, rows], 0.0, MASKED)
            for head in range(heads):
                at = slice(head * HEAD, (head + 1) * HEAD)
                base = 3 * head * HEAD
                q = scaled(x_ref[base : base + HEAD, rows])
                k = x_ref[base + HEAD : base + 2 * HEAD, :]
                v = x_ref[base + 2 * HEAD : base + 3 * HEAD, :]
                scores = dot_tn(k, q) + bias
                top = jnp.max(scores, axis=0, keepdims=True)
                weights = jnp.exp(scores - top)
                total = jnp.sum(weights, axis=0, keepdims=True)
                out_ref[at, rows] = (dot_nn(v, weights.astype(BF)) / total).astype(BF)
                lse_ref[head : head + 1, rows] = top + jnp.log(total)
            return carry

        lax.fori_loop(0, rows_all // chunk, one_chunk, 0)
        here_ref[...] = out_ref[:, :half]
        there_ref[...] = out_ref[:, half:]

    return pl.pallas_call(
        kernel,
        out_shape=(
            jax.ShapeDtypeStruct((group, half), BF),
            jax.ShapeDtypeStruct((group, half), BF),
            jax.ShapeDtypeStruct((heads, rows_all), F32),
        ),
        scratch_shapes=[pltpu.VMEM((wide, rows_all), BF), pltpu.VMEM((group, rows_all), BF)],
        compiler_params=VMEM_LIMIT,
        cost_estimate=attend_costs(rows_all, rows_all, heads, 4),
    )(mine, theirs, ids.reshape(1, rows_all), ids.reshape(rows_all, 1))


def attend_pair_back(mine, theirs, g_mine, g_theirs, lse, ids, heads):
    wide, half = mine.shape
    rows_all, group = 2 * half, heads * HEAD
    chunk = 256

    def kernel(
        mine_ref, theirs_ref, gm_ref, gt_ref, lse_ref, idq_ref, idk_ref, dmine_ref, dtheirs_ref,
        x_ref, g_ref, dq_ref, dk_ref, dv_ref,
    ):
        x_ref[:, :half] = mine_ref[...]
        x_ref[:, half:] = theirs_ref[...]
        g_ref[:, :half] = gm_ref[...]
        g_ref[:, half:] = gt_ref[...]
        dk_ref[...] = jnp.zeros_like(dk_ref)
        dv_ref[...] = jnp.zeros_like(dv_ref)

        def one_chunk(step, carry):
            rows = pl.ds(pl.multiple_of(step * chunk, chunk), chunk)
            bias = jnp.where(idk_ref[...] == idq_ref[:, rows], 0.0, MASKED)
            for head in range(heads):
                at = slice(head * HEAD, (head + 1) * HEAD)
                base = 3 * head * HEAD
                q = scaled(x_ref[base : base + HEAD, rows])
                g = g_ref[at, rows]
                k = x_ref[base + HEAD : base + 2 * HEAD, :]
                v = x_ref[base + 2 * HEAD : base + 3 * HEAD, :]
                probs = jnp.exp(dot_tn(k, q) + bias - lse_ref[head : head + 1, rows])
                dv_ref[at, :] += dot_nt(g, probs.astype(BF))
                both = probs * dot_tn(v, g)
                delta = jnp.sum(both, axis=0, keepdims=True)
                dscores = (both - probs * delta).astype(BF)
                dk_ref[at, :] += dot_nt(q, dscores)
                dq_ref[at, rows] = (dot_nn(k, dscores) * HEAD**-0.5).astype(BF)
            return carry

        lax.fori_loop(0, rows_all // chunk, one_chunk, 0)
        for out_ref, cols in ((dmine_ref, slice(0, half)), (dtheirs_ref, slice(half, rows_all))):
            for head in range(heads):
                at = slice(head * HEAD, (head + 1) * HEAD)
                base = 3 * head * HEAD
                out_ref[base : base + HEAD, :] = dq_ref[at, cols]
                out_ref[base + HEAD : base + 2 * HEAD, :] = dk_ref[at, cols].astype(BF)
                out_ref[base + 2 * HEAD : base + 3 * HEAD, :] = dv_ref[at, cols].astype(BF)

    return pl.pallas_call(
        kernel,
        out_shape=(jax.ShapeDtypeStruct((wide, half), BF), jax.ShapeDtypeStruct((wide, half), BF)),
        scratch_shapes=[
            pltpu.VMEM((wide, rows_all), BF),
            pltpu.VMEM((group, rows_all), BF),
            pltpu.VMEM((group, rows_all), BF),
            pltpu.VMEM((group, rows_all), F32),
            pltpu.VMEM((group, rows_all), F32),
        ],
        compiler_params=VMEM_LIMIT,
        cost_estimate=attend_costs(rows_all, rows_all, heads, 10),
    )(mine, theirs, g_mine, g_theirs, lse, ids.reshape(1, rows_all), ids.reshape(rows_all, 1))


def after(x, *others):
    anywhere = pl.BlockSpec(memory_space=pl.ANY)

    def kernel(*refs):
        pass

    return pl.pallas_call(
        kernel,
        out_shape=jax.ShapeDtypeStruct(x.shape, x.dtype),
        in_specs=[anywhere] * (1 + len(others)),
        out_specs=anywhere,
        input_output_aliases={0: 0},
    )(x, *others)


def lanes(n):
    return -(-n // 128) * 128


def packed(sums, rest, groups_of, shares):
    rows, columns = sums.shape[1], sums.shape[2]
    seqs, share, extra = rows // groups_of, columns // shares, rest.shape[2]
    wide = lanes(max(share, extra))

    def kernel(sums_ref, rest_ref, out_ref):
        for group in range(groups_of):
            for j in range(2):
                out_ref[group, 0, j * seqs : (j + 1) * seqs, :share] = sums_ref[
                    j, group * seqs : (group + 1) * seqs, :
                ]
            out_ref[group, 0, 2 * seqs : 2 * seqs + 2, :extra] = rest_ref[group, 0]

    if share % 128 == 0:
        sums_in, sums_spec = sums, pl.BlockSpec((2, rows, share), lambda k: (0, 0, k))
    else:
        sums_in = sums.reshape(2, rows, shares, share).transpose(2, 0, 1, 3)
        sums_spec = pl.BlockSpec((None, 2, rows, share), lambda k: (k, 0, 0, 0))
    out = pl.pallas_call(
        kernel,
        grid=(shares,),
        in_specs=[sums_spec, pl.BlockSpec((groups_of, 1, 2, extra), lambda k: (0, k, 0, 0))],
        out_specs=pl.BlockSpec((groups_of, 1, 8, wide), lambda k: (0, k, 0, 0)),
        out_shape=jax.ShapeDtypeStruct((groups_of, shares, 8, wide), F32),
    )(sums_in, rest.reshape(groups_of, shares, 2, extra))
    return out.reshape(groups_of * shares, 8, wide)


def normalized(x):
    centred = x - jnp.mean(x, axis=-1, keepdims=True)
    inverse = lax.rsqrt(jnp.mean(centred * centred, axis=-1, keepdims=True) + NORM_EPS)
    return centred * inverse, inverse


def norm_back(n, inverse, w):
    return (w - jnp.mean(w, axis=-1, keepdims=True) - n * jnp.mean(w * n, axis=-1, keepdims=True)) * inverse


def gelu_pair(u):
    c = 0.7978845608028654
    inner = jnp.tanh(c * (u + 0.044715 * u * u * u))
    value = 0.5 * u * (1.0 + inner)
    slope = 0.5 * (1.0 + inner) + 0.5 * u * (1.0 - inner * inner) * c * (1.0 + 3 * 0.044715 * u * u)
    return value.astype(BF), slope.astype(BF)


def shards(
    image_tokens,
    text_tokens,
    conditioning,
    image_seq_ids,
    text_seq_ids,
    ada_weight,
    qkv_weight,
    out_weight,
    up_weight,
    down_weight,
    biases,
    image_cotangent,
    text_cotangent,
):
    section = lax.axis_index("section")
    context = lax.axis_index("context")
    tensor = lax.axis_index("tensor")
    ncontext = lax.axis_size("context")
    ntensor = lax.axis_size("tensor")
    ndev = ncontext * ntensor
    first = section == 0
    micros, own_image, width = image_tokens.shape
    own_text = text_tokens.shape[1]
    seqs = conditioning.shape[1]
    rows_image, rows_text = micros * own_image, micros * own_text
    heads_here = HEADS // ntensor
    local = heads_here * HEAD
    hidden = up_weight.shape[3]
    bias_here = biases.shape[2]
    depth = qkv_weight.shape[2]
    mods = 6 * width
    table_rows = 2 * seqs
    per = ncontext // micros
    micro = context // per
    paired = per == 2 and heads_here % 2 == 0
    groups = 2 if paired else 1
    group_heads = heads_here // groups
    group = group_heads * HEAD
    side = context % per
    ctx_image, ctx_text = ntensor * rows_image, ntensor * rows_text
    ctx_rows = ctx_image + ctx_text

    order = (0, 2, 1, 3)

    def swapped(x, axis, bit):
        return lax.ppermute(x, axis, [(i, i ^ bit) for i in range(lax.axis_size(axis))])

    def sided(a, b):
        return jnp.where(side == 0, a, b), jnp.where(side == 0, b, a)

    def near(x):
        return swapped(x, "tensor", 1)

    def far(x):
        return swapped(x, "tensor", 2)

    def gather_tensor(x):
        beside = near(x)
        across = far(x)
        return x, across, beside, near(across)

    def reduce_tensor(x):
        n = x.shape[0] // 4
        got = near(x[2 * n :])
        mine = x[: 2 * n].astype(F32) + got.astype(F32)
        return mine[:n] + far(mine[n:].astype(BF)).astype(F32)

    def spread(rows):
        return jnp.concatenate(gather_tensor(rows), 0)

    def spread_both(rows):
        return [spread(rows[:rows_image]), spread(rows[rows_image:])]

    def collect(image_rows, text_rows):
        return jnp.concatenate(
            (reduce_tensor(image_rows.astype(BF)), reduce_tensor(text_rows.astype(BF))), 0
        )

    def gather_both(x):
        got = lax.all_gather(x, "tensor")
        got = lax.all_to_all(jnp.broadcast_to(got[None], (ncontext,) + got.shape), "context", 0, 0)
        return got.reshape((ndev,) + x.shape)

    def rounds(step, back):
        pairs = []
        for h in range(ncontext):
            m = (h + step) % micros
            pairs.append((h, m * per + h // micros))
        return [(b, a) for a, b in pairs] if back else pairs

    def to_work(image, text):
        pieces = []
        for step in range(micros):
            m = (context + step) % micros
            pieces.append(
                [
                    lax.ppermute(
                        lax.dynamic_index_in_dim(x, m, 0, keepdims=False), "context", rounds(step, False)
                    )
                    for x in (image, text)
                ]
            )
        return jnp.concatenate([p[0] for p in pieces] + [p[1] for p in pieces], 0).astype(F32)

    def to_home(rows):
        image, text = [], []
        for step in range(micros):
            image.append(
                lax.ppermute(
                    rows[step * own_image : (step + 1) * own_image], "context", rounds(step, True)
                )
            )
            at = rows_image + step * own_text
            text.append(lax.ppermute(rows[at : at + own_text], "context", rounds(step, True)))
        image, text = jnp.stack(image), jnp.stack(text)
        turns = [(m - context) % micros for m in range(micros)]
        return tuple(
            jnp.stack([lax.dynamic_index_in_dim(x, turn, 0, keepdims=False) for turn in turns])[None]
            for x in (image, text)
        )

    def gathered(w):
        return lax.all_gather(w, "context", axis=0, tiled=True)

    qkv_full = [gathered(qkv_weight[0, 0])]
    out_full = [gathered(out_weight[0, 0].T)]
    up_full = [gathered(up_weight[0, 0])]
    down_full = [gathered(down_weight[0, 0].T)]

    def ring(w, send_after=None):
        pieces = [w if send_after is None else after(w, send_after)]
        for step in range(1, ncontext):
            pieces.append(lax.ppermute(pieces[-1], "context", [(i, (i + 1) % ncontext) for i in range(ncontext)]))
        return pieces

    def laid(pieces):
        full = jnp.zeros((width, pieces[0].shape[1]), BF)
        for step, piece in enumerate(pieces):
            full = lax.dynamic_update_slice_in_dim(full, piece, (context - step) % ncontext * depth, 0)
        return full

    ring_first = ring(jnp.concatenate((qkv_weight[0, 1], out_weight[0, 1].T), axis=1))
    ring_second = ring(jnp.concatenate((up_weight[0, 1], down_weight[0, 1].T), axis=1), ring_first[-1])
    stage = (ncontext + 2) // 3

    cond_float = conditioning.astype(F32)
    silu_cond = jax.nn.silu(cond_float).astype(BF).reshape(micros * seqs, -1)
    ada_part = jnp.einsum("rc,jck->jrk", silu_cond, ada_weight[0], preferred_element_type=F32)
    sharing = [[m * per + u for u in range(per)] for m in range(micros)]
    shares = per * ntensor
    share = mods // shares
    bias_placed = lax.dynamic_update_slice_in_dim(
        jnp.zeros((2, bias_here * ndev), F32),
        biases[0].astype(F32),
        (context * ntensor + tensor) * bias_here,
        1,
    )
    ada_sent = packed(
        ada_part + bias_placed[:, None, :mods],
        jnp.broadcast_to(biases[0].astype(F32)[None], (ndev, 2, bias_here)),
        micros,
        shares,
    )
    ada_got = lax.all_to_all(ada_sent.astype(BF), BOTH, 0, 0)
    bias_full = ada_got[:, table_rows : table_rows + 2, :bias_here].transpose(1, 0, 2).reshape(2, -1).astype(F32)
    ada_sum = jnp.sum(ada_got[:, :table_rows, :share].astype(F32), axis=0).astype(BF)
    table = lax.all_gather(ada_sum, "tensor")
    if paired:
        table = jnp.stack(sided(table, swapped(table, "context", 1)))
    else:
        table = lax.all_gather(table, "context", axis_index_groups=sharing)
    table = after(table, ring_first[stage - 1])
    table = table.reshape(shares, table_rows, share).transpose(1, 0, 2).reshape(table_rows, mods)
    query_bias = lax.dynamic_slice_in_dim(bias_full, mods + tensor * local, local, 1)
    value_bias = lax.dynamic_slice_in_dim(bias_full, mods + width + tensor * local, local, 1)
    qkv_bias = jnp.stack(
        (
            query_bias.reshape(2, heads_here, HEAD),
            jnp.zeros((2, heads_here, HEAD), F32),
            value_bias.reshape(2, heads_here, HEAD),
        ),
        axis=2,
    ).reshape(2, 3 * local)
    out_bias = bias_full[:, mods + 2 * width : mods + 3 * width]
    at_up = mods + 3 * width
    up_bias = lax.dynamic_slice_in_dim(bias_full, at_up + tensor * hidden, hidden, 1)
    down_bias = bias_full[:, mods + 3 * width + hidden * ntensor :]

    def by_modality(pair):
        return jnp.concatenate(
            (
                jnp.broadcast_to(pair[0][None], (rows_image, width)),
                jnp.broadcast_to(pair[1][None], (rows_text, width)),
            ),
            0,
        )

    def ids_of(work_context):
        m, u = work_context // per, work_context % per
        homes = jnp.stack([u * micros + (m - step) % micros for step in range(micros)])
        places = homes[None, :] * ntensor + (tensor ^ jnp.array(order))[:, None]
        found = []
        for ids, own in ((image_seq_ids, own_image), (text_seq_ids, own_text)):
            table_ids = lax.dynamic_index_in_dim(ids, m, 0, keepdims=False).reshape(ndev, own)
            found.append(jnp.take(table_ids, places.reshape(-1), axis=0).reshape(-1))
        return found

    own_found = ids_of(context)
    own_ids = jnp.concatenate((own_found[0][:rows_image], own_found[1][:rows_text] + seqs))
    onehot = (own_ids[:, None] == jnp.arange(table_rows)[None, :]).astype(BF)
    row_mods = dot_nn(onehot, table).astype(BF)
    joint_ids = jnp.concatenate(own_found)
    if paired:
        attn_ids = jnp.concatenate([joint_ids] + ids_of(context ^ 1))
    else:
        attn_ids = jnp.concatenate([x for u in range(per) for x in ids_of(micro * per + u)])

    def row_mod(index):
        return row_mods[:, index * width : (index + 1) * width].astype(F32)

    def attention(joint):
        if paired:
            mine, theirs = sided(joint[: 3 * group], joint[3 * group :])
            theirs = swapped(theirs, "context", 1)
            here, there, lse = attend_pair(mine, theirs, attn_ids, group_heads)
            return jnp.concatenate(sided(here, swapped(there, "context", 1)), axis=0), (mine, theirs, lse)
        by_kind = joint.reshape(heads_here, 3, HEAD, ctx_rows)
        q, k, v = (by_kind[:, i].reshape(local, ctx_rows).T for i in range(3))
        k, v = (
            lax.all_gather(x, "context", axis=0, tiled=True, axis_index_groups=sharing) for x in (k, v)
        )
        attended, lse = attend(q, k, v, joint_ids, attn_ids, group_heads)
        return attended.T, (q, k, v, lse)

    def attention_back(grad, kept):
        if paired:
            mine, theirs, lse = kept
            g_mine, g_theirs = sided(grad[:group], grad[group:])
            g_theirs = swapped(g_theirs, "context", 1)
            d_mine, d_theirs = attend_pair_back(mine, theirs, g_mine, g_theirs, lse, attn_ids, group_heads)
            return jnp.concatenate(sided(d_mine, swapped(d_theirs, "context", 1)), axis=0)
        q, k, v, lse = kept
        dq, dk, dv = attend_back(q, k, v, grad.T, lse, joint_ids, attn_ids, group_heads)
        dk, dv = (
            lax.psum_scatter(x, "context", scatter_dimension=0, tiled=True, axis_index_groups=sharing)
            for x in (dk, dv)
        )
        kinds = [x.T.reshape(heads_here, HEAD, ctx_rows) for x in (dq, dk, dv)]
        return jnp.stack(kinds, axis=1).reshape(3 * local, ctx_rows)

    def forward(x):
        n1, inv1 = normalized(x)
        h1_rows = (n1 * (1.0 + row_mod(1)) + row_mod(0)).astype(BF)
        fresh = len(qkv_full) == 1
        if fresh:
            h1_rows = after(h1_rows, ring_first[2 * stage - 2])
            full = laid(ring_first)
            qkv_full.append(full[:, : 3 * local])
            out_full.append(full[:, 3 * local :])
        h1 = spread_both(h1_rows)
        joint = jnp.concatenate(
            [(dot_tt(qkv_full[j], h1[j]) + qkv_bias[j][:, None]).astype(BF) for j in range(2)], axis=1
        )
        attended, kept = attention(joint)
        if fresh:
            attended = after(attended, ring_second[stage - 1])
        branch = collect(
            dot_tt(attended, out_full[0])[:ctx_image], dot_tt(attended[:, ctx_image:], out_full[1])
        ) + by_modality(out_bias)
        middle = x + row_mod(2) * branch
        n2, inv2 = normalized(middle)
        h2_rows = (n2 * (1.0 + row_mod(4)) + row_mod(3)).astype(BF)
        if fresh:
            h2_rows = after(h2_rows, ring_second[2 * stage - 2])
            full = laid(ring_second)
            up_full.append(full[:, :hidden])
            down_full.append(full[:, hidden:])
        h2 = spread_both(h2_rows)
        pairs = [gelu_pair(dot_nn(h2[j], up_full[j]) + up_bias[j]) for j in range(2)]
        acts, slopes = [p[0] for p in pairs], [p[1] for p in pairs]
        down = collect(*(dot_nt(acts[j], down_full[j]) for j in range(2))) + by_modality(down_bias)
        out = middle + row_mod(5) * down
        saved = dict(
            x=x, h1=h1, kept=kept, attn=attended, branch=branch, middle=middle, h2=h2, acts=acts,
            slopes=slopes, down=down,
        )
        return out, saved

    def chosen(a, b):
        return jax.tree.map(lambda x, y: jnp.where(first, x, y), a, b)

    def scattered(full):
        return lax.psum_scatter(full.astype(BF), "context", scatter_dimension=0, tiled=True)

    def backward(saved, g_out, last=None):
        g_down = (row_mod(5) * g_out).astype(BF)
        gd = spread_both(g_down)
        g_up = [
            (dot_nn(gd[j], down_full[j]) * saved["slopes"][j].astype(F32)).astype(BF) for j in range(2)
        ]
        g_h2 = collect(*(dot_nt(g_up[j], up_full[j]) for j in range(2)))
        early = []
        if last:
            use = chosen(
                dict(h2=saved["h2"][0], acts=saved["acts"][0], gd=gd[0], g_up=g_up[0]),
                {k: last[k][0] for k in ("h2", "acts", "gd", "g_up")},
            )
            early = [
                dot_tn(use["gd"], use["acts"]).astype(BF),
                dot_tn(use["h2"], use["g_up"]).astype(BF),
            ]
            g_h2 = after(g_h2, *early)
            early = [scattered(part) for part in early]
        n2, inv2 = normalized(saved["middle"])
        g_middle = g_out + norm_back(n2, inv2, g_h2 * (1.0 + row_mod(4)))
        g_branch = (row_mod(2) * g_middle).astype(BF)
        gb = spread_both(g_branch)
        g_attn = jnp.concatenate([dot_tt(out_full[j], gb[j]).astype(BF) for j in range(2)], axis=1)
        if last:
            use = chosen(dict(gb=gb[0], attn=saved["attn"]), dict(gb=last["gb"][0], attn=last["attn"]))
            early.append(dot_tt(use["gb"], use["attn"][:, :ctx_image]).astype(BF))
            g_attn = after(g_attn, early[2])
        g_joint = attention_back(g_attn, saved["kept"])
        g_h1 = collect(
            dot_tt(g_joint, qkv_full[0])[:ctx_image], dot_tt(g_joint[:, ctx_image:], qkv_full[1])
        )
        if last:
            use = chosen(dict(h1=saved["h1"][0], g=g_joint), dict(h1=last["h1"][0], g=last["g_joint"]))
            early.append(dot_tt(use["h1"], use["g"][:, :ctx_image]).astype(BF))
            g_h1 = after(g_h1, early[3])
        n1, inv1 = normalized(saved["x"])
        g_x = g_middle + norm_back(n1, inv1, g_h1 * (1.0 + row_mod(1)))
        if last:
            g_x = after(g_x, *early[:2])
        row_grads = jnp.concatenate(
            [
                part.astype(BF)
                for part in (
                    g_h1, g_h1 * n1, g_middle * saved["branch"], g_h2, g_h2 * n2, g_out * saved["down"]
                )
            ],
            axis=1,
        )
        mod_grad = dot_tn(onehot, row_grads)
        tensors = dict(
            h1=saved["h1"], attn=saved["attn"], h2=saved["h2"], acts=saved["acts"], g_joint=g_joint,
            gb=gb, g_up=g_up, gd=gd, g_down=g_down, g_branch=g_branch, mod=mod_grad,
        )
        return g_x, tensors, early

    def blocks(rows):
        return rows.reshape(ctx_text, ncontext, depth).transpose(1, 0, 2)

    def copies(rows):
        return jnp.broadcast_to(rows[None], (ncontext,) + rows.shape)

    def text_round(parts):
        sent = jnp.concatenate(parts, axis=2)
        got = lax.all_to_all(sent, "context", 0, 0).reshape(ncontext * ctx_text, -1)
        cuts, at = [], 0
        for p in parts:
            cuts.append(got[:, at : at + p.shape[2]])
            at += p.shape[2]
        return cuts, got

    def handed(rows, by):
        return lax.ppermute(rows.astype(BF), "section", [(0, 1)] if by > 0 else [(1, 0)]).astype(F32)

    out_first, saved_first = forward(to_work(image_tokens, text_tokens))
    out_last, saved_last = forward(handed(out_first, 1))
    grad_last, tensors_last, unused = backward(saved_last, to_work(image_cotangent, text_cotangent))
    kept = chosen(
        dict(acts=saved_first["acts"][1], attn=saved_first["attn"][:, ctx_image:], h1=saved_first["h1"][1], h2=saved_first["h2"][1]),
        dict(acts=saved_last["acts"][1], attn=saved_last["attn"][:, ctx_image:], h1=saved_last["h1"][1], h2=saved_last["h2"][1]),
    )
    (acts_all, attn_all, h1_cols, h2_cols), acts_got = text_round(
        (copies(kept["acts"]), copies(kept["attn"].T), blocks(kept["h1"]), blocks(kept["h2"]))
    )
    out = to_home(jnp.where(first, out_first, out_last))
    returned = after(handed(grad_last, -1), acts_got, *out)
    grad_first, tensors_first, early = backward(saved_first, returned, tensors_last)
    grad = to_home(jnp.where(first, grad_first, grad_last))
    use = chosen(tensors_first, tensors_last)

    down_shard, up_shard, out_part, qkv_part = early
    out_shard = after(scattered(out_part), grad_first)
    qkv_shard = after(scattered(qkv_part), grad_first)

    (gd_cols, gb_cols, g_up_all), text_got = text_round(
        (blocks(use["gd"][1]), blocks(use["gb"][1]), copies(use["g_up"][1]))
    )
    def column_sums(parts):
        return jnp.stack([dot_nn(jnp.ones((8, p.shape[0]), BF), p)[0] for p in parts])

    def own_sums(rows):
        return column_sums((rows[:rows_image], rows[rows_image:]))

    qkv_sums = jnp.stack(
        [
            dot_nt(jnp.ones((8, part.shape[1]), BF), part)[0]
            for part in (use["g_joint"][:, :ctx_image], use["g_joint"][:, ctx_image:])
        ]
    ).reshape(2, heads_here, 3, HEAD)
    bias_part = jnp.zeros((2, bias_here * ndev), F32)
    for at, value in (
        (0, jnp.sum(use["mod"].reshape(2, seqs, mods), axis=1)),
        (mods + tensor * local, qkv_sums[:, :, 0].reshape(2, local)),
        (mods + width + tensor * local, qkv_sums[:, :, 2].reshape(2, local)),
        (mods + 2 * width, own_sums(use["g_branch"])),
        (mods + 3 * width + tensor * hidden, column_sums(use["g_up"])),
        (mods + 3 * width + ntensor * hidden, own_sums(use["g_down"])),
    ):
        bias_part = lax.dynamic_update_slice_in_dim(bias_part, value, at, 1)
    mod_sent = use["mod"].reshape(2, 1, seqs, mods)
    mod_sent = jnp.where(jnp.arange(micros)[None, :, None, None] == micro, mod_sent, 0.0)
    bias_sent = bias_part.reshape(2, ndev, bias_here).transpose(1, 0, 2)
    sent = packed(mod_sent.reshape(2, micros * seqs, mods), bias_sent, micros, shares).astype(BF)
    sent = after(sent, text_got)
    got = jnp.sum(lax.all_to_all(sent, BOTH, 0, 0).astype(F32), axis=0)
    bias_grad = got[table_rows:, :bias_here]
    mod_all = (
        gather_both(got[:table_rows, :share].astype(BF))
        .reshape(micros, shares, 2, seqs, share)
        .transpose(2, 0, 3, 1, 4)
        .reshape(2, micros * seqs, mods)
    )
    ada_grad = jnp.einsum("rc,jrk->jck", silu_cond, mod_all, preferred_element_type=F32)
    cond_inner = jnp.einsum("jrk,jck->rc", mod_all, ada_weight[0], preferred_element_type=F32)
    qkv_sent = copies(use["g_joint"][:, ctx_image:].T)
    g_qkv_all = after(lax.all_to_all(qkv_sent, "context", 0, 0), mod_all).reshape(ncontext * ctx_text, -1)
    down_grad = jnp.stack((down_shard.astype(F32).T, dot_tn(acts_all, gd_cols)))
    up_grad = jnp.stack((up_shard.astype(F32), dot_tn(h2_cols, g_up_all)))
    out_grad = jnp.stack((out_shard.astype(F32).T, dot_tn(attn_all, gb_cols)))
    qkv_grad = jnp.stack((qkv_shard.astype(F32), dot_tn(h1_cols, g_qkv_all)))
    unused, silu_back = jax.vjp(jax.nn.silu, cond_float)
    cond_grad = silu_back(lax.psum(cond_inner, "section").reshape(cond_float.shape))[0]
    return (
        *out,
        *grad,
        cond_grad,
        ada_grad[None],
        qkv_grad[None],
        out_grad[None],
        up_grad[None],
        down_grad[None],
        bias_grad[None],
    )


def solution(mesh):
    tokens = P(None, BOTH, None)
    block_rows = P("section", None, BOTH, None)
    by_rows = P("section", None, "context", "tensor")
    by_cols = P("section", None, "tensor", "context")
    block_biases = P("section", None, BOTH)
    in_specs = (
        tokens,
        tokens,
        P(None, None, BOTH),
        P(),
        P(),
        block_rows,
        by_rows,
        by_cols,
        by_rows,
        by_cols,
        block_biases,
        tokens,
        tokens,
    )
    out_specs = (
        block_rows,
        block_rows,
        block_rows,
        block_rows,
        P(None, None, BOTH),
        block_rows,
        by_rows,
        by_cols,
        by_rows,
        by_cols,
        block_biases,
    )
    return jax.shard_map(shards, mesh=mesh, in_specs=in_specs, out_specs=out_specs, check_vma=False)
```

```python
from functools import partial

import jax
import jax.numpy as jnp
from jax import lax
from jax.experimental import pallas as pl
from jax.experimental.pallas import tpu as pltpu
from jax.sharding import PartitionSpec as P

HEADS = 24
HEAD = 64
NORM_EPS = 1e-06
MASKED = -1e30
BF = jnp.bfloat16
F32 = jnp.float32
BOTH = ("context", "tensor")


def dot_nn(a, b):
    return lax.dot_general(a, b, (((1,), (0,)), ((), ())), preferred_element_type=F32)


def dot_nt(a, b):
    return lax.dot_general(a, b, (((1,), (1,)), ((), ())), preferred_element_type=F32)


def dot_tn(a, b):
    return lax.dot_general(a, b, (((0,), (0,)), ((), ())), preferred_element_type=F32)


def dot_tt(a, b):
    return lax.dot_general(a, b, (((0,), (1,)), ((), ())), preferred_element_type=F32)


def scaled(q):
    return q * jnp.asarray(HEAD**-0.5, BF)


def attend_body(heads, chunk, places, q_ref, k_ref, v_ref, idq_ref, idk_ref, store, lse_ref):
    at_q, at_k, at_v = places

    def one_chunk(step, carry):
        rows = pl.ds(pl.multiple_of(step * chunk, chunk), chunk)
        bias = jnp.where(idk_ref[...] == idq_ref[:, rows], 0.0, MASKED)
        outs = []
        for head in range(heads):
            at = head * HEAD
            q = scaled(q_ref[rows, at_q + at : at_q + at + HEAD])
            scores = dot_nt(k_ref[:, at_k + at : at_k + at + HEAD], q) + bias
            top = jnp.max(scores, axis=0, keepdims=True)
            weights = jnp.exp(scores - top)
            total = jnp.sum(weights, axis=0, keepdims=True)
            summed = dot_tn(v_ref[:, at_v + at : at_v + at + HEAD], weights.astype(BF))
            outs.append((summed / total).T)
            lse_ref[head : head + 1, rows] = top + jnp.log(total)
        store(rows, jnp.concatenate(outs, axis=1).astype(BF))
        return carry

    lax.fori_loop(0, idq_ref.shape[1] // chunk, one_chunk, 0)


def attend_back_body(
    heads, chunk, places, q_ref, k_ref, v_ref, g_ref, lse_ref, idq_ref, idk_ref, store_dq, dk_acc, dv_acc
):
    at_q, at_k, at_v = places
    dk_acc[...] = jnp.zeros_like(dk_acc)
    dv_acc[...] = jnp.zeros_like(dv_acc)

    def one_chunk(step, carry):
        rows = pl.ds(pl.multiple_of(step * chunk, chunk), chunk)
        bias = jnp.where(idk_ref[...] == idq_ref[:, rows], 0.0, MASKED)
        grads = []
        for head in range(heads):
            at = head * HEAD
            q = scaled(q_ref[rows, at_q + at : at_q + at + HEAD])
            g = g_ref[rows, at : at + HEAD]
            k = k_ref[:, at_k + at : at_k + at + HEAD]
            probs = jnp.exp(dot_nt(k, q) + bias - lse_ref[head : head + 1, rows])
            dv_acc[head] += dot_nn(probs.astype(BF), g)
            both = probs * dot_nt(v_ref[:, at_v + at : at_v + at + HEAD], g)
            delta = jnp.sum(both, axis=0, keepdims=True)
            dscores = (both - probs * delta).astype(BF)
            dk_acc[head] += dot_nn(dscores, q)
            grads.append((dot_tn(k, dscores) * HEAD**-0.5).T)
        store_dq(rows, jnp.concatenate(grads, axis=1).astype(BF))
        return carry

    lax.fori_loop(0, idq_ref.shape[1] // chunk, one_chunk, 0)


def heads_of(acc):
    return jnp.concatenate([acc[head] for head in range(acc.shape[0])], axis=1).astype(BF)


def attend_costs(queries, keys, heads, factor):
    return pl.CostEstimate(
        flops=factor * queries * keys * heads * HEAD,
        bytes_accessed=2 * (queries + 2 * keys) * heads * HEAD * factor // 4,
        transcendentals=queries * keys * heads,
    )


def chunk_for(keys):
    return 256 if keys <= 1024 else 128


VMEM_LIMIT = pltpu.CompilerParams(vmem_limit_bytes=56 * 2**20)


def attend(q, k, v, ids_q, ids_k, heads):
    queries, keys = q.shape[0], k.shape[0]

    def kernel(q_ref, k_ref, v_ref, idq_ref, idk_ref, out_ref, lse_ref):
        def store(rows, value):
            out_ref[rows, :] = value

        attend_body(
            heads, chunk_for(keys), (0, 0, 0), q_ref, k_ref, v_ref, idq_ref, idk_ref, store, lse_ref
        )

    return pl.pallas_call(
        kernel,
        out_shape=(
            jax.ShapeDtypeStruct((queries, heads * HEAD), BF),
            jax.ShapeDtypeStruct((heads, queries), F32),
        ),
        compiler_params=VMEM_LIMIT,
        cost_estimate=attend_costs(queries, keys, heads, 4),
    )(q, k, v, ids_q.reshape(1, queries), ids_k.reshape(keys, 1))


def attend_back(q, k, v, g, lse, ids_q, ids_k, heads):
    queries, keys = q.shape[0], k.shape[0]

    def kernel(
        q_ref, k_ref, v_ref, g_ref, lse_ref, idq_ref, idk_ref, dq_ref, dk_ref, dv_ref, dk_acc, dv_acc
    ):
        def store(rows, value):
            dq_ref[rows, :] = value

        attend_back_body(
            heads, chunk_for(keys), (0, 0, 0), q_ref, k_ref, v_ref, g_ref, lse_ref, idq_ref, idk_ref,
            store, dk_acc, dv_acc,
        )
        dk_ref[...] = heads_of(dk_acc)
        dv_ref[...] = heads_of(dv_acc)

    return pl.pallas_call(
        kernel,
        out_shape=(
            jax.ShapeDtypeStruct((queries, heads * HEAD), BF),
            jax.ShapeDtypeStruct((keys, heads * HEAD), BF),
            jax.ShapeDtypeStruct((keys, heads * HEAD), BF),
        ),
        scratch_shapes=[pltpu.VMEM((heads, keys, HEAD), F32), pltpu.VMEM((heads, keys, HEAD), F32)],
        compiler_params=VMEM_LIMIT,
        cost_estimate=attend_costs(queries, keys, heads, 10),
    )(q, k, v, g, lse, ids_q.reshape(1, queries), ids_k.reshape(keys, 1))


def attend_pair(mine, theirs, ids, heads):
    wide, half = mine.shape
    rows_all, group = 2 * half, heads * HEAD
    chunk = 256

    def kernel(mine_ref, theirs_ref, idq_ref, idk_ref, here_ref, there_ref, lse_ref, x_ref, out_ref):
        x_ref[:, :half] = mine_ref[...]
        x_ref[:, half:] = theirs_ref[...]

        def one_chunk(step, carry):
            rows = pl.ds(pl.multiple_of(step * chunk, chunk), chunk)
            bias = jnp.where(idk_ref[...] == idq_ref[:, rows], 0.0, MASKED)
            for head in range(heads):
                at = slice(head * HEAD, (head + 1) * HEAD)
                base = 3 * head * HEAD
                q = scaled(x_ref[base : base + HEAD, rows])
                k = x_ref[base + HEAD : base + 2 * HEAD, :]
                v = x_ref[base + 2 * HEAD : base + 3 * HEAD, :]
                scores = dot_tn(k, q) + bias
                top = jnp.max(scores, axis=0, keepdims=True)
                weights = jnp.exp(scores - top)
                total = jnp.sum(weights, axis=0, keepdims=True)
                out_ref[at, rows] = (dot_nn(v, weights.astype(BF)) / total).astype(BF)
                lse_ref[head : head + 1, rows] = top + jnp.log(total)
            return carry

        lax.fori_loop(0, rows_all // chunk, one_chunk, 0)
        here_ref[...] = out_ref[:, :half]
        there_ref[...] = out_ref[:, half:]

    return pl.pallas_call(
        kernel,
        out_shape=(
            jax.ShapeDtypeStruct((group, half), BF),
            jax.ShapeDtypeStruct((group, half), BF),
            jax.ShapeDtypeStruct((heads, rows_all), F32),
        ),
        scratch_shapes=[pltpu.VMEM((wide, rows_all), BF), pltpu.VMEM((group, rows_all), BF)],
        compiler_params=VMEM_LIMIT,
        cost_estimate=attend_costs(rows_all, rows_all, heads, 4),
    )(mine, theirs, ids.reshape(1, rows_all), ids.reshape(rows_all, 1))


def attend_pair_back(mine, theirs, g_mine, g_theirs, lse, ids, heads):
    wide, half = mine.shape
    rows_all, group = 2 * half, heads * HEAD
    chunk = 256

    def kernel(
        mine_ref, theirs_ref, gm_ref, gt_ref, lse_ref, idq_ref, idk_ref, dmine_ref, dtheirs_ref,
        x_ref, g_ref, dq_ref, dk_ref, dv_ref,
    ):
        x_ref[:, :half] = mine_ref[...]
        x_ref[:, half:] = theirs_ref[...]
        g_ref[:, :half] = gm_ref[...]
        g_ref[:, half:] = gt_ref[...]
        dk_ref[...] = jnp.zeros_like(dk_ref)
        dv_ref[...] = jnp.zeros_like(dv_ref)

        def one_chunk(step, carry):
            rows = pl.ds(pl.multiple_of(step * chunk, chunk), chunk)
            bias = jnp.where(idk_ref[...] == idq_ref[:, rows], 0.0, MASKED)
            for head in range(heads):
                at = slice(head * HEAD, (head + 1) * HEAD)
                base = 3 * head * HEAD
                q = scaled(x_ref[base : base + HEAD, rows])
                g = g_ref[at, rows]
                k = x_ref[base + HEAD : base + 2 * HEAD, :]
                v = x_ref[base + 2 * HEAD : base + 3 * HEAD, :]
                probs = jnp.exp(dot_tn(k, q) + bias - lse_ref[head : head + 1, rows])
                dv_ref[at, :] += dot_nt(g, probs.astype(BF))
                both = probs * dot_tn(v, g)
                delta = jnp.sum(both, axis=0, keepdims=True)
                dscores = (both - probs * delta).astype(BF)
                dk_ref[at, :] += dot_nt(q, dscores)
                dq_ref[at, rows] = (dot_nn(k, dscores) * HEAD**-0.5).astype(BF)
            return carry

        lax.fori_loop(0, rows_all // chunk, one_chunk, 0)
        for out_ref, cols in ((dmine_ref, slice(0, half)), (dtheirs_ref, slice(half, rows_all))):
            for head in range(heads):
                at = slice(head * HEAD, (head + 1) * HEAD)
                base = 3 * head * HEAD
                out_ref[base : base + HEAD, :] = dq_ref[at, cols]
                out_ref[base + HEAD : base + 2 * HEAD, :] = dk_ref[at, cols].astype(BF)
                out_ref[base + 2 * HEAD : base + 3 * HEAD, :] = dv_ref[at, cols].astype(BF)

    return pl.pallas_call(
        kernel,
        out_shape=(jax.ShapeDtypeStruct((wide, half), BF), jax.ShapeDtypeStruct((wide, half), BF)),
        scratch_shapes=[
            pltpu.VMEM((wide, rows_all), BF),
            pltpu.VMEM((group, rows_all), BF),
            pltpu.VMEM((group, rows_all), BF),
            pltpu.VMEM((group, rows_all), F32),
            pltpu.VMEM((group, rows_all), F32),
        ],
        compiler_params=VMEM_LIMIT,
        cost_estimate=attend_costs(rows_all, rows_all, heads, 10),
    )(mine, theirs, g_mine, g_theirs, lse, ids.reshape(1, rows_all), ids.reshape(rows_all, 1))


def after(x, *others):
    anywhere = pl.BlockSpec(memory_space=pl.ANY)

    def kernel(*refs):
        pass

    return pl.pallas_call(
        kernel,
        out_shape=jax.ShapeDtypeStruct(x.shape, x.dtype),
        in_specs=[anywhere] * (1 + len(others)),
        out_specs=anywhere,
        input_output_aliases={0: 0},
    )(x, *others)


def lanes(n):
    return -(-n // 128) * 128


def packed(sums, rest, groups_of, shares):
    rows, columns = sums.shape[1], sums.shape[2]
    seqs, share, extra = rows // groups_of, columns // shares, rest.shape[2]
    wide = lanes(max(share, extra))

    def kernel(sums_ref, rest_ref, out_ref):
        for group in range(groups_of):
            for j in range(2):
                out_ref[group, 0, j * seqs : (j + 1) * seqs, :share] = sums_ref[
                    j, group * seqs : (group + 1) * seqs, :
                ]
            out_ref[group, 0, 2 * seqs : 2 * seqs + 2, :extra] = rest_ref[group, 0]

    if share % 128 == 0:
        sums_in, sums_spec = sums, pl.BlockSpec((2, rows, share), lambda k: (0, 0, k))
    else:
        sums_in = sums.reshape(2, rows, shares, share).transpose(2, 0, 1, 3)
        sums_spec = pl.BlockSpec((None, 2, rows, share), lambda k: (k, 0, 0, 0))
    out = pl.pallas_call(
        kernel,
        grid=(shares,),
        in_specs=[sums_spec, pl.BlockSpec((groups_of, 1, 2, extra), lambda k: (0, k, 0, 0))],
        out_specs=pl.BlockSpec((groups_of, 1, 8, wide), lambda k: (0, k, 0, 0)),
        out_shape=jax.ShapeDtypeStruct((groups_of, shares, 8, wide), F32),
    )(sums_in, rest.reshape(groups_of, shares, 2, extra))
    return out.reshape(groups_of * shares, 8, wide)


def text_packed(blocked, copied, stacked, count):
    rows = (blocked + copied)[0].shape[0] if blocked or copied else stacked[0].shape[1]
    widths = [x.shape[1] // count for x in blocked] + [x.shape[1] for x in copied]
    widths += [x.shape[0] * x.shape[2] for x in stacked]
    if any(x.shape[1] // count % 128 for x in blocked) or any(w % 128 for w in widths):
        parts = [x.reshape(rows, count, -1).transpose(1, 0, 2) for x in blocked]
        whole = list(copied) + [x.transpose(1, 0, 2).reshape(rows, -1) for x in stacked]
        parts += [jnp.broadcast_to(x[None], (count,) + x.shape) for x in whole]
        return jnp.concatenate(parts, axis=2)
    nblocked, ncopied = len(blocked), len(copied)

    def kernel(*refs):
        out_ref = refs[-1]
        for k in range(count):
            at = 0
            for i, ref in enumerate(refs[:-1]):
                wide = widths[i]
                if i < nblocked:
                    out_ref[k, :, at : at + wide] = ref[:, k * wide : (k + 1) * wide]
                elif i < nblocked + ncopied:
                    out_ref[k, :, at : at + wide] = ref[...]
                else:
                    part = ref.shape[2]
                    for t in range(ref.shape[0]):
                        out_ref[k, :, at + t * part : at + (t + 1) * part] = ref[t]
                at += wide

    return pl.pallas_call(
        kernel, out_shape=jax.ShapeDtypeStruct((count, rows, sum(widths)), BF), compiler_params=VMEM_LIMIT
    )(*blocked, *copied, *stacked)


def normalized(x):
    centred = x - jnp.mean(x, axis=-1, keepdims=True)
    inverse = lax.rsqrt(jnp.mean(centred * centred, axis=-1, keepdims=True) + NORM_EPS)
    return centred * inverse, inverse


def norm_back(n, inverse, w):
    return (w - jnp.mean(w, axis=-1, keepdims=True) - n * jnp.mean(w * n, axis=-1, keepdims=True)) * inverse


def gelu_pair(u):
    c = 0.7978845608028654
    inner = jnp.tanh(c * (u + 0.044715 * u * u * u))
    value = 0.5 * u * (1.0 + inner)
    slope = 0.5 * (1.0 + inner) + 0.5 * u * (1.0 - inner * inner) * c * (1.0 + 3 * 0.044715 * u * u)
    return value.astype(BF), slope.astype(BF)


def shards(
    image_tokens,
    text_tokens,
    conditioning,
    image_seq_ids,
    text_seq_ids,
    ada_weight,
    qkv_weight,
    out_weight,
    up_weight,
    down_weight,
    biases,
    image_cotangent,
    text_cotangent,
):
    section = lax.axis_index("section")
    context = lax.axis_index("context")
    tensor = lax.axis_index("tensor")
    ncontext = lax.axis_size("context")
    ntensor = lax.axis_size("tensor")
    ndev = ncontext * ntensor
    first = section == 0
    micros, own_image, width = image_tokens.shape
    own_text = text_tokens.shape[1]
    seqs = conditioning.shape[1]
    rows_image, rows_text = micros * own_image, micros * own_text
    heads_here = HEADS // ntensor
    local = heads_here * HEAD
    hidden = up_weight.shape[3]
    bias_here = biases.shape[2]
    depth = qkv_weight.shape[2]
    mods = 6 * width
    table_rows = 2 * seqs
    per = ncontext // micros
    micro = context // per
    paired = per == 2 and heads_here % 2 == 0
    groups = 2 if paired else 1
    group_heads = heads_here // groups
    group = group_heads * HEAD
    side = context % per
    ctx_image, ctx_text = ntensor * rows_image, ntensor * rows_text
    ctx_rows = ctx_image + ctx_text

    order = (0, 2, 1, 3)

    def swapped(x, axis, bit):
        return lax.ppermute(x, axis, [(i, i ^ bit) for i in range(lax.axis_size(axis))])

    def sided(a, b):
        return jnp.where(side == 0, a, b), jnp.where(side == 0, b, a)

    def near(x):
        return swapped(x, "tensor", 1)

    def far(x):
        return swapped(x, "tensor", 2)

    def gather_tensor(x):
        beside = near(x)
        across = far(x)
        return x, across, beside, near(across)

    def reduce_tensor(x):
        n = x.shape[0] // 4
        got = near(x[2 * n :])
        mine = x[: 2 * n].astype(F32) + got.astype(F32)
        return mine[:n] + far(mine[n:].astype(BF)).astype(F32)

    def spread(rows):
        return jnp.concatenate(gather_tensor(rows), 0)

    def spread_both(rows):
        return [spread(rows[:rows_image]), spread(rows[rows_image:])]

    def collect(image_rows, text_rows):
        return jnp.concatenate(
            (reduce_tensor(image_rows.astype(BF)), reduce_tensor(text_rows.astype(BF))), 0
        )

    def text_gather(rows):
        sent = jnp.broadcast_to(rows[None], (ncontext,) + rows.shape)
        return lax.all_to_all(sent, "context", 0, 0).reshape(ncontext * rows_text, width)

    def text_scatter(partial_sums):
        sent = partial_sums.astype(BF).reshape(ncontext, rows_text, width)
        return jnp.sum(lax.all_to_all(sent, "context", 0, 0).astype(F32), axis=0)

    def by_tensor(x, axis):
        places = [jnp.array(order)[tensor ^ k] for k in range(ntensor)]
        return jnp.stack([lax.dynamic_index_in_dim(x, at, axis, keepdims=False) for at in places], axis)

    def in_group(x, axis):
        places = [tensor ^ bit for bit in order]
        return jnp.stack([lax.dynamic_index_in_dim(x, at, axis, keepdims=False) for at in places], axis)

    def gather_both(x):
        got = lax.all_gather(x, "tensor")
        got = lax.all_to_all(jnp.broadcast_to(got[None], (ncontext,) + got.shape), "context", 0, 0)
        return got.reshape((ndev,) + x.shape)

    def rounds(step, back):
        pairs = []
        for h in range(ncontext):
            m = (h + step) % micros
            pairs.append((h, m * per + h // micros))
        return [(b, a) for a, b in pairs] if back else pairs

    def to_work(image, text):
        pieces = []
        for step in range(micros):
            m = (context + step) % micros
            pieces.append(
                [
                    lax.ppermute(
                        lax.dynamic_index_in_dim(x, m, 0, keepdims=False), "context", rounds(step, False)
                    )
                    for x in (image, text)
                ]
            )
        return jnp.concatenate([p[0] for p in pieces] + [p[1] for p in pieces], 0).astype(F32)

    def to_home(rows):
        image, text = [], []
        for step in range(micros):
            image.append(
                lax.ppermute(
                    rows[step * own_image : (step + 1) * own_image], "context", rounds(step, True)
                )
            )
            at = rows_image + step * own_text
            text.append(lax.ppermute(rows[at : at + own_text], "context", rounds(step, True)))
        image, text = jnp.stack(image), jnp.stack(text)
        turns = [(m - context) % micros for m in range(micros)]
        return tuple(
            jnp.stack([lax.dynamic_index_in_dim(x, turn, 0, keepdims=False) for turn in turns])[None]
            for x in (image, text)
        )

    def gathered(w):
        return lax.all_gather(w, "context", axis=0, tiled=True)

    qkv_full = [gathered(qkv_weight[0, 0])]
    out_full = [gathered(out_weight[0, 0].T)]
    up_full = [gathered(up_weight[0, 0])]
    down_full = [gathered(down_weight[0, 0].T)]

    def ring(w, send_after=None):
        pieces = [w if send_after is None else after(w, send_after)]
        for step in range(1, ncontext):
            pieces.append(lax.ppermute(pieces[-1], "context", [(i, (i + 1) % ncontext) for i in range(ncontext)]))
        return pieces

    def laid(pieces):
        full = jnp.zeros((width, pieces[0].shape[1]), BF)
        for step, piece in enumerate(pieces):
            full = lax.dynamic_update_slice_in_dim(full, piece, (context - step) % ncontext * depth, 0)
        return full

    ring_first = ring(jnp.concatenate((qkv_weight[0, 1], out_weight[0, 1].T), axis=1))
    stage = (ncontext + 2) // 3
    part = hidden // ncontext
    text_sent = jnp.concatenate(
        [w.reshape(ncontext, part, depth) for w in (up_weight[0, 1].T, down_weight[0, 1])], axis=1
    )
    text_moved = lax.all_to_all(after(text_sent, ring_first[-1]), "context", 0, 0)
    feed = []

    cond_float = conditioning.astype(F32)
    silu_cond = jax.nn.silu(cond_float).astype(BF).reshape(micros * seqs, -1)
    ada_part = jnp.einsum("rc,jck->jrk", silu_cond, ada_weight[0], preferred_element_type=F32)
    sharing = [[m * per + u for u in range(per)] for m in range(micros)]
    shares = per * ntensor
    share = mods // shares
    bias_placed = lax.dynamic_update_slice_in_dim(
        jnp.zeros((2, bias_here * ndev), F32),
        biases[0].astype(F32),
        (context * ntensor + tensor) * bias_here,
        1,
    )
    ada_sent = packed(
        ada_part + bias_placed[:, None, :mods],
        jnp.broadcast_to(biases[0].astype(F32)[None], (ndev, 2, bias_here)),
        micros,
        shares,
    )
    ada_got = lax.all_to_all(ada_sent.astype(BF), BOTH, 0, 0)
    bias_full = ada_got[:, table_rows : table_rows + 2, :bias_here].transpose(1, 0, 2).reshape(2, -1).astype(F32)
    ada_sum = jnp.sum(ada_got[:, :table_rows, :share].astype(F32), axis=0).astype(BF)
    table = lax.all_gather(ada_sum, "tensor")
    if paired:
        table = jnp.stack(sided(table, swapped(table, "context", 1)))
    else:
        table = lax.all_gather(table, "context", axis_index_groups=sharing)
    table = after(table, ring_first[stage - 1])
    table = table.reshape(shares, table_rows, share).transpose(1, 0, 2).reshape(table_rows, mods)
    query_bias = lax.dynamic_slice_in_dim(bias_full, mods + tensor * local, local, 1)
    value_bias = lax.dynamic_slice_in_dim(bias_full, mods + width + tensor * local, local, 1)
    qkv_bias = jnp.stack(
        (
            query_bias.reshape(2, heads_here, HEAD),
            jnp.zeros((2, heads_here, HEAD), F32),
            value_bias.reshape(2, heads_here, HEAD),
        ),
        axis=2,
    ).reshape(2, 3 * local)
    out_bias = bias_full[:, mods + 2 * width : mods + 3 * width]
    at_up = mods + 3 * width
    up_bias = lax.dynamic_slice_in_dim(bias_full[0], at_up + tensor * hidden, hidden, 0)
    up_bias_text = bias_full[1, at_up : at_up + ntensor * hidden].reshape(ntensor, ncontext, part)
    up_bias_text = in_group(lax.dynamic_index_in_dim(up_bias_text, context, 1, keepdims=False), 0).reshape(-1)
    down_bias = bias_full[:, mods + 3 * width + hidden * ntensor :]

    def by_modality(pair):
        return jnp.concatenate(
            (
                jnp.broadcast_to(pair[0][None], (rows_image, width)),
                jnp.broadcast_to(pair[1][None], (rows_text, width)),
            ),
            0,
        )

    def ids_of(work_context):
        m, u = work_context // per, work_context % per
        homes = jnp.stack([u * micros + (m - step) % micros for step in range(micros)])
        places = homes[None, :] * ntensor + (tensor ^ jnp.array(order))[:, None]
        found = []
        for ids, own in ((image_seq_ids, own_image), (text_seq_ids, own_text)):
            table_ids = lax.dynamic_index_in_dim(ids, m, 0, keepdims=False).reshape(ndev, own)
            found.append(jnp.take(table_ids, places.reshape(-1), axis=0).reshape(-1))
        return found

    own_found = ids_of(context)
    own_ids = jnp.concatenate((own_found[0][:rows_image], own_found[1][:rows_text] + seqs))
    onehot = (own_ids[:, None] == jnp.arange(table_rows)[None, :]).astype(BF)
    row_mods = dot_nn(onehot, table).astype(BF)
    joint_ids = jnp.concatenate(own_found)
    if paired:
        attn_ids = jnp.concatenate([joint_ids] + ids_of(context ^ 1))
    else:
        attn_ids = jnp.concatenate([x for u in range(per) for x in ids_of(micro * per + u)])

    def row_mod(index):
        return row_mods[:, index * width : (index + 1) * width].astype(F32)

    def attention(joint):
        if paired:
            mine, theirs = sided(joint[: 3 * group], joint[3 * group :])
            theirs = swapped(theirs, "context", 1)
            here, there, lse = attend_pair(mine, theirs, attn_ids, group_heads)
            return jnp.concatenate(sided(here, swapped(there, "context", 1)), axis=0), (mine, theirs, lse)
        by_kind = joint.reshape(heads_here, 3, HEAD, ctx_rows)
        q, k, v = (by_kind[:, i].reshape(local, ctx_rows).T for i in range(3))
        k, v = (
            lax.all_gather(x, "context", axis=0, tiled=True, axis_index_groups=sharing) for x in (k, v)
        )
        attended, lse = attend(q, k, v, joint_ids, attn_ids, group_heads)
        return attended.T, (q, k, v, lse)

    def attention_back(grad, kept):
        if paired:
            mine, theirs, lse = kept
            g_mine, g_theirs = sided(grad[:group], grad[group:])
            g_theirs = swapped(g_theirs, "context", 1)
            d_mine, d_theirs = attend_pair_back(mine, theirs, g_mine, g_theirs, lse, attn_ids, group_heads)
            return jnp.concatenate(sided(d_mine, swapped(d_theirs, "context", 1)), axis=0)
        q, k, v, lse = kept
        dq, dk, dv = attend_back(q, k, v, grad.T, lse, joint_ids, attn_ids, group_heads)
        dk, dv = (
            lax.psum_scatter(x, "context", scatter_dimension=0, tiled=True, axis_index_groups=sharing)
            for x in (dk, dv)
        )
        kinds = [x.T.reshape(heads_here, HEAD, ctx_rows) for x in (dq, dk, dv)]
        return jnp.stack(kinds, axis=1).reshape(3 * local, ctx_rows)

    def forward(x):
        n1, inv1 = normalized(x)
        h1_rows = (n1 * (1.0 + row_mod(1)) + row_mod(0)).astype(BF)
        fresh = len(qkv_full) == 1
        if fresh:
            h1_rows = after(h1_rows, ring_first[2 * stage - 2])
            full = laid(ring_first)
            qkv_full.append(full[:, : 3 * local])
            out_full.append(full[:, 3 * local :])
        h1 = spread_both(h1_rows)
        joint = jnp.concatenate(
            [(dot_tt(qkv_full[j], h1[j]) + qkv_bias[j][:, None]).astype(BF) for j in range(2)], axis=1
        )
        attended, kept = attention(joint)
        if fresh:
            attended = after(attended, text_moved)
            moved = gather_tensor(text_moved.transpose(1, 0, 2).reshape(2 * part, width))
            feed.append(jnp.concatenate([b[:part] for b in moved], 0))
            feed.append(jnp.concatenate([b[part:] for b in moved], 0))
        branch = collect(
            dot_tt(attended, out_full[0])[:ctx_image], dot_tt(attended[:, ctx_image:], out_full[1])
        ) + by_modality(out_bias)
        middle = x + row_mod(2) * branch
        n2, inv2 = normalized(middle)
        h2_rows = (n2 * (1.0 + row_mod(4)) + row_mod(3)).astype(BF)
        up_text, down_text = feed
        h2 = [spread(h2_rows[:rows_image]), text_gather(h2_rows[rows_image:])]
        pairs = [
            gelu_pair(dot_nn(h2[0], up_full[0]) + up_bias),
            gelu_pair(dot_nt(h2[1], up_text) + up_bias_text),
        ]
        acts, slopes = [p[0] for p in pairs], [p[1] for p in pairs]
        down = jnp.concatenate(
            (
                reduce_tensor(dot_nt(acts[0], down_full[0]).astype(BF)),
                text_scatter(dot_nn(acts[1], down_text)),
            ),
            0,
        ) + by_modality(down_bias)
        out = middle + row_mod(5) * down
        saved = dict(
            x=x, h1=h1, kept=kept, attn=attended, branch=branch, middle=middle, h2=h2, acts=acts,
            slopes=slopes, down=down,
        )
        return out, saved

    def chosen(a, b):
        return jax.tree.map(lambda x, y: jnp.where(first, x, y), a, b)

    def scattered(full):
        return lax.psum_scatter(full.astype(BF), "context", scatter_dimension=0, tiled=True)

    def backward(saved, g_out, last=None):
        g_down = (row_mod(5) * g_out).astype(BF)
        up_text, down_text = feed
        gd = [spread(g_down[:rows_image]), text_gather(g_down[rows_image:])]
        g_up = [
            (dot_nn(gd[0], down_full[0]) * saved["slopes"][0].astype(F32)).astype(BF),
            (dot_nt(gd[1], down_text) * saved["slopes"][1].astype(F32)).astype(BF),
        ]
        g_h2 = jnp.concatenate(
            (
                reduce_tensor(dot_nt(g_up[0], up_full[0]).astype(BF)),
                text_scatter(dot_nn(g_up[1], up_text)),
            ),
            0,
        )
        early = []
        if last:
            use = chosen(
                dict(h2=saved["h2"][0], acts=saved["acts"][0], gd=gd[0], g_up=g_up[0]),
                {k: last[k][0] for k in ("h2", "acts", "gd", "g_up")},
            )
            early = [
                dot_tn(use["gd"], use["acts"]).astype(BF),
                dot_tn(use["h2"], use["g_up"]).astype(BF),
            ]
            g_h2 = after(g_h2, *early)
            early = [scattered(part) for part in early]
        n2, inv2 = normalized(saved["middle"])
        g_middle = g_out + norm_back(n2, inv2, g_h2 * (1.0 + row_mod(4)))
        g_branch = (row_mod(2) * g_middle).astype(BF)
        gb = spread_both(g_branch)
        g_attn = jnp.concatenate([dot_tt(out_full[j], gb[j]).astype(BF) for j in range(2)], axis=1)
        if last:
            use = chosen(dict(gb=gb[0], attn=saved["attn"]), dict(gb=last["gb"][0], attn=last["attn"]))
            early.append(dot_tt(use["gb"], use["attn"][:, :ctx_image]).astype(BF))
            g_attn = after(g_attn, early[2])
        g_joint = attention_back(g_attn, saved["kept"])
        g_h1 = collect(
            dot_tt(g_joint, qkv_full[0])[:ctx_image], dot_tt(g_joint[:, ctx_image:], qkv_full[1])
        )
        if last:
            use = chosen(dict(h1=saved["h1"][0], g=g_joint), dict(h1=last["h1"][0], g=last["g_joint"]))
            early.append(dot_tt(use["h1"], use["g"][:, :ctx_image]).astype(BF))
            g_h1 = after(g_h1, early[3])
        n1, inv1 = normalized(saved["x"])
        g_x = g_middle + norm_back(n1, inv1, g_h1 * (1.0 + row_mod(1)))
        if last:
            g_x = after(g_x, *early[:2])
        row_grads = jnp.concatenate(
            [
                part.astype(BF)
                for part in (
                    g_h1, g_h1 * n1, g_middle * saved["branch"], g_h2, g_h2 * n2, g_out * saved["down"]
                )
            ],
            axis=1,
        )
        mod_grad = dot_tn(onehot, row_grads)
        tensors = dict(
            h1=saved["h1"], attn=saved["attn"], h2=saved["h2"], acts=saved["acts"], g_joint=g_joint,
            gb=gb, g_up=g_up, gd=gd, g_down=g_down, g_branch=g_branch, mod=mod_grad,
        )
        return g_x, tensors, early

    def own_hidden(rows):
        return lax.all_to_all(
            by_tensor(rows.reshape(rows.shape[0], ntensor, part), 1).transpose(1, 0, 2), "tensor", 0, 0
        )

    def own_columns(arrays):
        cols = [lax.dynamic_slice_in_dim(x, context * depth, depth, 1) for x in arrays]
        got = lax.all_gather(jnp.concatenate(cols, axis=1), "tensor")
        return [got[:, :, i * depth : (i + 1) * depth] for i in range(len(arrays))]

    def text_round(blocked, copied, stacked):
        if stacked and blocked + copied and stacked[0].shape[1] != (blocked + copied)[0].shape[0]:
            one, got_one = text_round(blocked, copied, [])
            two, got_two = text_round([], [], stacked)
            return one + two, after(got_one, got_two)
        got = lax.all_to_all(text_packed(blocked, copied, stacked, ncontext), "context", 0, 0)
        cuts, at = [], 0
        for x in blocked + copied:
            wide = depth if len(cuts) < len(blocked) else x.shape[1]
            cuts.append(got[:, :, at : at + wide].reshape(ncontext * ctx_text, wide))
            at += wide
        for x in stacked:
            wide = ntensor * part
            cuts.append(got[:, :, at : at + wide].reshape(ncontext, -1, ntensor, part))
            at += wide
        return cuts, got

    def handed(rows, by):
        return lax.ppermute(rows.astype(BF), "section", [(0, 1)] if by > 0 else [(1, 0)]).astype(F32)

    out_first, saved_first = forward(to_work(image_tokens, text_tokens))
    out_last, saved_last = forward(handed(out_first, 1))
    grad_last, tensors_last, unused = backward(saved_last, to_work(image_cotangent, text_cotangent))
    kept = chosen(
        [saved_first[n][1] for n in ("acts", "h1", "h2")] + [saved_first["attn"][:, ctx_image:]],
        [saved_last[n][1] for n in ("acts", "h1", "h2")] + [saved_last["attn"][:, ctx_image:]],
    )
    (h1_cols, attn_all, acts_all), acts_got = text_round(
        [kept[1]], [kept[3].T], [own_hidden(kept[0])]
    )
    out = to_home(jnp.where(first, out_first, out_last))
    returned = after(handed(grad_last, -1), acts_got, *out)
    grad_first, tensors_first, early = backward(saved_first, returned, tensors_last)
    grad = to_home(jnp.where(first, grad_first, grad_last))
    use = chosen(tensors_first, tensors_last)

    down_shard, up_shard, out_part, qkv_part = early
    out_shard = after(scattered(out_part), grad_first)
    qkv_shard = after(scattered(qkv_part), grad_first)

    (gb_cols, g_up_all), text_got = text_round([use["gb"][1]], [], [own_hidden(use["g_up"][1])])
    gd_cols, h2_cols = own_columns([use["gd"][1], kept[2]])

    def column_sums(parts):
        return jnp.stack([dot_nn(jnp.ones((8, p.shape[0]), BF), p)[0] for p in parts])

    def own_sums(rows):
        return column_sums((rows[:rows_image], rows[rows_image:]))

    qkv_sums = jnp.stack(
        [
            dot_nt(jnp.ones((8, part.shape[1]), BF), part)[0]
            for part in (use["g_joint"][:, :ctx_image], use["g_joint"][:, ctx_image:])
        ]
    ).reshape(2, heads_here, 3, HEAD)
    up_sums_text = lax.dynamic_update_slice_in_dim(
        jnp.zeros((ntensor, ncontext, part), F32),
        by_tensor(column_sums((use["g_up"][1],)).reshape(ntensor, 1, part), 0),
        context,
        1,
    ).reshape(1, -1)
    up_sums_image = lax.dynamic_update_slice_in_dim(
        jnp.zeros((1, ntensor * hidden), F32), column_sums((use["g_up"][0],)), tensor * hidden, 1
    )
    bias_part = jnp.zeros((2, bias_here * ndev), F32)
    for at, value in (
        (0, jnp.sum(use["mod"].reshape(2, seqs, mods), axis=1)),
        (mods + tensor * local, qkv_sums[:, :, 0].reshape(2, local)),
        (mods + width + tensor * local, qkv_sums[:, :, 2].reshape(2, local)),
        (mods + 2 * width, own_sums(use["g_branch"])),
        (mods + 3 * width, jnp.concatenate((up_sums_image, up_sums_text), 0)),
        (mods + 3 * width + ntensor * hidden, own_sums(use["g_down"])),
    ):
        bias_part = lax.dynamic_update_slice_in_dim(bias_part, value, at, 1)
    mod_sent = use["mod"].reshape(2, 1, seqs, mods)
    mod_sent = jnp.where(jnp.arange(micros)[None, :, None, None] == micro, mod_sent, 0.0)
    bias_sent = bias_part.reshape(2, ndev, bias_here).transpose(1, 0, 2)
    sent = packed(mod_sent.reshape(2, micros * seqs, mods), bias_sent, micros, shares).astype(BF)
    sent = after(sent, text_got, *grad)
    got = jnp.sum(lax.all_to_all(sent, BOTH, 0, 0).astype(F32), axis=0)
    bias_grad = got[table_rows:, :bias_here]
    mod_all = (
        gather_both(got[:table_rows, :share].astype(BF))
        .reshape(micros, shares, 2, seqs, share)
        .transpose(2, 0, 3, 1, 4)
        .reshape(2, micros * seqs, mods)
    )
    ada_grad = jnp.einsum("rc,jrk->jck", silu_cond, mod_all, preferred_element_type=F32)
    cond_inner = jnp.einsum("jrk,jck->rc", mod_all, ada_weight[0], preferred_element_type=F32)
    qkv_sent = text_packed([], [use["g_joint"][:, ctx_image:].T], [], ncontext)
    g_qkv_all = after(lax.all_to_all(qkv_sent, "context", 0, 0), mod_all).reshape(ncontext * ctx_text, -1)
    down_grad = jnp.stack((down_shard.astype(F32).T, jnp.einsum("crtj,trd->cjd", acts_all, gd_cols, preferred_element_type=F32).reshape(hidden, depth)))
    up_grad = jnp.stack((up_shard.astype(F32), jnp.einsum("trk,crtj->kcj", h2_cols, g_up_all, preferred_element_type=F32).reshape(depth, hidden)))
    out_grad = jnp.stack((out_shard.astype(F32).T, dot_tn(attn_all, gb_cols)))
    qkv_grad = jnp.stack((qkv_shard.astype(F32), dot_tn(h1_cols, g_qkv_all)))
    unused, silu_back = jax.vjp(jax.nn.silu, cond_float)
    cond_grad = silu_back(lax.psum(cond_inner, "section").reshape(cond_float.shape))[0]
    return (
        *out,
        *grad,
        cond_grad,
        ada_grad[None],
        qkv_grad[None],
        out_grad[None],
        up_grad[None],
        down_grad[None],
        bias_grad[None],
    )


def solution(mesh):
    tokens = P(None, BOTH, None)
    block_rows = P("section", None, BOTH, None)
    by_rows = P("section", None, "context", "tensor")
    by_cols = P("section", None, "tensor", "context")
    block_biases = P("section", None, BOTH)
    in_specs = (
        tokens,
        tokens,
        P(None, None, BOTH),
        P(),
        P(),
        block_rows,
        by_rows,
        by_cols,
        by_rows,
        by_cols,
        block_biases,
        tokens,
        tokens,
    )
    out_specs = (
        block_rows,
        block_rows,
        block_rows,
        block_rows,
        P(None, None, BOTH),
        block_rows,
        by_rows,
        by_cols,
        by_rows,
        by_cols,
        block_biases,
    )
    return jax.shard_map(shards, mesh=mesh, in_specs=in_specs, out_specs=out_specs, check_vma=False)
```

```python
from functools import partial

import jax
import jax.numpy as jnp
from jax import lax
from jax.experimental import pallas as pl
from jax.experimental.pallas import tpu as pltpu
from jax.sharding import PartitionSpec as P

HEADS = 24
HEAD = 64
NORM_EPS = 1e-06
MASKED = -1e30
BF = jnp.bfloat16
F32 = jnp.float32
BOTH = ("context", "tensor")


def dot_nn(a, b):
    return lax.dot_general(a, b, (((1,), (0,)), ((), ())), preferred_element_type=F32)


def dot_nt(a, b):
    return lax.dot_general(a, b, (((1,), (1,)), ((), ())), preferred_element_type=F32)


def dot_tn(a, b):
    return lax.dot_general(a, b, (((0,), (0,)), ((), ())), preferred_element_type=F32)


def dot_tt(a, b):
    return lax.dot_general(a, b, (((0,), (1,)), ((), ())), preferred_element_type=F32)


def scaled(q):
    return q * jnp.asarray(HEAD**-0.5, BF)


def attend_body(heads, chunk, places, q_ref, k_ref, v_ref, idq_ref, idk_ref, store, lse_ref):
    at_q, at_k, at_v = places

    def one_chunk(step, carry):
        rows = pl.ds(pl.multiple_of(step * chunk, chunk), chunk)
        bias = jnp.where(idk_ref[...] == idq_ref[:, rows], 0.0, MASKED)
        outs = []
        for head in range(heads):
            at = head * HEAD
            q = scaled(q_ref[rows, at_q + at : at_q + at + HEAD])
            scores = dot_nt(k_ref[:, at_k + at : at_k + at + HEAD], q) + bias
            top = jnp.max(scores, axis=0, keepdims=True)
            weights = jnp.exp(scores - top)
            total = jnp.sum(weights, axis=0, keepdims=True)
            summed = dot_tn(v_ref[:, at_v + at : at_v + at + HEAD], weights.astype(BF))
            outs.append((summed / total).T)
            lse_ref[head : head + 1, rows] = top + jnp.log(total)
        store(rows, jnp.concatenate(outs, axis=1).astype(BF))
        return carry

    lax.fori_loop(0, idq_ref.shape[1] // chunk, one_chunk, 0)


def attend_back_body(
    heads, chunk, places, q_ref, k_ref, v_ref, g_ref, lse_ref, idq_ref, idk_ref, store_dq, dk_acc, dv_acc
):
    at_q, at_k, at_v = places
    dk_acc[...] = jnp.zeros_like(dk_acc)
    dv_acc[...] = jnp.zeros_like(dv_acc)

    def one_chunk(step, carry):
        rows = pl.ds(pl.multiple_of(step * chunk, chunk), chunk)
        bias = jnp.where(idk_ref[...] == idq_ref[:, rows], 0.0, MASKED)
        grads = []
        for head in range(heads):
            at = head * HEAD
            q = scaled(q_ref[rows, at_q + at : at_q + at + HEAD])
            g = g_ref[rows, at : at + HEAD]
            k = k_ref[:, at_k + at : at_k + at + HEAD]
            probs = jnp.exp(dot_nt(k, q) + bias - lse_ref[head : head + 1, rows])
            dv_acc[head] += dot_nn(probs.astype(BF), g)
            both = probs * dot_nt(v_ref[:, at_v + at : at_v + at + HEAD], g)
            delta = jnp.sum(both, axis=0, keepdims=True)
            dscores = (both - probs * delta).astype(BF)
            dk_acc[head] += dot_nn(dscores, q)
            grads.append((dot_tn(k, dscores) * HEAD**-0.5).T)
        store_dq(rows, jnp.concatenate(grads, axis=1).astype(BF))
        return carry

    lax.fori_loop(0, idq_ref.shape[1] // chunk, one_chunk, 0)


def heads_of(acc):
    return jnp.concatenate([acc[head] for head in range(acc.shape[0])], axis=1).astype(BF)


def attend_costs(queries, keys, heads, factor):
    return pl.CostEstimate(
        flops=factor * queries * keys * heads * HEAD,
        bytes_accessed=2 * (queries + 2 * keys) * heads * HEAD * factor // 4,
        transcendentals=queries * keys * heads,
    )


def chunk_for(keys):
    return 256 if keys <= 1024 else 128


VMEM_LIMIT = pltpu.CompilerParams(vmem_limit_bytes=56 * 2**20)


def attend(q, k, v, ids_q, ids_k, heads):
    queries, keys = q.shape[0], k.shape[0]

    def kernel(q_ref, k_ref, v_ref, idq_ref, idk_ref, out_ref, lse_ref):
        def store(rows, value):
            out_ref[rows, :] = value

        attend_body(
            heads, chunk_for(keys), (0, 0, 0), q_ref, k_ref, v_ref, idq_ref, idk_ref, store, lse_ref
        )

    return pl.pallas_call(
        kernel,
        out_shape=(
            jax.ShapeDtypeStruct((queries, heads * HEAD), BF),
            jax.ShapeDtypeStruct((heads, queries), F32),
        ),
        compiler_params=VMEM_LIMIT,
        cost_estimate=attend_costs(queries, keys, heads, 4),
    )(q, k, v, ids_q.reshape(1, queries), ids_k.reshape(keys, 1))


def attend_back(q, k, v, g, lse, ids_q, ids_k, heads):
    queries, keys = q.shape[0], k.shape[0]

    def kernel(
        q_ref, k_ref, v_ref, g_ref, lse_ref, idq_ref, idk_ref, dq_ref, dk_ref, dv_ref, dk_acc, dv_acc
    ):
        def store(rows, value):
            dq_ref[rows, :] = value

        attend_back_body(
            heads, chunk_for(keys), (0, 0, 0), q_ref, k_ref, v_ref, g_ref, lse_ref, idq_ref, idk_ref,
            store, dk_acc, dv_acc,
        )
        dk_ref[...] = heads_of(dk_acc)
        dv_ref[...] = heads_of(dv_acc)

    return pl.pallas_call(
        kernel,
        out_shape=(
            jax.ShapeDtypeStruct((queries, heads * HEAD), BF),
            jax.ShapeDtypeStruct((keys, heads * HEAD), BF),
            jax.ShapeDtypeStruct((keys, heads * HEAD), BF),
        ),
        scratch_shapes=[pltpu.VMEM((heads, keys, HEAD), F32), pltpu.VMEM((heads, keys, HEAD), F32)],
        compiler_params=VMEM_LIMIT,
        cost_estimate=attend_costs(queries, keys, heads, 10),
    )(q, k, v, g, lse, ids_q.reshape(1, queries), ids_k.reshape(keys, 1))


def attend_pair(mine, theirs, ids, heads):
    wide, half = mine.shape
    rows_all, group = 2 * half, heads * HEAD
    chunk = 256

    def kernel(mine_ref, theirs_ref, idq_ref, idk_ref, here_ref, there_ref, lse_ref, x_ref, out_ref):
        x_ref[:, :half] = mine_ref[...]
        x_ref[:, half:] = theirs_ref[...]

        def one_chunk(step, carry):
            rows = pl.ds(pl.multiple_of(step * chunk, chunk), chunk)
            bias = jnp.where(idk_ref[...] == idq_ref[:, rows], 0.0, MASKED)
            for head in range(heads):
                at = slice(head * HEAD, (head + 1) * HEAD)
                base = 3 * head * HEAD
                q = scaled(x_ref[base : base + HEAD, rows])
                k = x_ref[base + HEAD : base + 2 * HEAD, :]
                v = x_ref[base + 2 * HEAD : base + 3 * HEAD, :]
                scores = dot_tn(k, q) + bias
                top = jnp.max(scores, axis=0, keepdims=True)
                weights = jnp.exp(scores - top)
                total = jnp.sum(weights, axis=0, keepdims=True)
                out_ref[at, rows] = (dot_nn(v, weights.astype(BF)) / total).astype(BF)
                lse_ref[head : head + 1, rows] = top + jnp.log(total)
            return carry

        lax.fori_loop(0, rows_all // chunk, one_chunk, 0)
        here_ref[...] = out_ref[:, :half]
        there_ref[...] = out_ref[:, half:]

    return pl.pallas_call(
        kernel,
        out_shape=(
            jax.ShapeDtypeStruct((group, half), BF),
            jax.ShapeDtypeStruct((group, half), BF),
            jax.ShapeDtypeStruct((heads, rows_all), F32),
        ),
        scratch_shapes=[pltpu.VMEM((wide, rows_all), BF), pltpu.VMEM((group, rows_all), BF)],
        compiler_params=VMEM_LIMIT,
        cost_estimate=attend_costs(rows_all, rows_all, heads, 4),
    )(mine, theirs, ids.reshape(1, rows_all), ids.reshape(rows_all, 1))


def attend_pair_back(mine, theirs, g_mine, g_theirs, lse, ids, heads):
    wide, half = mine.shape
    rows_all, group = 2 * half, heads * HEAD
    chunk = 256

    def kernel(
        mine_ref, theirs_ref, gm_ref, gt_ref, lse_ref, idq_ref, idk_ref, dmine_ref, dtheirs_ref,
        x_ref, g_ref, dq_ref, dk_ref, dv_ref,
    ):
        x_ref[:, :half] = mine_ref[...]
        x_ref[:, half:] = theirs_ref[...]
        g_ref[:, :half] = gm_ref[...]
        g_ref[:, half:] = gt_ref[...]
        dk_ref[...] = jnp.zeros_like(dk_ref)
        dv_ref[...] = jnp.zeros_like(dv_ref)

        def one_chunk(step, carry):
            rows = pl.ds(pl.multiple_of(step * chunk, chunk), chunk)
            bias = jnp.where(idk_ref[...] == idq_ref[:, rows], 0.0, MASKED)
            for head in range(heads):
                at = slice(head * HEAD, (head + 1) * HEAD)
                base = 3 * head * HEAD
                q = scaled(x_ref[base : base + HEAD, rows])
                g = g_ref[at, rows]
                k = x_ref[base + HEAD : base + 2 * HEAD, :]
                v = x_ref[base + 2 * HEAD : base + 3 * HEAD, :]
                probs = jnp.exp(dot_tn(k, q) + bias - lse_ref[head : head + 1, rows])
                dv_ref[at, :] += dot_nt(g, probs.astype(BF))
                both = probs * dot_tn(v, g)
                delta = jnp.sum(both, axis=0, keepdims=True)
                dscores = (both - probs * delta).astype(BF)
                dk_ref[at, :] += dot_nt(q, dscores)
                dq_ref[at, rows] = (dot_nn(k, dscores) * HEAD**-0.5).astype(BF)
            return carry

        lax.fori_loop(0, rows_all // chunk, one_chunk, 0)
        for out_ref, cols in ((dmine_ref, slice(0, half)), (dtheirs_ref, slice(half, rows_all))):
            for head in range(heads):
                at = slice(head * HEAD, (head + 1) * HEAD)
                base = 3 * head * HEAD
                out_ref[base : base + HEAD, :] = dq_ref[at, cols]
                out_ref[base + HEAD : base + 2 * HEAD, :] = dk_ref[at, cols].astype(BF)
                out_ref[base + 2 * HEAD : base + 3 * HEAD, :] = dv_ref[at, cols].astype(BF)

    return pl.pallas_call(
        kernel,
        out_shape=(jax.ShapeDtypeStruct((wide, half), BF), jax.ShapeDtypeStruct((wide, half), BF)),
        scratch_shapes=[
            pltpu.VMEM((wide, rows_all), BF),
            pltpu.VMEM((group, rows_all), BF),
            pltpu.VMEM((group, rows_all), BF),
            pltpu.VMEM((group, rows_all), F32),
            pltpu.VMEM((group, rows_all), F32),
        ],
        compiler_params=VMEM_LIMIT,
        cost_estimate=attend_costs(rows_all, rows_all, heads, 10),
    )(mine, theirs, g_mine, g_theirs, lse, ids.reshape(1, rows_all), ids.reshape(rows_all, 1))


def after(x, *others):
    anywhere = pl.BlockSpec(memory_space=pl.ANY)

    def kernel(*refs):
        pass

    return pl.pallas_call(
        kernel,
        out_shape=jax.ShapeDtypeStruct(x.shape, x.dtype),
        in_specs=[anywhere] * (1 + len(others)),
        out_specs=anywhere,
        input_output_aliases={0: 0},
    )(x, *others)


def lanes(n):
    return -(-n // 128) * 128


def packed(sums, rest, groups_of, shares):
    rows, columns = sums.shape[1], sums.shape[2]
    seqs, share, extra = rows // groups_of, columns // shares, rest.shape[2]
    wide = lanes(max(share, extra))

    def kernel(sums_ref, rest_ref, out_ref):
        for group in range(groups_of):
            for j in range(2):
                out_ref[group, 0, j * seqs : (j + 1) * seqs, :share] = sums_ref[
                    j, group * seqs : (group + 1) * seqs, :
                ]
            out_ref[group, 0, 2 * seqs : 2 * seqs + 2, :extra] = rest_ref[group, 0]

    if share % 128 == 0:
        sums_in, sums_spec = sums, pl.BlockSpec((2, rows, share), lambda k: (0, 0, k))
    else:
        sums_in = sums.reshape(2, rows, shares, share).transpose(2, 0, 1, 3)
        sums_spec = pl.BlockSpec((None, 2, rows, share), lambda k: (k, 0, 0, 0))
    out = pl.pallas_call(
        kernel,
        grid=(shares,),
        in_specs=[sums_spec, pl.BlockSpec((groups_of, 1, 2, extra), lambda k: (0, k, 0, 0))],
        out_specs=pl.BlockSpec((groups_of, 1, 8, wide), lambda k: (0, k, 0, 0)),
        out_shape=jax.ShapeDtypeStruct((groups_of, shares, 8, wide), F32),
    )(sums_in, rest.reshape(groups_of, shares, 2, extra))
    return out.reshape(groups_of * shares, 8, wide)


def text_packed(blocked, turned, stacked, part, count):
    rows = blocked[0].shape[0] if blocked else turned[0].shape[1]
    widths = [x.shape[1] // count for x in blocked] + [x.shape[0] for x in turned]
    widths += [x.shape[0] * part for x in stacked]
    nblocked, nturned = len(blocked), len(turned)

    def kernel(*refs):
        out_ref = refs[-1]
        at = 0
        for i, ref in enumerate(refs[:-1]):
            wide = widths[i]
            if i < nblocked:
                for k in range(count):
                    out_ref[k, :, at : at + wide] = ref[:, k * wide : (k + 1) * wide]
            elif i < nblocked + nturned:
                value = ref[...].astype(F32).T.astype(BF)
                for k in range(count):
                    out_ref[k, :, at : at + wide] = value
            else:
                for t in range(ref.shape[0]):
                    for k in range(count):
                        out_ref[k, :, at + t * part : at + (t + 1) * part] = ref[t, :, :part]
            at += wide

    return pl.pallas_call(
        kernel, out_shape=jax.ShapeDtypeStruct((count, rows, sum(widths)), BF), compiler_params=VMEM_LIMIT
    )(*blocked, *turned, *stacked)


def tensor_packed(places, hidden_rows, wide_rows, part, depth):
    count = places.shape[0] - 1
    rows = hidden_rows.shape[0]

    def kernel(places_ref, hidden_ref, wide_ref, out_ref):
        own = wide_ref[:, pl.ds(pl.multiple_of(places_ref[count] * depth, 128), depth)]
        for k in range(count):
            at = pl.multiple_of(places_ref[k] * part, 128)
            out_ref[k, :, :part] = hidden_ref[:, pl.ds(at, part)]
            out_ref[k, :, part:] = own

    return pl.pallas_call(
        kernel,
        in_specs=[pl.BlockSpec(memory_space=pltpu.SMEM)] + [pl.BlockSpec(memory_space=pltpu.VMEM)] * 2,
        out_shape=jax.ShapeDtypeStruct((count, rows, part + depth), BF),
    )(places, hidden_rows, wide_rows)


def tail_packed(micro, mod, rest, groups_of, shares):
    rows, mods = mod.shape
    share, seqs = mods // shares, rows // 2
    extra = (mods + rest.shape[1]) // (groups_of * shares)
    wide = lanes(max(share, extra))

    def kernel(micro_ref, mod_ref, rest_ref, out_ref, bias_ref, piece_ref):
        for j in range(2):
            bias_ref[j : j + 1, :mods] = jnp.sum(mod_ref[j * seqs : (j + 1) * seqs, :], axis=0, keepdims=True)
        bias_ref[:, mods:] = rest_ref[...]
        piece_ref[...] = jnp.zeros_like(piece_ref)
        for group in range(groups_of):
            mine = jnp.where(micro_ref[0] == group, 1.0, 0.0)
            for k in range(shares):
                device = group * shares + k
                piece_ref[device, :rows, :share] = mod_ref[:, k * share : (k + 1) * share] * mine
                piece_ref[device, rows : rows + 2, :extra] = bias_ref[:, device * extra : (device + 1) * extra]
        out_ref[...] = piece_ref[...].astype(BF)

    return pl.pallas_call(
        kernel,
        in_specs=[pl.BlockSpec(memory_space=pltpu.SMEM)] + [pl.BlockSpec(memory_space=pltpu.VMEM)] * 2,
        out_shape=jax.ShapeDtypeStruct((groups_of * shares, 8, wide), BF),
        scratch_shapes=[
            pltpu.VMEM((2, mods + rest.shape[1]), F32),
            pltpu.VMEM((groups_of * shares, 8, wide), F32),
        ],
    )(micro.reshape(1), mod, rest)


def finish_down(shard, hidden_got, at, cols, part):
    depth, hidden = shard.shape
    count, rows, wide = hidden_got.shape

    def kernel(shard_ref, got_ref, cols_ref, out_ref):
        out_ref[0] = shard_ref[...].astype(F32).T
        total = jnp.zeros((part, depth), F32)
        for t in range(cols.shape[0]):
            lane = at + t * part
            total += dot_tn(got_ref[0, :, lane : lane + part], cols_ref[t, :, part:])
        out_ref[1] = total

    return pl.pallas_call(
        kernel,
        grid=(count,),
        in_specs=[
            pl.BlockSpec((depth, part), lambda c: (0, c)),
            pl.BlockSpec((1, rows, wide), lambda c: (c, 0, 0)),
            pl.BlockSpec(cols.shape, lambda c: (0, 0, 0)),
        ],
        out_specs=pl.BlockSpec((2, part, depth), lambda c: (0, c, 0)),
        out_shape=jax.ShapeDtypeStruct((2, hidden, depth), F32),
    )(shard, hidden_got, cols)


def finish_up(shard, hidden_got, at, cols, part):
    depth, hidden = shard.shape
    count, rows, wide = hidden_got.shape

    def kernel(shard_ref, got_ref, cols_ref, out_ref):
        out_ref[0] = shard_ref[...].astype(F32)
        total = jnp.zeros((depth, part), F32)
        for t in range(cols.shape[0]):
            lane = at + t * part
            total += dot_tn(cols_ref[t, :, part:], got_ref[0, :, lane : lane + part])
        out_ref[1] = total

    return pl.pallas_call(
        kernel,
        grid=(count,),
        in_specs=[
            pl.BlockSpec((depth, part), lambda c: (0, c)),
            pl.BlockSpec((1, rows, wide), lambda c: (c, 0, 0)),
            pl.BlockSpec(cols.shape, lambda c: (0, 0, 0)),
        ],
        out_specs=pl.BlockSpec((2, depth, part), lambda c: (0, 0, c)),
        out_shape=jax.ShapeDtypeStruct((2, depth, hidden), F32),
    )(shard, hidden_got, cols)


def finish_rows(shard, left_got, left, right_got, right, turned):
    m, n = left[1] - left[0], right[1] - right[0]

    def kernel(shard_ref, left_ref, right_ref, out_ref):
        image = shard_ref[...].astype(F32)
        out_ref[0] = image.T if turned else image
        total = jnp.zeros((m, n), F32)
        for c in range(left_got.shape[0]):
            total += dot_tn(left_ref[c, :, left[0] : left[1]], right_ref[c, :, right[0] : right[1]])
        out_ref[1] = total

    return pl.pallas_call(
        kernel, out_shape=jax.ShapeDtypeStruct((2, m, n), F32), compiler_params=VMEM_LIMIT
    )(shard, left_got, right_got)


def normalized(x):
    centred = x - jnp.mean(x, axis=-1, keepdims=True)
    inverse = lax.rsqrt(jnp.mean(centred * centred, axis=-1, keepdims=True) + NORM_EPS)
    return centred * inverse, inverse


def norm_back(n, inverse, w):
    return (w - jnp.mean(w, axis=-1, keepdims=True) - n * jnp.mean(w * n, axis=-1, keepdims=True)) * inverse


def gelu_pair(u):
    c = 0.7978845608028654
    inner = jnp.tanh(c * (u + 0.044715 * u * u * u))
    value = 0.5 * u * (1.0 + inner)
    slope = 0.5 * (1.0 + inner) + 0.5 * u * (1.0 - inner * inner) * c * (1.0 + 3 * 0.044715 * u * u)
    return value.astype(BF), slope.astype(BF)


def shards(
    image_tokens,
    text_tokens,
    conditioning,
    image_seq_ids,
    text_seq_ids,
    ada_weight,
    qkv_weight,
    out_weight,
    up_weight,
    down_weight,
    biases,
    image_cotangent,
    text_cotangent,
):
    section = lax.axis_index("section")
    context = lax.axis_index("context")
    tensor = lax.axis_index("tensor")
    ncontext = lax.axis_size("context")
    ntensor = lax.axis_size("tensor")
    ndev = ncontext * ntensor
    first = section == 0
    micros, own_image, width = image_tokens.shape
    own_text = text_tokens.shape[1]
    seqs = conditioning.shape[1]
    rows_image, rows_text = micros * own_image, micros * own_text
    heads_here = HEADS // ntensor
    local = heads_here * HEAD
    hidden = up_weight.shape[3]
    bias_here = biases.shape[2]
    depth = qkv_weight.shape[2]
    mods = 6 * width
    table_rows = 2 * seqs
    per = ncontext // micros
    micro = context // per
    paired = per == 2 and heads_here % 2 == 0
    groups = 2 if paired else 1
    group_heads = heads_here // groups
    group = group_heads * HEAD
    side = context % per
    ctx_image, ctx_text = ntensor * rows_image, ntensor * rows_text
    ctx_rows = ctx_image + ctx_text

    order = (0, 2, 1, 3)

    def swapped(x, axis, bit):
        return lax.ppermute(x, axis, [(i, i ^ bit) for i in range(lax.axis_size(axis))])

    def sided(a, b):
        return jnp.where(side == 0, a, b), jnp.where(side == 0, b, a)

    def near(x):
        return swapped(x, "tensor", 1)

    def far(x):
        return swapped(x, "tensor", 2)

    def gather_tensor(x):
        beside = near(x)
        across = far(x)
        return x, across, beside, near(across)

    def reduce_tensor(x):
        n = x.shape[0] // 4
        got = near(x[2 * n :])
        mine = x[: 2 * n].astype(F32) + got.astype(F32)
        return mine[:n] + far(mine[n:].astype(BF)).astype(F32)

    def spread(rows):
        return jnp.concatenate(gather_tensor(rows), 0)

    def spread_both(rows):
        return [spread(rows[:rows_image]), spread(rows[rows_image:])]

    def collect(image_rows, text_rows):
        return jnp.concatenate(
            (reduce_tensor(image_rows.astype(BF)), reduce_tensor(text_rows.astype(BF))), 0
        )

    def text_gather(rows):
        sent = jnp.broadcast_to(rows[None], (ncontext,) + rows.shape)
        return lax.all_to_all(sent, "context", 0, 0).reshape(ncontext * rows_text, width)

    def text_scatter(partial_sums):
        sent = partial_sums.astype(BF).reshape(ncontext, rows_text, width)
        return jnp.sum(lax.all_to_all(sent, "context", 0, 0).astype(F32), axis=0)

    def by_tensor(x, axis):
        places = [jnp.array(order)[tensor ^ k] for k in range(ntensor)]
        return jnp.stack([lax.dynamic_index_in_dim(x, at, axis, keepdims=False) for at in places], axis)

    def in_group(x, axis):
        places = [tensor ^ bit for bit in order]
        return jnp.stack([lax.dynamic_index_in_dim(x, at, axis, keepdims=False) for at in places], axis)

    def gather_both(x):
        got = lax.all_gather(x, "tensor")
        got = lax.all_to_all(jnp.broadcast_to(got[None], (ncontext,) + got.shape), "context", 0, 0)
        return got.reshape((ndev,) + x.shape)

    def rounds(step, back):
        pairs = []
        for h in range(ncontext):
            m = (h + step) % micros
            pairs.append((h, m * per + h // micros))
        return [(b, a) for a, b in pairs] if back else pairs

    def to_work(image, text):
        pieces = []
        for step in range(micros):
            m = (context + step) % micros
            pieces.append(
                [
                    lax.ppermute(
                        lax.dynamic_index_in_dim(x, m, 0, keepdims=False), "context", rounds(step, False)
                    )
                    for x in (image, text)
                ]
            )
        return jnp.concatenate([p[0] for p in pieces] + [p[1] for p in pieces], 0).astype(F32)

    def to_home(rows):
        image, text = [], []
        rows = rows.astype(BF)
        for step in range(micros):
            image.append(
                lax.ppermute(
                    rows[step * own_image : (step + 1) * own_image], "context", rounds(step, True)
                )
            )
            at = rows_image + step * own_text
            text.append(lax.ppermute(rows[at : at + own_text], "context", rounds(step, True)))
        image, text = jnp.stack(image), jnp.stack(text)
        turns = [(m - context) % micros for m in range(micros)]
        return tuple(
            jnp.stack([lax.dynamic_index_in_dim(x, turn, 0, keepdims=False) for turn in turns])[None].astype(F32)
            for x in (image, text)
        )

    def gathered(w):
        return lax.all_gather(w, "context", axis=0, tiled=True)

    qkv_full = [gathered(qkv_weight[0, 0])]
    out_full = [gathered(out_weight[0, 0].T)]
    up_full = [gathered(up_weight[0, 0])]
    down_full = [gathered(down_weight[0, 0].T)]

    def ring(w, send_after=None):
        pieces = [w if send_after is None else after(w, send_after)]
        for step in range(1, ncontext):
            pieces.append(lax.ppermute(pieces[-1], "context", [(i, (i + 1) % ncontext) for i in range(ncontext)]))
        return pieces

    def laid(pieces):
        full = jnp.zeros((width, pieces[0].shape[1]), BF)
        for step, piece in enumerate(pieces):
            full = lax.dynamic_update_slice_in_dim(full, piece, (context - step) % ncontext * depth, 0)
        return full

    ring_first = ring(jnp.concatenate((qkv_weight[0, 1], out_weight[0, 1].T), axis=1))
    stage = (ncontext + 2) // 3
    part = hidden // ncontext
    text_sent = jnp.concatenate(
        [w.reshape(ncontext, part, depth) for w in (up_weight[0, 1].T, down_weight[0, 1])], axis=1
    )
    text_moved = lax.all_to_all(after(text_sent, ring_first[-1]), "context", 0, 0)
    feed = []

    cond_float = conditioning.astype(F32)
    silu_cond = jax.nn.silu(cond_float).astype(BF).reshape(micros * seqs, -1)
    ada_part = jnp.einsum("rc,jck->jrk", silu_cond, ada_weight[0], preferred_element_type=F32)
    sharing = [[m * per + u for u in range(per)] for m in range(micros)]
    shares = per * ntensor
    share = mods // shares
    bias_placed = lax.dynamic_update_slice_in_dim(
        jnp.zeros((2, bias_here * ndev), F32),
        biases[0].astype(F32),
        (context * ntensor + tensor) * bias_here,
        1,
    )
    ada_sent = packed(
        ada_part + bias_placed[:, None, :mods],
        jnp.broadcast_to(biases[0].astype(F32)[None], (ndev, 2, bias_here)),
        micros,
        shares,
    )
    ada_got = lax.all_to_all(ada_sent.astype(BF), BOTH, 0, 0)
    bias_full = ada_got[:, table_rows : table_rows + 2, :bias_here].transpose(1, 0, 2).reshape(2, -1).astype(F32)
    ada_sum = jnp.sum(ada_got[:, :table_rows, :share].astype(F32), axis=0).astype(BF)
    table = lax.all_gather(ada_sum, "tensor")
    if paired:
        table = jnp.stack(sided(table, swapped(table, "context", 1)))
    else:
        table = lax.all_gather(table, "context", axis_index_groups=sharing)
    table = after(table, ring_first[stage - 1])
    table = table.reshape(shares, table_rows, share).transpose(1, 0, 2).reshape(table_rows, mods)
    query_bias = lax.dynamic_slice_in_dim(bias_full, mods + tensor * local, local, 1)
    value_bias = lax.dynamic_slice_in_dim(bias_full, mods + width + tensor * local, local, 1)
    qkv_bias = jnp.stack(
        (
            query_bias.reshape(2, heads_here, HEAD),
            jnp.zeros((2, heads_here, HEAD), F32),
            value_bias.reshape(2, heads_here, HEAD),
        ),
        axis=2,
    ).reshape(2, 3 * local)
    out_bias = bias_full[:, mods + 2 * width : mods + 3 * width]
    at_up = mods + 3 * width
    up_bias = lax.dynamic_slice_in_dim(bias_full[0], at_up + tensor * hidden, hidden, 0)
    up_bias_text = bias_full[1, at_up : at_up + ntensor * hidden].reshape(ntensor, ncontext, part)
    up_bias_text = in_group(lax.dynamic_index_in_dim(up_bias_text, context, 1, keepdims=False), 0).reshape(-1)
    down_bias = bias_full[:, mods + 3 * width + hidden * ntensor :]

    def by_modality(pair):
        return jnp.concatenate(
            (
                jnp.broadcast_to(pair[0][None], (rows_image, width)),
                jnp.broadcast_to(pair[1][None], (rows_text, width)),
            ),
            0,
        )

    def ids_of(work_context):
        m, u = work_context // per, work_context % per
        homes = jnp.stack([u * micros + (m - step) % micros for step in range(micros)])
        places = homes[None, :] * ntensor + (tensor ^ jnp.array(order))[:, None]
        found = []
        for ids, own in ((image_seq_ids, own_image), (text_seq_ids, own_text)):
            table_ids = lax.dynamic_index_in_dim(ids, m, 0, keepdims=False).reshape(ndev, own)
            found.append(jnp.take(table_ids, places.reshape(-1), axis=0).reshape(-1))
        return found

    own_found = ids_of(context)
    own_ids = jnp.concatenate((own_found[0][:rows_image], own_found[1][:rows_text] + seqs))
    onehot = (own_ids[:, None] == jnp.arange(table_rows)[None, :]).astype(BF)
    row_mods = dot_nn(onehot, table).astype(BF)
    joint_ids = jnp.concatenate(own_found)
    if paired:
        attn_ids = jnp.concatenate([joint_ids] + ids_of(context ^ 1))
    else:
        attn_ids = jnp.concatenate([x for u in range(per) for x in ids_of(micro * per + u)])

    def row_mod(index):
        return row_mods[:, index * width : (index + 1) * width].astype(F32)

    def attention(joint):
        if paired:
            mine, theirs = sided(joint[: 3 * group], joint[3 * group :])
            theirs = swapped(theirs, "context", 1)
            here, there, lse = attend_pair(mine, theirs, attn_ids, group_heads)
            return jnp.concatenate(sided(here, swapped(there, "context", 1)), axis=0), (mine, theirs, lse)
        by_kind = joint.reshape(heads_here, 3, HEAD, ctx_rows)
        q, k, v = (by_kind[:, i].reshape(local, ctx_rows).T for i in range(3))
        k, v = (
            lax.all_gather(x, "context", axis=0, tiled=True, axis_index_groups=sharing) for x in (k, v)
        )
        attended, lse = attend(q, k, v, joint_ids, attn_ids, group_heads)
        return attended.T, (q, k, v, lse)

    def attention_back(grad, kept):
        if paired:
            mine, theirs, lse = kept
            g_mine, g_theirs = sided(grad[:group], grad[group:])
            g_theirs = swapped(g_theirs, "context", 1)
            d_mine, d_theirs = attend_pair_back(mine, theirs, g_mine, g_theirs, lse, attn_ids, group_heads)
            return jnp.concatenate(sided(d_mine, swapped(d_theirs, "context", 1)), axis=0)
        q, k, v, lse = kept
        dq, dk, dv = attend_back(q, k, v, grad.T, lse, joint_ids, attn_ids, group_heads)
        dk, dv = (
            lax.psum_scatter(x, "context", scatter_dimension=0, tiled=True, axis_index_groups=sharing)
            for x in (dk, dv)
        )
        kinds = [x.T.reshape(heads_here, HEAD, ctx_rows) for x in (dq, dk, dv)]
        return jnp.stack(kinds, axis=1).reshape(3 * local, ctx_rows)

    def forward(x, late=False):
        n1, inv1 = normalized(x)
        h1_rows = (n1 * (1.0 + row_mod(1)) + row_mod(0)).astype(BF)
        fresh = len(qkv_full) == 1
        if fresh:
            h1_rows = after(h1_rows, ring_first[2 * stage - 2])
            full = laid(ring_first)
            qkv_full.append(full[:, : 3 * local])
            out_full.append(full[:, 3 * local :])
        h1 = spread_both(h1_rows)
        joint = jnp.concatenate(
            [(dot_tt(qkv_full[j], h1[j]) + qkv_bias[j][:, None]).astype(BF) for j in range(2)], axis=1
        )
        attended, kept = attention(joint)
        if fresh:
            attended = after(attended, text_moved)
            moved = gather_tensor(text_moved.transpose(1, 0, 2).reshape(2 * part, width))
            feed.append(jnp.concatenate([b[:part] for b in moved], 0))
            feed.append(jnp.concatenate([b[part:] for b in moved], 0))
        branch = collect(
            dot_tt(attended, out_full[0])[:ctx_image], dot_tt(attended[:, ctx_image:], out_full[1])
        ) + by_modality(out_bias)
        middle = x + row_mod(2) * branch
        if fresh:
            middle = after(middle, *feed)
        n2, inv2 = normalized(middle)
        h2_rows = (n2 * (1.0 + row_mod(4)) + row_mod(3)).astype(BF)
        up_text, down_text = feed
        h2 = [spread(h2_rows[:rows_image]), text_gather(h2_rows[rows_image:])]
        pairs = [
            gelu_pair(dot_nn(h2[0], up_full[0]) + up_bias),
            gelu_pair(dot_nt(h2[1], up_text) + up_bias_text),
        ]
        acts, slopes = [p[0] for p in pairs], [p[1] for p in pairs]
        saved = dict(
            x=x, h1=h1, kept=kept, attn=attended, branch=branch, middle=middle, h2=h2, acts=acts,
            slopes=slopes,
        )

        def finish(gate):
            if gate is not None:
                saved["acts"] = [after(act, gate) for act in acts]
            down = jnp.concatenate(
                (
                    reduce_tensor(dot_nt(saved["acts"][0], down_full[0]).astype(BF)),
                    text_scatter(dot_nn(saved["acts"][1], down_text)),
                ),
                0,
            ) + by_modality(down_bias)
            saved["down"] = down
            saved["out"] = middle + row_mod(5) * down

        saved["finish"] = finish
        if not late:
            finish(None)
        return saved

    def chosen(a, b):
        return jax.tree.map(lambda x, y: jnp.where(first, x, y), a, b)

    def scattered(full):
        return lax.psum_scatter(full.astype(BF), "context", scatter_dimension=0, tiled=True)

    def backward(saved, g_out, last=None):
        g_down = (row_mod(5) * g_out).astype(BF)
        up_text, down_text = feed
        gd = [spread(g_down[:rows_image]), text_gather(g_down[rows_image:])]
        g_up = [
            (dot_nn(gd[0], down_full[0]) * saved["slopes"][0].astype(F32)).astype(BF),
            (dot_nt(gd[1], down_text) * saved["slopes"][1].astype(F32)).astype(BF),
        ]
        g_h2 = jnp.concatenate(
            (
                reduce_tensor(dot_nt(g_up[0], up_full[0]).astype(BF)),
                text_scatter(dot_nn(g_up[1], up_text)),
            ),
            0,
        )
        early = []
        if last:
            use = chosen(
                dict(h2=saved["h2"][0], acts=saved["acts"][0], gd=gd[0], g_up=g_up[0]),
                {k: last[k][0] for k in ("h2", "acts", "gd", "g_up")},
            )
            early = [
                dot_tn(use["gd"], use["acts"]).astype(BF),
                dot_tn(use["h2"], use["g_up"]).astype(BF),
            ]
            g_h2 = after(g_h2, *early)
            early = [scattered(part) for part in early]
        n2, inv2 = normalized(saved["middle"])
        g_middle = g_out + norm_back(n2, inv2, g_h2 * (1.0 + row_mod(4)))
        g_branch = (row_mod(2) * g_middle).astype(BF)
        gb = spread_both(g_branch)
        if "down" not in saved:
            saved["finish"](gb[0])
        g_attn = jnp.concatenate([dot_tt(out_full[j], gb[j]).astype(BF) for j in range(2)], axis=1)
        if last:
            use = chosen(dict(gb=gb[0], attn=saved["attn"]), dict(gb=last["gb"][0], attn=last["attn"]))
            early.append(dot_tt(use["gb"], use["attn"][:, :ctx_image]).astype(BF))
            g_attn = after(g_attn, early[2])
        g_joint = attention_back(g_attn, saved["kept"])
        g_h1 = collect(
            dot_tt(g_joint, qkv_full[0])[:ctx_image], dot_tt(g_joint[:, ctx_image:], qkv_full[1])
        )
        if last:
            use = chosen(dict(h1=saved["h1"][0], g=g_joint), dict(h1=last["h1"][0], g=last["g_joint"]))
            early.append(dot_tt(use["h1"], use["g"][:, :ctx_image]).astype(BF))
            g_h1 = after(g_h1, early[3])
        n1, inv1 = normalized(saved["x"])
        g_x = g_middle + norm_back(n1, inv1, g_h1 * (1.0 + row_mod(1)))
        if last:
            g_x = after(g_x, *early[:2])
        row_grads = jnp.concatenate(
            [
                part.astype(BF)
                for part in (
                    g_h1, g_h1 * n1, g_middle * saved["branch"], g_h2, g_h2 * n2, g_out * saved["down"]
                )
            ],
            axis=1,
        )
        mod_grad = dot_tn(onehot, row_grads)
        tensors = dict(
            h1=saved["h1"], attn=saved["attn"], h2=saved["h2"], acts=saved["acts"], g_joint=g_joint,
            gb=gb, g_up=g_up, gd=gd, g_down=g_down, g_branch=g_branch, mod=mod_grad,
        )
        return g_x, tensors, early

    aligned = part % 128 == 0 and depth % 128 == 0 and local % 128 == 0 and ncontext == ntensor
    offsets = tensor ^ jnp.arange(ntensor, dtype=jnp.int32)
    places = jnp.concatenate(((offsets & 1) * 2 + offsets // 2, context.reshape(1).astype(jnp.int32)))

    def tensor_round(hidden_rows, wide_rows):
        if aligned:
            sent = tensor_packed(places, hidden_rows, wide_rows, part, depth)
        else:
            pieces = by_tensor(hidden_rows.reshape(hidden_rows.shape[0], ntensor, part), 1).transpose(1, 0, 2)
            own = lax.dynamic_slice_in_dim(wide_rows, context * depth, depth, 1)
            sent = jnp.concatenate((pieces, jnp.broadcast_to(own[None], (ntensor,) + own.shape)), axis=2)
        return lax.all_to_all(sent, "tensor", 0, 0)

    def context_round(blocked, turned, stacked):
        if aligned:
            return [lax.all_to_all(text_packed(blocked, turned, stacked, part, ncontext), "context", 0, 0)]
        parts = [x.reshape(x.shape[0], ncontext, -1).transpose(1, 0, 2) for x in blocked]
        parts += [jnp.broadcast_to(x.T[None], (ncontext,) + x.T.shape) for x in turned]
        stacks = [x[:, :, :part].transpose(1, 0, 2).reshape(x.shape[1], -1) for x in stacked]
        stacks = [jnp.broadcast_to(x[None], (ncontext,) + x.shape) for x in stacks]
        return [
            lax.all_to_all(jnp.concatenate(group, axis=2), "context", 0, 0) for group in (parts, stacks) if group
        ]

    def handed(rows, by):
        return lax.ppermute(rows.astype(BF), "section", [(0, 1)] if by > 0 else [(1, 0)]).astype(F32)

    saved_first = forward(to_work(image_tokens, text_tokens))
    saved_last = forward(handed(saved_first["out"], 1), late=True)
    grad_last, tensors_last, unused = backward(saved_last, to_work(image_cotangent, text_cotangent))
    kept = chosen(
        [saved_first[n][1] for n in ("acts", "h1", "h2")] + [saved_first["attn"][:, ctx_image:]],
        [saved_last[n][1] for n in ("acts", "h1", "h2")] + [saved_last["attn"][:, ctx_image:]],
    )
    kept[0] = after(kept[0], tensors_last["g_joint"])
    ours_before = tensor_round(kept[0], kept[2])
    got_before = context_round([kept[1]], [kept[3]], [ours_before])
    out = to_home(after(jnp.where(first, saved_first["out"], saved_last["out"]), tensors_last["g_joint"]))
    returned = after(handed(grad_last, -1), *got_before, *out)
    grad_first, tensors_first, early = backward(saved_first, returned, tensors_last)
    grad = to_home(jnp.where(first, grad_first, grad_last))
    use = chosen(tensors_first, tensors_last)

    down_shard, up_shard, out_part, qkv_part = early
    out_shard = after(scattered(out_part), grad_first)
    qkv_shard = after(scattered(qkv_part), grad_first)

    ours_after = tensor_round(use["g_up"][1], use["gd"][1])
    got_after = context_round([after(use["gb"][1], tensors_first["g_joint"])], [], [ours_after])

    def column_sums(parts):
        return jnp.stack([dot_nn(jnp.ones((8, p.shape[0]), BF), p)[0] for p in parts])

    def own_sums(rows):
        return column_sums((rows[:rows_image], rows[rows_image:]))

    qkv_sums = jnp.stack(
        [
            dot_nt(jnp.ones((8, part.shape[1]), BF), part)[0]
            for part in (use["g_joint"][:, :ctx_image], use["g_joint"][:, ctx_image:])
        ]
    ).reshape(2, heads_here, 3, HEAD)
    up_sums_text = lax.dynamic_update_slice_in_dim(
        jnp.zeros((ntensor, ncontext, part), F32),
        by_tensor(column_sums((use["g_up"][1],)).reshape(ntensor, 1, part), 0),
        context,
        1,
    ).reshape(1, -1)
    up_sums_image = lax.dynamic_update_slice_in_dim(
        jnp.zeros((1, ntensor * hidden), F32), column_sums((use["g_up"][0],)), tensor * hidden, 1
    )
    rest = jnp.zeros((2, bias_here * ndev - mods), F32)
    for at, value in (
        (tensor * local, qkv_sums[:, :, 0].reshape(2, local)),
        (width + tensor * local, qkv_sums[:, :, 2].reshape(2, local)),
        (2 * width, own_sums(use["g_branch"])),
        (3 * width, jnp.concatenate((up_sums_image, up_sums_text), 0)),
        (3 * width + ntensor * hidden, own_sums(use["g_down"])),
    ):
        rest = lax.dynamic_update_slice_in_dim(rest, value, at, 1)
    if aligned:
        sent = tail_packed(micro.astype(jnp.int32), use["mod"], rest, micros, shares)
    else:
        bias_part = jnp.concatenate((jnp.sum(use["mod"].reshape(2, seqs, mods), axis=1), rest), axis=1)
        mod_sent = use["mod"].reshape(2, 1, seqs, mods)
        mod_sent = jnp.where(jnp.arange(micros)[None, :, None, None] == micro, mod_sent, 0.0)
        bias_sent = bias_part.reshape(2, ndev, bias_here).transpose(1, 0, 2)
        sent = packed(mod_sent.reshape(2, micros * seqs, mods), bias_sent, micros, shares).astype(BF)
    got = jnp.sum(lax.all_to_all(sent, BOTH, 0, 0).astype(F32), axis=0)
    bias_grad = got[table_rows:, :bias_here]
    got = after(got, *got_after)
    mod_all = (
        gather_both(got[:table_rows, :share].astype(BF))
        .reshape(micros, shares, 2, seqs, share)
        .transpose(2, 0, 3, 1, 4)
        .reshape(2, micros * seqs, mods)
    )
    ada_grad = jnp.einsum("rc,jrk->jck", silu_cond, mod_all, preferred_element_type=F32)
    cond_inner = jnp.einsum("jrk,jck->rc", mod_all, ada_weight[0], preferred_element_type=F32)
    got_qkv = after(context_round([], [use["g_joint"][:, ctx_image:]], [])[0], mod_all)
    if aligned:
        down_grad = finish_down(down_shard, got_before[0], depth + local, ours_after, part)
        up_grad = finish_up(up_shard, got_after[0], depth, ours_before, part)
        out_grad = finish_rows(
            out_shard, got_before[0], (depth, depth + local), got_after[0], (0, depth), True
        )
        qkv_grad = finish_rows(qkv_shard, got_before[0], (0, depth), got_qkv, (0, 3 * local), False)
    else:
        acts_all = got_before[1].reshape(ncontext, -1, ntensor, part)
        g_up_all = got_after[1].reshape(ncontext, -1, ntensor, part)
        text_down = jnp.einsum("crtj,trd->cjd", acts_all, ours_after[:, :, part:], preferred_element_type=F32)
        text_up = jnp.einsum("trk,crtj->kcj", ours_before[:, :, part:], g_up_all, preferred_element_type=F32)
        text_out = jnp.einsum(
            "crh,crd->hd", got_before[0][:, :, depth:], got_after[0], preferred_element_type=F32
        )
        text_qkv = jnp.einsum("crk,crh->kh", got_before[0][:, :, :depth], got_qkv, preferred_element_type=F32)
        down_grad = jnp.stack((down_shard.astype(F32).T, text_down.reshape(hidden, depth)))
        up_grad = jnp.stack((up_shard.astype(F32), text_up.reshape(depth, hidden)))
        out_grad = jnp.stack((out_shard.astype(F32).T, text_out))
        qkv_grad = jnp.stack((qkv_shard.astype(F32), text_qkv))
    unused, silu_back = jax.vjp(jax.nn.silu, cond_float)
    cond_grad = silu_back(lax.psum(cond_inner, "section").reshape(cond_float.shape))[0]
    return (
        *out,
        *grad,
        cond_grad,
        ada_grad[None],
        qkv_grad[None],
        out_grad[None],
        up_grad[None],
        down_grad[None],
        bias_grad[None],
    )


def solution(mesh):
    tokens = P(None, BOTH, None)
    block_rows = P("section", None, BOTH, None)
    by_rows = P("section", None, "context", "tensor")
    by_cols = P("section", None, "tensor", "context")
    block_biases = P("section", None, BOTH)
    in_specs = (
        tokens,
        tokens,
        P(None, None, BOTH),
        P(),
        P(),
        block_rows,
        by_rows,
        by_cols,
        by_rows,
        by_cols,
        block_biases,
        tokens,
        tokens,
    )
    out_specs = (
        block_rows,
        block_rows,
        block_rows,
        block_rows,
        P(None, None, BOTH),
        block_rows,
        by_rows,
        by_cols,
        by_rows,
        by_cols,
        block_biases,
    )
    return jax.shard_map(shards, mesh=mesh, in_specs=in_specs, out_specs=out_specs, check_vma=False)
```

```python
from functools import partial

import jax
import jax.numpy as jnp
from jax import lax
from jax.experimental import pallas as pl
from jax.experimental.pallas import tpu as pltpu
from jax.sharding import PartitionSpec as P

HEADS = 24
HEAD = 64
NORM_EPS = 1e-06
MASKED = -1e30
BF = jnp.bfloat16
F32 = jnp.float32
BOTH = ("context", "tensor")


def dot_nn(a, b):
    return lax.dot_general(a, b, (((1,), (0,)), ((), ())), preferred_element_type=F32)


def dot_nt(a, b):
    return lax.dot_general(a, b, (((1,), (1,)), ((), ())), preferred_element_type=F32)


def dot_tn(a, b):
    return lax.dot_general(a, b, (((0,), (0,)), ((), ())), preferred_element_type=F32)


def dot_tt(a, b):
    return lax.dot_general(a, b, (((0,), (1,)), ((), ())), preferred_element_type=F32)


def scaled(q):
    return q * jnp.asarray(HEAD**-0.5, BF)


def attend_body(heads, chunk, places, q_ref, k_ref, v_ref, idq_ref, idk_ref, store, lse_ref):
    at_q, at_k, at_v = places

    def one_chunk(step, carry):
        rows = pl.ds(pl.multiple_of(step * chunk, chunk), chunk)
        bias = jnp.where(idk_ref[...] == idq_ref[:, rows], 0.0, MASKED)
        outs = []
        for head in range(heads):
            at = head * HEAD
            q = scaled(q_ref[rows, at_q + at : at_q + at + HEAD])
            scores = dot_nt(k_ref[:, at_k + at : at_k + at + HEAD], q) + bias
            top = jnp.max(scores, axis=0, keepdims=True)
            weights = jnp.exp(scores - top)
            total = jnp.sum(weights, axis=0, keepdims=True)
            summed = dot_tn(v_ref[:, at_v + at : at_v + at + HEAD], weights.astype(BF))
            outs.append((summed / total).T)
            lse_ref[head : head + 1, rows] = top + jnp.log(total)
        store(rows, jnp.concatenate(outs, axis=1).astype(BF))
        return carry

    lax.fori_loop(0, idq_ref.shape[1] // chunk, one_chunk, 0)


def attend_back_body(
    heads, chunk, places, q_ref, k_ref, v_ref, g_ref, lse_ref, idq_ref, idk_ref, store_dq, dk_acc, dv_acc
):
    at_q, at_k, at_v = places
    dk_acc[...] = jnp.zeros_like(dk_acc)
    dv_acc[...] = jnp.zeros_like(dv_acc)

    def one_chunk(step, carry):
        rows = pl.ds(pl.multiple_of(step * chunk, chunk), chunk)
        bias = jnp.where(idk_ref[...] == idq_ref[:, rows], 0.0, MASKED)
        grads = []
        for head in range(heads):
            at = head * HEAD
            q = scaled(q_ref[rows, at_q + at : at_q + at + HEAD])
            g = g_ref[rows, at : at + HEAD]
            k = k_ref[:, at_k + at : at_k + at + HEAD]
            probs = jnp.exp(dot_nt(k, q) + bias - lse_ref[head : head + 1, rows])
            dv_acc[head] += dot_nn(probs.astype(BF), g)
            both = probs * dot_nt(v_ref[:, at_v + at : at_v + at + HEAD], g)
            delta = jnp.sum(both, axis=0, keepdims=True)
            dscores = (both - probs * delta).astype(BF)
            dk_acc[head] += dot_nn(dscores, q)
            grads.append((dot_tn(k, dscores) * HEAD**-0.5).T)
        store_dq(rows, jnp.concatenate(grads, axis=1).astype(BF))
        return carry

    lax.fori_loop(0, idq_ref.shape[1] // chunk, one_chunk, 0)


def heads_of(acc):
    return jnp.concatenate([acc[head] for head in range(acc.shape[0])], axis=1).astype(BF)


def attend_costs(queries, keys, heads, factor):
    return pl.CostEstimate(
        flops=factor * queries * keys * heads * HEAD,
        bytes_accessed=2 * (queries + 2 * keys) * heads * HEAD * factor // 4,
        transcendentals=queries * keys * heads,
    )


def chunk_for(keys):
    return 256 if keys <= 1024 else 128


VMEM_LIMIT = pltpu.CompilerParams(vmem_limit_bytes=56 * 2**20)


def attend(q, k, v, ids_q, ids_k, heads):
    queries, keys = q.shape[0], k.shape[0]

    def kernel(q_ref, k_ref, v_ref, idq_ref, idk_ref, out_ref, lse_ref):
        def store(rows, value):
            out_ref[rows, :] = value

        attend_body(
            heads, chunk_for(keys), (0, 0, 0), q_ref, k_ref, v_ref, idq_ref, idk_ref, store, lse_ref
        )

    return pl.pallas_call(
        kernel,
        out_shape=(
            jax.ShapeDtypeStruct((queries, heads * HEAD), BF),
            jax.ShapeDtypeStruct((heads, queries), F32),
        ),
        compiler_params=VMEM_LIMIT,
        cost_estimate=attend_costs(queries, keys, heads, 4),
    )(q, k, v, ids_q.reshape(1, queries), ids_k.reshape(keys, 1))


def attend_back(q, k, v, g, lse, ids_q, ids_k, heads):
    queries, keys = q.shape[0], k.shape[0]

    def kernel(
        q_ref, k_ref, v_ref, g_ref, lse_ref, idq_ref, idk_ref, dq_ref, dk_ref, dv_ref, dk_acc, dv_acc
    ):
        def store(rows, value):
            dq_ref[rows, :] = value

        attend_back_body(
            heads, chunk_for(keys), (0, 0, 0), q_ref, k_ref, v_ref, g_ref, lse_ref, idq_ref, idk_ref,
            store, dk_acc, dv_acc,
        )
        dk_ref[...] = heads_of(dk_acc)
        dv_ref[...] = heads_of(dv_acc)

    return pl.pallas_call(
        kernel,
        out_shape=(
            jax.ShapeDtypeStruct((queries, heads * HEAD), BF),
            jax.ShapeDtypeStruct((keys, heads * HEAD), BF),
            jax.ShapeDtypeStruct((keys, heads * HEAD), BF),
        ),
        scratch_shapes=[pltpu.VMEM((heads, keys, HEAD), F32), pltpu.VMEM((heads, keys, HEAD), F32)],
        compiler_params=VMEM_LIMIT,
        cost_estimate=attend_costs(queries, keys, heads, 10),
    )(q, k, v, g, lse, ids_q.reshape(1, queries), ids_k.reshape(keys, 1))


def attend_pair(mine, theirs, ids, heads):
    wide, half = mine.shape
    rows_all, group = 2 * half, heads * HEAD
    chunk = 256

    def kernel(mine_ref, theirs_ref, idq_ref, idk_ref, here_ref, there_ref, lse_ref, x_ref, out_ref):
        x_ref[:, :half] = mine_ref[...]
        x_ref[:, half:] = theirs_ref[...]

        def one_chunk(step, carry):
            rows = pl.ds(pl.multiple_of(step * chunk, chunk), chunk)
            bias = jnp.where(idk_ref[...] == idq_ref[:, rows], 0.0, MASKED)
            for head in range(heads):
                at = slice(head * HEAD, (head + 1) * HEAD)
                base = 3 * head * HEAD
                q = scaled(x_ref[base : base + HEAD, rows])
                k = x_ref[base + HEAD : base + 2 * HEAD, :]
                v = x_ref[base + 2 * HEAD : base + 3 * HEAD, :]
                scores = dot_tn(k, q) + bias
                top = jnp.max(scores, axis=0, keepdims=True)
                weights = jnp.exp(scores - top)
                total = jnp.sum(weights, axis=0, keepdims=True)
                out_ref[at, rows] = (dot_nn(v, weights.astype(BF)) / total).astype(BF)
                lse_ref[head : head + 1, rows] = top + jnp.log(total)
            return carry

        lax.fori_loop(0, rows_all // chunk, one_chunk, 0)
        here_ref[...] = out_ref[:, :half]
        there_ref[...] = out_ref[:, half:]

    return pl.pallas_call(
        kernel,
        out_shape=(
            jax.ShapeDtypeStruct((group, half), BF),
            jax.ShapeDtypeStruct((group, half), BF),
            jax.ShapeDtypeStruct((heads, rows_all), F32),
        ),
        scratch_shapes=[pltpu.VMEM((wide, rows_all), BF), pltpu.VMEM((group, rows_all), BF)],
        compiler_params=VMEM_LIMIT,
        cost_estimate=attend_costs(rows_all, rows_all, heads, 4),
    )(mine, theirs, ids.reshape(1, rows_all), ids.reshape(rows_all, 1))


def attend_pair_back(mine, theirs, g_mine, g_theirs, lse, ids, heads):
    wide, half = mine.shape
    rows_all, group = 2 * half, heads * HEAD
    chunk = 256

    def kernel(
        mine_ref, theirs_ref, gm_ref, gt_ref, lse_ref, idq_ref, idk_ref, dmine_ref, dtheirs_ref,
        x_ref, g_ref, dq_ref, dk_ref, dv_ref,
    ):
        x_ref[:, :half] = mine_ref[...]
        x_ref[:, half:] = theirs_ref[...]
        g_ref[:, :half] = gm_ref[...]
        g_ref[:, half:] = gt_ref[...]
        dk_ref[...] = jnp.zeros_like(dk_ref)
        dv_ref[...] = jnp.zeros_like(dv_ref)

        def one_chunk(step, carry):
            rows = pl.ds(pl.multiple_of(step * chunk, chunk), chunk)
            bias = jnp.where(idk_ref[...] == idq_ref[:, rows], 0.0, MASKED)
            for head in range(heads):
                at = slice(head * HEAD, (head + 1) * HEAD)
                base = 3 * head * HEAD
                q = scaled(x_ref[base : base + HEAD, rows])
                g = g_ref[at, rows]
                k = x_ref[base + HEAD : base + 2 * HEAD, :]
                v = x_ref[base + 2 * HEAD : base + 3 * HEAD, :]
                probs = jnp.exp(dot_tn(k, q) + bias - lse_ref[head : head + 1, rows])
                dv_ref[at, :] += dot_nt(g, probs.astype(BF))
                both = probs * dot_tn(v, g)
                delta = jnp.sum(both, axis=0, keepdims=True)
                dscores = (both - probs * delta).astype(BF)
                dk_ref[at, :] += dot_nt(q, dscores)
                dq_ref[at, rows] = (dot_nn(k, dscores) * HEAD**-0.5).astype(BF)
            return carry

        lax.fori_loop(0, rows_all // chunk, one_chunk, 0)
        for out_ref, cols in ((dmine_ref, slice(0, half)), (dtheirs_ref, slice(half, rows_all))):
            for head in range(heads):
                at = slice(head * HEAD, (head + 1) * HEAD)
                base = 3 * head * HEAD
                out_ref[base : base + HEAD, :] = dq_ref[at, cols]
                out_ref[base + HEAD : base + 2 * HEAD, :] = dk_ref[at, cols].astype(BF)
                out_ref[base + 2 * HEAD : base + 3 * HEAD, :] = dv_ref[at, cols].astype(BF)

    return pl.pallas_call(
        kernel,
        out_shape=(jax.ShapeDtypeStruct((wide, half), BF), jax.ShapeDtypeStruct((wide, half), BF)),
        scratch_shapes=[
            pltpu.VMEM((wide, rows_all), BF),
            pltpu.VMEM((group, rows_all), BF),
            pltpu.VMEM((group, rows_all), BF),
            pltpu.VMEM((group, rows_all), F32),
            pltpu.VMEM((group, rows_all), F32),
        ],
        compiler_params=VMEM_LIMIT,
        cost_estimate=attend_costs(rows_all, rows_all, heads, 10),
    )(mine, theirs, g_mine, g_theirs, lse, ids.reshape(1, rows_all), ids.reshape(rows_all, 1))


def after(x, *others):
    anywhere = pl.BlockSpec(memory_space=pl.ANY)

    def kernel(*refs):
        pass

    return pl.pallas_call(
        kernel,
        out_shape=jax.ShapeDtypeStruct(x.shape, x.dtype),
        in_specs=[anywhere] * (1 + len(others)),
        out_specs=anywhere,
        input_output_aliases={0: 0},
    )(x, *others)


def lanes(n):
    return -(-n // 128) * 128


def packed(sums, rest, groups_of, shares):
    rows, columns = sums.shape[1], sums.shape[2]
    seqs, share, extra = rows // groups_of, columns // shares, rest.shape[2]
    wide = lanes(max(share, extra))

    def kernel(sums_ref, rest_ref, out_ref):
        for group in range(groups_of):
            for j in range(2):
                out_ref[group, 0, j * seqs : (j + 1) * seqs, :share] = sums_ref[
                    j, group * seqs : (group + 1) * seqs, :
                ]
            out_ref[group, 0, 2 * seqs : 2 * seqs + 2, :extra] = rest_ref[group, 0]

    if share % 128 == 0:
        sums_in, sums_spec = sums, pl.BlockSpec((2, rows, share), lambda k: (0, 0, k))
    else:
        sums_in = sums.reshape(2, rows, shares, share).transpose(2, 0, 1, 3)
        sums_spec = pl.BlockSpec((None, 2, rows, share), lambda k: (k, 0, 0, 0))
    out = pl.pallas_call(
        kernel,
        grid=(shares,),
        in_specs=[sums_spec, pl.BlockSpec((groups_of, 1, 2, extra), lambda k: (0, k, 0, 0))],
        out_specs=pl.BlockSpec((groups_of, 1, 8, wide), lambda k: (0, k, 0, 0)),
        out_shape=jax.ShapeDtypeStruct((groups_of, shares, 8, wide), F32),
    )(sums_in, rest.reshape(groups_of, shares, 2, extra))
    return out.reshape(groups_of * shares, 8, wide)


def text_packed(blocked, turned, stacked, part, count):
    rows = blocked[0].shape[0] if blocked else turned[0].shape[1]
    widths = [x.shape[1] // count for x in blocked] + [x.shape[0] for x in turned]
    widths += [x.shape[0] * part for x in stacked]
    nblocked, nturned = len(blocked), len(turned)

    def kernel(*refs):
        out_ref = refs[-1]
        at = 0
        for i, ref in enumerate(refs[:-1]):
            wide = widths[i]
            if i < nblocked:
                for k in range(count):
                    out_ref[k, :, at : at + wide] = ref[:, k * wide : (k + 1) * wide]
            elif i < nblocked + nturned:
                value = ref[...].astype(F32).T.astype(BF)
                for k in range(count):
                    out_ref[k, :, at : at + wide] = value
            else:
                for t in range(ref.shape[0]):
                    for k in range(count):
                        out_ref[k, :, at + t * part : at + (t + 1) * part] = ref[t, :, :part]
            at += wide

    return pl.pallas_call(
        kernel, out_shape=jax.ShapeDtypeStruct((count, rows, sum(widths)), BF), compiler_params=VMEM_LIMIT
    )(*blocked, *turned, *stacked)


def tensor_packed(places, hidden_rows, wide_rows, part, depth):
    count = places.shape[0] - 1
    rows = hidden_rows.shape[0]

    def kernel(places_ref, hidden_ref, wide_ref, out_ref):
        own = wide_ref[:, pl.ds(pl.multiple_of(places_ref[count] * depth, 128), depth)]
        for k in range(count):
            at = pl.multiple_of(places_ref[k] * part, 128)
            out_ref[k, :, :part] = hidden_ref[:, pl.ds(at, part)]
            out_ref[k, :, part:] = own

    return pl.pallas_call(
        kernel,
        in_specs=[pl.BlockSpec(memory_space=pltpu.SMEM)] + [pl.BlockSpec(memory_space=pltpu.VMEM)] * 2,
        out_shape=jax.ShapeDtypeStruct((count, rows, part + depth), BF),
    )(places, hidden_rows, wide_rows)


def tail_packed(micro, mod, rest, groups_of, shares):
    rows, mods = mod.shape
    share, seqs = mods // shares, rows // 2
    extra = (mods + rest.shape[1]) // (groups_of * shares)
    wide = lanes(max(share, extra))

    def kernel(micro_ref, mod_ref, rest_ref, out_ref, bias_ref, piece_ref):
        for j in range(2):
            bias_ref[j : j + 1, :mods] = jnp.sum(mod_ref[j * seqs : (j + 1) * seqs, :], axis=0, keepdims=True)
        bias_ref[:, mods:] = rest_ref[...]
        piece_ref[...] = jnp.zeros_like(piece_ref)
        for group in range(groups_of):
            mine = jnp.where(micro_ref[0] == group, 1.0, 0.0)
            for k in range(shares):
                device = group * shares + k
                piece_ref[device, :rows, :share] = mod_ref[:, k * share : (k + 1) * share] * mine
                piece_ref[device, rows : rows + 2, :extra] = bias_ref[:, device * extra : (device + 1) * extra]
        out_ref[...] = piece_ref[...].astype(BF)

    return pl.pallas_call(
        kernel,
        in_specs=[pl.BlockSpec(memory_space=pltpu.SMEM)] + [pl.BlockSpec(memory_space=pltpu.VMEM)] * 2,
        out_shape=jax.ShapeDtypeStruct((groups_of * shares, 8, wide), BF),
        scratch_shapes=[
            pltpu.VMEM((2, mods + rest.shape[1]), F32),
            pltpu.VMEM((groups_of * shares, 8, wide), F32),
        ],
    )(micro.reshape(1), mod, rest)


def finish_down(shard, hidden_got, at, cols, part):
    depth, hidden = shard.shape
    count, rows, wide = hidden_got.shape

    def kernel(shard_ref, got_ref, cols_ref, out_ref):
        out_ref[0] = shard_ref[...].astype(F32).T
        total = jnp.zeros((part, depth), F32)
        for t in range(cols.shape[0]):
            lane = at + t * part
            total += dot_tn(got_ref[0, :, lane : lane + part], cols_ref[t, :, part:])
        out_ref[1] = total

    return pl.pallas_call(
        kernel,
        grid=(count,),
        in_specs=[
            pl.BlockSpec((depth, part), lambda c: (0, c)),
            pl.BlockSpec((1, rows, wide), lambda c: (c, 0, 0)),
            pl.BlockSpec(cols.shape, lambda c: (0, 0, 0)),
        ],
        out_specs=pl.BlockSpec((2, part, depth), lambda c: (0, c, 0)),
        out_shape=jax.ShapeDtypeStruct((2, hidden, depth), F32),
    )(shard, hidden_got, cols)


def finish_up(shard, hidden_got, at, cols, part):
    depth, hidden = shard.shape
    count, rows, wide = hidden_got.shape

    def kernel(shard_ref, got_ref, cols_ref, out_ref):
        out_ref[0] = shard_ref[...].astype(F32)
        total = jnp.zeros((depth, part), F32)
        for t in range(cols.shape[0]):
            lane = at + t * part
            total += dot_tn(cols_ref[t, :, part:], got_ref[0, :, lane : lane + part])
        out_ref[1] = total

    return pl.pallas_call(
        kernel,
        grid=(count,),
        in_specs=[
            pl.BlockSpec((depth, part), lambda c: (0, c)),
            pl.BlockSpec((1, rows, wide), lambda c: (c, 0, 0)),
            pl.BlockSpec(cols.shape, lambda c: (0, 0, 0)),
        ],
        out_specs=pl.BlockSpec((2, depth, part), lambda c: (0, 0, c)),
        out_shape=jax.ShapeDtypeStruct((2, depth, hidden), F32),
    )(shard, hidden_got, cols)


def finish_rows(shard, left_got, left, right_got, right, turned):
    m, n = left[1] - left[0], right[1] - right[0]

    def kernel(shard_ref, left_ref, right_ref, out_ref):
        image = shard_ref[...].astype(F32)
        out_ref[0] = image.T if turned else image
        total = jnp.zeros((m, n), F32)
        for c in range(left_got.shape[0]):
            total += dot_tn(left_ref[c, :, left[0] : left[1]], right_ref[c, :, right[0] : right[1]])
        out_ref[1] = total

    return pl.pallas_call(
        kernel, out_shape=jax.ShapeDtypeStruct((2, m, n), F32), compiler_params=VMEM_LIMIT
    )(shard, left_got, right_got)


def normalized(x):
    centred = x - jnp.mean(x, axis=-1, keepdims=True)
    inverse = lax.rsqrt(jnp.mean(centred * centred, axis=-1, keepdims=True) + NORM_EPS)
    return centred * inverse, inverse


def norm_back(n, inverse, w):
    return (w - jnp.mean(w, axis=-1, keepdims=True) - n * jnp.mean(w * n, axis=-1, keepdims=True)) * inverse


def gelu_pair(u):
    c = 0.7978845608028654
    inner = jnp.tanh(c * (u + 0.044715 * u * u * u))
    value = 0.5 * u * (1.0 + inner)
    slope = 0.5 * (1.0 + inner) + 0.5 * u * (1.0 - inner * inner) * c * (1.0 + 3 * 0.044715 * u * u)
    return value.astype(BF), slope.astype(BF)


def shards(
    image_tokens,
    text_tokens,
    conditioning,
    image_seq_ids,
    text_seq_ids,
    ada_weight,
    qkv_weight,
    out_weight,
    up_weight,
    down_weight,
    biases,
    image_cotangent,
    text_cotangent,
):
    section = lax.axis_index("section")
    context = lax.axis_index("context")
    tensor = lax.axis_index("tensor")
    ncontext = lax.axis_size("context")
    ntensor = lax.axis_size("tensor")
    ndev = ncontext * ntensor
    first = section == 0
    micros, own_image, width = image_tokens.shape
    own_text = text_tokens.shape[1]
    seqs = conditioning.shape[1]
    rows_image, rows_text = micros * own_image, micros * own_text
    heads_here = HEADS // ntensor
    local = heads_here * HEAD
    hidden = up_weight.shape[3]
    bias_here = biases.shape[2]
    depth = qkv_weight.shape[2]
    mods = 6 * width
    table_rows = 2 * seqs
    per = ncontext // micros
    micro = context // per
    paired = per == 2 and heads_here % 2 == 0
    groups = 2 if paired else 1
    group_heads = heads_here // groups
    group = group_heads * HEAD
    side = context % per
    ctx_image, ctx_text = ntensor * rows_image, ntensor * rows_text
    ctx_rows = ctx_image + ctx_text

    order = (0, 2, 1, 3)

    def swapped(x, axis, bit):
        return lax.ppermute(x, axis, [(i, i ^ bit) for i in range(lax.axis_size(axis))])

    def sided(a, b):
        return jnp.where(side == 0, a, b), jnp.where(side == 0, b, a)

    def near(x):
        return swapped(x, "tensor", 1)

    def far(x):
        return swapped(x, "tensor", 2)

    def gather_tensor(x):
        beside = near(x)
        across = far(x)
        return x, across, beside, near(across)

    def reduce_tensor(x):
        n = x.shape[0] // 4
        got = near(x[2 * n :])
        mine = x[: 2 * n].astype(F32) + got.astype(F32)
        return mine[:n] + far(mine[n:].astype(BF)).astype(F32)

    def spread(rows):
        return jnp.concatenate(gather_tensor(rows), 0)

    def spread_both(rows):
        return [spread(rows[:rows_image]), spread(rows[rows_image:])]

    def collect(image_rows, text_rows):
        return jnp.concatenate(
            (reduce_tensor(image_rows.astype(BF)), reduce_tensor(text_rows.astype(BF))), 0
        )

    def text_gather(rows):
        sent = jnp.broadcast_to(rows[None], (ncontext,) + rows.shape)
        return lax.all_to_all(sent, "context", 0, 0).reshape(ncontext * rows_text, width)

    def text_scatter(partial_sums):
        sent = partial_sums.astype(BF).reshape(ncontext, rows_text, width)
        return jnp.sum(lax.all_to_all(sent, "context", 0, 0).astype(F32), axis=0)

    def by_tensor(x, axis):
        places = [jnp.array(order)[tensor ^ k] for k in range(ntensor)]
        return jnp.stack([lax.dynamic_index_in_dim(x, at, axis, keepdims=False) for at in places], axis)

    def in_group(x, axis):
        places = [tensor ^ bit for bit in order]
        return jnp.stack([lax.dynamic_index_in_dim(x, at, axis, keepdims=False) for at in places], axis)

    def gather_both(x):
        got = lax.all_gather(x, "tensor")
        got = lax.all_to_all(jnp.broadcast_to(got[None], (ncontext,) + got.shape), "context", 0, 0)
        return got.reshape((ndev,) + x.shape)

    def rounds(step, back):
        pairs = []
        for h in range(ncontext):
            m = (h + step) % micros
            pairs.append((h, m * per + h // micros))
        return [(b, a) for a, b in pairs] if back else pairs

    def to_work(image, text):
        pieces = []
        for step in range(micros):
            m = (context + step) % micros
            pieces.append(
                [
                    lax.ppermute(
                        lax.dynamic_index_in_dim(x, m, 0, keepdims=False), "context", rounds(step, False)
                    )
                    for x in (image, text)
                ]
            )
        return jnp.concatenate([p[0] for p in pieces] + [p[1] for p in pieces], 0).astype(F32)

    def to_home(rows):
        rows = rows.astype(BF)
        pieces = []
        for step in range(micros):
            at, below = step * own_image, rows_image + step * own_text
            both = jnp.concatenate((rows[at : at + own_image], rows[below : below + own_text]), 0)
            pieces.append(lax.ppermute(both, "context", rounds(step, True)))
        pieces = jnp.stack(pieces).astype(F32)
        image, text = pieces[:, :own_image], pieces[:, own_image:]
        turns = [(m - context) % micros for m in range(micros)]
        return tuple(
            jnp.stack([lax.dynamic_index_in_dim(x, turn, 0, keepdims=False) for turn in turns])[None]
            for x in (image, text)
        )

    def gathered(w):
        return lax.all_gather(w, "context", axis=0, tiled=True)

    qkv_full = [gathered(qkv_weight[0, 0])]
    out_full = [gathered(out_weight[0, 0].T)]
    up_full = [gathered(up_weight[0, 0])]
    down_full = [gathered(down_weight[0, 0].T)]
    down_first = []

    def ring(w, send_after=None):
        pieces = [w if send_after is None else after(w, send_after)]
        for step in range(1, ncontext):
            pieces.append(lax.ppermute(pieces[-1], "context", [(i, (i + 1) % ncontext) for i in range(ncontext)]))
        return pieces

    def laid(pieces):
        full = jnp.zeros((width, pieces[0].shape[1]), BF)
        for step, piece in enumerate(pieces):
            full = lax.dynamic_update_slice_in_dim(full, piece, (context - step) % ncontext * depth, 0)
        return full

    ring_first = ring(jnp.concatenate((qkv_weight[0, 1], out_weight[0, 1].T), axis=1))
    stage = (ncontext + 2) // 3
    down_here = down_weight[0, 0].T
    helped = [lax.ppermute(down_here, "section", [(0, 1)])]
    for step in range(1, ncontext):
        pairs = [(ncontext + i, ncontext + (i + 1) % ncontext) for i in range(ncontext)]
        helped.append(lax.ppermute(helped[-1], ("section", "context"), pairs))
    handed_back = [down_here] + [lax.ppermute(x, "section", [(1, 0)]) for x in helped[1:]]
    part = hidden // ncontext
    text_sent = jnp.concatenate(
        [w.reshape(ncontext, part, depth) for w in (up_weight[0, 1].T, down_weight[0, 1])], axis=1
    )
    text_moved = lax.all_to_all(after(text_sent, ring_first[-1]), "context", 0, 0)
    feed = []

    cond_float = conditioning.astype(F32)
    silu_cond = jax.nn.silu(cond_float).astype(BF).reshape(micros * seqs, -1)
    ada_part = jnp.einsum("rc,jck->jrk", silu_cond, ada_weight[0], preferred_element_type=F32)
    sharing = [[m * per + u for u in range(per)] for m in range(micros)]
    shares = per * ntensor
    share = mods // shares
    bias_placed = lax.dynamic_update_slice_in_dim(
        jnp.zeros((2, bias_here * ndev), F32),
        biases[0].astype(F32),
        (context * ntensor + tensor) * bias_here,
        1,
    )
    ada_sent = packed(
        ada_part + bias_placed[:, None, :mods],
        jnp.broadcast_to(biases[0].astype(F32)[None], (ndev, 2, bias_here)),
        micros,
        shares,
    )
    ada_got = lax.all_to_all(ada_sent.astype(BF), BOTH, 0, 0)
    bias_full = ada_got[:, table_rows : table_rows + 2, :bias_here].transpose(1, 0, 2).reshape(2, -1).astype(F32)
    ada_sum = jnp.sum(ada_got[:, :table_rows, :share].astype(F32), axis=0).astype(BF)
    table = lax.all_gather(ada_sum, "tensor")
    if paired:
        table = jnp.stack(sided(table, swapped(table, "context", 1)))
    else:
        table = lax.all_gather(table, "context", axis_index_groups=sharing)
    table = after(table, ring_first[stage - 1], helped[0])
    table = table.reshape(shares, table_rows, share).transpose(1, 0, 2).reshape(table_rows, mods)
    query_bias = lax.dynamic_slice_in_dim(bias_full, mods + tensor * local, local, 1)
    value_bias = lax.dynamic_slice_in_dim(bias_full, mods + width + tensor * local, local, 1)
    qkv_bias = jnp.stack(
        (
            query_bias.reshape(2, heads_here, HEAD),
            jnp.zeros((2, heads_here, HEAD), F32),
            value_bias.reshape(2, heads_here, HEAD),
        ),
        axis=2,
    ).reshape(2, 3 * local)
    out_bias = bias_full[:, mods + 2 * width : mods + 3 * width]
    at_up = mods + 3 * width
    up_bias = lax.dynamic_slice_in_dim(bias_full[0], at_up + tensor * hidden, hidden, 0)
    up_bias_text = bias_full[1, at_up : at_up + ntensor * hidden].reshape(ntensor, ncontext, part)
    up_bias_text = in_group(lax.dynamic_index_in_dim(up_bias_text, context, 1, keepdims=False), 0).reshape(-1)
    down_bias = bias_full[:, mods + 3 * width + hidden * ntensor :]

    def by_modality(pair):
        return jnp.concatenate(
            (
                jnp.broadcast_to(pair[0][None], (rows_image, width)),
                jnp.broadcast_to(pair[1][None], (rows_text, width)),
            ),
            0,
        )

    def ids_of(work_context):
        m, u = work_context // per, work_context % per
        homes = jnp.stack([u * micros + (m - step) % micros for step in range(micros)])
        places = homes[None, :] * ntensor + (tensor ^ jnp.array(order))[:, None]
        found = []
        for ids, own in ((image_seq_ids, own_image), (text_seq_ids, own_text)):
            table_ids = lax.dynamic_index_in_dim(ids, m, 0, keepdims=False).reshape(ndev, own)
            found.append(jnp.take(table_ids, places.reshape(-1), axis=0).reshape(-1))
        return found

    own_found = ids_of(context)
    own_ids = jnp.concatenate((own_found[0][:rows_image], own_found[1][:rows_text] + seqs))
    onehot = (own_ids[:, None] == jnp.arange(table_rows)[None, :]).astype(BF)
    row_mods = dot_nn(onehot, table).astype(BF)
    joint_ids = jnp.concatenate(own_found)
    if paired:
        attn_ids = jnp.concatenate([joint_ids] + ids_of(context ^ 1))
    else:
        attn_ids = jnp.concatenate([x for u in range(per) for x in ids_of(micro * per + u)])

    def row_mod(index):
        return row_mods[:, index * width : (index + 1) * width].astype(F32)

    def attention(joint):
        if paired:
            mine, theirs = sided(joint[: 3 * group], joint[3 * group :])
            theirs = swapped(theirs, "context", 1)
            here, there, lse = attend_pair(mine, theirs, attn_ids, group_heads)
            return jnp.concatenate(sided(here, swapped(there, "context", 1)), axis=0), (mine, theirs, lse)
        by_kind = joint.reshape(heads_here, 3, HEAD, ctx_rows)
        q, k, v = (by_kind[:, i].reshape(local, ctx_rows).T for i in range(3))
        k, v = (
            lax.all_gather(x, "context", axis=0, tiled=True, axis_index_groups=sharing) for x in (k, v)
        )
        attended, lse = attend(q, k, v, joint_ids, attn_ids, group_heads)
        return attended.T, (q, k, v, lse)

    def attention_back(grad, kept):
        if paired:
            mine, theirs, lse = kept
            g_mine, g_theirs = sided(grad[:group], grad[group:])
            g_theirs = swapped(g_theirs, "context", 1)
            d_mine, d_theirs = attend_pair_back(mine, theirs, g_mine, g_theirs, lse, attn_ids, group_heads)
            return jnp.concatenate(sided(d_mine, swapped(d_theirs, "context", 1)), axis=0)
        q, k, v, lse = kept
        dq, dk, dv = attend_back(q, k, v, grad.T, lse, joint_ids, attn_ids, group_heads)
        dk, dv = (
            lax.psum_scatter(x, "context", scatter_dimension=0, tiled=True, axis_index_groups=sharing)
            for x in (dk, dv)
        )
        kinds = [x.T.reshape(heads_here, HEAD, ctx_rows) for x in (dq, dk, dv)]
        return jnp.stack(kinds, axis=1).reshape(3 * local, ctx_rows)

    def forward(x, late=False):
        n1, inv1 = normalized(x)
        h1_rows = (n1 * (1.0 + row_mod(1)) + row_mod(0)).astype(BF)
        fresh = len(qkv_full) == 1
        if fresh:
            h1_rows = after(h1_rows, ring_first[2 * stage - 2], helped[stage - 1])
            full = laid(ring_first)
            qkv_full.append(full[:, : 3 * local])
            out_full.append(full[:, 3 * local :])
        h1 = spread_both(h1_rows)
        joint = jnp.concatenate(
            [(dot_tt(qkv_full[j], h1[j]) + qkv_bias[j][:, None]).astype(BF) for j in range(2)], axis=1
        )
        attended, kept = attention(joint)
        if fresh:
            attended = after(attended, text_moved, helped[2 * stage - 2], handed_back[stage - 1])
            moved = gather_tensor(text_moved.transpose(1, 0, 2).reshape(2 * part, width))
            feed.append(jnp.concatenate([b[:part] for b in moved], 0))
            feed.append(jnp.concatenate([b[part:] for b in moved], 0))
        branch = collect(
            dot_tt(attended, out_full[0])[:ctx_image], dot_tt(attended[:, ctx_image:], out_full[1])
        ) + by_modality(out_bias)
        middle = x + row_mod(2) * branch
        if fresh:
            middle = after(middle, helped[-1], handed_back[2 * stage - 2], *feed)
            down_first.append(laid(handed_back))
        n2, inv2 = normalized(middle)
        h2_rows = (n2 * (1.0 + row_mod(4)) + row_mod(3)).astype(BF)
        up_text, down_text = feed
        h2 = [spread(h2_rows[:rows_image]), text_gather(h2_rows[rows_image:])]
        pairs = [
            gelu_pair(dot_nn(h2[0], up_full[0]) + up_bias),
            gelu_pair(dot_nt(h2[1], up_text) + up_bias_text),
        ]
        acts, slopes = [p[0] for p in pairs], [p[1] for p in pairs]
        saved = dict(
            x=x, h1=h1, kept=kept, attn=attended, branch=branch, middle=middle, h2=h2, acts=acts,
            slopes=slopes,
        )

        def finish(gate):
            if gate is not None:
                saved["acts"] = [after(act, gate) for act in acts]
            down = jnp.concatenate(
                (
                    reduce_tensor(
                        dot_nt(saved["acts"][0], (down_first if fresh else down_full)[0]).astype(BF)
                    ),
                    text_scatter(dot_nn(saved["acts"][1], down_text)),
                ),
                0,
            ) + by_modality(down_bias)
            saved["down"] = down
            saved["out"] = middle + row_mod(5) * down

        saved["finish"] = finish
        if not late:
            finish(None)
        return saved

    def chosen(a, b):
        return jax.tree.map(lambda x, y: jnp.where(first, x, y), a, b)

    def scattered(full):
        return lax.psum_scatter(full.astype(BF), "context", scatter_dimension=0, tiled=True)

    def backward(saved, g_out, last=None):
        g_down = (row_mod(5) * g_out).astype(BF)
        up_text, down_text = feed
        gd = [spread(g_down[:rows_image]), text_gather(g_down[rows_image:])]
        g_up = [
            (dot_nn(gd[0], down_full[0]) * saved["slopes"][0].astype(F32)).astype(BF),
            (dot_nt(gd[1], down_text) * saved["slopes"][1].astype(F32)).astype(BF),
        ]
        g_h2 = jnp.concatenate(
            (
                reduce_tensor(dot_nt(g_up[0], up_full[0]).astype(BF)),
                text_scatter(dot_nn(g_up[1], up_text)),
            ),
            0,
        )
        early = []
        if last:
            use = chosen(
                dict(h2=saved["h2"][0], acts=saved["acts"][0], gd=gd[0], g_up=g_up[0]),
                {k: last[k][0] for k in ("h2", "acts", "gd", "g_up")},
            )
            early = [
                dot_tn(use["gd"], use["acts"]).astype(BF),
                dot_tn(use["h2"], use["g_up"]).astype(BF),
            ]
            g_h2 = after(g_h2, *early)
            early = [scattered(part) for part in early]
        n2, inv2 = normalized(saved["middle"])
        g_middle = g_out + norm_back(n2, inv2, g_h2 * (1.0 + row_mod(4)))
        g_branch = (row_mod(2) * g_middle).astype(BF)
        gb = spread_both(g_branch)
        if "down" not in saved:
            saved["finish"](gb[0])
        g_attn = jnp.concatenate([dot_tt(out_full[j], gb[j]).astype(BF) for j in range(2)], axis=1)
        if last:
            use = chosen(dict(gb=gb[0], attn=saved["attn"]), dict(gb=last["gb"][0], attn=last["attn"]))
            early.append(dot_tt(use["gb"], use["attn"][:, :ctx_image]).astype(BF))
            g_attn = after(g_attn, early[2])
        g_joint = attention_back(g_attn, saved["kept"])
        g_h1 = collect(
            dot_tt(g_joint, qkv_full[0])[:ctx_image], dot_tt(g_joint[:, ctx_image:], qkv_full[1])
        )
        if last:
            use = chosen(dict(h1=saved["h1"][0], g=g_joint), dict(h1=last["h1"][0], g=last["g_joint"]))
            early.append(dot_tt(use["h1"], use["g"][:, :ctx_image]).astype(BF))
            g_h1 = after(g_h1, early[3])
        n1, inv1 = normalized(saved["x"])
        g_x = g_middle + norm_back(n1, inv1, g_h1 * (1.0 + row_mod(1)))
        if last:
            g_x = after(g_x, *early[:2])
        row_grads = jnp.concatenate(
            [
                part.astype(BF)
                for part in (
                    g_h1, g_h1 * n1, g_middle * saved["branch"], g_h2, g_h2 * n2, g_out * saved["down"]
                )
            ],
            axis=1,
        )
        mod_grad = dot_tn(onehot, row_grads)
        tensors = dict(
            h1=saved["h1"], attn=saved["attn"], h2=saved["h2"], acts=saved["acts"], g_joint=g_joint,
            gb=gb, g_up=g_up, gd=gd, g_down=g_down, g_branch=g_branch, mod=mod_grad,
        )
        return g_x, tensors, early

    aligned = part % 128 == 0 and depth % 128 == 0 and local % 128 == 0 and ncontext == ntensor
    offsets = tensor ^ jnp.arange(ntensor, dtype=jnp.int32)
    places = jnp.concatenate(((offsets & 1) * 2 + offsets // 2, context.reshape(1).astype(jnp.int32)))

    def tensor_round(hidden_rows, wide_rows):
        if aligned:
            sent = tensor_packed(places, hidden_rows, wide_rows, part, depth)
        else:
            pieces = by_tensor(hidden_rows.reshape(hidden_rows.shape[0], ntensor, part), 1).transpose(1, 0, 2)
            own = lax.dynamic_slice_in_dim(wide_rows, context * depth, depth, 1)
            sent = jnp.concatenate((pieces, jnp.broadcast_to(own[None], (ntensor,) + own.shape)), axis=2)
        return lax.all_to_all(sent, "tensor", 0, 0)

    def context_round(blocked, turned, stacked):
        if aligned:
            return [lax.all_to_all(text_packed(blocked, turned, stacked, part, ncontext), "context", 0, 0)]
        parts = [x.reshape(x.shape[0], ncontext, -1).transpose(1, 0, 2) for x in blocked]
        parts += [jnp.broadcast_to(x.T[None], (ncontext,) + x.T.shape) for x in turned]
        stacks = [x[:, :, :part].transpose(1, 0, 2).reshape(x.shape[1], -1) for x in stacked]
        stacks = [jnp.broadcast_to(x[None], (ncontext,) + x.shape) for x in stacks]
        return [
            lax.all_to_all(jnp.concatenate(group, axis=2), "context", 0, 0) for group in (parts, stacks) if group
        ]

    def handed(rows, by):
        return lax.ppermute(rows.astype(BF), "section", [(0, 1)] if by > 0 else [(1, 0)]).astype(F32)

    saved_first = forward(to_work(image_tokens, text_tokens))
    saved_last = forward(handed(saved_first["out"], 1), late=True)
    grad_last, tensors_last, unused = backward(saved_last, to_work(image_cotangent, text_cotangent))
    kept = chosen(
        [saved_first[n][1] for n in ("acts", "h1", "h2")] + [saved_first["attn"][:, ctx_image:]],
        [saved_last[n][1] for n in ("acts", "h1", "h2")] + [saved_last["attn"][:, ctx_image:]],
    )
    kept[0] = after(kept[0], tensors_last["g_joint"])
    ours_before = tensor_round(kept[0], kept[2])
    got_before = context_round([kept[1]], [kept[3]], [ours_before])
    out = to_home(after(jnp.where(first, saved_first["out"], saved_last["out"]), tensors_last["g_joint"]))
    returned = after(handed(grad_last, -1), *got_before, *out)
    grad_first, tensors_first, early = backward(saved_first, returned, tensors_last)
    grad = to_home(jnp.where(first, grad_first, grad_last))
    use = chosen(tensors_first, tensors_last)

    down_shard, up_shard, out_part, qkv_part = early
    out_shard = after(scattered(out_part), grad_first)
    qkv_shard = after(scattered(qkv_part), grad_first)

    ours_after = tensor_round(use["g_up"][1], use["gd"][1])
    got_after = context_round([after(use["gb"][1], tensors_first["g_joint"])], [], [ours_after])

    def column_sums(parts):
        return jnp.stack([dot_nn(jnp.ones((8, p.shape[0]), BF), p)[0] for p in parts])

    def own_sums(rows):
        return column_sums((rows[:rows_image], rows[rows_image:]))

    qkv_sums = jnp.stack(
        [
            dot_nt(jnp.ones((8, part.shape[1]), BF), part)[0]
            for part in (use["g_joint"][:, :ctx_image], use["g_joint"][:, ctx_image:])
        ]
    ).reshape(2, heads_here, 3, HEAD)
    up_sums_text = lax.dynamic_update_slice_in_dim(
        jnp.zeros((ntensor, ncontext, part), F32),
        by_tensor(column_sums((use["g_up"][1],)).reshape(ntensor, 1, part), 0),
        context,
        1,
    ).reshape(1, -1)
    up_sums_image = lax.dynamic_update_slice_in_dim(
        jnp.zeros((1, ntensor * hidden), F32), column_sums((use["g_up"][0],)), tensor * hidden, 1
    )
    rest = jnp.zeros((2, bias_here * ndev - mods), F32)
    for at, value in (
        (tensor * local, qkv_sums[:, :, 0].reshape(2, local)),
        (width + tensor * local, qkv_sums[:, :, 2].reshape(2, local)),
        (2 * width, own_sums(use["g_branch"])),
        (3 * width, jnp.concatenate((up_sums_image, up_sums_text), 0)),
        (3 * width + ntensor * hidden, own_sums(use["g_down"])),
    ):
        rest = lax.dynamic_update_slice_in_dim(rest, value, at, 1)
    if aligned:
        sent = tail_packed(micro.astype(jnp.int32), use["mod"], rest, micros, shares)
    else:
        bias_part = jnp.concatenate((jnp.sum(use["mod"].reshape(2, seqs, mods), axis=1), rest), axis=1)
        mod_sent = use["mod"].reshape(2, 1, seqs, mods)
        mod_sent = jnp.where(jnp.arange(micros)[None, :, None, None] == micro, mod_sent, 0.0)
        bias_sent = bias_part.reshape(2, ndev, bias_here).transpose(1, 0, 2)
        sent = packed(mod_sent.reshape(2, micros * seqs, mods), bias_sent, micros, shares).astype(BF)
    got = jnp.sum(lax.all_to_all(sent, BOTH, 0, 0).astype(F32), axis=0)
    bias_grad = got[table_rows:, :bias_here]
    mod_all = (
        gather_both(got[:table_rows, :share].astype(BF))
        .reshape(micros, shares, 2, seqs, share)
        .transpose(2, 0, 3, 1, 4)
        .reshape(2, micros * seqs, mods)
    )
    ada_grad = jnp.einsum("rc,jrk->jck", silu_cond, mod_all, preferred_element_type=F32)
    cond_inner = jnp.einsum("jrk,jck->rc", mod_all, ada_weight[0], preferred_element_type=F32)
    got_qkv = after(context_round([], [use["g_joint"][:, ctx_image:]], [])[0], got)
    if aligned:
        down_grad = finish_down(down_shard, got_before[0], depth + local, ours_after, part)
        up_grad = finish_up(up_shard, got_after[0], depth, ours_before, part)
        out_grad = finish_rows(
            out_shard, got_before[0], (depth, depth + local), got_after[0], (0, depth), True
        )
        qkv_grad = finish_rows(qkv_shard, got_before[0], (0, depth), got_qkv, (0, 3 * local), False)
    else:
        acts_all = got_before[1].reshape(ncontext, -1, ntensor, part)
        g_up_all = got_after[1].reshape(ncontext, -1, ntensor, part)
        text_down = jnp.einsum("crtj,trd->cjd", acts_all, ours_after[:, :, part:], preferred_element_type=F32)
        text_up = jnp.einsum("trk,crtj->kcj", ours_before[:, :, part:], g_up_all, preferred_element_type=F32)
        text_out = jnp.einsum(
            "crh,crd->hd", got_before[0][:, :, depth:], got_after[0], preferred_element_type=F32
        )
        text_qkv = jnp.einsum("crk,crh->kh", got_before[0][:, :, :depth], got_qkv, preferred_element_type=F32)
        down_grad = jnp.stack((down_shard.astype(F32).T, text_down.reshape(hidden, depth)))
        up_grad = jnp.stack((up_shard.astype(F32), text_up.reshape(depth, hidden)))
        out_grad = jnp.stack((out_shard.astype(F32).T, text_out))
        qkv_grad = jnp.stack((qkv_shard.astype(F32), text_qkv))
    unused, silu_back = jax.vjp(jax.nn.silu, cond_float)
    cond_grad = silu_back(lax.psum(cond_inner, "section").reshape(cond_float.shape))[0]
    return (
        *out,
        *grad,
        cond_grad,
        ada_grad[None],
        qkv_grad[None],
        out_grad[None],
        up_grad[None],
        down_grad[None],
        bias_grad[None],
    )


def solution(mesh):
    tokens = P(None, BOTH, None)
    block_rows = P("section", None, BOTH, None)
    by_rows = P("section", None, "context", "tensor")
    by_cols = P("section", None, "tensor", "context")
    block_biases = P("section", None, BOTH)
    in_specs = (
        tokens,
        tokens,
        P(None, None, BOTH),
        P(),
        P(),
        block_rows,
        by_rows,
        by_cols,
        by_rows,
        by_cols,
        block_biases,
        tokens,
        tokens,
    )
    out_specs = (
        block_rows,
        block_rows,
        block_rows,
        block_rows,
        P(None, None, BOTH),
        block_rows,
        by_rows,
        by_cols,
        by_rows,
        by_cols,
        block_biases,
    )
    return jax.shard_map(shards, mesh=mesh, in_specs=in_specs, out_specs=out_specs, check_vma=False)
```

```python
from functools import partial

import jax
import jax.numpy as jnp
from jax import lax
from jax.experimental import pallas as pl
from jax.experimental.pallas import tpu as pltpu
from jax.sharding import PartitionSpec as P

HEADS = 24
HEAD = 64
NORM_EPS = 1e-06
MASKED = -1e30
BF = jnp.bfloat16
F32 = jnp.float32
BOTH = ("context", "tensor")


def dot_nn(a, b):
    return lax.dot_general(a, b, (((1,), (0,)), ((), ())), preferred_element_type=F32)


def dot_nt(a, b):
    return lax.dot_general(a, b, (((1,), (1,)), ((), ())), preferred_element_type=F32)


def dot_tn(a, b):
    return lax.dot_general(a, b, (((0,), (0,)), ((), ())), preferred_element_type=F32)


def dot_tt(a, b):
    return lax.dot_general(a, b, (((0,), (1,)), ((), ())), preferred_element_type=F32)


def scaled(q):
    return q * jnp.asarray(HEAD**-0.5, BF)


def attend_body(heads, chunk, places, q_ref, k_ref, v_ref, idq_ref, idk_ref, store, lse_ref):
    at_q, at_k, at_v = places

    def one_chunk(step, carry):
        rows = pl.ds(pl.multiple_of(step * chunk, chunk), chunk)
        bias = jnp.where(idk_ref[...] == idq_ref[:, rows], 0.0, MASKED)
        outs = []
        for head in range(heads):
            at = head * HEAD
            q = scaled(q_ref[rows, at_q + at : at_q + at + HEAD])
            scores = dot_nt(k_ref[:, at_k + at : at_k + at + HEAD], q) + bias
            top = jnp.max(scores, axis=0, keepdims=True)
            weights = jnp.exp(scores - top)
            total = jnp.sum(weights, axis=0, keepdims=True)
            summed = dot_tn(v_ref[:, at_v + at : at_v + at + HEAD], weights.astype(BF))
            outs.append((summed / total).T)
            lse_ref[head : head + 1, rows] = top + jnp.log(total)
        store(rows, jnp.concatenate(outs, axis=1).astype(BF))
        return carry

    lax.fori_loop(0, idq_ref.shape[1] // chunk, one_chunk, 0)


def attend_back_body(
    heads, chunk, places, q_ref, k_ref, v_ref, g_ref, lse_ref, idq_ref, idk_ref, store_dq, dk_acc, dv_acc
):
    at_q, at_k, at_v = places
    dk_acc[...] = jnp.zeros_like(dk_acc)
    dv_acc[...] = jnp.zeros_like(dv_acc)

    def one_chunk(step, carry):
        rows = pl.ds(pl.multiple_of(step * chunk, chunk), chunk)
        bias = jnp.where(idk_ref[...] == idq_ref[:, rows], 0.0, MASKED)
        grads = []
        for head in range(heads):
            at = head * HEAD
            q = scaled(q_ref[rows, at_q + at : at_q + at + HEAD])
            g = g_ref[rows, at : at + HEAD]
            k = k_ref[:, at_k + at : at_k + at + HEAD]
            probs = jnp.exp(dot_nt(k, q) + bias - lse_ref[head : head + 1, rows])
            dv_acc[head] += dot_nn(probs.astype(BF), g)
            both = probs * dot_nt(v_ref[:, at_v + at : at_v + at + HEAD], g)
            delta = jnp.sum(both, axis=0, keepdims=True)
            dscores = (both - probs * delta).astype(BF)
            dk_acc[head] += dot_nn(dscores, q)
            grads.append((dot_tn(k, dscores) * HEAD**-0.5).T)
        store_dq(rows, jnp.concatenate(grads, axis=1).astype(BF))
        return carry

    lax.fori_loop(0, idq_ref.shape[1] // chunk, one_chunk, 0)


def heads_of(acc):
    return jnp.concatenate([acc[head] for head in range(acc.shape[0])], axis=1).astype(BF)


def attend_costs(queries, keys, heads, factor):
    return pl.CostEstimate(
        flops=factor * queries * keys * heads * HEAD,
        bytes_accessed=2 * (queries + 2 * keys) * heads * HEAD * factor // 4,
        transcendentals=queries * keys * heads,
    )


def chunk_for(keys):
    return 256 if keys <= 1024 else 128


VMEM_LIMIT = pltpu.CompilerParams(vmem_limit_bytes=56 * 2**20)


def attend(q, k, v, ids_q, ids_k, heads):
    queries, keys = q.shape[0], k.shape[0]

    def kernel(q_ref, k_ref, v_ref, idq_ref, idk_ref, out_ref, lse_ref):
        def store(rows, value):
            out_ref[rows, :] = value

        attend_body(
            heads, chunk_for(keys), (0, 0, 0), q_ref, k_ref, v_ref, idq_ref, idk_ref, store, lse_ref
        )

    return pl.pallas_call(
        kernel,
        out_shape=(
            jax.ShapeDtypeStruct((queries, heads * HEAD), BF),
            jax.ShapeDtypeStruct((heads, queries), F32),
        ),
        compiler_params=VMEM_LIMIT,
        cost_estimate=attend_costs(queries, keys, heads, 4),
    )(q, k, v, ids_q.reshape(1, queries), ids_k.reshape(keys, 1))


def attend_back(q, k, v, g, lse, ids_q, ids_k, heads):
    queries, keys = q.shape[0], k.shape[0]

    def kernel(
        q_ref, k_ref, v_ref, g_ref, lse_ref, idq_ref, idk_ref, dq_ref, dk_ref, dv_ref, dk_acc, dv_acc
    ):
        def store(rows, value):
            dq_ref[rows, :] = value

        attend_back_body(
            heads, chunk_for(keys), (0, 0, 0), q_ref, k_ref, v_ref, g_ref, lse_ref, idq_ref, idk_ref,
            store, dk_acc, dv_acc,
        )
        dk_ref[...] = heads_of(dk_acc)
        dv_ref[...] = heads_of(dv_acc)

    return pl.pallas_call(
        kernel,
        out_shape=(
            jax.ShapeDtypeStruct((queries, heads * HEAD), BF),
            jax.ShapeDtypeStruct((keys, heads * HEAD), BF),
            jax.ShapeDtypeStruct((keys, heads * HEAD), BF),
        ),
        scratch_shapes=[pltpu.VMEM((heads, keys, HEAD), F32), pltpu.VMEM((heads, keys, HEAD), F32)],
        compiler_params=VMEM_LIMIT,
        cost_estimate=attend_costs(queries, keys, heads, 10),
    )(q, k, v, g, lse, ids_q.reshape(1, queries), ids_k.reshape(keys, 1))


def attend_pair(mine, theirs, ids, heads):
    wide, half = mine.shape
    rows_all, group = 2 * half, heads * HEAD
    chunk = 256

    def kernel(mine_ref, theirs_ref, idq_ref, idk_ref, here_ref, there_ref, lse_ref, x_ref, out_ref):
        x_ref[:, :half] = mine_ref[...]
        x_ref[:, half:] = theirs_ref[...]

        def one_chunk(step, carry):
            rows = pl.ds(pl.multiple_of(step * chunk, chunk), chunk)
            bias = jnp.where(idk_ref[...] == idq_ref[:, rows], 0.0, MASKED)
            for head in range(heads):
                at = slice(head * HEAD, (head + 1) * HEAD)
                base = 3 * head * HEAD
                q = scaled(x_ref[base : base + HEAD, rows])
                k = x_ref[base + HEAD : base + 2 * HEAD, :]
                v = x_ref[base + 2 * HEAD : base + 3 * HEAD, :]
                scores = dot_tn(k, q) + bias
                top = jnp.max(scores, axis=0, keepdims=True)
                weights = jnp.exp(scores - top)
                total = jnp.sum(weights, axis=0, keepdims=True)
                out_ref[at, rows] = (dot_nn(v, weights.astype(BF)) / total).astype(BF)
                lse_ref[head : head + 1, rows] = top + jnp.log(total)
            return carry

        lax.fori_loop(0, rows_all // chunk, one_chunk, 0)
        here_ref[...] = out_ref[:, :half]
        there_ref[...] = out_ref[:, half:]

    return pl.pallas_call(
        kernel,
        out_shape=(
            jax.ShapeDtypeStruct((group, half), BF),
            jax.ShapeDtypeStruct((group, half), BF),
            jax.ShapeDtypeStruct((heads, rows_all), F32),
        ),
        scratch_shapes=[pltpu.VMEM((wide, rows_all), BF), pltpu.VMEM((group, rows_all), BF)],
        compiler_params=VMEM_LIMIT,
        cost_estimate=attend_costs(rows_all, rows_all, heads, 4),
    )(mine, theirs, ids.reshape(1, rows_all), ids.reshape(rows_all, 1))


def attend_pair_back(mine, theirs, g_mine, g_theirs, lse, ids, heads):
    wide, half = mine.shape
    rows_all, group = 2 * half, heads * HEAD
    chunk = 256

    def kernel(
        mine_ref, theirs_ref, gm_ref, gt_ref, lse_ref, idq_ref, idk_ref, dmine_ref, dtheirs_ref,
        x_ref, g_ref, dq_ref, dk_ref, dv_ref,
    ):
        x_ref[:, :half] = mine_ref[...]
        x_ref[:, half:] = theirs_ref[...]
        g_ref[:, :half] = gm_ref[...]
        g_ref[:, half:] = gt_ref[...]
        dk_ref[...] = jnp.zeros_like(dk_ref)
        dv_ref[...] = jnp.zeros_like(dv_ref)

        def one_chunk(step, carry):
            rows = pl.ds(pl.multiple_of(step * chunk, chunk), chunk)
            bias = jnp.where(idk_ref[...] == idq_ref[:, rows], 0.0, MASKED)
            for head in range(heads):
                at = slice(head * HEAD, (head + 1) * HEAD)
                base = 3 * head * HEAD
                q = scaled(x_ref[base : base + HEAD, rows])
                g = g_ref[at, rows]
                k = x_ref[base + HEAD : base + 2 * HEAD, :]
                v = x_ref[base + 2 * HEAD : base + 3 * HEAD, :]
                probs = jnp.exp(dot_tn(k, q) + bias - lse_ref[head : head + 1, rows])
                dv_ref[at, :] += dot_nt(g, probs.astype(BF))
                both = probs * dot_tn(v, g)
                delta = jnp.sum(both, axis=0, keepdims=True)
                dscores = (both - probs * delta).astype(BF)
                dk_ref[at, :] += dot_nt(q, dscores)
                dq_ref[at, rows] = (dot_nn(k, dscores) * HEAD**-0.5).astype(BF)
            return carry

        lax.fori_loop(0, rows_all // chunk, one_chunk, 0)
        for out_ref, cols in ((dmine_ref, slice(0, half)), (dtheirs_ref, slice(half, rows_all))):
            for head in range(heads):
                at = slice(head * HEAD, (head + 1) * HEAD)
                base = 3 * head * HEAD
                out_ref[base : base + HEAD, :] = dq_ref[at, cols]
                out_ref[base + HEAD : base + 2 * HEAD, :] = dk_ref[at, cols].astype(BF)
                out_ref[base + 2 * HEAD : base + 3 * HEAD, :] = dv_ref[at, cols].astype(BF)

    return pl.pallas_call(
        kernel,
        out_shape=(jax.ShapeDtypeStruct((wide, half), BF), jax.ShapeDtypeStruct((wide, half), BF)),
        scratch_shapes=[
            pltpu.VMEM((wide, rows_all), BF),
            pltpu.VMEM((group, rows_all), BF),
            pltpu.VMEM((group, rows_all), BF),
            pltpu.VMEM((group, rows_all), F32),
            pltpu.VMEM((group, rows_all), F32),
        ],
        compiler_params=VMEM_LIMIT,
        cost_estimate=attend_costs(rows_all, rows_all, heads, 10),
    )(mine, theirs, g_mine, g_theirs, lse, ids.reshape(1, rows_all), ids.reshape(rows_all, 1))


def after(x, *others):
    anywhere = pl.BlockSpec(memory_space=pl.ANY)

    def kernel(*refs):
        pass

    return pl.pallas_call(
        kernel,
        out_shape=jax.ShapeDtypeStruct(x.shape, x.dtype),
        in_specs=[anywhere] * (1 + len(others)),
        out_specs=anywhere,
        input_output_aliases={0: 0},
    )(x, *others)


def lanes(n):
    return -(-n // 128) * 128


def packed(sums, rest, groups_of, shares):
    rows, columns = sums.shape[1], sums.shape[2]
    seqs, share, extra = rows // groups_of, columns // shares, rest.shape[2]
    wide = lanes(max(share, extra))

    def kernel(sums_ref, rest_ref, out_ref):
        for group in range(groups_of):
            for j in range(2):
                out_ref[group, 0, j * seqs : (j + 1) * seqs, :share] = sums_ref[
                    j, group * seqs : (group + 1) * seqs, :
                ]
            out_ref[group, 0, 2 * seqs : 2 * seqs + 2, :extra] = rest_ref[group, 0]

    if share % 128 == 0:
        sums_in, sums_spec = sums, pl.BlockSpec((2, rows, share), lambda k: (0, 0, k))
    else:
        sums_in = sums.reshape(2, rows, shares, share).transpose(2, 0, 1, 3)
        sums_spec = pl.BlockSpec((None, 2, rows, share), lambda k: (k, 0, 0, 0))
    out = pl.pallas_call(
        kernel,
        grid=(shares,),
        in_specs=[sums_spec, pl.BlockSpec((groups_of, 1, 2, extra), lambda k: (0, k, 0, 0))],
        out_specs=pl.BlockSpec((groups_of, 1, 8, wide), lambda k: (0, k, 0, 0)),
        out_shape=jax.ShapeDtypeStruct((groups_of, shares, 8, wide), F32),
    )(sums_in, rest.reshape(groups_of, shares, 2, extra))
    return out.reshape(groups_of * shares, 8, wide)


def text_packed(blocked, turned, stacked, part, count):
    rows = blocked[0].shape[0] if blocked else turned[0].shape[1]
    widths = [x.shape[1] // count for x in blocked] + [x.shape[0] for x in turned]
    widths += [x.shape[0] * part for x in stacked]
    nblocked, nturned = len(blocked), len(turned)

    def kernel(*refs):
        out_ref = refs[-1]
        at = 0
        for i, ref in enumerate(refs[:-1]):
            wide = widths[i]
            if i < nblocked:
                for k in range(count):
                    out_ref[k, :, at : at + wide] = ref[:, k * wide : (k + 1) * wide]
            elif i < nblocked + nturned:
                value = ref[...].astype(F32).T.astype(BF)
                for k in range(count):
                    out_ref[k, :, at : at + wide] = value
            else:
                for t in range(ref.shape[0]):
                    for k in range(count):
                        out_ref[k, :, at + t * part : at + (t + 1) * part] = ref[t, :, :part]
            at += wide

    return pl.pallas_call(
        kernel, out_shape=jax.ShapeDtypeStruct((count, rows, sum(widths)), BF), compiler_params=VMEM_LIMIT
    )(*blocked, *turned, *stacked)


def tensor_packed(places, hidden_rows, wide_rows, part, depth):
    count = places.shape[0] - 1
    rows = hidden_rows.shape[0]

    def kernel(places_ref, hidden_ref, wide_ref, out_ref):
        own = wide_ref[:, pl.ds(pl.multiple_of(places_ref[count] * depth, 128), depth)]
        for k in range(count):
            at = pl.multiple_of(places_ref[k] * part, 128)
            out_ref[k, :, :part] = hidden_ref[:, pl.ds(at, part)]
            out_ref[k, :, part:] = own

    return pl.pallas_call(
        kernel,
        in_specs=[pl.BlockSpec(memory_space=pltpu.SMEM)] + [pl.BlockSpec(memory_space=pltpu.VMEM)] * 2,
        out_shape=jax.ShapeDtypeStruct((count, rows, part + depth), BF),
    )(places, hidden_rows, wide_rows)


def tail_packed(micro, mod, rest, groups_of, shares):
    rows, mods = mod.shape
    share, seqs = mods // shares, rows // 2
    extra = (mods + rest.shape[1]) // (groups_of * shares)
    wide = lanes(max(share, extra))

    def kernel(micro_ref, mod_ref, rest_ref, out_ref, bias_ref, piece_ref):
        for j in range(2):
            bias_ref[j : j + 1, :mods] = jnp.sum(mod_ref[j * seqs : (j + 1) * seqs, :], axis=0, keepdims=True)
        bias_ref[:, mods:] = rest_ref[...]
        piece_ref[...] = jnp.zeros_like(piece_ref)
        for group in range(groups_of):
            mine = jnp.where(micro_ref[0] == group, 1.0, 0.0)
            for k in range(shares):
                device = group * shares + k
                piece_ref[device, :rows, :share] = mod_ref[:, k * share : (k + 1) * share] * mine
                piece_ref[device, rows : rows + 2, :extra] = bias_ref[:, device * extra : (device + 1) * extra]
        out_ref[...] = piece_ref[...].astype(BF)

    return pl.pallas_call(
        kernel,
        in_specs=[pl.BlockSpec(memory_space=pltpu.SMEM)] + [pl.BlockSpec(memory_space=pltpu.VMEM)] * 2,
        out_shape=jax.ShapeDtypeStruct((groups_of * shares, 8, wide), BF),
        scratch_shapes=[
            pltpu.VMEM((2, mods + rest.shape[1]), F32),
            pltpu.VMEM((groups_of * shares, 8, wide), F32),
        ],
    )(micro.reshape(1), mod, rest)


def finish_down(shard, hidden_got, at, cols, part):
    depth, hidden = shard.shape
    count, rows, wide = hidden_got.shape

    def kernel(shard_ref, got_ref, cols_ref, out_ref):
        out_ref[0] = shard_ref[...].astype(F32).T
        total = jnp.zeros((part, depth), F32)
        for t in range(cols.shape[0]):
            lane = at + t * part
            total += dot_tn(got_ref[0, :, lane : lane + part], cols_ref[t, :, part:])
        out_ref[1] = total

    return pl.pallas_call(
        kernel,
        grid=(count,),
        in_specs=[
            pl.BlockSpec((depth, part), lambda c: (0, c)),
            pl.BlockSpec((1, rows, wide), lambda c: (c, 0, 0)),
            pl.BlockSpec(cols.shape, lambda c: (0, 0, 0)),
        ],
        out_specs=pl.BlockSpec((2, part, depth), lambda c: (0, c, 0)),
        out_shape=jax.ShapeDtypeStruct((2, hidden, depth), F32),
    )(shard, hidden_got, cols)


def finish_up(shard, hidden_got, at, cols, part):
    depth, hidden = shard.shape
    count, rows, wide = hidden_got.shape

    def kernel(shard_ref, got_ref, cols_ref, out_ref):
        out_ref[0] = shard_ref[...].astype(F32)
        total = jnp.zeros((depth, part), F32)
        for t in range(cols.shape[0]):
            lane = at + t * part
            total += dot_tn(cols_ref[t, :, part:], got_ref[0, :, lane : lane + part])
        out_ref[1] = total

    return pl.pallas_call(
        kernel,
        grid=(count,),
        in_specs=[
            pl.BlockSpec((depth, part), lambda c: (0, c)),
            pl.BlockSpec((1, rows, wide), lambda c: (c, 0, 0)),
            pl.BlockSpec(cols.shape, lambda c: (0, 0, 0)),
        ],
        out_specs=pl.BlockSpec((2, depth, part), lambda c: (0, 0, c)),
        out_shape=jax.ShapeDtypeStruct((2, depth, hidden), F32),
    )(shard, hidden_got, cols)


def finish_rows(shard, left_got, left, right_got, right, turned):
    m, n = left[1] - left[0], right[1] - right[0]

    def kernel(shard_ref, left_ref, right_ref, out_ref):
        image = shard_ref[...].astype(F32)
        out_ref[0] = image.T if turned else image
        total = jnp.zeros((m, n), F32)
        for c in range(left_got.shape[0]):
            total += dot_tn(left_ref[c, :, left[0] : left[1]], right_ref[c, :, right[0] : right[1]])
        out_ref[1] = total

    return pl.pallas_call(
        kernel, out_shape=jax.ShapeDtypeStruct((2, m, n), F32), compiler_params=VMEM_LIMIT
    )(shard, left_got, right_got)


def normalized(x):
    centred = x - jnp.mean(x, axis=-1, keepdims=True)
    inverse = lax.rsqrt(jnp.mean(centred * centred, axis=-1, keepdims=True) + NORM_EPS)
    return centred * inverse, inverse


def norm_back(n, inverse, w):
    return (w - jnp.mean(w, axis=-1, keepdims=True) - n * jnp.mean(w * n, axis=-1, keepdims=True)) * inverse


def row_call(kernel, row_mods, indices, arrays, outs):
    rows, width = row_mods.shape[0], row_mods.shape[1] // 6

    def whole(x):
        return pl.BlockSpec(x.shape, lambda i: (0,) * len(x.shape))

    return pl.pallas_call(
        kernel,
        grid=(1,),
        in_specs=[pl.BlockSpec((rows, width), lambda i, at=at: (0, at)) for at in indices]
        + [whole(x) for x in arrays],
        out_specs=tuple(whole(x) for x in outs),
        out_shape=tuple(outs),
        compiler_params=VMEM_LIMIT,
    )(*[row_mods] * len(indices), *arrays)


def enter_rows(row_mods, x, cut):
    rows, width = x.shape

    def kernel(shift_ref, scale_ref, x_ref, image_ref, text_ref):
        n = normalized(x_ref[...])[0]
        h = (n * (1.0 + scale_ref[...].astype(F32)) + shift_ref[...].astype(F32)).astype(BF)
        image_ref[...] = h[:cut]
        text_ref[...] = h[cut:]

    outs = [jax.ShapeDtypeStruct((cut, width), BF), jax.ShapeDtypeStruct((rows - cut, width), BF)]
    return row_call(kernel, row_mods, (0, 1), (x,), outs)


def middle_rows(row_mods, x, image_sum, text_sum, bias):
    rows, width = x.shape
    cut = image_sum.shape[0]

    def kernel(
        gate_ref, shift_ref, scale_ref, x_ref, image_ref, text_ref, bias_ref,
        branch_ref, middle_ref, himage_ref, htext_ref,
    ):
        branch_ref[:cut] = image_ref[...] + bias_ref[0:1, :]
        branch_ref[cut:] = text_ref[...] + bias_ref[1:2, :]
        middle = x_ref[...] + gate_ref[...].astype(F32) * branch_ref[...]
        middle_ref[...] = middle
        n = normalized(middle)[0]
        h = (n * (1.0 + scale_ref[...].astype(F32)) + shift_ref[...].astype(F32)).astype(BF)
        himage_ref[...] = h[:cut]
        htext_ref[...] = h[cut:]

    outs = [jax.ShapeDtypeStruct((rows, width), F32)] * 2
    outs += [jax.ShapeDtypeStruct((cut, width), BF), jax.ShapeDtypeStruct((rows - cut, width), BF)]
    return row_call(kernel, row_mods, (2, 3, 4), (x, image_sum, text_sum, bias), outs)


def halves_sum(rows, cut):
    return jnp.concatenate(
        (jnp.sum(rows[:cut], axis=0, keepdims=True), jnp.sum(rows[cut:], axis=0, keepdims=True)), 0
    )


def gated_rows(row_mods, g_out, cut):
    rows, width = g_out.shape

    def kernel(gate_ref, g_ref, image_ref, text_ref, sums_ref):
        g = (gate_ref[...].astype(F32) * g_ref[...]).astype(BF)
        image_ref[...] = g[:cut]
        text_ref[...] = g[cut:]
        sums_ref[...] = halves_sum(g.astype(F32), cut)

    outs = [jax.ShapeDtypeStruct((cut, width), BF), jax.ShapeDtypeStruct((rows - cut, width), BF)]
    outs += [jax.ShapeDtypeStruct((2, width), F32)]
    return row_call(kernel, row_mods, (5,), (g_out,), outs)


def middle_rows_back(row_mods, image_sum, text_sum, middle, g_out, branch, picks):
    rows, width = middle.shape
    cut = image_sum.shape[0]

    def kernel(
        gate_ref, scale_ref, image_ref, text_ref, middle_ref, g_ref, branch_ref, picks_ref,
        gmiddle_ref, gimage_ref, gtext_ref, sums_ref, mod_ref, gh_ref,
    ):
        gh_ref[:cut] = image_ref[...]
        gh_ref[cut:] = text_ref[...]
        gh = gh_ref[...]
        n, inverse = normalized(middle_ref[...])
        g_middle = g_ref[...] + norm_back(n, inverse, gh * (1.0 + scale_ref[...].astype(F32)))
        gmiddle_ref[...] = g_middle
        g_branch = (gate_ref[...].astype(F32) * g_middle).astype(BF)
        gimage_ref[...] = g_branch[:cut]
        gtext_ref[...] = g_branch[cut:]
        sums_ref[...] = halves_sum(g_branch.astype(F32), cut)
        for at, part in enumerate((g_middle * branch_ref[...], gh, gh * n)):
            mod_ref[:, at * width : (at + 1) * width] = dot_nn(picks_ref[...], part.astype(BF))

    outs = [jax.ShapeDtypeStruct((rows, width), F32), jax.ShapeDtypeStruct((cut, width), BF)]
    outs += [jax.ShapeDtypeStruct((rows - cut, width), BF), jax.ShapeDtypeStruct((2, width), F32)]
    outs += [jax.ShapeDtypeStruct((picks.shape[0], 3 * width), F32)]
    scratch = jax.ShapeDtypeStruct((rows, width), F32)
    return row_call(
        kernel, row_mods, (2, 4), (image_sum, text_sum, middle, g_out, branch, picks), outs + [scratch]
    )[:5]


def enter_rows_back(row_mods, image_sum, text_sum, x, g_middle, g_out, down, picks):
    rows, width = x.shape
    cut = image_sum.shape[0]

    def kernel(
        scale_ref, image_ref, text_ref, x_ref, gm_ref, g_ref, down_ref, picks_ref, gx_ref, mod_ref, gh_ref
    ):
        gh_ref[:cut] = image_ref[...]
        gh_ref[cut:] = text_ref[...]
        gh = gh_ref[...]
        n, inverse = normalized(x_ref[...])
        gx_ref[...] = gm_ref[...] + norm_back(n, inverse, gh * (1.0 + scale_ref[...].astype(F32)))
        for at, part in enumerate((gh, gh * n, g_ref[...] * down_ref[...])):
            mod_ref[:, at * width : (at + 1) * width] = dot_nn(picks_ref[...], part.astype(BF))

    outs = [jax.ShapeDtypeStruct((rows, width), F32), jax.ShapeDtypeStruct((picks.shape[0], 3 * width), F32)]
    scratch = jax.ShapeDtypeStruct((rows, width), F32)
    return row_call(
        kernel, row_mods, (1,), (image_sum, text_sum, x, g_middle, g_out, down, picks), outs + [scratch]
    )[:2]


def gelu_pair(u):
    c = 0.7978845608028654
    inner = jnp.tanh(c * (u + 0.044715 * u * u * u))
    value = 0.5 * u * (1.0 + inner)
    slope = 0.5 * (1.0 + inner) + 0.5 * u * (1.0 - inner * inner) * c * (1.0 + 3 * 0.044715 * u * u)
    return value.astype(BF), slope.astype(BF)


def shards(
    image_tokens,
    text_tokens,
    conditioning,
    image_seq_ids,
    text_seq_ids,
    ada_weight,
    qkv_weight,
    out_weight,
    up_weight,
    down_weight,
    biases,
    image_cotangent,
    text_cotangent,
):
    section = lax.axis_index("section")
    context = lax.axis_index("context")
    tensor = lax.axis_index("tensor")
    ncontext = lax.axis_size("context")
    ntensor = lax.axis_size("tensor")
    ndev = ncontext * ntensor
    first = section == 0
    micros, own_image, width = image_tokens.shape
    own_text = text_tokens.shape[1]
    seqs = conditioning.shape[1]
    rows_image, rows_text = micros * own_image, micros * own_text
    heads_here = HEADS // ntensor
    local = heads_here * HEAD
    hidden = up_weight.shape[3]
    bias_here = biases.shape[2]
    depth = qkv_weight.shape[2]
    mods = 6 * width
    table_rows = 2 * seqs
    per = ncontext // micros
    micro = context // per
    paired = per == 2 and heads_here % 2 == 0
    groups = 2 if paired else 1
    group_heads = heads_here // groups
    group = group_heads * HEAD
    side = context % per
    ctx_image, ctx_text = ntensor * rows_image, ntensor * rows_text
    ctx_rows = ctx_image + ctx_text

    order = (0, 2, 1, 3)

    def swapped(x, axis, bit):
        return lax.ppermute(x, axis, [(i, i ^ bit) for i in range(lax.axis_size(axis))])

    def sided(a, b):
        return jnp.where(side == 0, a, b), jnp.where(side == 0, b, a)

    def near(x):
        return swapped(x, "tensor", 1)

    def far(x):
        return swapped(x, "tensor", 2)

    def gather_tensor(x):
        beside = near(x)
        across = far(x)
        return x, across, beside, near(across)

    def reduce_tensor(x):
        n = x.shape[0] // 4
        got = near(x[2 * n :])
        mine = x[: 2 * n].astype(F32) + got.astype(F32)
        return mine[:n] + far(mine[n:].astype(BF)).astype(F32)

    def spread(rows):
        return jnp.concatenate(gather_tensor(rows), 0)

    def text_gather(rows):
        sent = jnp.broadcast_to(rows[None], (ncontext,) + rows.shape)
        return lax.all_to_all(sent, "context", 0, 0).reshape(ncontext * rows_text, width)

    def text_scatter(partial_sums):
        sent = partial_sums.astype(BF).reshape(ncontext, rows_text, width)
        return jnp.sum(lax.all_to_all(sent, "context", 0, 0).astype(F32), axis=0)

    def by_tensor(x, axis):
        places = [jnp.array(order)[tensor ^ k] for k in range(ntensor)]
        return jnp.stack([lax.dynamic_index_in_dim(x, at, axis, keepdims=False) for at in places], axis)

    def in_group(x, axis):
        places = [tensor ^ bit for bit in order]
        return jnp.stack([lax.dynamic_index_in_dim(x, at, axis, keepdims=False) for at in places], axis)

    def gather_both(x):
        got = lax.all_gather(x, "tensor")
        got = lax.all_to_all(jnp.broadcast_to(got[None], (ncontext,) + got.shape), "context", 0, 0)
        return got.reshape((ndev,) + x.shape)

    def rounds(step, back):
        pairs = []
        for h in range(ncontext):
            m = (h + step) % micros
            pairs.append((h, m * per + h // micros))
        return [(b, a) for a, b in pairs] if back else pairs

    def to_work(image, text):
        pieces = []
        for step in range(micros):
            m = (context + step) % micros
            pieces.append(
                [
                    lax.ppermute(
                        lax.dynamic_index_in_dim(x, m, 0, keepdims=False), "context", rounds(step, False)
                    )
                    for x in (image, text)
                ]
            )
        return jnp.concatenate([p[0] for p in pieces] + [p[1] for p in pieces], 0).astype(F32)

    def to_home(rows):
        rows = rows.astype(BF)
        pieces = []
        for step in range(micros):
            at, below = step * own_image, rows_image + step * own_text
            both = jnp.concatenate((rows[at : at + own_image], rows[below : below + own_text]), 0)
            pieces.append(lax.ppermute(both, "context", rounds(step, True)))
        pieces = jnp.stack(pieces).astype(F32)
        image, text = pieces[:, :own_image], pieces[:, own_image:]
        turns = [(m - context) % micros for m in range(micros)]
        return tuple(
            jnp.stack([lax.dynamic_index_in_dim(x, turn, 0, keepdims=False) for turn in turns])[None]
            for x in (image, text)
        )

    def gathered(w):
        return lax.all_gather(w, "context", axis=0, tiled=True)

    qkv_full = [gathered(qkv_weight[0, 0])]
    out_full = [gathered(out_weight[0, 0].T)]
    up_full = [gathered(up_weight[0, 0])]
    down_full = [gathered(down_weight[0, 0].T)]

    def ring(w, send_after=None):
        pieces = [w if send_after is None else after(w, send_after)]
        for step in range(1, ncontext):
            pieces.append(lax.ppermute(pieces[-1], "context", [(i, (i + 1) % ncontext) for i in range(ncontext)]))
        return pieces

    def laid(pieces):
        full = jnp.zeros((width, pieces[0].shape[1]), BF)
        for step, piece in enumerate(pieces):
            full = lax.dynamic_update_slice_in_dim(full, piece, (context - step) % ncontext * depth, 0)
        return full

    ring_first = ring(jnp.concatenate((qkv_weight[0, 1], out_weight[0, 1].T), axis=1))
    stage = (ncontext + 2) // 3
    part = hidden // ncontext
    text_sent = jnp.concatenate(
        [w.reshape(ncontext, part, depth) for w in (up_weight[0, 1].T, down_weight[0, 1])], axis=1
    )
    text_moved = lax.all_to_all(after(text_sent, ring_first[-1]), "context", 0, 0)
    feed = []

    cond_float = conditioning.astype(F32)
    silu_cond = jax.nn.silu(cond_float).astype(BF).reshape(micros * seqs, -1)
    ada_part = jnp.einsum("rc,jck->jrk", silu_cond, ada_weight[0], preferred_element_type=F32)
    sharing = [[m * per + u for u in range(per)] for m in range(micros)]
    shares = per * ntensor
    share = mods // shares
    bias_placed = lax.dynamic_update_slice_in_dim(
        jnp.zeros((2, bias_here * ndev), F32),
        biases[0].astype(F32),
        (context * ntensor + tensor) * bias_here,
        1,
    )
    ada_sent = packed(
        ada_part + bias_placed[:, None, :mods],
        jnp.broadcast_to(biases[0].astype(F32)[None], (ndev, 2, bias_here)),
        micros,
        shares,
    )
    ada_got = lax.all_to_all(ada_sent.astype(BF), BOTH, 0, 0)
    bias_full = ada_got[:, table_rows : table_rows + 2, :bias_here].transpose(1, 0, 2).reshape(2, -1).astype(F32)
    ada_sum = jnp.sum(ada_got[:, :table_rows, :share].astype(F32), axis=0).astype(BF)
    table = lax.all_gather(ada_sum, "tensor")
    if paired:
        table = jnp.stack(sided(table, swapped(table, "context", 1)))
    else:
        table = lax.all_gather(table, "context", axis_index_groups=sharing)
    table = after(table, ring_first[stage - 1])
    table = table.reshape(shares, table_rows, share).transpose(1, 0, 2).reshape(table_rows, mods)
    query_bias = lax.dynamic_slice_in_dim(bias_full, mods + tensor * local, local, 1)
    value_bias = lax.dynamic_slice_in_dim(bias_full, mods + width + tensor * local, local, 1)
    qkv_bias = jnp.stack(
        (
            query_bias.reshape(2, heads_here, HEAD),
            jnp.zeros((2, heads_here, HEAD), F32),
            value_bias.reshape(2, heads_here, HEAD),
        ),
        axis=2,
    ).reshape(2, 3 * local)
    out_bias = bias_full[:, mods + 2 * width : mods + 3 * width]
    at_up = mods + 3 * width
    up_bias = lax.dynamic_slice_in_dim(bias_full[0], at_up + tensor * hidden, hidden, 0)
    up_bias_text = bias_full[1, at_up : at_up + ntensor * hidden].reshape(ntensor, ncontext, part)
    up_bias_text = in_group(lax.dynamic_index_in_dim(up_bias_text, context, 1, keepdims=False), 0).reshape(-1)
    down_bias = bias_full[:, mods + 3 * width + hidden * ntensor :]

    def by_modality(pair):
        return jnp.concatenate(
            (
                jnp.broadcast_to(pair[0][None], (rows_image, width)),
                jnp.broadcast_to(pair[1][None], (rows_text, width)),
            ),
            0,
        )

    def ids_of(work_context):
        m, u = work_context // per, work_context % per
        homes = jnp.stack([u * micros + (m - step) % micros for step in range(micros)])
        places = homes[None, :] * ntensor + (tensor ^ jnp.array(order))[:, None]
        found = []
        for ids, own in ((image_seq_ids, own_image), (text_seq_ids, own_text)):
            table_ids = lax.dynamic_index_in_dim(ids, m, 0, keepdims=False).reshape(ndev, own)
            found.append(jnp.take(table_ids, places.reshape(-1), axis=0).reshape(-1))
        return found

    own_found = ids_of(context)
    own_ids = jnp.concatenate((own_found[0][:rows_image], own_found[1][:rows_text] + seqs))
    onehot = (own_ids[:, None] == jnp.arange(table_rows)[None, :]).astype(BF)
    row_mods = dot_nn(onehot, table).astype(BF)
    picks = onehot.T
    joint_ids = jnp.concatenate(own_found)
    if paired:
        attn_ids = jnp.concatenate([joint_ids] + ids_of(context ^ 1))
    else:
        attn_ids = jnp.concatenate([x for u in range(per) for x in ids_of(micro * per + u)])

    def row_mod(index):
        return row_mods[:, index * width : (index + 1) * width].astype(F32)

    def attention(joint):
        if paired:
            mine, theirs = sided(joint[: 3 * group], joint[3 * group :])
            theirs = swapped(theirs, "context", 1)
            here, there, lse = attend_pair(mine, theirs, attn_ids, group_heads)
            return jnp.concatenate(sided(here, swapped(there, "context", 1)), axis=0), (mine, theirs, lse)
        by_kind = joint.reshape(heads_here, 3, HEAD, ctx_rows)
        q, k, v = (by_kind[:, i].reshape(local, ctx_rows).T for i in range(3))
        k, v = (
            lax.all_gather(x, "context", axis=0, tiled=True, axis_index_groups=sharing) for x in (k, v)
        )
        attended, lse = attend(q, k, v, joint_ids, attn_ids, group_heads)
        return attended.T, (q, k, v, lse)

    def attention_back(grad, kept):
        if paired:
            mine, theirs, lse = kept
            g_mine, g_theirs = sided(grad[:group], grad[group:])
            g_theirs = swapped(g_theirs, "context", 1)
            d_mine, d_theirs = attend_pair_back(mine, theirs, g_mine, g_theirs, lse, attn_ids, group_heads)
            return jnp.concatenate(sided(d_mine, swapped(d_theirs, "context", 1)), axis=0)
        q, k, v, lse = kept
        dq, dk, dv = attend_back(q, k, v, grad.T, lse, joint_ids, attn_ids, group_heads)
        dk, dv = (
            lax.psum_scatter(x, "context", scatter_dimension=0, tiled=True, axis_index_groups=sharing)
            for x in (dk, dv)
        )
        kinds = [x.T.reshape(heads_here, HEAD, ctx_rows) for x in (dq, dk, dv)]
        return jnp.stack(kinds, axis=1).reshape(3 * local, ctx_rows)

    def forward(x, late=False):
        h1_image, h1_text = enter_rows(row_mods, x, rows_image)
        fresh = len(qkv_full) == 1
        if fresh:
            h1_image = after(h1_image, ring_first[2 * stage - 2])
            full = laid(ring_first)
            qkv_full.append(full[:, : 3 * local])
            out_full.append(full[:, 3 * local :])
        h1 = [spread(h1_image), spread(h1_text)]
        joint = jnp.concatenate(
            [(dot_tt(qkv_full[j], h1[j]) + qkv_bias[j][:, None]).astype(BF) for j in range(2)], axis=1
        )
        attended, kept = attention(joint)
        if fresh:
            attended = after(attended, text_moved)
            moved = gather_tensor(text_moved.transpose(1, 0, 2).reshape(2 * part, width))
            feed.append(jnp.concatenate([b[:part] for b in moved], 0))
            feed.append(jnp.concatenate([b[part:] for b in moved], 0))
        image_sum = reduce_tensor(dot_tt(attended, out_full[0])[:ctx_image].astype(BF))
        text_sum = reduce_tensor(dot_tt(attended[:, ctx_image:], out_full[1]).astype(BF))
        if fresh:
            image_sum = after(image_sum, *feed)
        branch, middle, h2_image, h2_text = middle_rows(row_mods, x, image_sum, text_sum, out_bias)
        up_text, down_text = feed
        h2 = [spread(h2_image), text_gather(h2_text)]
        pairs = [
            gelu_pair(dot_nn(h2[0], up_full[0]) + up_bias),
            gelu_pair(dot_nt(h2[1], up_text) + up_bias_text),
        ]
        acts, slopes = [p[0] for p in pairs], [p[1] for p in pairs]
        saved = dict(
            x=x, h1=h1, kept=kept, attn=attended, branch=branch, middle=middle, h2=h2, acts=acts,
            slopes=slopes,
        )

        def finish(gate):
            if gate is not None:
                saved["acts"] = [after(act, gate) for act in acts]
            down = jnp.concatenate(
                (
                    reduce_tensor(dot_nt(saved["acts"][0], down_full[0]).astype(BF)),
                    text_scatter(dot_nn(saved["acts"][1], down_text)),
                ),
                0,
            ) + by_modality(down_bias)
            saved["down"] = down
            saved["out"] = middle + row_mod(5) * down

        saved["finish"] = finish
        if not late:
            finish(None)
        return saved

    def chosen(a, b):
        return jax.tree.map(lambda x, y: jnp.where(first, x, y), a, b)

    def scattered(full):
        return lax.psum_scatter(full.astype(BF), "context", scatter_dimension=0, tiled=True)

    def backward(saved, g_out, last=None):
        gd_image, gd_text, gd_sums = gated_rows(row_mods, g_out, rows_image)
        up_text, down_text = feed
        gd = [spread(gd_image), text_gather(gd_text)]
        g_up = [
            (dot_nn(gd[0], down_full[0]) * saved["slopes"][0].astype(F32)).astype(BF),
            (dot_nt(gd[1], down_text) * saved["slopes"][1].astype(F32)).astype(BF),
        ]
        g_h2_image = reduce_tensor(dot_nt(g_up[0], up_full[0]).astype(BF))
        g_h2_text = text_scatter(dot_nn(g_up[1], up_text))
        early = []
        if last:
            use = chosen(
                dict(h2=saved["h2"][0], acts=saved["acts"][0], gd=gd[0], g_up=g_up[0]),
                {k: last[k][0] for k in ("h2", "acts", "gd", "g_up")},
            )
            early = [
                dot_tn(use["gd"], use["acts"]).astype(BF),
                dot_tn(use["h2"], use["g_up"]).astype(BF),
            ]
            g_h2_image = after(g_h2_image, *early)
            early = [scattered(part) for part in early]
        g_middle, gb_image, gb_text, gb_sums, mod_late = middle_rows_back(
            row_mods, g_h2_image, g_h2_text, saved["middle"], g_out, saved["branch"], picks
        )
        gb = [spread(gb_image), spread(gb_text)]
        if "down" not in saved:
            saved["finish"](gb[0])
        g_attn = jnp.concatenate([dot_tt(out_full[j], gb[j]).astype(BF) for j in range(2)], axis=1)
        if last:
            use = chosen(dict(gb=gb[0], attn=saved["attn"]), dict(gb=last["gb"][0], attn=last["attn"]))
            early.append(dot_tt(use["gb"], use["attn"][:, :ctx_image]).astype(BF))
            g_attn = after(g_attn, early[2])
        g_joint = attention_back(g_attn, saved["kept"])
        g_h1_image = reduce_tensor(dot_tt(g_joint, qkv_full[0])[:ctx_image].astype(BF))
        g_h1_text = reduce_tensor(dot_tt(g_joint[:, ctx_image:], qkv_full[1]).astype(BF))
        if last:
            use = chosen(dict(h1=saved["h1"][0], g=g_joint), dict(h1=last["h1"][0], g=last["g_joint"]))
            early.append(dot_tt(use["h1"], use["g"][:, :ctx_image]).astype(BF))
            g_h1_image = after(g_h1_image, early[3])
        g_x, mod_early = enter_rows_back(
            row_mods, g_h1_image, g_h1_text, saved["x"], g_middle, g_out, saved["down"], picks
        )
        if last:
            g_x = after(g_x, *early[:2])
        mod_grad = jnp.concatenate((mod_early[:, : 2 * width], mod_late, mod_early[:, 2 * width :]), axis=1)
        tensors = dict(
            h1=saved["h1"], attn=saved["attn"], h2=saved["h2"], acts=saved["acts"], g_joint=g_joint,
            gb=gb, g_up=g_up, gd=gd, gd_sums=gd_sums, gb_sums=gb_sums, mod=mod_grad,
        )
        return g_x, tensors, early

    aligned = part % 128 == 0 and depth % 128 == 0 and local % 128 == 0 and ncontext == ntensor
    offsets = tensor ^ jnp.arange(ntensor, dtype=jnp.int32)
    places = jnp.concatenate(((offsets & 1) * 2 + offsets // 2, context.reshape(1).astype(jnp.int32)))

    def tensor_round(hidden_rows, wide_rows):
        if aligned:
            sent = tensor_packed(places, hidden_rows, wide_rows, part, depth)
        else:
            pieces = by_tensor(hidden_rows.reshape(hidden_rows.shape[0], ntensor, part), 1).transpose(1, 0, 2)
            own = lax.dynamic_slice_in_dim(wide_rows, context * depth, depth, 1)
            sent = jnp.concatenate((pieces, jnp.broadcast_to(own[None], (ntensor,) + own.shape)), axis=2)
        return lax.all_to_all(sent, "tensor", 0, 0)

    def context_round(blocked, turned, stacked):
        if aligned:
            return [lax.all_to_all(text_packed(blocked, turned, stacked, part, ncontext), "context", 0, 0)]
        parts = [x.reshape(x.shape[0], ncontext, -1).transpose(1, 0, 2) for x in blocked]
        parts += [jnp.broadcast_to(x.T[None], (ncontext,) + x.T.shape) for x in turned]
        stacks = [x[:, :, :part].transpose(1, 0, 2).reshape(x.shape[1], -1) for x in stacked]
        stacks = [jnp.broadcast_to(x[None], (ncontext,) + x.shape) for x in stacks]
        return [
            lax.all_to_all(jnp.concatenate(group, axis=2), "context", 0, 0) for group in (parts, stacks) if group
        ]

    def handed(rows, by):
        return lax.ppermute(rows.astype(BF), "section", [(0, 1)] if by > 0 else [(1, 0)]).astype(F32)

    saved_first = forward(to_work(image_tokens, text_tokens))
    saved_last = forward(handed(saved_first["out"], 1), late=True)
    grad_last, tensors_last, unused = backward(saved_last, to_work(image_cotangent, text_cotangent))
    kept = chosen(
        [saved_first[n][1] for n in ("acts", "h1", "h2")] + [saved_first["attn"][:, ctx_image:]],
        [saved_last[n][1] for n in ("acts", "h1", "h2")] + [saved_last["attn"][:, ctx_image:]],
    )
    kept[0] = after(kept[0], tensors_last["g_joint"])
    ours_before = tensor_round(kept[0], kept[2])
    got_before = context_round([kept[1]], [kept[3]], [ours_before])
    out = to_home(after(jnp.where(first, saved_first["out"], saved_last["out"]), tensors_last["g_joint"]))
    returned = after(handed(grad_last, -1), *got_before, *out)
    grad_first, tensors_first, early = backward(saved_first, returned, tensors_last)
    grad = to_home(jnp.where(first, grad_first, grad_last))
    use = chosen(tensors_first, tensors_last)

    down_shard, up_shard, out_part, qkv_part = early
    out_shard = after(scattered(out_part), grad_first)
    qkv_shard = after(scattered(qkv_part), grad_first)

    ours_after = tensor_round(use["g_up"][1], use["gd"][1])
    got_after = context_round([after(use["gb"][1], tensors_first["g_joint"])], [], [ours_after])

    def column_sums(parts):
        return jnp.stack([dot_nn(jnp.ones((8, p.shape[0]), BF), p)[0] for p in parts])

    qkv_sums = jnp.stack(
        [
            dot_nt(jnp.ones((8, part.shape[1]), BF), part)[0]
            for part in (use["g_joint"][:, :ctx_image], use["g_joint"][:, ctx_image:])
        ]
    ).reshape(2, heads_here, 3, HEAD)
    up_sums_text = lax.dynamic_update_slice_in_dim(
        jnp.zeros((ntensor, ncontext, part), F32),
        by_tensor(column_sums((use["g_up"][1],)).reshape(ntensor, 1, part), 0),
        context,
        1,
    ).reshape(1, -1)
    up_sums_image = lax.dynamic_update_slice_in_dim(
        jnp.zeros((1, ntensor * hidden), F32), column_sums((use["g_up"][0],)), tensor * hidden, 1
    )
    rest = jnp.zeros((2, bias_here * ndev - mods), F32)
    for at, value in (
        (tensor * local, qkv_sums[:, :, 0].reshape(2, local)),
        (width + tensor * local, qkv_sums[:, :, 2].reshape(2, local)),
        (2 * width, use["gb_sums"]),
        (3 * width, jnp.concatenate((up_sums_image, up_sums_text), 0)),
        (3 * width + ntensor * hidden, use["gd_sums"]),
    ):
        rest = lax.dynamic_update_slice_in_dim(rest, value, at, 1)
    if aligned:
        sent = tail_packed(micro.astype(jnp.int32), use["mod"], rest, micros, shares)
    else:
        bias_part = jnp.concatenate((jnp.sum(use["mod"].reshape(2, seqs, mods), axis=1), rest), axis=1)
        mod_sent = use["mod"].reshape(2, 1, seqs, mods)
        mod_sent = jnp.where(jnp.arange(micros)[None, :, None, None] == micro, mod_sent, 0.0)
        bias_sent = bias_part.reshape(2, ndev, bias_here).transpose(1, 0, 2)
        sent = packed(mod_sent.reshape(2, micros * seqs, mods), bias_sent, micros, shares).astype(BF)
    got = jnp.sum(lax.all_to_all(sent, BOTH, 0, 0).astype(F32), axis=0)
    bias_grad = got[table_rows:, :bias_here]
    mod_all = (
        gather_both(got[:table_rows, :share].astype(BF))
        .reshape(micros, shares, 2, seqs, share)
        .transpose(2, 0, 3, 1, 4)
        .reshape(2, micros * seqs, mods)
    )
    ada_grad = jnp.einsum("rc,jrk->jck", silu_cond, mod_all, preferred_element_type=F32)
    cond_inner = jnp.einsum("jrk,jck->rc", mod_all, ada_weight[0], preferred_element_type=F32)
    got_after = [after(x, mod_all) for x in got_after]
    got_qkv = after(context_round([], [use["g_joint"][:, ctx_image:]], [])[0], mod_all)
    if aligned:
        down_grad = finish_down(down_shard, got_before[0], depth + local, ours_after, part)
        up_grad = finish_up(up_shard, got_after[0], depth, ours_before, part)
        out_grad = finish_rows(
            out_shard, got_before[0], (depth, depth + local), got_after[0], (0, depth), True
        )
        qkv_grad = finish_rows(qkv_shard, got_before[0], (0, depth), got_qkv, (0, 3 * local), False)
    else:
        acts_all = got_before[1].reshape(ncontext, -1, ntensor, part)
        g_up_all = got_after[1].reshape(ncontext, -1, ntensor, part)
        text_down = jnp.einsum("crtj,trd->cjd", acts_all, ours_after[:, :, part:], preferred_element_type=F32)
        text_up = jnp.einsum("trk,crtj->kcj", ours_before[:, :, part:], g_up_all, preferred_element_type=F32)
        text_out = jnp.einsum(
            "crh,crd->hd", got_before[0][:, :, depth:], got_after[0], preferred_element_type=F32
        )
        text_qkv = jnp.einsum("crk,crh->kh", got_before[0][:, :, :depth], got_qkv, preferred_element_type=F32)
        down_grad = jnp.stack((down_shard.astype(F32).T, text_down.reshape(hidden, depth)))
        up_grad = jnp.stack((up_shard.astype(F32), text_up.reshape(depth, hidden)))
        out_grad = jnp.stack((out_shard.astype(F32).T, text_out))
        qkv_grad = jnp.stack((qkv_shard.astype(F32), text_qkv))
    unused, silu_back = jax.vjp(jax.nn.silu, cond_float)
    cond_inner = cond_inner + lax.ppermute(cond_inner, "section", [(0, 1), (1, 0)])
    cond_grad = silu_back(cond_inner.reshape(cond_float.shape))[0]
    return (
        *out,
        *grad,
        cond_grad,
        ada_grad[None],
        qkv_grad[None],
        out_grad[None],
        up_grad[None],
        down_grad[None],
        bias_grad[None],
    )


def solution(mesh):
    tokens = P(None, BOTH, None)
    block_rows = P("section", None, BOTH, None)
    by_rows = P("section", None, "context", "tensor")
    by_cols = P("section", None, "tensor", "context")
    block_biases = P("section", None, BOTH)
    in_specs = (
        tokens,
        tokens,
        P(None, None, BOTH),
        P(),
        P(),
        block_rows,
        by_rows,
        by_cols,
        by_rows,
        by_cols,
        block_biases,
        tokens,
        tokens,
    )
    out_specs = (
        block_rows,
        block_rows,
        block_rows,
        block_rows,
        P(None, None, BOTH),
        block_rows,
        by_rows,
        by_cols,
        by_rows,
        by_cols,
        block_biases,
    )
    return jax.shard_map(shards, mesh=mesh, in_specs=in_specs, out_specs=out_specs, check_vma=False)
```

```python
from functools import partial

import jax
import jax.numpy as jnp
from jax import lax
from jax.experimental import pallas as pl
from jax.experimental.pallas import tpu as pltpu
from jax.sharding import PartitionSpec as P

HEADS = 24
HEAD = 64
NORM_EPS = 1e-06
MASKED = -1e30
BF = jnp.bfloat16
F32 = jnp.float32
BOTH = ("context", "tensor")


def dot_nn(a, b):
    return lax.dot_general(a, b, (((1,), (0,)), ((), ())), preferred_element_type=F32)


def dot_nt(a, b):
    return lax.dot_general(a, b, (((1,), (1,)), ((), ())), preferred_element_type=F32)


def dot_tn(a, b):
    return lax.dot_general(a, b, (((0,), (0,)), ((), ())), preferred_element_type=F32)


def dot_tt(a, b):
    return lax.dot_general(a, b, (((0,), (1,)), ((), ())), preferred_element_type=F32)


def scaled(q):
    return q * jnp.asarray(HEAD**-0.5, BF)


def attend_body(heads, chunk, places, q_ref, k_ref, v_ref, idq_ref, idk_ref, store, lse_ref):
    at_q, at_k, at_v = places

    def one_chunk(step, carry):
        rows = pl.ds(pl.multiple_of(step * chunk, chunk), chunk)
        bias = jnp.where(idk_ref[...] == idq_ref[:, rows], 0.0, MASKED)
        outs = []
        for head in range(heads):
            at = head * HEAD
            q = scaled(q_ref[rows, at_q + at : at_q + at + HEAD])
            scores = dot_nt(k_ref[:, at_k + at : at_k + at + HEAD], q) + bias
            top = jnp.max(scores, axis=0, keepdims=True)
            weights = jnp.exp(scores - top)
            total = jnp.sum(weights, axis=0, keepdims=True)
            summed = dot_tn(v_ref[:, at_v + at : at_v + at + HEAD], weights.astype(BF))
            outs.append((summed / total).T)
            lse_ref[head : head + 1, rows] = top + jnp.log(total)
        store(rows, jnp.concatenate(outs, axis=1).astype(BF))
        return carry

    lax.fori_loop(0, idq_ref.shape[1] // chunk, one_chunk, 0)


def attend_back_body(
    heads, chunk, places, q_ref, k_ref, v_ref, g_ref, lse_ref, idq_ref, idk_ref, store_dq, dk_acc, dv_acc
):
    at_q, at_k, at_v = places
    dk_acc[...] = jnp.zeros_like(dk_acc)
    dv_acc[...] = jnp.zeros_like(dv_acc)

    def one_chunk(step, carry):
        rows = pl.ds(pl.multiple_of(step * chunk, chunk), chunk)
        bias = jnp.where(idk_ref[...] == idq_ref[:, rows], 0.0, MASKED)
        grads = []
        for head in range(heads):
            at = head * HEAD
            q = scaled(q_ref[rows, at_q + at : at_q + at + HEAD])
            g = g_ref[rows, at : at + HEAD]
            k = k_ref[:, at_k + at : at_k + at + HEAD]
            probs = jnp.exp(dot_nt(k, q) + bias - lse_ref[head : head + 1, rows])
            dv_acc[head] += dot_nn(probs.astype(BF), g)
            both = probs * dot_nt(v_ref[:, at_v + at : at_v + at + HEAD], g)
            delta = jnp.sum(both, axis=0, keepdims=True)
            dscores = (both - probs * delta).astype(BF)
            dk_acc[head] += dot_nn(dscores, q)
            grads.append((dot_tn(k, dscores) * HEAD**-0.5).T)
        store_dq(rows, jnp.concatenate(grads, axis=1).astype(BF))
        return carry

    lax.fori_loop(0, idq_ref.shape[1] // chunk, one_chunk, 0)


def heads_of(acc):
    return jnp.concatenate([acc[head] for head in range(acc.shape[0])], axis=1).astype(BF)


def attend_costs(queries, keys, heads, factor):
    return pl.CostEstimate(
        flops=factor * queries * keys * heads * HEAD,
        bytes_accessed=2 * (queries + 2 * keys) * heads * HEAD * factor // 4,
        transcendentals=queries * keys * heads,
    )


def chunk_for(keys):
    return 256 if keys <= 1024 else 128


VMEM_LIMIT = pltpu.CompilerParams(vmem_limit_bytes=56 * 2**20)


def attend(q, k, v, ids_q, ids_k, heads):
    queries, keys = q.shape[0], k.shape[0]

    def kernel(q_ref, k_ref, v_ref, idq_ref, idk_ref, out_ref, lse_ref):
        def store(rows, value):
            out_ref[rows, :] = value

        attend_body(
            heads, chunk_for(keys), (0, 0, 0), q_ref, k_ref, v_ref, idq_ref, idk_ref, store, lse_ref
        )

    return pl.pallas_call(
        kernel,
        out_shape=(
            jax.ShapeDtypeStruct((queries, heads * HEAD), BF),
            jax.ShapeDtypeStruct((heads, queries), F32),
        ),
        compiler_params=VMEM_LIMIT,
        cost_estimate=attend_costs(queries, keys, heads, 4),
    )(q, k, v, ids_q.reshape(1, queries), ids_k.reshape(keys, 1))


def attend_back(q, k, v, g, lse, ids_q, ids_k, heads):
    queries, keys = q.shape[0], k.shape[0]

    def kernel(
        q_ref, k_ref, v_ref, g_ref, lse_ref, idq_ref, idk_ref, dq_ref, dk_ref, dv_ref, dk_acc, dv_acc
    ):
        def store(rows, value):
            dq_ref[rows, :] = value

        attend_back_body(
            heads, chunk_for(keys), (0, 0, 0), q_ref, k_ref, v_ref, g_ref, lse_ref, idq_ref, idk_ref,
            store, dk_acc, dv_acc,
        )
        dk_ref[...] = heads_of(dk_acc)
        dv_ref[...] = heads_of(dv_acc)

    return pl.pallas_call(
        kernel,
        out_shape=(
            jax.ShapeDtypeStruct((queries, heads * HEAD), BF),
            jax.ShapeDtypeStruct((keys, heads * HEAD), BF),
            jax.ShapeDtypeStruct((keys, heads * HEAD), BF),
        ),
        scratch_shapes=[pltpu.VMEM((heads, keys, HEAD), F32), pltpu.VMEM((heads, keys, HEAD), F32)],
        compiler_params=VMEM_LIMIT,
        cost_estimate=attend_costs(queries, keys, heads, 10),
    )(q, k, v, g, lse, ids_q.reshape(1, queries), ids_k.reshape(keys, 1))


def attend_pair(mine, theirs, ids, heads):
    wide, half = mine.shape
    rows_all, group = 2 * half, heads * HEAD
    chunk = 256

    def kernel(mine_ref, theirs_ref, idq_ref, idk_ref, here_ref, there_ref, lse_ref, x_ref, out_ref):
        x_ref[:, :half] = mine_ref[...]
        x_ref[:, half:] = theirs_ref[...]

        def one_chunk(step, carry):
            rows = pl.ds(pl.multiple_of(step * chunk, chunk), chunk)
            bias = jnp.where(idk_ref[...] == idq_ref[:, rows], 0.0, MASKED)
            for head in range(heads):
                at = slice(head * HEAD, (head + 1) * HEAD)
                base = 3 * head * HEAD
                q = scaled(x_ref[base : base + HEAD, rows])
                k = x_ref[base + HEAD : base + 2 * HEAD, :]
                v = x_ref[base + 2 * HEAD : base + 3 * HEAD, :]
                scores = dot_tn(k, q) + bias
                top = jnp.max(scores, axis=0, keepdims=True)
                weights = jnp.exp(scores - top)
                total = jnp.sum(weights, axis=0, keepdims=True)
                out_ref[at, rows] = (dot_nn(v, weights.astype(BF)) / total).astype(BF)
                lse_ref[head : head + 1, rows] = top + jnp.log(total)
            return carry

        lax.fori_loop(0, rows_all // chunk, one_chunk, 0)
        here_ref[...] = out_ref[:, :half]
        there_ref[...] = out_ref[:, half:]

    return pl.pallas_call(
        kernel,
        out_shape=(
            jax.ShapeDtypeStruct((group, half), BF),
            jax.ShapeDtypeStruct((group, half), BF),
            jax.ShapeDtypeStruct((heads, rows_all), F32),
        ),
        scratch_shapes=[pltpu.VMEM((wide, rows_all), BF), pltpu.VMEM((group, rows_all), BF)],
        compiler_params=VMEM_LIMIT,
        cost_estimate=attend_costs(rows_all, rows_all, heads, 4),
    )(mine, theirs, ids.reshape(1, rows_all), ids.reshape(rows_all, 1))


def attend_pair_back(mine, theirs, g_mine, g_theirs, lse, ids, heads):
    wide, half = mine.shape
    rows_all, group = 2 * half, heads * HEAD
    chunk = 256

    def kernel(
        mine_ref, theirs_ref, gm_ref, gt_ref, lse_ref, idq_ref, idk_ref, dmine_ref, dtheirs_ref,
        x_ref, g_ref, dq_ref, dk_ref, dv_ref,
    ):
        x_ref[:, :half] = mine_ref[...]
        x_ref[:, half:] = theirs_ref[...]
        g_ref[:, :half] = gm_ref[...]
        g_ref[:, half:] = gt_ref[...]
        dk_ref[...] = jnp.zeros_like(dk_ref)
        dv_ref[...] = jnp.zeros_like(dv_ref)

        def one_chunk(step, carry):
            rows = pl.ds(pl.multiple_of(step * chunk, chunk), chunk)
            bias = jnp.where(idk_ref[...] == idq_ref[:, rows], 0.0, MASKED)
            for head in range(heads):
                at = slice(head * HEAD, (head + 1) * HEAD)
                base = 3 * head * HEAD
                q = scaled(x_ref[base : base + HEAD, rows])
                g = g_ref[at, rows]
                k = x_ref[base + HEAD : base + 2 * HEAD, :]
                v = x_ref[base + 2 * HEAD : base + 3 * HEAD, :]
                probs = jnp.exp(dot_tn(k, q) + bias - lse_ref[head : head + 1, rows])
                dv_ref[at, :] += dot_nt(g, probs.astype(BF))
                both = probs * dot_tn(v, g)
                delta = jnp.sum(both, axis=0, keepdims=True)
                dscores = (both - probs * delta).astype(BF)
                dk_ref[at, :] += dot_nt(q, dscores)
                dq_ref[at, rows] = (dot_nn(k, dscores) * HEAD**-0.5).astype(BF)
            return carry

        lax.fori_loop(0, rows_all // chunk, one_chunk, 0)
        for out_ref, cols in ((dmine_ref, slice(0, half)), (dtheirs_ref, slice(half, rows_all))):
            for head in range(heads):
                at = slice(head * HEAD, (head + 1) * HEAD)
                base = 3 * head * HEAD
                out_ref[base : base + HEAD, :] = dq_ref[at, cols]
                out_ref[base + HEAD : base + 2 * HEAD, :] = dk_ref[at, cols].astype(BF)
                out_ref[base + 2 * HEAD : base + 3 * HEAD, :] = dv_ref[at, cols].astype(BF)

    return pl.pallas_call(
        kernel,
        out_shape=(jax.ShapeDtypeStruct((wide, half), BF), jax.ShapeDtypeStruct((wide, half), BF)),
        scratch_shapes=[
            pltpu.VMEM((wide, rows_all), BF),
            pltpu.VMEM((group, rows_all), BF),
            pltpu.VMEM((group, rows_all), BF),
            pltpu.VMEM((group, rows_all), F32),
            pltpu.VMEM((group, rows_all), F32),
        ],
        compiler_params=VMEM_LIMIT,
        cost_estimate=attend_costs(rows_all, rows_all, heads, 10),
    )(mine, theirs, g_mine, g_theirs, lse, ids.reshape(1, rows_all), ids.reshape(rows_all, 1))


def after(x, *others):
    anywhere = pl.BlockSpec(memory_space=pl.ANY)

    def kernel(*refs):
        pass

    return pl.pallas_call(
        kernel,
        out_shape=jax.ShapeDtypeStruct(x.shape, x.dtype),
        in_specs=[anywhere] * (1 + len(others)),
        out_specs=anywhere,
        input_output_aliases={0: 0},
    )(x, *others)


def lanes(n):
    return -(-n // 128) * 128


def packed(sums, rest, groups_of, shares):
    rows, columns = sums.shape[1], sums.shape[2]
    seqs, share, extra = rows // groups_of, columns // shares, rest.shape[2]
    wide = lanes(max(share, extra))

    def kernel(sums_ref, rest_ref, out_ref):
        for group in range(groups_of):
            for j in range(2):
                out_ref[group, 0, j * seqs : (j + 1) * seqs, :share] = sums_ref[
                    j, group * seqs : (group + 1) * seqs, :
                ]
            out_ref[group, 0, 2 * seqs : 2 * seqs + 2, :extra] = rest_ref[group, 0]

    if share % 128 == 0:
        sums_in, sums_spec = sums, pl.BlockSpec((2, rows, share), lambda k: (0, 0, k))
    else:
        sums_in = sums.reshape(2, rows, shares, share).transpose(2, 0, 1, 3)
        sums_spec = pl.BlockSpec((None, 2, rows, share), lambda k: (k, 0, 0, 0))
    out = pl.pallas_call(
        kernel,
        grid=(shares,),
        in_specs=[sums_spec, pl.BlockSpec((groups_of, 1, 2, extra), lambda k: (0, k, 0, 0))],
        out_specs=pl.BlockSpec((groups_of, 1, 8, wide), lambda k: (0, k, 0, 0)),
        out_shape=jax.ShapeDtypeStruct((groups_of, shares, 8, wide), F32),
    )(sums_in, rest.reshape(groups_of, shares, 2, extra))
    return out.reshape(groups_of * shares, 8, wide)


def joined(*groups):
    sizes = [len(group) for group in groups]

    def kernel(*refs):
        taken = 0
        for out_ref, size in zip(refs[sum(sizes) :], sizes):
            at = 0
            for ref in refs[taken : taken + size]:
                out_ref[at : at + ref.shape[0], :] = ref[...]
                at += ref.shape[0]
            taken += size

    outs = [
        jax.ShapeDtypeStruct((sum(x.shape[0] for x in group), group[0].shape[1]), group[0].dtype)
        for group in groups
    ]
    return pl.pallas_call(kernel, out_shape=tuple(outs), compiler_params=VMEM_LIMIT)(
        *[x for group in groups for x in group]
    )


def text_packed(context, blocked, turned, stacked, part, count):
    rows = blocked[0].shape[0] if blocked else turned[0].shape[1]
    widths = [x.shape[1] // count for x in blocked] + [x.shape[0] for x in turned]
    widths += [x.shape[0] * part for x in stacked]
    nblocked, nturned = len(blocked), len(turned)
    ninputs = nblocked + nturned + len(stacked)

    def kernel(context_ref, *refs):
        ins, outs = refs[:ninputs], refs[ninputs:]
        at = 0
        for i, ref in enumerate(ins):
            wide = widths[i]
            if i < nblocked:
                for k in range(count):
                    lane = pl.multiple_of((context_ref[0] + k) % count * wide, 128)
                    outs[k][:, at : at + wide] = ref[:, pl.ds(lane, wide)]
            elif i < nblocked + nturned:
                value = ref[...].astype(F32).T.astype(BF)
                for k in range(count):
                    outs[k][:, at : at + wide] = value
            else:
                for t in range(ref.shape[0]):
                    for k in range(count):
                        outs[k][:, at + t * part : at + (t + 1) * part] = ref[t, :, :part]
            at += wide

    return pl.pallas_call(
        kernel,
        in_specs=[pl.BlockSpec(memory_space=pltpu.SMEM)] + [pl.BlockSpec(memory_space=pltpu.VMEM)] * ninputs,
        out_shape=tuple([jax.ShapeDtypeStruct((rows, sum(widths)), BF)] * count),
        compiler_params=VMEM_LIMIT,
    )(context, *blocked, *turned, *stacked)


def tensor_packed(places, hidden_rows, wide_rows, part, depth, count):
    tensors = places.shape[0] - 1
    rows = hidden_rows.shape[0]
    own = rows // count

    def kernel(places_ref, hidden_ref, wide_ref, out_ref):
        context = places_ref[tensors]
        lane = pl.multiple_of(context * depth, 128)
        for j in range(count):
            source = pl.ds(pl.multiple_of((context + count - j) % count * own, own), own)
            here = slice(j * own, (j + 1) * own)
            columns = wide_ref[source, pl.ds(lane, depth)]
            for k in range(tensors):
                at = pl.multiple_of(places_ref[k] * part, 128)
                out_ref[k, here, :part] = hidden_ref[source, pl.ds(at, part)]
                out_ref[k, here, part:] = columns

    return pl.pallas_call(
        kernel,
        in_specs=[pl.BlockSpec(memory_space=pltpu.SMEM)] + [pl.BlockSpec(memory_space=pltpu.VMEM)] * 2,
        out_shape=jax.ShapeDtypeStruct((tensors, rows, part + depth), BF),
    )(places, hidden_rows, wide_rows)


def tail_packed(micro, mod, rest, groups_of, shares):
    rows, mods = mod.shape
    share, seqs = mods // shares, rows // 2
    extra = (mods + rest.shape[1]) // (groups_of * shares)
    wide = lanes(max(share, extra))

    def kernel(micro_ref, mod_ref, rest_ref, out_ref, bias_ref, piece_ref):
        for j in range(2):
            bias_ref[j : j + 1, :mods] = jnp.sum(mod_ref[j * seqs : (j + 1) * seqs, :], axis=0, keepdims=True)
        bias_ref[:, mods:] = rest_ref[...]
        piece_ref[...] = jnp.zeros_like(piece_ref)
        for group in range(groups_of):
            mine = jnp.where(micro_ref[0] == group, 1.0, 0.0)
            for k in range(shares):
                device = group * shares + k
                piece_ref[device, :rows, :share] = mod_ref[:, k * share : (k + 1) * share] * mine
                piece_ref[device, rows : rows + 2, :extra] = bias_ref[:, device * extra : (device + 1) * extra]
        out_ref[...] = piece_ref[...].astype(BF)

    return pl.pallas_call(
        kernel,
        in_specs=[pl.BlockSpec(memory_space=pltpu.SMEM)] + [pl.BlockSpec(memory_space=pltpu.VMEM)] * 2,
        out_shape=jax.ShapeDtypeStruct((groups_of * shares, 8, wide), BF),
        scratch_shapes=[
            pltpu.VMEM((2, mods + rest.shape[1]), F32),
            pltpu.VMEM((groups_of * shares, 8, wide), F32),
        ],
    )(micro.reshape(1), mod, rest)


def finish_hidden(context, image, got, at, cols, part, turned):
    count, tensors = len(got), cols.shape[0]
    rows, *steps = image
    depth = cols.shape[2] - part
    hidden = rows.shape[-1]
    shape = (2, hidden, depth) if turned else (2, depth, hidden)

    def kernel(context_ref, image_ref, cols_ref, *refs):
        out_ref = refs[-1]
        if steps:
            product = 0.0
            for k in range(count):
                product += dot_tn(refs[count + k][...], image_ref[(context_ref[0] + count - k) % count])
        else:
            product = image_ref[...].astype(F32)
        out_ref[0] = product.T if turned else product
        for k in range(count):
            block = pl.ds(pl.multiple_of((context_ref[0] + count - k) % count * part, 128), part)
            total = 0.0
            for t in range(tensors):
                lane = at + t * part
                pair = (refs[k][:, lane : lane + part], cols_ref[t, :, part:])
                total += dot_tn(*pair) if turned else dot_tn(*pair[::-1])
            if turned:
                out_ref[1, block, :] = total
            else:
                out_ref[1, :, block] = total

    return pl.pallas_call(
        kernel,
        in_specs=[pl.BlockSpec(memory_space=pltpu.SMEM)]
        + [pl.BlockSpec(memory_space=pltpu.VMEM)] * (2 + count + len(steps)),
        out_shape=jax.ShapeDtypeStruct(shape, F32),
        compiler_params=VMEM_LIMIT,
    )(context, rows, cols, *got, *steps)


def finish_rows(shard, left_got, left, right_got, right, turned):
    m, n = left[1] - left[0], right[1] - right[0]
    count = len(left_got)

    def kernel(shard_ref, *refs):
        out_ref = refs[-1]
        image = shard_ref[...].astype(F32)
        out_ref[0] = image.T if turned else image
        total = 0.0
        for k in range(count):
            total += dot_tn(refs[k][:, left[0] : left[1]], refs[count + k][:, right[0] : right[1]])
        out_ref[1] = total

    return pl.pallas_call(
        kernel, out_shape=jax.ShapeDtypeStruct((2, m, n), F32), compiler_params=VMEM_LIMIT
    )(shard, *left_got, *right_got)


def normalized(x):
    centred = x - jnp.mean(x, axis=-1, keepdims=True)
    inverse = lax.rsqrt(jnp.mean(centred * centred, axis=-1, keepdims=True) + NORM_EPS)
    return centred * inverse, inverse


def norm_back(n, inverse, w):
    return (w - jnp.mean(w, axis=-1, keepdims=True) - n * jnp.mean(w * n, axis=-1, keepdims=True)) * inverse


def row_call(kernel, row_mods, indices, arrays, outs):
    rows, width = row_mods.shape[0], row_mods.shape[1] // 6

    def whole(x):
        return pl.BlockSpec(x.shape, lambda i: (0,) * len(x.shape))

    return pl.pallas_call(
        kernel,
        grid=(1,),
        in_specs=[pl.BlockSpec((rows, width), lambda i, at=at: (0, at)) for at in indices]
        + [whole(x) for x in arrays],
        out_specs=tuple(whole(x) for x in outs),
        out_shape=tuple(outs),
        compiler_params=VMEM_LIMIT,
    )(*[row_mods] * len(indices), *arrays)


def enter_rows(row_mods, x, cut):
    rows, width = x.shape

    def kernel(shift_ref, scale_ref, x_ref, image_ref, text_ref):
        n = normalized(x_ref[...])[0]
        h = (n * (1.0 + scale_ref[...].astype(F32)) + shift_ref[...].astype(F32)).astype(BF)
        image_ref[...] = h[:cut]
        text_ref[...] = h[cut:]

    outs = [jax.ShapeDtypeStruct((cut, width), BF), jax.ShapeDtypeStruct((rows - cut, width), BF)]
    return row_call(kernel, row_mods, (0, 1), (x,), outs)


def middle_rows(row_mods, x, image_sum, text_sum, bias):
    rows, width = x.shape
    cut = image_sum.shape[0]

    def kernel(
        gate_ref, shift_ref, scale_ref, x_ref, image_ref, text_ref, bias_ref,
        branch_ref, middle_ref, himage_ref, htext_ref,
    ):
        branch_ref[:cut] = image_ref[...] + bias_ref[0:1, :]
        branch_ref[cut:] = text_ref[...] + bias_ref[1:2, :]
        middle = x_ref[...] + gate_ref[...].astype(F32) * branch_ref[...]
        middle_ref[...] = middle
        n = normalized(middle)[0]
        h = (n * (1.0 + scale_ref[...].astype(F32)) + shift_ref[...].astype(F32)).astype(BF)
        himage_ref[...] = h[:cut]
        htext_ref[...] = h[cut:]

    outs = [jax.ShapeDtypeStruct((rows, width), F32)] * 2
    outs += [jax.ShapeDtypeStruct((cut, width), BF), jax.ShapeDtypeStruct((rows - cut, width), BF)]
    return row_call(kernel, row_mods, (2, 3, 4), (x, image_sum, text_sum, bias), outs)


def halves_sum(rows, cut):
    return jnp.concatenate(
        (jnp.sum(rows[:cut], axis=0, keepdims=True), jnp.sum(rows[cut:], axis=0, keepdims=True)), 0
    )


def gated_rows(row_mods, g_out, cut):
    rows, width = g_out.shape

    def kernel(gate_ref, g_ref, image_ref, text_ref, sums_ref):
        g = (gate_ref[...].astype(F32) * g_ref[...]).astype(BF)
        image_ref[...] = g[:cut]
        text_ref[...] = g[cut:]
        sums_ref[...] = halves_sum(g.astype(F32), cut)

    outs = [jax.ShapeDtypeStruct((cut, width), BF), jax.ShapeDtypeStruct((rows - cut, width), BF)]
    outs += [jax.ShapeDtypeStruct((2, width), F32)]
    return row_call(kernel, row_mods, (5,), (g_out,), outs)


def middle_rows_back(row_mods, image_sum, text_sum, middle, g_out, branch, picks):
    rows, width = middle.shape
    cut = image_sum.shape[0]

    def kernel(
        gate_ref, scale_ref, image_ref, text_ref, middle_ref, g_ref, branch_ref, picks_ref,
        gmiddle_ref, gimage_ref, gtext_ref, sums_ref, mod_ref, gh_ref,
    ):
        gh_ref[:cut] = image_ref[...]
        gh_ref[cut:] = text_ref[...]
        gh = gh_ref[...]
        n, inverse = normalized(middle_ref[...])
        g_middle = g_ref[...] + norm_back(n, inverse, gh * (1.0 + scale_ref[...].astype(F32)))
        gmiddle_ref[...] = g_middle
        g_branch = (gate_ref[...].astype(F32) * g_middle).astype(BF)
        gimage_ref[...] = g_branch[:cut]
        gtext_ref[...] = g_branch[cut:]
        sums_ref[...] = halves_sum(g_branch.astype(F32), cut)
        for at, part in enumerate((g_middle * branch_ref[...], gh, gh * n)):
            mod_ref[:, at * width : (at + 1) * width] = dot_nn(picks_ref[...], part.astype(BF))

    outs = [jax.ShapeDtypeStruct((rows, width), F32), jax.ShapeDtypeStruct((cut, width), BF)]
    outs += [jax.ShapeDtypeStruct((rows - cut, width), BF), jax.ShapeDtypeStruct((2, width), F32)]
    outs += [jax.ShapeDtypeStruct((picks.shape[0], 3 * width), F32)]
    scratch = jax.ShapeDtypeStruct((rows, width), F32)
    return row_call(
        kernel, row_mods, (2, 4), (image_sum, text_sum, middle, g_out, branch, picks), outs + [scratch]
    )[:5]


def enter_rows_back(row_mods, image_sum, text_sum, x, g_middle, g_out, down, picks):
    rows, width = x.shape
    cut = image_sum.shape[0]

    def kernel(
        scale_ref, image_ref, text_ref, x_ref, gm_ref, g_ref, down_ref, picks_ref, gx_ref, mod_ref, gh_ref
    ):
        gh_ref[:cut] = image_ref[...]
        gh_ref[cut:] = text_ref[...]
        gh = gh_ref[...]
        n, inverse = normalized(x_ref[...])
        gx_ref[...] = gm_ref[...] + norm_back(n, inverse, gh * (1.0 + scale_ref[...].astype(F32)))
        for at, part in enumerate((gh, gh * n, g_ref[...] * down_ref[...])):
            mod_ref[:, at * width : (at + 1) * width] = dot_nn(picks_ref[...], part.astype(BF))

    outs = [jax.ShapeDtypeStruct((rows, width), F32), jax.ShapeDtypeStruct((picks.shape[0], 3 * width), F32)]
    scratch = jax.ShapeDtypeStruct((rows, width), F32)
    return row_call(
        kernel, row_mods, (1,), (image_sum, text_sum, x, g_middle, g_out, down, picks), outs + [scratch]
    )[:2]


def gelu_pair(u):
    c = 0.7978845608028654
    inner = jnp.tanh(c * (u + 0.044715 * u * u * u))
    value = 0.5 * u * (1.0 + inner)
    slope = 0.5 * (1.0 + inner) + 0.5 * u * (1.0 - inner * inner) * c * (1.0 + 3 * 0.044715 * u * u)
    return value.astype(BF), slope.astype(BF)


def shards(
    image_tokens,
    text_tokens,
    conditioning,
    image_seq_ids,
    text_seq_ids,
    ada_weight,
    qkv_weight,
    out_weight,
    up_weight,
    down_weight,
    biases,
    image_cotangent,
    text_cotangent,
):
    section = lax.axis_index("section")
    context = lax.axis_index("context")
    tensor = lax.axis_index("tensor")
    ncontext = lax.axis_size("context")
    ntensor = lax.axis_size("tensor")
    ndev = ncontext * ntensor
    first = section == 0
    micros, own_image, width = image_tokens.shape
    own_text = text_tokens.shape[1]
    seqs = conditioning.shape[1]
    rows_image, rows_text = micros * own_image, micros * own_text
    heads_here = HEADS // ntensor
    local = heads_here * HEAD
    hidden = up_weight.shape[3]
    bias_here = biases.shape[2]
    depth = qkv_weight.shape[2]
    mods = 6 * width
    table_rows = 2 * seqs
    per = ncontext // micros
    micro = context // per
    paired = per == 2 and heads_here % 2 == 0
    groups = 2 if paired else 1
    group_heads = heads_here // groups
    group = group_heads * HEAD
    side = context % per
    ctx_image, ctx_text = ntensor * rows_image, ntensor * rows_text
    ctx_rows = ctx_image + ctx_text

    order = (0, 2, 1, 3)

    def swapped(x, axis, bit):
        return lax.ppermute(x, axis, [(i, i ^ bit) for i in range(lax.axis_size(axis))])

    def sided(a, b):
        return jnp.where(side == 0, a, b), jnp.where(side == 0, b, a)

    def near(x):
        return swapped(x, "tensor", 1)

    def far(x):
        return swapped(x, "tensor", 2)

    def gather_tensor(x):
        beside = near(x)
        across = far(x)
        return x, across, beside, near(across)

    def reduce_tensor(x):
        n = x.shape[0] // 4
        got = near(x[2 * n :])
        mine = x[: 2 * n].astype(F32) + got.astype(F32)
        return mine[:n] + far(mine[n:].astype(BF)).astype(F32)

    def spread_both(image, text):
        return joined(gather_tensor(image), gather_tensor(text))

    def turned_by(x, by):
        return lax.ppermute(x, "context", [(i, (i + by) % ncontext) for i in range(ncontext)])

    def text_gather(rows):
        return [rows] + [turned_by(rows, k) for k in range(1, ncontext)]

    def text_scatter(partial_sums):
        sums = partial_sums.astype(BF).reshape(ncontext, rows_text, width)
        total = sums[0].astype(F32)
        for k in range(1, ncontext):
            total += turned_by(sums[k], -k).astype(F32)
        return total

    def spread_and_gather(image, text):
        return joined(gather_tensor(image)) + joined(text_gather(text))

    def by_tensor(x, axis):
        places = [jnp.array(order)[tensor ^ k] for k in range(ntensor)]
        return jnp.stack([lax.dynamic_index_in_dim(x, at, axis, keepdims=False) for at in places], axis)

    def in_group(x, axis):
        places = [tensor ^ bit for bit in order]
        return jnp.stack([lax.dynamic_index_in_dim(x, at, axis, keepdims=False) for at in places], axis)

    def gather_both(x):
        got = lax.all_gather(x, "tensor")
        got = lax.all_to_all(jnp.broadcast_to(got[None], (ncontext,) + got.shape), "context", 0, 0)
        return got.reshape((ndev,) + x.shape)

    def rounds(step, back):
        pairs = []
        for h in range(ncontext):
            m = (h + step) % micros
            pairs.append((h, m * per + h // micros))
        return [(b, a) for a, b in pairs] if back else pairs

    def to_work(image, text):
        pieces = []
        for step in range(micros):
            m = (context + step) % micros
            pieces.append(
                [
                    lax.ppermute(
                        lax.dynamic_index_in_dim(x, m, 0, keepdims=False), "context", rounds(step, False)
                    )
                    for x in (image, text)
                ]
            )
        return jnp.concatenate([p[0] for p in pieces] + [p[1] for p in pieces], 0).astype(F32)

    def to_home(rows):
        rows = rows.astype(BF)
        pieces = []
        for step in range(micros):
            at, below = step * own_image, rows_image + step * own_text
            both = jnp.concatenate((rows[at : at + own_image], rows[below : below + own_text]), 0)
            pieces.append(lax.ppermute(both, "context", rounds(step, True)))
        pieces = jnp.stack(pieces).astype(F32)
        image, text = pieces[:, :own_image], pieces[:, own_image:]
        turns = [(m - context) % micros for m in range(micros)]
        return tuple(
            jnp.stack([lax.dynamic_index_in_dim(x, turn, 0, keepdims=False) for turn in turns])[None]
            for x in (image, text)
        )

    def gathered(w):
        return lax.all_gather(w, "context", axis=0, tiled=True)

    qkv_full = [gathered(qkv_weight[0, 0])]
    out_full = [gathered(out_weight[0, 0].T)]
    up_full = [gathered(up_weight[0, 0])]
    down_full = [gathered(down_weight[0, 0].T)]

    def ring(w, send_after=None):
        pieces = [w if send_after is None else after(w, send_after)]
        for step in range(1, ncontext):
            pieces.append(lax.ppermute(pieces[-1], "context", [(i, (i + 1) % ncontext) for i in range(ncontext)]))
        return pieces

    def laid(pieces):
        full = jnp.zeros((width, pieces[0].shape[1]), BF)
        for step, piece in enumerate(pieces):
            full = lax.dynamic_update_slice_in_dim(full, piece, (context - step) % ncontext * depth, 0)
        return full

    ring_first = ring(jnp.concatenate((qkv_weight[0, 1], out_weight[0, 1].T), axis=1))
    stage = (ncontext + 2) // 3
    part = hidden // ncontext
    aligned = part % 128 == 0 and depth % 128 == 0 and local % 128 == 0 and ncontext == ntensor
    text_sent = jnp.concatenate(
        [w.reshape(ncontext, part, depth) for w in (up_weight[0, 1].T, down_weight[0, 1])], axis=1
    )
    text_moved = lax.all_to_all(after(text_sent, ring_first[-1]), "context", 0, 0)
    feed = []

    cond_float = conditioning.astype(F32)
    silu_cond = jax.nn.silu(cond_float).astype(BF).reshape(micros * seqs, -1)
    ada_part = jnp.einsum("rc,jck->jrk", silu_cond, ada_weight[0], preferred_element_type=F32)
    sharing = [[m * per + u for u in range(per)] for m in range(micros)]
    shares = per * ntensor
    share = mods // shares
    bias_placed = lax.dynamic_update_slice_in_dim(
        jnp.zeros((2, bias_here * ndev), F32),
        biases[0].astype(F32),
        (context * ntensor + tensor) * bias_here,
        1,
    )
    ada_sent = packed(
        ada_part + bias_placed[:, None, :mods],
        jnp.broadcast_to(biases[0].astype(F32)[None], (ndev, 2, bias_here)),
        micros,
        shares,
    )
    ada_got = lax.all_to_all(ada_sent.astype(BF), BOTH, 0, 0)
    bias_full = ada_got[:, table_rows : table_rows + 2, :bias_here].transpose(1, 0, 2).reshape(2, -1).astype(F32)
    ada_sum = jnp.sum(ada_got[:, :table_rows, :share].astype(F32), axis=0).astype(BF)
    table = lax.all_gather(ada_sum, "tensor")
    if paired:
        table = jnp.stack(sided(table, swapped(table, "context", 1)))
    else:
        table = lax.all_gather(table, "context", axis_index_groups=sharing)
    table = after(table, ring_first[stage - 1])
    table = table.reshape(shares, table_rows, share).transpose(1, 0, 2).reshape(table_rows, mods)
    query_bias = lax.dynamic_slice_in_dim(bias_full, mods + tensor * local, local, 1)
    value_bias = lax.dynamic_slice_in_dim(bias_full, mods + width + tensor * local, local, 1)
    qkv_bias = jnp.stack(
        (
            query_bias.reshape(2, heads_here, HEAD),
            jnp.zeros((2, heads_here, HEAD), F32),
            value_bias.reshape(2, heads_here, HEAD),
        ),
        axis=2,
    ).reshape(2, 3 * local)
    out_bias = bias_full[:, mods + 2 * width : mods + 3 * width]
    at_up = mods + 3 * width
    up_bias = lax.dynamic_slice_in_dim(bias_full[0], at_up + tensor * hidden, hidden, 0)
    up_bias_text = bias_full[1, at_up : at_up + ntensor * hidden].reshape(ntensor, ncontext, part)
    up_bias_text = in_group(lax.dynamic_index_in_dim(up_bias_text, context, 1, keepdims=False), 0).reshape(-1)
    down_bias = bias_full[:, mods + 3 * width + hidden * ntensor :]

    def by_modality(pair):
        return jnp.concatenate(
            (
                jnp.broadcast_to(pair[0][None], (rows_image, width)),
                jnp.broadcast_to(pair[1][None], (rows_text, width)),
            ),
            0,
        )

    def ids_of(work_context):
        m, u = work_context // per, work_context % per
        homes = jnp.stack([u * micros + (m - step) % micros for step in range(micros)])
        places = homes[None, :] * ntensor + (tensor ^ jnp.array(order))[:, None]
        found = []
        for ids, own in ((image_seq_ids, own_image), (text_seq_ids, own_text)):
            table_ids = lax.dynamic_index_in_dim(ids, m, 0, keepdims=False).reshape(ndev, own)
            found.append(jnp.take(table_ids, places.reshape(-1), axis=0).reshape(-1))
        return found

    own_found = ids_of(context)
    own_ids = jnp.concatenate((own_found[0][:rows_image], own_found[1][:rows_text] + seqs))
    onehot = (own_ids[:, None] == jnp.arange(table_rows)[None, :]).astype(BF)
    row_mods = dot_nn(onehot, table).astype(BF)
    picks = onehot.T
    joint_ids = jnp.concatenate(own_found)
    if paired:
        attn_ids = jnp.concatenate([joint_ids] + ids_of(context ^ 1))
    else:
        attn_ids = jnp.concatenate([x for u in range(per) for x in ids_of(micro * per + u)])

    def row_mod(index):
        return row_mods[:, index * width : (index + 1) * width].astype(F32)

    def attention(joint):
        if paired:
            mine, theirs = sided(joint[: 3 * group], joint[3 * group :])
            theirs = swapped(theirs, "context", 1)
            here, there, lse = attend_pair(mine, theirs, attn_ids, group_heads)
            return jnp.concatenate(sided(here, swapped(there, "context", 1)), axis=0), (mine, theirs, lse)
        by_kind = joint.reshape(heads_here, 3, HEAD, ctx_rows)
        q, k, v = (by_kind[:, i].reshape(local, ctx_rows).T for i in range(3))
        k, v = (
            lax.all_gather(x, "context", axis=0, tiled=True, axis_index_groups=sharing) for x in (k, v)
        )
        attended, lse = attend(q, k, v, joint_ids, attn_ids, group_heads)
        return attended.T, (q, k, v, lse)

    def attention_back(grad, kept):
        if paired:
            mine, theirs, lse = kept
            g_mine, g_theirs = sided(grad[:group], grad[group:])
            g_theirs = swapped(g_theirs, "context", 1)
            d_mine, d_theirs = attend_pair_back(mine, theirs, g_mine, g_theirs, lse, attn_ids, group_heads)
            return jnp.concatenate(sided(d_mine, swapped(d_theirs, "context", 1)), axis=0)
        q, k, v, lse = kept
        dq, dk, dv = attend_back(q, k, v, grad.T, lse, joint_ids, attn_ids, group_heads)
        dk, dv = (
            lax.psum_scatter(x, "context", scatter_dimension=0, tiled=True, axis_index_groups=sharing)
            for x in (dk, dv)
        )
        kinds = [x.T.reshape(heads_here, HEAD, ctx_rows) for x in (dq, dk, dv)]
        return jnp.stack(kinds, axis=1).reshape(3 * local, ctx_rows)

    own_context = context.reshape(1).astype(jnp.int32)

    def context_round(blocked, turned, stacked):
        if aligned:
            sent = text_packed(own_context, blocked, turned, stacked, part, ncontext)
            return [turned_by(x, k) if k else x for k, x in enumerate(sent)]
        parts = [x.reshape(x.shape[0], ncontext, -1).transpose(1, 0, 2) for x in blocked]
        parts += [jnp.broadcast_to(x.T[None], (ncontext,) + x.T.shape) for x in turned]
        stacks = [x[:, :, :part].transpose(1, 0, 2).reshape(x.shape[1], -1) for x in stacked]
        stacks = [jnp.broadcast_to(x[None], (ncontext,) + x.shape) for x in stacks]
        return [
            lax.all_to_all(jnp.concatenate(group, axis=2), "context", 0, 0) for group in (parts, stacks) if group
        ]

    def forward(x, late=False):
        h1_image, h1_text = enter_rows(row_mods, x, rows_image)
        fresh = len(qkv_full) == 1
        if fresh:
            h1_image = after(h1_image, ring_first[2 * stage - 2])
            full = laid(ring_first)
            qkv_full.append(full[:, : 3 * local])
            out_full.append(full[:, 3 * local :])
        h1 = spread_both(h1_image, h1_text)
        joint = jnp.concatenate(
            [(dot_tt(qkv_full[j], h1[j]) + qkv_bias[j][:, None]).astype(BF) for j in range(2)], axis=1
        )
        attended, kept = attention(joint)
        if fresh:
            attended = after(attended, text_moved)
            moved = gather_tensor(text_moved.transpose(1, 0, 2).reshape(2 * part, width))
            feed.append(jnp.concatenate([b[:part] for b in moved], 0))
            feed.append(jnp.concatenate([b[part:] for b in moved], 0))
        image_sum = reduce_tensor(dot_tt(attended, out_full[0])[:ctx_image].astype(BF))
        text_sum = reduce_tensor(dot_tt(attended[:, ctx_image:], out_full[1]).astype(BF))
        if fresh:
            image_sum = after(image_sum, *feed)
        branch, middle, h2_image, h2_text = middle_rows(row_mods, x, image_sum, text_sum, out_bias)
        up_text, down_text = feed
        h2 = spread_and_gather(h2_image, h2_text)
        pairs = [
            gelu_pair(dot_nn(h2[0], up_full[0]) + up_bias),
            gelu_pair(dot_nt(h2[1], up_text) + up_bias_text),
        ]
        acts, slopes = [p[0] for p in pairs], [p[1] for p in pairs]
        saved = dict(
            x=x, h1=h1, kept=kept, attn=attended, branch=branch, middle=middle, h2=h2, acts=acts,
            slopes=slopes, raw=acts[0],
        )

        def finish(gate):
            if gate is not None:
                saved["acts"] = [after(act, gate) for act in acts]
            down = jnp.concatenate(
                (
                    reduce_tensor(dot_nt(saved["acts"][0], down_full[0]).astype(BF)),
                    text_scatter(dot_nn(saved["acts"][1], down_text)),
                ),
                0,
            ) + by_modality(down_bias)
            saved["down"] = down
            saved["out"] = middle + row_mod(5) * down

        saved["finish"] = finish
        if not late:
            finish(None)
        return saved

    def chosen(a, b):
        return jax.tree.map(lambda x, y: jnp.where(first, x, y), a, b)

    def scattered(full):
        return lax.psum_scatter(full.astype(BF), "context", scatter_dimension=0, tiled=True)

    def backward(saved, g_out, last=None):
        gd_image, gd_text, gd_sums = gated_rows(row_mods, g_out, rows_image)
        up_text, down_text = feed
        gd = spread_and_gather(gd_image, gd_text)
        g_up = [
            (dot_nn(gd[0], down_full[0]) * saved["slopes"][0].astype(F32)).astype(BF),
            (dot_nt(gd[1], down_text) * saved["slopes"][1].astype(F32)).astype(BF),
        ]
        g_h2_image = reduce_tensor(dot_nt(g_up[0], up_full[0]).astype(BF))
        g_h2_text = text_scatter(dot_nn(g_up[1], up_text))
        early = {}
        if last:
            use = chosen(
                dict(h2=saved["h2"][0], acts=saved["raw"], gd=gd[0], g_up=g_up[0]),
                dict(h2=last["h2"][0], acts=last["raw"], gd=last["gd"][0], g_up=last["g_up"][0]),
            )
            early["up"] = dot_tn(use["h2"], use["g_up"]).astype(BF)
            if aligned:
                early["columns"] = context_round([use["gd"]], [], [])
                g_h2_image = after(g_h2_image, early["up"])
            else:
                early["down"] = dot_tn(use["gd"], use["acts"]).astype(BF)
                g_h2_image = after(g_h2_image, early["up"], early["down"])
                early["down"] = scattered(early["down"])
            early["up"] = scattered(early["up"])
        g_middle, gb_image, gb_text, gb_sums, mod_late = middle_rows_back(
            row_mods, g_h2_image, g_h2_text, saved["middle"], g_out, saved["branch"], picks
        )
        gb = spread_both(gb_image, gb_text)
        if "down" not in saved:
            saved["finish"](gb[0])
        g_attn = jnp.concatenate([dot_tt(out_full[j], gb[j]).astype(BF) for j in range(2)], axis=1)
        if last:
            use = chosen(dict(gb=gb[0], attn=saved["attn"]), dict(gb=last["gb"][0], attn=last["attn"]))
            early["out"] = dot_tt(use["gb"], use["attn"][:, :ctx_image]).astype(BF)
            g_attn = after(g_attn, early["out"], *early.get("columns", ()))
        g_joint = attention_back(g_attn, saved["kept"])
        g_h1_image = reduce_tensor(dot_tt(g_joint, qkv_full[0])[:ctx_image].astype(BF))
        g_h1_text = reduce_tensor(dot_tt(g_joint[:, ctx_image:], qkv_full[1]).astype(BF))
        if last:
            use = chosen(dict(h1=saved["h1"][0], g=g_joint), dict(h1=last["h1"][0], g=last["g_joint"]))
            early["qkv"] = dot_tt(use["h1"], use["g"][:, :ctx_image]).astype(BF)
            g_h1_image = after(g_h1_image, early["qkv"])
        g_x, mod_early = enter_rows_back(
            row_mods, g_h1_image, g_h1_text, saved["x"], g_middle, g_out, saved["down"], picks
        )
        if last:
            g_x = after(g_x, *[early[name] for name in ("down", "up") if name in early])
        mod_grad = jnp.concatenate((mod_early[:, : 2 * width], mod_late, mod_early[:, 2 * width :]), axis=1)
        tensors = dict(
            raw=saved["raw"], h1=saved["h1"], attn=saved["attn"], h2=saved["h2"], acts=saved["acts"], g_joint=g_joint,
            gb=gb, g_up=g_up, gd=gd, gd_sums=gd_sums, gb_sums=gb_sums, mod=mod_grad,
        )
        return g_x, tensors, early

    offsets = tensor ^ jnp.arange(ntensor, dtype=jnp.int32)
    places = jnp.concatenate(((offsets & 1) * 2 + offsets // 2, context.reshape(1).astype(jnp.int32)))

    def tensor_round(hidden_rows, wide_rows):
        if aligned:
            sent = tensor_packed(places, hidden_rows, wide_rows, part, depth, ncontext)
        else:
            back = (context - jnp.arange(ncontext)) % ncontext
            hidden_rows, wide_rows = (
                jnp.take(x.reshape(ncontext, rows_text, -1), back, axis=0).reshape(x.shape)
                for x in (hidden_rows, wide_rows)
            )
            pieces = by_tensor(hidden_rows.reshape(hidden_rows.shape[0], ntensor, part), 1).transpose(1, 0, 2)
            own = lax.dynamic_slice_in_dim(wide_rows, context * depth, depth, 1)
            sent = jnp.concatenate((pieces, jnp.broadcast_to(own[None], (ntensor,) + own.shape)), axis=2)
        return lax.all_to_all(sent, "tensor", 0, 0)

    def handed(rows, by):
        return lax.ppermute(rows.astype(BF), "section", [(0, 1)] if by > 0 else [(1, 0)]).astype(F32)

    saved_first = forward(to_work(image_tokens, text_tokens))
    saved_last = forward(handed(saved_first["out"], 1), late=True)
    grad_last, tensors_last, unused = backward(saved_last, to_work(image_cotangent, text_cotangent))
    kept = chosen(
        [saved_first[n][1] for n in ("acts", "h1", "h2")] + [saved_first["attn"][:, ctx_image:]],
        [saved_last[n][1] for n in ("acts", "h1", "h2")] + [saved_last["attn"][:, ctx_image:]],
    )
    kept[0] = after(kept[0], tensors_last["g_joint"])
    ours_before = tensor_round(kept[0], kept[2])
    got_before = context_round([kept[1]], [kept[3]], [ours_before])
    out = to_home(after(jnp.where(first, saved_first["out"], saved_last["out"]), tensors_last["g_joint"]))
    acts_all = ()
    if aligned:
        acts_all = gathered(jnp.where(first, saved_first["raw"], saved_last["raw"]))
        acts_all = (acts_all.reshape(ncontext, ctx_image, hidden),)
    returned = after(handed(grad_last, -1), *got_before, *out, *acts_all)
    grad_first, tensors_first, early = backward(saved_first, returned, tensors_last)
    grad = to_home(jnp.where(first, grad_first, grad_last))
    use = chosen(tensors_first, tensors_last)

    up_shard, out_part, qkv_part = early["up"], early["out"], early["qkv"]
    out_shard = after(scattered(out_part), grad_first)
    qkv_shard = after(scattered(qkv_part), grad_first)

    ours_after = tensor_round(use["g_up"][1], use["gd"][1])
    got_after = context_round([after(use["gb"][1], tensors_first["g_joint"])], [], [ours_after])

    def column_sums(parts):
        return jnp.stack([dot_nn(jnp.ones((8, p.shape[0]), BF), p)[0] for p in parts])

    qkv_sums = jnp.stack(
        [
            dot_nt(jnp.ones((8, part.shape[1]), BF), part)[0]
            for part in (use["g_joint"][:, :ctx_image], use["g_joint"][:, ctx_image:])
        ]
    ).reshape(2, heads_here, 3, HEAD)
    up_sums_text = lax.dynamic_update_slice_in_dim(
        jnp.zeros((ntensor, ncontext, part), F32),
        by_tensor(column_sums((use["g_up"][1],)).reshape(ntensor, 1, part), 0),
        context,
        1,
    ).reshape(1, -1)
    up_sums_image = lax.dynamic_update_slice_in_dim(
        jnp.zeros((1, ntensor * hidden), F32), column_sums((use["g_up"][0],)), tensor * hidden, 1
    )
    rest = jnp.zeros((2, bias_here * ndev - mods), F32)
    for at, value in (
        (tensor * local, qkv_sums[:, :, 0].reshape(2, local)),
        (width + tensor * local, qkv_sums[:, :, 2].reshape(2, local)),
        (2 * width, use["gb_sums"]),
        (3 * width, jnp.concatenate((up_sums_image, up_sums_text), 0)),
        (3 * width + ntensor * hidden, use["gd_sums"]),
    ):
        rest = lax.dynamic_update_slice_in_dim(rest, value, at, 1)
    if aligned:
        sent = tail_packed(micro.astype(jnp.int32), use["mod"], rest, micros, shares)
    else:
        bias_part = jnp.concatenate((jnp.sum(use["mod"].reshape(2, seqs, mods), axis=1), rest), axis=1)
        mod_sent = use["mod"].reshape(2, 1, seqs, mods)
        mod_sent = jnp.where(jnp.arange(micros)[None, :, None, None] == micro, mod_sent, 0.0)
        bias_sent = bias_part.reshape(2, ndev, bias_here).transpose(1, 0, 2)
        sent = packed(mod_sent.reshape(2, micros * seqs, mods), bias_sent, micros, shares).astype(BF)
    got = jnp.sum(lax.all_to_all(sent, BOTH, 0, 0).astype(F32), axis=0)
    bias_grad = got[table_rows:, :bias_here]
    mod_all = (
        gather_both(got[:table_rows, :share].astype(BF))
        .reshape(micros, shares, 2, seqs, share)
        .transpose(2, 0, 3, 1, 4)
        .reshape(2, micros * seqs, mods)
    )
    ada_grad = jnp.einsum("rc,jrk->jck", silu_cond, mod_all, preferred_element_type=F32)
    cond_inner = jnp.einsum("jrk,jck->rc", mod_all, ada_weight[0], preferred_element_type=F32)
    got_qkv = context_round([], [use["g_joint"][:, ctx_image:]], [])
    if aligned:
        down_grad = finish_hidden(own_context, acts_all + tuple(early["columns"]), got_before, depth + local, ours_after, part, True)
        up_grad = finish_hidden(own_context, (up_shard,), got_after, depth, ours_before, part, False)
        out_grad = finish_rows(out_shard, got_before, (depth, depth + local), got_after, (0, depth), True)
        qkv_grad = finish_rows(qkv_shard, got_before, (0, depth), got_qkv, (0, 3 * local), False)
    else:
        acts_all = got_before[1].reshape(ncontext, -1, ntensor, part)
        g_up_all = got_after[1].reshape(ncontext, -1, ntensor, part)
        text_down = jnp.einsum("crtj,trd->cjd", acts_all, ours_after[:, :, part:], preferred_element_type=F32)
        text_up = jnp.einsum("trk,crtj->kcj", ours_before[:, :, part:], g_up_all, preferred_element_type=F32)
        text_out = jnp.einsum(
            "crh,crd->hd", got_before[0][:, :, depth:], got_after[0], preferred_element_type=F32
        )
        text_qkv = jnp.einsum("crk,crh->kh", got_before[0][:, :, :depth], got_qkv[0], preferred_element_type=F32)
        down_grad = jnp.stack((early["down"].astype(F32).T, text_down.reshape(hidden, depth)))
        up_grad = jnp.stack((up_shard.astype(F32), text_up.reshape(depth, hidden)))
        out_grad = jnp.stack((out_shard.astype(F32).T, text_out))
        qkv_grad = jnp.stack((qkv_shard.astype(F32), text_qkv))
    unused, silu_back = jax.vjp(jax.nn.silu, cond_float)
    cond_inner = cond_inner + lax.ppermute(cond_inner, "section", [(0, 1), (1, 0)])
    cond_grad = silu_back(cond_inner.reshape(cond_float.shape))[0]
    return (
        *out,
        *grad,
        cond_grad,
        ada_grad[None],
        qkv_grad[None],
        out_grad[None],
        up_grad[None],
        down_grad[None],
        bias_grad[None],
    )


def solution(mesh):
    tokens = P(None, BOTH, None)
    block_rows = P("section", None, BOTH, None)
    by_rows = P("section", None, "context", "tensor")
    by_cols = P("section", None, "tensor", "context")
    block_biases = P("section", None, BOTH)
    in_specs = (
        tokens,
        tokens,
        P(None, None, BOTH),
        P(),
        P(),
        block_rows,
        by_rows,
        by_cols,
        by_rows,
        by_cols,
        block_biases,
        tokens,
        tokens,
    )
    out_specs = (
        block_rows,
        block_rows,
        block_rows,
        block_rows,
        P(None, None, BOTH),
        block_rows,
        by_rows,
        by_cols,
        by_rows,
        by_cols,
        block_biases,
    )
    return jax.shard_map(shards, mesh=mesh, in_specs=in_specs, out_specs=out_specs, check_vma=False)
```

```python
from functools import partial

import jax
import jax.numpy as jnp
from jax import lax
from jax.experimental import pallas as pl
from jax.experimental.pallas import tpu as pltpu
from jax.sharding import PartitionSpec as P

HEADS = 24
HEAD = 64
NORM_EPS = 1e-06
MASKED = -1e30
BF = jnp.bfloat16
F32 = jnp.float32
BOTH = ("context", "tensor")


def dot_nn(a, b):
    return lax.dot_general(a, b, (((1,), (0,)), ((), ())), preferred_element_type=F32)


def dot_nt(a, b):
    return lax.dot_general(a, b, (((1,), (1,)), ((), ())), preferred_element_type=F32)


def dot_tn(a, b):
    return lax.dot_general(a, b, (((0,), (0,)), ((), ())), preferred_element_type=F32)


def dot_tt(a, b):
    return lax.dot_general(a, b, (((0,), (1,)), ((), ())), preferred_element_type=F32)


def scaled(q):
    return q * jnp.asarray(HEAD**-0.5, BF)


def attend_body(heads, chunk, places, q_ref, k_ref, v_ref, idq_ref, idk_ref, store, lse_ref):
    at_q, at_k, at_v = places

    def one_chunk(step, carry):
        rows = pl.ds(pl.multiple_of(step * chunk, chunk), chunk)
        bias = jnp.where(idk_ref[...] == idq_ref[:, rows], 0.0, MASKED)
        outs = []
        for head in range(heads):
            at = head * HEAD
            q = scaled(q_ref[rows, at_q + at : at_q + at + HEAD])
            scores = dot_nt(k_ref[:, at_k + at : at_k + at + HEAD], q) + bias
            top = jnp.max(scores, axis=0, keepdims=True)
            weights = jnp.exp(scores - top)
            total = jnp.sum(weights, axis=0, keepdims=True)
            summed = dot_tn(v_ref[:, at_v + at : at_v + at + HEAD], weights.astype(BF))
            outs.append((summed / total).T)
            lse_ref[head : head + 1, rows] = top + jnp.log(total)
        store(rows, jnp.concatenate(outs, axis=1).astype(BF))
        return carry

    lax.fori_loop(0, idq_ref.shape[1] // chunk, one_chunk, 0)


def attend_back_body(
    heads, chunk, places, q_ref, k_ref, v_ref, g_ref, lse_ref, idq_ref, idk_ref, store_dq, dk_acc, dv_acc
):
    at_q, at_k, at_v = places
    dk_acc[...] = jnp.zeros_like(dk_acc)
    dv_acc[...] = jnp.zeros_like(dv_acc)

    def one_chunk(step, carry):
        rows = pl.ds(pl.multiple_of(step * chunk, chunk), chunk)
        bias = jnp.where(idk_ref[...] == idq_ref[:, rows], 0.0, MASKED)
        grads = []
        for head in range(heads):
            at = head * HEAD
            q = scaled(q_ref[rows, at_q + at : at_q + at + HEAD])
            g = g_ref[rows, at : at + HEAD]
            k = k_ref[:, at_k + at : at_k + at + HEAD]
            probs = jnp.exp(dot_nt(k, q) + bias - lse_ref[head : head + 1, rows])
            dv_acc[head] += dot_nn(probs.astype(BF), g)
            both = probs * dot_nt(v_ref[:, at_v + at : at_v + at + HEAD], g)
            delta = jnp.sum(both, axis=0, keepdims=True)
            dscores = (both - probs * delta).astype(BF)
            dk_acc[head] += dot_nn(dscores, q)
            grads.append((dot_tn(k, dscores) * HEAD**-0.5).T)
        store_dq(rows, jnp.concatenate(grads, axis=1).astype(BF))
        return carry

    lax.fori_loop(0, idq_ref.shape[1] // chunk, one_chunk, 0)


def heads_of(acc):
    return jnp.concatenate([acc[head] for head in range(acc.shape[0])], axis=1).astype(BF)


def attend_costs(queries, keys, heads, factor):
    return pl.CostEstimate(
        flops=factor * queries * keys * heads * HEAD,
        bytes_accessed=2 * (queries + 2 * keys) * heads * HEAD * factor // 4,
        transcendentals=queries * keys * heads,
    )


def chunk_for(keys):
    return 256 if keys <= 1024 else 128


VMEM_LIMIT = pltpu.CompilerParams(vmem_limit_bytes=56 * 2**20)


def attend(q, k, v, ids_q, ids_k, heads):
    queries, keys = q.shape[0], k.shape[0]

    def kernel(q_ref, k_ref, v_ref, idq_ref, idk_ref, out_ref, lse_ref):
        def store(rows, value):
            out_ref[rows, :] = value

        attend_body(
            heads, chunk_for(keys), (0, 0, 0), q_ref, k_ref, v_ref, idq_ref, idk_ref, store, lse_ref
        )

    return pl.pallas_call(
        kernel,
        out_shape=(
            jax.ShapeDtypeStruct((queries, heads * HEAD), BF),
            jax.ShapeDtypeStruct((heads, queries), F32),
        ),
        compiler_params=VMEM_LIMIT,
        cost_estimate=attend_costs(queries, keys, heads, 4),
    )(q, k, v, ids_q.reshape(1, queries), ids_k.reshape(keys, 1))


def attend_back(q, k, v, g, lse, ids_q, ids_k, heads):
    queries, keys = q.shape[0], k.shape[0]

    def kernel(
        q_ref, k_ref, v_ref, g_ref, lse_ref, idq_ref, idk_ref, dq_ref, dk_ref, dv_ref, dk_acc, dv_acc
    ):
        def store(rows, value):
            dq_ref[rows, :] = value

        attend_back_body(
            heads, chunk_for(keys), (0, 0, 0), q_ref, k_ref, v_ref, g_ref, lse_ref, idq_ref, idk_ref,
            store, dk_acc, dv_acc,
        )
        dk_ref[...] = heads_of(dk_acc)
        dv_ref[...] = heads_of(dv_acc)

    return pl.pallas_call(
        kernel,
        out_shape=(
            jax.ShapeDtypeStruct((queries, heads * HEAD), BF),
            jax.ShapeDtypeStruct((keys, heads * HEAD), BF),
            jax.ShapeDtypeStruct((keys, heads * HEAD), BF),
        ),
        scratch_shapes=[pltpu.VMEM((heads, keys, HEAD), F32), pltpu.VMEM((heads, keys, HEAD), F32)],
        compiler_params=VMEM_LIMIT,
        cost_estimate=attend_costs(queries, keys, heads, 10),
    )(q, k, v, g, lse, ids_q.reshape(1, queries), ids_k.reshape(keys, 1))


def attend_pair(mine, theirs, ids, heads):
    wide, half = mine.shape
    rows_all, group = 2 * half, heads * HEAD
    chunk = 256

    def kernel(mine_ref, theirs_ref, idq_ref, idk_ref, here_ref, there_ref, lse_ref, x_ref, out_ref):
        x_ref[:, :half] = mine_ref[...]
        x_ref[:, half:] = theirs_ref[...]

        def one_chunk(step, carry):
            rows = pl.ds(pl.multiple_of(step * chunk, chunk), chunk)
            bias = jnp.where(idk_ref[...] == idq_ref[:, rows], 0.0, MASKED)
            for head in range(heads):
                at = slice(head * HEAD, (head + 1) * HEAD)
                base = 3 * head * HEAD
                q = scaled(x_ref[base : base + HEAD, rows])
                k = x_ref[base + HEAD : base + 2 * HEAD, :]
                v = x_ref[base + 2 * HEAD : base + 3 * HEAD, :]
                scores = dot_tn(k, q) + bias
                top = jnp.max(scores, axis=0, keepdims=True)
                weights = jnp.exp(scores - top)
                total = jnp.sum(weights, axis=0, keepdims=True)
                out_ref[at, rows] = (dot_nn(v, weights.astype(BF)) / total).astype(BF)
                lse_ref[head : head + 1, rows] = top + jnp.log(total)
            return carry

        lax.fori_loop(0, rows_all // chunk, one_chunk, 0)
        here_ref[...] = out_ref[:, :half]
        there_ref[...] = out_ref[:, half:]

    return pl.pallas_call(
        kernel,
        out_shape=(
            jax.ShapeDtypeStruct((group, half), BF),
            jax.ShapeDtypeStruct((group, half), BF),
            jax.ShapeDtypeStruct((heads, rows_all), F32),
        ),
        scratch_shapes=[pltpu.VMEM((wide, rows_all), BF), pltpu.VMEM((group, rows_all), BF)],
        compiler_params=VMEM_LIMIT,
        cost_estimate=attend_costs(rows_all, rows_all, heads, 4),
    )(mine, theirs, ids.reshape(1, rows_all), ids.reshape(rows_all, 1))


def attend_pair_back(mine, theirs, g_mine, g_theirs, lse, ids, heads):
    wide, half = mine.shape
    rows_all, group = 2 * half, heads * HEAD
    chunk = 256

    def kernel(
        mine_ref, theirs_ref, gm_ref, gt_ref, lse_ref, idq_ref, idk_ref, dmine_ref, dtheirs_ref,
        x_ref, g_ref, dq_ref, dk_ref, dv_ref,
    ):
        x_ref[:, :half] = mine_ref[...]
        x_ref[:, half:] = theirs_ref[...]
        g_ref[:, :half] = gm_ref[...]
        g_ref[:, half:] = gt_ref[...]
        dk_ref[...] = jnp.zeros_like(dk_ref)
        dv_ref[...] = jnp.zeros_like(dv_ref)

        def one_chunk(step, carry):
            rows = pl.ds(pl.multiple_of(step * chunk, chunk), chunk)
            bias = jnp.where(idk_ref[...] == idq_ref[:, rows], 0.0, MASKED)
            for head in range(heads):
                at = slice(head * HEAD, (head + 1) * HEAD)
                base = 3 * head * HEAD
                q = scaled(x_ref[base : base + HEAD, rows])
                g = g_ref[at, rows]
                k = x_ref[base + HEAD : base + 2 * HEAD, :]
                v = x_ref[base + 2 * HEAD : base + 3 * HEAD, :]
                probs = jnp.exp(dot_tn(k, q) + bias - lse_ref[head : head + 1, rows])
                dv_ref[at, :] += dot_nt(g, probs.astype(BF))
                both = probs * dot_tn(v, g)
                delta = jnp.sum(both, axis=0, keepdims=True)
                dscores = (both - probs * delta).astype(BF)
                dk_ref[at, :] += dot_nt(q, dscores)
                dq_ref[at, rows] = (dot_nn(k, dscores) * HEAD**-0.5).astype(BF)
            return carry

        lax.fori_loop(0, rows_all // chunk, one_chunk, 0)
        for out_ref, cols in ((dmine_ref, slice(0, half)), (dtheirs_ref, slice(half, rows_all))):
            for head in range(heads):
                at = slice(head * HEAD, (head + 1) * HEAD)
                base = 3 * head * HEAD
                out_ref[base : base + HEAD, :] = dq_ref[at, cols]
                out_ref[base + HEAD : base + 2 * HEAD, :] = dk_ref[at, cols].astype(BF)
                out_ref[base + 2 * HEAD : base + 3 * HEAD, :] = dv_ref[at, cols].astype(BF)

    return pl.pallas_call(
        kernel,
        out_shape=(jax.ShapeDtypeStruct((wide, half), BF), jax.ShapeDtypeStruct((wide, half), BF)),
        scratch_shapes=[
            pltpu.VMEM((wide, rows_all), BF),
            pltpu.VMEM((group, rows_all), BF),
            pltpu.VMEM((group, rows_all), BF),
            pltpu.VMEM((group, rows_all), F32),
            pltpu.VMEM((group, rows_all), F32),
        ],
        compiler_params=VMEM_LIMIT,
        cost_estimate=attend_costs(rows_all, rows_all, heads, 10),
    )(mine, theirs, g_mine, g_theirs, lse, ids.reshape(1, rows_all), ids.reshape(rows_all, 1))


def after(x, *others):
    anywhere = pl.BlockSpec(memory_space=pl.ANY)

    def kernel(*refs):
        pass

    return pl.pallas_call(
        kernel,
        out_shape=jax.ShapeDtypeStruct(x.shape, x.dtype),
        in_specs=[anywhere] * (1 + len(others)),
        out_specs=anywhere,
        input_output_aliases={0: 0},
    )(x, *others)


def lanes(n):
    return -(-n // 128) * 128


def packed(sums, rest, groups_of, shares):
    rows, columns = sums.shape[1], sums.shape[2]
    seqs, share, extra = rows // groups_of, columns // shares, rest.shape[2]
    wide = lanes(max(share, extra))

    def kernel(sums_ref, rest_ref, out_ref):
        for group in range(groups_of):
            for j in range(2):
                out_ref[group, 0, j * seqs : (j + 1) * seqs, :share] = sums_ref[
                    j, group * seqs : (group + 1) * seqs, :
                ]
            out_ref[group, 0, 2 * seqs : 2 * seqs + 2, :extra] = rest_ref[group, 0]

    if share % 128 == 0:
        sums_in, sums_spec = sums, pl.BlockSpec((2, rows, share), lambda k: (0, 0, k))
    else:
        sums_in = sums.reshape(2, rows, shares, share).transpose(2, 0, 1, 3)
        sums_spec = pl.BlockSpec((None, 2, rows, share), lambda k: (k, 0, 0, 0))
    out = pl.pallas_call(
        kernel,
        grid=(shares,),
        in_specs=[sums_spec, pl.BlockSpec((groups_of, 1, 2, extra), lambda k: (0, k, 0, 0))],
        out_specs=pl.BlockSpec((groups_of, 1, 8, wide), lambda k: (0, k, 0, 0)),
        out_shape=jax.ShapeDtypeStruct((groups_of, shares, 8, wide), F32),
    )(sums_in, rest.reshape(groups_of, shares, 2, extra))
    return out.reshape(groups_of * shares, 8, wide)


def joined(*groups):
    sizes = [len(group) for group in groups]

    def kernel(*refs):
        taken = 0
        for out_ref, size in zip(refs[sum(sizes) :], sizes):
            at = 0
            for ref in refs[taken : taken + size]:
                out_ref[at : at + ref.shape[0], :] = ref[...]
                at += ref.shape[0]
            taken += size

    outs = [
        jax.ShapeDtypeStruct((sum(x.shape[0] for x in group), group[0].shape[1]), group[0].dtype)
        for group in groups
    ]
    return pl.pallas_call(kernel, out_shape=tuple(outs), compiler_params=VMEM_LIMIT)(
        *[x for group in groups for x in group]
    )


def text_packed(context, blocked, turned, stacked, part, count):
    rows = blocked[0].shape[0] if blocked else turned[0].shape[1]
    widths = [x.shape[1] // count for x in blocked] + [x.shape[0] for x in turned]
    widths += [x.shape[0] * part for x in stacked]
    nblocked, nturned = len(blocked), len(turned)
    ninputs = nblocked + nturned + len(stacked)

    def kernel(context_ref, *refs):
        ins, outs = refs[:ninputs], refs[ninputs:]
        at = 0
        for i, ref in enumerate(ins):
            wide = widths[i]
            if i < nblocked:
                for k in range(count):
                    lane = pl.multiple_of((context_ref[0] + k) % count * wide, 128)
                    outs[k][:, at : at + wide] = ref[:, pl.ds(lane, wide)]
            elif i < nblocked + nturned:
                value = ref[...].astype(F32).T.astype(BF)
                for k in range(count):
                    outs[k][:, at : at + wide] = value
            else:
                for t in range(ref.shape[0]):
                    for k in range(count):
                        outs[k][:, at + t * part : at + (t + 1) * part] = ref[t, :, :part]
            at += wide

    return pl.pallas_call(
        kernel,
        in_specs=[pl.BlockSpec(memory_space=pltpu.SMEM)] + [pl.BlockSpec(memory_space=pltpu.VMEM)] * ninputs,
        out_shape=tuple([jax.ShapeDtypeStruct((rows, sum(widths)), BF)] * count),
        compiler_params=VMEM_LIMIT,
    )(context, *blocked, *turned, *stacked)


def tensor_packed(places, hidden_rows, wide_rows, part, depth, count):
    tensors = places.shape[0] - 1
    rows = hidden_rows.shape[0]
    own = rows // count

    def kernel(places_ref, hidden_ref, wide_ref, out_ref):
        context = places_ref[tensors]
        lane = pl.multiple_of(context * depth, 128)
        for j in range(count):
            source = pl.ds(pl.multiple_of((context + count - j) % count * own, own), own)
            here = slice(j * own, (j + 1) * own)
            columns = wide_ref[source, pl.ds(lane, depth)]
            for k in range(tensors):
                at = pl.multiple_of(places_ref[k] * part, 128)
                out_ref[k, here, :part] = hidden_ref[source, pl.ds(at, part)]
                out_ref[k, here, part:] = columns

    return pl.pallas_call(
        kernel,
        in_specs=[pl.BlockSpec(memory_space=pltpu.SMEM)] + [pl.BlockSpec(memory_space=pltpu.VMEM)] * 2,
        out_shape=jax.ShapeDtypeStruct((tensors, rows, part + depth), BF),
    )(places, hidden_rows, wide_rows)


def tail_packed(micro, mod, rest, groups_of, shares):
    rows, mods = mod.shape
    share, seqs = mods // shares, rows // 2
    extra = (mods + rest.shape[1]) // (groups_of * shares)
    wide = lanes(max(share, extra))

    def kernel(micro_ref, mod_ref, rest_ref, out_ref, bias_ref, piece_ref):
        for j in range(2):
            bias_ref[j : j + 1, :mods] = jnp.sum(mod_ref[j * seqs : (j + 1) * seqs, :], axis=0, keepdims=True)
        bias_ref[:, mods:] = rest_ref[...]
        piece_ref[...] = jnp.zeros_like(piece_ref)
        for group in range(groups_of):
            mine = jnp.where(micro_ref[0] == group, 1.0, 0.0)
            for k in range(shares):
                device = group * shares + k
                piece_ref[device, :rows, :share] = mod_ref[:, k * share : (k + 1) * share] * mine
                piece_ref[device, rows : rows + 2, :extra] = bias_ref[:, device * extra : (device + 1) * extra]
        out_ref[...] = piece_ref[...].astype(BF)

    return pl.pallas_call(
        kernel,
        in_specs=[pl.BlockSpec(memory_space=pltpu.SMEM)] + [pl.BlockSpec(memory_space=pltpu.VMEM)] * 2,
        out_shape=jax.ShapeDtypeStruct((groups_of * shares, 8, wide), BF),
        scratch_shapes=[
            pltpu.VMEM((2, mods + rest.shape[1]), F32),
            pltpu.VMEM((groups_of * shares, 8, wide), F32),
        ],
    )(micro.reshape(1), mod, rest)


def finish_hidden(context, shard, got, at, cols, part, turned):
    depth, hidden = shard.shape
    count, tensors = len(got), cols.shape[0]
    shape = (2, hidden, depth) if turned else (2, depth, hidden)

    def kernel(context_ref, shard_ref, cols_ref, *refs):
        out_ref = refs[-1]
        image = shard_ref[...].astype(F32)
        out_ref[0] = image.T if turned else image
        for k in range(count):
            block = pl.ds(pl.multiple_of((context_ref[0] + count - k) % count * part, 128), part)
            total = 0.0
            for t in range(tensors):
                lane = at + t * part
                pair = (refs[k][:, lane : lane + part], cols_ref[t, :, part:])
                total += dot_tn(*pair) if turned else dot_tn(*pair[::-1])
            if turned:
                out_ref[1, block, :] = total
            else:
                out_ref[1, :, block] = total

    return pl.pallas_call(
        kernel,
        in_specs=[pl.BlockSpec(memory_space=pltpu.SMEM)]
        + [pl.BlockSpec(memory_space=pltpu.VMEM)] * (2 + count),
        out_shape=jax.ShapeDtypeStruct(shape, F32),
        compiler_params=VMEM_LIMIT,
    )(context, shard, cols, *got)


def finish_rows(shard, left_got, left, right_got, right, turned):
    m, n = left[1] - left[0], right[1] - right[0]
    count = len(left_got)

    def kernel(shard_ref, *refs):
        out_ref = refs[-1]
        image = shard_ref[...].astype(F32)
        out_ref[0] = image.T if turned else image
        total = 0.0
        for k in range(count):
            total += dot_tn(refs[k][:, left[0] : left[1]], refs[count + k][:, right[0] : right[1]])
        out_ref[1] = total

    return pl.pallas_call(
        kernel, out_shape=jax.ShapeDtypeStruct((2, m, n), F32), compiler_params=VMEM_LIMIT
    )(shard, *left_got, *right_got)


def normalized(x):
    centred = x - jnp.mean(x, axis=-1, keepdims=True)
    inverse = lax.rsqrt(jnp.mean(centred * centred, axis=-1, keepdims=True) + NORM_EPS)
    return centred * inverse, inverse


def norm_back(n, inverse, w):
    return (w - jnp.mean(w, axis=-1, keepdims=True) - n * jnp.mean(w * n, axis=-1, keepdims=True)) * inverse


def row_call(kernel, row_mods, indices, arrays, outs):
    rows, width = row_mods.shape[0], row_mods.shape[1] // 6

    def whole(x):
        return pl.BlockSpec(x.shape, lambda i: (0,) * len(x.shape))

    return pl.pallas_call(
        kernel,
        grid=(1,),
        in_specs=[pl.BlockSpec((rows, width), lambda i, at=at: (0, at)) for at in indices]
        + [whole(x) for x in arrays],
        out_specs=tuple(whole(x) for x in outs),
        out_shape=tuple(outs),
        compiler_params=VMEM_LIMIT,
    )(*[row_mods] * len(indices), *arrays)


def enter_rows(row_mods, x, cut):
    rows, width = x.shape

    def kernel(shift_ref, scale_ref, x_ref, image_ref, text_ref):
        n = normalized(x_ref[...])[0]
        h = (n * (1.0 + scale_ref[...].astype(F32)) + shift_ref[...].astype(F32)).astype(BF)
        image_ref[...] = h[:cut]
        text_ref[...] = h[cut:]

    outs = [jax.ShapeDtypeStruct((cut, width), BF), jax.ShapeDtypeStruct((rows - cut, width), BF)]
    return row_call(kernel, row_mods, (0, 1), (x,), outs)


def middle_rows(row_mods, x, image_sum, text_sum, bias):
    rows, width = x.shape
    cut = image_sum.shape[0]

    def kernel(
        gate_ref, shift_ref, scale_ref, x_ref, image_ref, text_ref, bias_ref,
        branch_ref, middle_ref, himage_ref, htext_ref,
    ):
        branch_ref[:cut] = image_ref[...] + bias_ref[0:1, :]
        branch_ref[cut:] = text_ref[...] + bias_ref[1:2, :]
        middle = x_ref[...] + gate_ref[...].astype(F32) * branch_ref[...]
        middle_ref[...] = middle
        n = normalized(middle)[0]
        h = (n * (1.0 + scale_ref[...].astype(F32)) + shift_ref[...].astype(F32)).astype(BF)
        himage_ref[...] = h[:cut]
        htext_ref[...] = h[cut:]

    outs = [jax.ShapeDtypeStruct((rows, width), F32)] * 2
    outs += [jax.ShapeDtypeStruct((cut, width), BF), jax.ShapeDtypeStruct((rows - cut, width), BF)]
    return row_call(kernel, row_mods, (2, 3, 4), (x, image_sum, text_sum, bias), outs)


def halves_sum(rows, cut):
    return jnp.concatenate(
        (jnp.sum(rows[:cut], axis=0, keepdims=True), jnp.sum(rows[cut:], axis=0, keepdims=True)), 0
    )


def gated_rows(row_mods, g_out, cut):
    rows, width = g_out.shape

    def kernel(gate_ref, g_ref, image_ref, text_ref, sums_ref):
        g = (gate_ref[...].astype(F32) * g_ref[...]).astype(BF)
        image_ref[...] = g[:cut]
        text_ref[...] = g[cut:]
        sums_ref[...] = halves_sum(g.astype(F32), cut)

    outs = [jax.ShapeDtypeStruct((cut, width), BF), jax.ShapeDtypeStruct((rows - cut, width), BF)]
    outs += [jax.ShapeDtypeStruct((2, width), F32)]
    return row_call(kernel, row_mods, (5,), (g_out,), outs)


def middle_rows_back(row_mods, image_sum, text_sum, middle, g_out, branch, picks):
    rows, width = middle.shape
    cut = image_sum.shape[0]

    def kernel(
        gate_ref, scale_ref, image_ref, text_ref, middle_ref, g_ref, branch_ref, picks_ref,
        gmiddle_ref, gimage_ref, gtext_ref, sums_ref, mod_ref, gh_ref,
    ):
        gh_ref[:cut] = image_ref[...]
        gh_ref[cut:] = text_ref[...]
        gh = gh_ref[...]
        n, inverse = normalized(middle_ref[...])
        g_middle = g_ref[...] + norm_back(n, inverse, gh * (1.0 + scale_ref[...].astype(F32)))
        gmiddle_ref[...] = g_middle
        g_branch = (gate_ref[...].astype(F32) * g_middle).astype(BF)
        gimage_ref[...] = g_branch[:cut]
        gtext_ref[...] = g_branch[cut:]
        sums_ref[...] = halves_sum(g_branch.astype(F32), cut)
        for at, part in enumerate((g_middle * branch_ref[...], gh, gh * n)):
            mod_ref[:, at * width : (at + 1) * width] = dot_nn(picks_ref[...], part.astype(BF))

    outs = [jax.ShapeDtypeStruct((rows, width), F32), jax.ShapeDtypeStruct((cut, width), BF)]
    outs += [jax.ShapeDtypeStruct((rows - cut, width), BF), jax.ShapeDtypeStruct((2, width), F32)]
    outs += [jax.ShapeDtypeStruct((picks.shape[0], 3 * width), F32)]
    scratch = jax.ShapeDtypeStruct((rows, width), F32)
    return row_call(
        kernel, row_mods, (2, 4), (image_sum, text_sum, middle, g_out, branch, picks), outs + [scratch]
    )[:5]


def enter_rows_back(row_mods, image_sum, text_sum, x, g_middle, g_out, down, picks):
    rows, width = x.shape
    cut = image_sum.shape[0]

    def kernel(
        scale_ref, image_ref, text_ref, x_ref, gm_ref, g_ref, down_ref, picks_ref, gx_ref, mod_ref, gh_ref
    ):
        gh_ref[:cut] = image_ref[...]
        gh_ref[cut:] = text_ref[...]
        gh = gh_ref[...]
        n, inverse = normalized(x_ref[...])
        gx_ref[...] = gm_ref[...] + norm_back(n, inverse, gh * (1.0 + scale_ref[...].astype(F32)))
        for at, part in enumerate((gh, gh * n, g_ref[...] * down_ref[...])):
            mod_ref[:, at * width : (at + 1) * width] = dot_nn(picks_ref[...], part.astype(BF))

    outs = [jax.ShapeDtypeStruct((rows, width), F32), jax.ShapeDtypeStruct((picks.shape[0], 3 * width), F32)]
    scratch = jax.ShapeDtypeStruct((rows, width), F32)
    return row_call(
        kernel, row_mods, (1,), (image_sum, text_sum, x, g_middle, g_out, down, picks), outs + [scratch]
    )[:2]


def gelu_pair(u):
    c = 0.7978845608028654
    inner = jnp.tanh(c * (u + 0.044715 * u * u * u))
    value = 0.5 * u * (1.0 + inner)
    slope = 0.5 * (1.0 + inner) + 0.5 * u * (1.0 - inner * inner) * c * (1.0 + 3 * 0.044715 * u * u)
    return value.astype(BF), slope.astype(BF)


def shards(
    image_tokens,
    text_tokens,
    conditioning,
    image_seq_ids,
    text_seq_ids,
    ada_weight,
    qkv_weight,
    out_weight,
    up_weight,
    down_weight,
    biases,
    image_cotangent,
    text_cotangent,
):
    section = lax.axis_index("section")
    context = lax.axis_index("context")
    tensor = lax.axis_index("tensor")
    ncontext = lax.axis_size("context")
    ntensor = lax.axis_size("tensor")
    ndev = ncontext * ntensor
    first = section == 0
    micros, own_image, width = image_tokens.shape
    own_text = text_tokens.shape[1]
    seqs = conditioning.shape[1]
    rows_image, rows_text = micros * own_image, micros * own_text
    heads_here = HEADS // ntensor
    local = heads_here * HEAD
    hidden = up_weight.shape[3]
    bias_here = biases.shape[2]
    depth = qkv_weight.shape[2]
    mods = 6 * width
    table_rows = 2 * seqs
    per = ncontext // micros
    micro = context // per
    paired = per == 2 and heads_here % 2 == 0
    groups = 2 if paired else 1
    group_heads = heads_here // groups
    group = group_heads * HEAD
    side = context % per
    ctx_image, ctx_text = ntensor * rows_image, ntensor * rows_text
    ctx_rows = ctx_image + ctx_text

    order = (0, 2, 1, 3)

    def swapped(x, axis, bit):
        return lax.ppermute(x, axis, [(i, i ^ bit) for i in range(lax.axis_size(axis))])

    def sided(a, b):
        return jnp.where(side == 0, a, b), jnp.where(side == 0, b, a)

    def near(x):
        return swapped(x, "tensor", 1)

    def far(x):
        return swapped(x, "tensor", 2)

    def gather_tensor(x):
        beside = near(x)
        across = far(x)
        return x, across, beside, near(across)

    def reduce_tensor(x):
        n = x.shape[0] // 4
        got = near(x[2 * n :])
        mine = x[: 2 * n].astype(F32) + got.astype(F32)
        return mine[:n] + far(mine[n:].astype(BF)).astype(F32)

    def spread_both(image, text):
        return joined(gather_tensor(image), gather_tensor(text))

    def turned_by(x, by):
        return lax.ppermute(x, "context", [(i, (i + by) % ncontext) for i in range(ncontext)])

    def text_gather(rows):
        return [rows] + [turned_by(rows, k) for k in range(1, ncontext)]

    def text_scatter(partial_sums):
        sums = partial_sums.astype(BF).reshape(ncontext, rows_text, width)
        total = sums[0].astype(F32)
        for k in range(1, ncontext):
            total += turned_by(sums[k], -k).astype(F32)
        return total

    def spread_and_gather(image, text):
        return joined(gather_tensor(image)) + joined(text_gather(text))

    def by_tensor(x, axis):
        places = [jnp.array(order)[tensor ^ k] for k in range(ntensor)]
        return jnp.stack([lax.dynamic_index_in_dim(x, at, axis, keepdims=False) for at in places], axis)

    def in_group(x, axis):
        places = [tensor ^ bit for bit in order]
        return jnp.stack([lax.dynamic_index_in_dim(x, at, axis, keepdims=False) for at in places], axis)

    def gather_both(x):
        got = lax.all_gather(x, "tensor")
        got = lax.all_to_all(jnp.broadcast_to(got[None], (ncontext,) + got.shape), "context", 0, 0)
        return got.reshape((ndev,) + x.shape)

    def rounds(step, back):
        pairs = []
        for h in range(ncontext):
            m = (h + step) % micros
            pairs.append((h, m * per + h // micros))
        return [(b, a) for a, b in pairs] if back else pairs

    def to_work(image, text):
        pieces = []
        for step in range(micros):
            m = (context + step) % micros
            pieces.append(
                [
                    lax.ppermute(
                        lax.dynamic_index_in_dim(x, m, 0, keepdims=False), "context", rounds(step, False)
                    )
                    for x in (image, text)
                ]
            )
        return jnp.concatenate([p[0] for p in pieces] + [p[1] for p in pieces], 0).astype(F32)

    def to_home(rows):
        rows = rows.astype(BF)
        pieces = []
        for step in range(micros):
            at, below = step * own_image, rows_image + step * own_text
            both = jnp.concatenate((rows[at : at + own_image], rows[below : below + own_text]), 0)
            pieces.append(lax.ppermute(both, "context", rounds(step, True)))
        pieces = jnp.stack(pieces).astype(F32)
        image, text = pieces[:, :own_image], pieces[:, own_image:]
        turns = [(m - context) % micros for m in range(micros)]
        return tuple(
            jnp.stack([lax.dynamic_index_in_dim(x, turn, 0, keepdims=False) for turn in turns])[None]
            for x in (image, text)
        )

    def gathered(w):
        return lax.all_gather(w, "context", axis=0, tiled=True)

    qkv_full = [gathered(qkv_weight[0, 0])]
    out_full = [gathered(out_weight[0, 0].T)]
    up_full = [gathered(up_weight[0, 0])]
    down_full = [gathered(down_weight[0, 0].T)]

    def ring(w, send_after=None):
        pieces = [w if send_after is None else after(w, send_after)]
        for step in range(1, ncontext):
            pieces.append(lax.ppermute(pieces[-1], "context", [(i, (i + 1) % ncontext) for i in range(ncontext)]))
        return pieces

    def laid(pieces):
        full = jnp.zeros((width, pieces[0].shape[1]), BF)
        for step, piece in enumerate(pieces):
            full = lax.dynamic_update_slice_in_dim(full, piece, (context - step) % ncontext * depth, 0)
        return full

    ring_first = ring(jnp.concatenate((qkv_weight[0, 1], out_weight[0, 1].T), axis=1))
    stage = (ncontext + 2) // 3
    part = hidden // ncontext
    text_sent = jnp.concatenate(
        [w.reshape(ncontext, part, depth) for w in (up_weight[0, 1].T, down_weight[0, 1])], axis=1
    )
    text_moved = lax.all_to_all(after(text_sent, ring_first[-1]), "context", 0, 0)
    feed = []

    cond_float = conditioning.astype(F32)
    silu_cond = jax.nn.silu(cond_float).astype(BF).reshape(micros * seqs, -1)
    ada_part = jnp.einsum("rc,jck->jrk", silu_cond, ada_weight[0], preferred_element_type=F32)
    sharing = [[m * per + u for u in range(per)] for m in range(micros)]
    shares = per * ntensor
    share = mods // shares
    bias_placed = lax.dynamic_update_slice_in_dim(
        jnp.zeros((2, bias_here * ndev), F32),
        biases[0].astype(F32),
        (context * ntensor + tensor) * bias_here,
        1,
    )
    ada_sent = packed(
        ada_part + bias_placed[:, None, :mods],
        jnp.broadcast_to(biases[0].astype(F32)[None], (ndev, 2, bias_here)),
        micros,
        shares,
    )
    ada_got = lax.all_to_all(ada_sent.astype(BF), BOTH, 0, 0)
    bias_full = ada_got[:, table_rows : table_rows + 2, :bias_here].transpose(1, 0, 2).reshape(2, -1).astype(F32)
    ada_sum = jnp.sum(ada_got[:, :table_rows, :share].astype(F32), axis=0).astype(BF)
    table = lax.all_gather(ada_sum, "tensor")
    if paired:
        table = jnp.stack(sided(table, swapped(table, "context", 1)))
    else:
        table = lax.all_gather(table, "context", axis_index_groups=sharing)
    table = after(table, ring_first[stage - 1])
    table = table.reshape(shares, table_rows, share).transpose(1, 0, 2).reshape(table_rows, mods)
    query_bias = lax.dynamic_slice_in_dim(bias_full, mods + tensor * local, local, 1)
    value_bias = lax.dynamic_slice_in_dim(bias_full, mods + width + tensor * local, local, 1)
    qkv_bias = jnp.stack(
        (
            query_bias.reshape(2, heads_here, HEAD),
            jnp.zeros((2, heads_here, HEAD), F32),
            value_bias.reshape(2, heads_here, HEAD),
        ),
        axis=2,
    ).reshape(2, 3 * local)
    out_bias = bias_full[:, mods + 2 * width : mods + 3 * width]
    at_up = mods + 3 * width
    up_bias = lax.dynamic_slice_in_dim(bias_full[0], at_up + tensor * hidden, hidden, 0)
    up_bias_text = bias_full[1, at_up : at_up + ntensor * hidden].reshape(ntensor, ncontext, part)
    up_bias_text = in_group(lax.dynamic_index_in_dim(up_bias_text, context, 1, keepdims=False), 0).reshape(-1)
    down_bias = bias_full[:, mods + 3 * width + hidden * ntensor :]

    def by_modality(pair):
        return jnp.concatenate(
            (
                jnp.broadcast_to(pair[0][None], (rows_image, width)),
                jnp.broadcast_to(pair[1][None], (rows_text, width)),
            ),
            0,
        )

    def ids_of(work_context):
        m, u = work_context // per, work_context % per
        homes = jnp.stack([u * micros + (m - step) % micros for step in range(micros)])
        places = homes[None, :] * ntensor + (tensor ^ jnp.array(order))[:, None]
        found = []
        for ids, own in ((image_seq_ids, own_image), (text_seq_ids, own_text)):
            table_ids = lax.dynamic_index_in_dim(ids, m, 0, keepdims=False).reshape(ndev, own)
            found.append(jnp.take(table_ids, places.reshape(-1), axis=0).reshape(-1))
        return found

    own_found = ids_of(context)
    own_ids = jnp.concatenate((own_found[0][:rows_image], own_found[1][:rows_text] + seqs))
    onehot = (own_ids[:, None] == jnp.arange(table_rows)[None, :]).astype(BF)
    row_mods = dot_nn(onehot, table).astype(BF)
    picks = onehot.T
    joint_ids = jnp.concatenate(own_found)
    if paired:
        attn_ids = jnp.concatenate([joint_ids] + ids_of(context ^ 1))
    else:
        attn_ids = jnp.concatenate([x for u in range(per) for x in ids_of(micro * per + u)])

    def row_mod(index):
        return row_mods[:, index * width : (index + 1) * width].astype(F32)

    def attention(joint):
        if paired:
            mine, theirs = sided(joint[: 3 * group], joint[3 * group :])
            theirs = swapped(theirs, "context", 1)
            here, there, lse = attend_pair(mine, theirs, attn_ids, group_heads)
            return jnp.concatenate(sided(here, swapped(there, "context", 1)), axis=0), (mine, theirs, lse)
        by_kind = joint.reshape(heads_here, 3, HEAD, ctx_rows)
        q, k, v = (by_kind[:, i].reshape(local, ctx_rows).T for i in range(3))
        k, v = (
            lax.all_gather(x, "context", axis=0, tiled=True, axis_index_groups=sharing) for x in (k, v)
        )
        attended, lse = attend(q, k, v, joint_ids, attn_ids, group_heads)
        return attended.T, (q, k, v, lse)

    def attention_back(grad, kept):
        if paired:
            mine, theirs, lse = kept
            g_mine, g_theirs = sided(grad[:group], grad[group:])
            g_theirs = swapped(g_theirs, "context", 1)
            d_mine, d_theirs = attend_pair_back(mine, theirs, g_mine, g_theirs, lse, attn_ids, group_heads)
            return jnp.concatenate(sided(d_mine, swapped(d_theirs, "context", 1)), axis=0)
        q, k, v, lse = kept
        dq, dk, dv = attend_back(q, k, v, grad.T, lse, joint_ids, attn_ids, group_heads)
        dk, dv = (
            lax.psum_scatter(x, "context", scatter_dimension=0, tiled=True, axis_index_groups=sharing)
            for x in (dk, dv)
        )
        kinds = [x.T.reshape(heads_here, HEAD, ctx_rows) for x in (dq, dk, dv)]
        return jnp.stack(kinds, axis=1).reshape(3 * local, ctx_rows)

    def forward(x, late=False, ahead=()):
        h1_image, h1_text = enter_rows(row_mods, x, rows_image)
        fresh = len(qkv_full) == 1
        if fresh:
            h1_image = after(h1_image, ring_first[2 * stage - 2])
            full = laid(ring_first)
            qkv_full.append(full[:, : 3 * local])
            out_full.append(full[:, 3 * local :])
        h1 = spread_both(h1_image, h1_text)
        joint = jnp.concatenate(
            [(dot_tt(qkv_full[j], h1[j]) + qkv_bias[j][:, None]).astype(BF) for j in range(2)], axis=1
        )
        attended, kept = attention(joint)
        if fresh:
            attended = after(attended, text_moved)
            moved = gather_tensor(text_moved.transpose(1, 0, 2).reshape(2 * part, width))
            feed.append(jnp.concatenate([b[:part] for b in moved], 0))
            feed.append(jnp.concatenate([b[part:] for b in moved], 0))
        if ahead:
            attended = after(attended, *ahead)
        image_sum = reduce_tensor(dot_tt(attended, out_full[0])[:ctx_image].astype(BF))
        text_sum = reduce_tensor(dot_tt(attended[:, ctx_image:], out_full[1]).astype(BF))
        if fresh:
            image_sum = after(image_sum, *feed)
        branch, middle, h2_image, h2_text = middle_rows(row_mods, x, image_sum, text_sum, out_bias)
        up_text, down_text = feed
        h2 = spread_and_gather(h2_image, h2_text)
        pairs = [
            gelu_pair(dot_nn(h2[0], up_full[0]) + up_bias),
            gelu_pair(dot_nt(h2[1], up_text) + up_bias_text),
        ]
        acts, slopes = [p[0] for p in pairs], [p[1] for p in pairs]
        saved = dict(
            x=x, h1=h1, kept=kept, attn=attended, branch=branch, middle=middle, h2=h2, acts=acts,
            slopes=slopes, raw=[None, acts[1]],
        )

        def finish(gate):
            if gate is not None:
                saved["acts"] = [after(acts[0], gate), acts[1]]
            down = jnp.concatenate(
                (
                    reduce_tensor(dot_nt(saved["acts"][0], down_full[0]).astype(BF)),
                    text_scatter(dot_nn(saved["acts"][1], down_text)),
                ),
                0,
            ) + by_modality(down_bias)
            saved["down"] = down
            saved["out"] = middle + row_mod(5) * down

        saved["finish"] = finish
        if not late:
            finish(None)
        return saved

    def chosen(a, b):
        return jax.tree.map(lambda x, y: jnp.where(first, x, y), a, b)

    def scattered(full):
        return lax.psum_scatter(full.astype(BF), "context", scatter_dimension=0, tiled=True)

    def begin_back(g_out):
        gd_image, gd_text, gd_sums = gated_rows(row_mods, g_out, rows_image)
        return spread_and_gather(gd_image, gd_text), gd_sums

    def backward(saved, g_out, begun, last=None, beside=None):
        up_text, down_text = feed
        gd, gd_sums = begun
        g_up = [
            (dot_nn(gd[0], down_full[0]) * saved["slopes"][0].astype(F32)).astype(BF),
            (dot_nt(gd[1], down_text) * saved["slopes"][1].astype(F32)).astype(BF),
        ]
        g_h2_image = reduce_tensor(dot_nt(g_up[0], up_full[0]).astype(BF))
        g_h2_text = text_scatter(dot_nn(g_up[1], up_text))
        early = []
        if beside:
            g_h2_image = after(g_h2_image, beside["first"](g_up[0]))
        if last:
            use = chosen(
                dict(h2=saved["h2"][0], acts=saved["acts"][0], gd=gd[0], g_up=g_up[0]),
                {k: last[k][0] for k in ("h2", "acts", "gd", "g_up")},
            )
            early = [
                dot_tn(use["gd"], use["acts"]).astype(BF),
                dot_tn(use["h2"], use["g_up"]).astype(BF),
            ]
            g_h2_image = after(g_h2_image, *early)
            early = [scattered(part) for part in early]
        g_middle, gb_image, gb_text, gb_sums, mod_late = middle_rows_back(
            row_mods, g_h2_image, g_h2_text, saved["middle"], g_out, saved["branch"], picks
        )
        gb = spread_both(gb_image, gb_text)
        if "down" not in saved:
            saved["finish"](gb[0])
        g_attn = jnp.concatenate([dot_tt(out_full[j], gb[j]).astype(BF) for j in range(2)], axis=1)
        if last:
            use = chosen(dict(gb=gb[0], attn=saved["attn"]), dict(gb=last["gb"][0], attn=last["attn"]))
            early.append(dot_tt(use["gb"], use["attn"][:, :ctx_image]).astype(BF))
            g_attn = after(g_attn, early[2])
        if beside:
            g_attn = after(g_attn, *beside["second"](gb[0]))
        g_joint = attention_back(g_attn, saved["kept"])
        g_h1_image = reduce_tensor(dot_tt(g_joint, qkv_full[0])[:ctx_image].astype(BF))
        g_h1_text = reduce_tensor(dot_tt(g_joint[:, ctx_image:], qkv_full[1]).astype(BF))
        if last:
            use = chosen(dict(h1=saved["h1"][0], g=g_joint), dict(h1=last["h1"][0], g=last["g_joint"]))
            early.append(dot_tt(use["h1"], use["g"][:, :ctx_image]).astype(BF))
            g_h1_image = after(g_h1_image, early[3])
        g_x, mod_early = enter_rows_back(
            row_mods, g_h1_image, g_h1_text, saved["x"], g_middle, g_out, saved["down"], picks
        )
        if last:
            g_x = after(g_x, *early[:2])
        mod_grad = jnp.concatenate((mod_early[:, : 2 * width], mod_late, mod_early[:, 2 * width :]), axis=1)
        tensors = dict(
            h1=saved["h1"], attn=saved["attn"], h2=saved["h2"], acts=saved["acts"], g_joint=g_joint,
            gb=gb, g_up=g_up, gd=gd, gd_sums=gd_sums, gb_sums=gb_sums, mod=mod_grad,
        )
        return g_x, tensors, early

    aligned = part % 128 == 0 and depth % 128 == 0 and local % 128 == 0 and ncontext == ntensor
    offsets = tensor ^ jnp.arange(ntensor, dtype=jnp.int32)
    places = jnp.concatenate(((offsets & 1) * 2 + offsets // 2, context.reshape(1).astype(jnp.int32)))

    own_context = context.reshape(1).astype(jnp.int32)

    def tensor_round(hidden_rows, wide_rows):
        if aligned:
            sent = tensor_packed(places, hidden_rows, wide_rows, part, depth, ncontext)
        else:
            back = (context - jnp.arange(ncontext)) % ncontext
            hidden_rows, wide_rows = (
                jnp.take(x.reshape(ncontext, rows_text, -1), back, axis=0).reshape(x.shape)
                for x in (hidden_rows, wide_rows)
            )
            pieces = by_tensor(hidden_rows.reshape(hidden_rows.shape[0], ntensor, part), 1).transpose(1, 0, 2)
            own = lax.dynamic_slice_in_dim(wide_rows, context * depth, depth, 1)
            sent = jnp.concatenate((pieces, jnp.broadcast_to(own[None], (ntensor,) + own.shape)), axis=2)
        return lax.all_to_all(sent, "tensor", 0, 0)

    def context_round(blocked, turned, stacked):
        if aligned:
            sent = text_packed(own_context, blocked, turned, stacked, part, ncontext)
            return [turned_by(x, k) if k else x for k, x in enumerate(sent)]
        parts = [x.reshape(x.shape[0], ncontext, -1).transpose(1, 0, 2) for x in blocked]
        parts += [jnp.broadcast_to(x.T[None], (ncontext,) + x.T.shape) for x in turned]
        stacks = [x[:, :, :part].transpose(1, 0, 2).reshape(x.shape[1], -1) for x in stacked]
        stacks = [jnp.broadcast_to(x[None], (ncontext,) + x.shape) for x in stacks]
        return [
            lax.all_to_all(jnp.concatenate(group, axis=2), "context", 0, 0) for group in (parts, stacks) if group
        ]

    def handed(rows, by):
        return lax.ppermute(rows.astype(BF), "section", [(0, 1)] if by > 0 else [(1, 0)]).astype(F32)

    saved_first = forward(to_work(image_tokens, text_tokens))
    g_last = to_work(image_cotangent, text_cotangent)
    begun = begin_back(g_last)
    saved_last = forward(handed(saved_first["out"], 1), late=True, ahead=begun[0])

    rounds_done = {}

    def kept_rows():
        return chosen(
            [saved_first[n][1] for n in ("acts", "h1", "h2")] + [saved_first["attn"][:, ctx_image:]],
            [saved_last[n][1] for n in ("raw", "h1", "h2")] + [saved_last["attn"][:, ctx_image:]],
        )

    def tensor_first(gate):
        kept = kept_rows()
        rounds_done["ours"] = tensor_round(after(kept[0], gate), kept[2])
        return rounds_done["ours"]

    def context_second(gate):
        kept = kept_rows()
        rounds_done["got"] = context_round([after(kept[1], gate)], [kept[3]], [rounds_done["ours"]])
        return rounds_done["got"]

    grad_last, tensors_last, unused = backward(
        saved_last, g_last, begun, beside=dict(first=tensor_first, second=context_second)
    )
    ours_before, got_before = rounds_done["ours"], rounds_done["got"]
    out = to_home(after(jnp.where(first, saved_first["out"], saved_last["out"]), tensors_last["g_joint"]))
    returned = after(handed(grad_last, -1), *out)
    grad_first, tensors_first, early = backward(
        saved_first, returned, begin_back(returned), tensors_last
    )
    grad = to_home(jnp.where(first, grad_first, grad_last))
    use = chosen(tensors_first, tensors_last)

    down_shard, up_shard, out_part, qkv_part = early
    out_shard = after(scattered(out_part), grad_first)
    qkv_shard = after(scattered(qkv_part), grad_first)

    ours_after = tensor_round(use["g_up"][1], use["gd"][1])
    got_after = context_round([after(use["gb"][1], tensors_first["g_joint"])], [], [ours_after])

    def column_sums(parts):
        return jnp.stack([dot_nn(jnp.ones((8, p.shape[0]), BF), p)[0] for p in parts])

    qkv_sums = jnp.stack(
        [
            dot_nt(jnp.ones((8, part.shape[1]), BF), part)[0]
            for part in (use["g_joint"][:, :ctx_image], use["g_joint"][:, ctx_image:])
        ]
    ).reshape(2, heads_here, 3, HEAD)
    up_sums_text = lax.dynamic_update_slice_in_dim(
        jnp.zeros((ntensor, ncontext, part), F32),
        by_tensor(column_sums((use["g_up"][1],)).reshape(ntensor, 1, part), 0),
        context,
        1,
    ).reshape(1, -1)
    up_sums_image = lax.dynamic_update_slice_in_dim(
        jnp.zeros((1, ntensor * hidden), F32), column_sums((use["g_up"][0],)), tensor * hidden, 1
    )
    rest = jnp.zeros((2, bias_here * ndev - mods), F32)
    for at, value in (
        (tensor * local, qkv_sums[:, :, 0].reshape(2, local)),
        (width + tensor * local, qkv_sums[:, :, 2].reshape(2, local)),
        (2 * width, use["gb_sums"]),
        (3 * width, jnp.concatenate((up_sums_image, up_sums_text), 0)),
        (3 * width + ntensor * hidden, use["gd_sums"]),
    ):
        rest = lax.dynamic_update_slice_in_dim(rest, value, at, 1)
    if aligned:
        sent = tail_packed(micro.astype(jnp.int32), use["mod"], rest, micros, shares)
    else:
        bias_part = jnp.concatenate((jnp.sum(use["mod"].reshape(2, seqs, mods), axis=1), rest), axis=1)
        mod_sent = use["mod"].reshape(2, 1, seqs, mods)
        mod_sent = jnp.where(jnp.arange(micros)[None, :, None, None] == micro, mod_sent, 0.0)
        bias_sent = bias_part.reshape(2, ndev, bias_here).transpose(1, 0, 2)
        sent = packed(mod_sent.reshape(2, micros * seqs, mods), bias_sent, micros, shares).astype(BF)
    got = jnp.sum(lax.all_to_all(sent, BOTH, 0, 0).astype(F32), axis=0)
    bias_grad = got[table_rows:, :bias_here]
    mod_all = (
        gather_both(got[:table_rows, :share].astype(BF))
        .reshape(micros, shares, 2, seqs, share)
        .transpose(2, 0, 3, 1, 4)
        .reshape(2, micros * seqs, mods)
    )
    ada_grad = jnp.einsum("rc,jrk->jck", silu_cond, mod_all, preferred_element_type=F32)
    cond_inner = jnp.einsum("jrk,jck->rc", mod_all, ada_weight[0], preferred_element_type=F32)
    got_qkv = context_round([], [use["g_joint"][:, ctx_image:]], [])
    if aligned:
        down_grad = finish_hidden(own_context, down_shard, got_before, depth + local, ours_after, part, True)
        up_grad = finish_hidden(own_context, up_shard, got_after, depth, ours_before, part, False)
        out_grad = finish_rows(out_shard, got_before, (depth, depth + local), got_after, (0, depth), True)
        qkv_grad = finish_rows(qkv_shard, got_before, (0, depth), got_qkv, (0, 3 * local), False)
    else:
        acts_all = got_before[1].reshape(ncontext, -1, ntensor, part)
        g_up_all = got_after[1].reshape(ncontext, -1, ntensor, part)
        text_down = jnp.einsum("crtj,trd->cjd", acts_all, ours_after[:, :, part:], preferred_element_type=F32)
        text_up = jnp.einsum("trk,crtj->kcj", ours_before[:, :, part:], g_up_all, preferred_element_type=F32)
        text_out = jnp.einsum(
            "crh,crd->hd", got_before[0][:, :, depth:], got_after[0], preferred_element_type=F32
        )
        text_qkv = jnp.einsum("crk,crh->kh", got_before[0][:, :, :depth], got_qkv[0], preferred_element_type=F32)
        down_grad = jnp.stack((down_shard.astype(F32).T, text_down.reshape(hidden, depth)))
        up_grad = jnp.stack((up_shard.astype(F32), text_up.reshape(depth, hidden)))
        out_grad = jnp.stack((out_shard.astype(F32).T, text_out))
        qkv_grad = jnp.stack((qkv_shard.astype(F32), text_qkv))
    unused, silu_back = jax.vjp(jax.nn.silu, cond_float)
    cond_inner = cond_inner + lax.ppermute(cond_inner, "section", [(0, 1), (1, 0)])
    cond_grad = silu_back(cond_inner.reshape(cond_float.shape))[0]
    return (
        *out,
        *grad,
        cond_grad,
        ada_grad[None],
        qkv_grad[None],
        out_grad[None],
        up_grad[None],
        down_grad[None],
        bias_grad[None],
    )


def solution(mesh):
    tokens = P(None, BOTH, None)
    block_rows = P("section", None, BOTH, None)
    by_rows = P("section", None, "context", "tensor")
    by_cols = P("section", None, "tensor", "context")
    block_biases = P("section", None, BOTH)
    in_specs = (
        tokens,
        tokens,
        P(None, None, BOTH),
        P(),
        P(),
        block_rows,
        by_rows,
        by_cols,
        by_rows,
        by_cols,
        block_biases,
        tokens,
        tokens,
    )
    out_specs = (
        block_rows,
        block_rows,
        block_rows,
        block_rows,
        P(None, None, BOTH),
        block_rows,
        by_rows,
        by_cols,
        by_rows,
        by_cols,
        block_biases,
    )
    return jax.shard_map(shards, mesh=mesh, in_specs=in_specs, out_specs=out_specs, check_vma=False)
```

```python
from functools import partial

import jax
import jax.numpy as jnp
from jax import lax
from jax.experimental import pallas as pl
from jax.experimental.pallas import tpu as pltpu
from jax.sharding import PartitionSpec as P

HEADS = 24
HEAD = 64
NORM_EPS = 1e-06
MASKED = -1e30
BF = jnp.bfloat16
F32 = jnp.float32
BOTH = ("context", "tensor")


def dot_nn(a, b):
    return lax.dot_general(a, b, (((1,), (0,)), ((), ())), preferred_element_type=F32)


def dot_nt(a, b):
    return lax.dot_general(a, b, (((1,), (1,)), ((), ())), preferred_element_type=F32)


def dot_tn(a, b):
    return lax.dot_general(a, b, (((0,), (0,)), ((), ())), preferred_element_type=F32)


def dot_tt(a, b):
    return lax.dot_general(a, b, (((0,), (1,)), ((), ())), preferred_element_type=F32)


def scaled(q):
    return q * jnp.asarray(HEAD**-0.5, BF)


def attend_body(heads, chunk, places, q_ref, k_ref, v_ref, idq_ref, idk_ref, store, lse_ref):
    at_q, at_k, at_v = places

    def one_chunk(step, carry):
        rows = pl.ds(pl.multiple_of(step * chunk, chunk), chunk)
        bias = jnp.where(idk_ref[...] == idq_ref[:, rows], 0.0, MASKED)
        outs = []
        for head in range(heads):
            at = head * HEAD
            q = scaled(q_ref[rows, at_q + at : at_q + at + HEAD])
            scores = dot_nt(k_ref[:, at_k + at : at_k + at + HEAD], q) + bias
            top = jnp.max(scores, axis=0, keepdims=True)
            weights = jnp.exp(scores - top)
            total = jnp.sum(weights, axis=0, keepdims=True)
            summed = dot_tn(v_ref[:, at_v + at : at_v + at + HEAD], weights.astype(BF))
            outs.append((summed / total).T)
            lse_ref[head : head + 1, rows] = top + jnp.log(total)
        store(rows, jnp.concatenate(outs, axis=1).astype(BF))
        return carry

    lax.fori_loop(0, idq_ref.shape[1] // chunk, one_chunk, 0)


def attend_back_body(
    heads, chunk, places, q_ref, k_ref, v_ref, g_ref, lse_ref, idq_ref, idk_ref, store_dq, dk_acc, dv_acc
):
    at_q, at_k, at_v = places
    dk_acc[...] = jnp.zeros_like(dk_acc)
    dv_acc[...] = jnp.zeros_like(dv_acc)

    def one_chunk(step, carry):
        rows = pl.ds(pl.multiple_of(step * chunk, chunk), chunk)
        bias = jnp.where(idk_ref[...] == idq_ref[:, rows], 0.0, MASKED)
        grads = []
        for head in range(heads):
            at = head * HEAD
            q = scaled(q_ref[rows, at_q + at : at_q + at + HEAD])
            g = g_ref[rows, at : at + HEAD]
            k = k_ref[:, at_k + at : at_k + at + HEAD]
            probs = jnp.exp(dot_nt(k, q) + bias - lse_ref[head : head + 1, rows])
            dv_acc[head] += dot_nn(probs.astype(BF), g)
            both = probs * dot_nt(v_ref[:, at_v + at : at_v + at + HEAD], g)
            delta = jnp.sum(both, axis=0, keepdims=True)
            dscores = (both - probs * delta).astype(BF)
            dk_acc[head] += dot_nn(dscores, q)
            grads.append((dot_tn(k, dscores) * HEAD**-0.5).T)
        store_dq(rows, jnp.concatenate(grads, axis=1).astype(BF))
        return carry

    lax.fori_loop(0, idq_ref.shape[1] // chunk, one_chunk, 0)


def heads_of(acc):
    return jnp.concatenate([acc[head] for head in range(acc.shape[0])], axis=1).astype(BF)


def attend_costs(queries, keys, heads, factor):
    return pl.CostEstimate(
        flops=factor * queries * keys * heads * HEAD,
        bytes_accessed=2 * (queries + 2 * keys) * heads * HEAD * factor // 4,
        transcendentals=queries * keys * heads,
    )


def chunk_for(keys):
    return 256 if keys <= 1024 else 128


VMEM_LIMIT = pltpu.CompilerParams(vmem_limit_bytes=56 * 2**20)


def attend(q, k, v, ids_q, ids_k, heads):
    queries, keys = q.shape[0], k.shape[0]

    def kernel(q_ref, k_ref, v_ref, idq_ref, idk_ref, out_ref, lse_ref):
        def store(rows, value):
            out_ref[rows, :] = value

        attend_body(
            heads, chunk_for(keys), (0, 0, 0), q_ref, k_ref, v_ref, idq_ref, idk_ref, store, lse_ref
        )

    return pl.pallas_call(
        kernel,
        out_shape=(
            jax.ShapeDtypeStruct((queries, heads * HEAD), BF),
            jax.ShapeDtypeStruct((heads, queries), F32),
        ),
        compiler_params=VMEM_LIMIT,
        cost_estimate=attend_costs(queries, keys, heads, 4),
    )(q, k, v, ids_q.reshape(1, queries), ids_k.reshape(keys, 1))


def attend_back(q, k, v, g, lse, ids_q, ids_k, heads):
    queries, keys = q.shape[0], k.shape[0]

    def kernel(
        q_ref, k_ref, v_ref, g_ref, lse_ref, idq_ref, idk_ref, dq_ref, dk_ref, dv_ref, dk_acc, dv_acc
    ):
        def store(rows, value):
            dq_ref[rows, :] = value

        attend_back_body(
            heads, chunk_for(keys), (0, 0, 0), q_ref, k_ref, v_ref, g_ref, lse_ref, idq_ref, idk_ref,
            store, dk_acc, dv_acc,
        )
        dk_ref[...] = heads_of(dk_acc)
        dv_ref[...] = heads_of(dv_acc)

    return pl.pallas_call(
        kernel,
        out_shape=(
            jax.ShapeDtypeStruct((queries, heads * HEAD), BF),
            jax.ShapeDtypeStruct((keys, heads * HEAD), BF),
            jax.ShapeDtypeStruct((keys, heads * HEAD), BF),
        ),
        scratch_shapes=[pltpu.VMEM((heads, keys, HEAD), F32), pltpu.VMEM((heads, keys, HEAD), F32)],
        compiler_params=VMEM_LIMIT,
        cost_estimate=attend_costs(queries, keys, heads, 10),
    )(q, k, v, g, lse, ids_q.reshape(1, queries), ids_k.reshape(keys, 1))


def attend_pair(mine, theirs, ids, heads):
    wide, half = mine.shape
    rows_all, group = 2 * half, heads * HEAD
    chunk = 256

    def kernel(mine_ref, theirs_ref, idq_ref, idk_ref, here_ref, there_ref, lse_ref, x_ref, out_ref):
        x_ref[:, :half] = mine_ref[...]
        x_ref[:, half:] = theirs_ref[...]

        def one_chunk(step, carry):
            rows = pl.ds(pl.multiple_of(step * chunk, chunk), chunk)
            bias = jnp.where(idk_ref[...] == idq_ref[:, rows], 0.0, MASKED)
            for head in range(heads):
                at = slice(head * HEAD, (head + 1) * HEAD)
                base = 3 * head * HEAD
                q = scaled(x_ref[base : base + HEAD, rows])
                k = x_ref[base + HEAD : base + 2 * HEAD, :]
                v = x_ref[base + 2 * HEAD : base + 3 * HEAD, :]
                scores = dot_tn(k, q) + bias
                top = jnp.max(scores, axis=0, keepdims=True)
                weights = jnp.exp(scores - top)
                total = jnp.sum(weights, axis=0, keepdims=True)
                out_ref[at, rows] = (dot_nn(v, weights.astype(BF)) / total).astype(BF)
                lse_ref[head : head + 1, rows] = top + jnp.log(total)
            return carry

        lax.fori_loop(0, rows_all // chunk, one_chunk, 0)
        here_ref[...] = out_ref[:, :half]
        there_ref[...] = out_ref[:, half:]

    return pl.pallas_call(
        kernel,
        out_shape=(
            jax.ShapeDtypeStruct((group, half), BF),
            jax.ShapeDtypeStruct((group, half), BF),
            jax.ShapeDtypeStruct((heads, rows_all), F32),
        ),
        scratch_shapes=[pltpu.VMEM((wide, rows_all), BF), pltpu.VMEM((group, rows_all), BF)],
        compiler_params=VMEM_LIMIT,
        cost_estimate=attend_costs(rows_all, rows_all, heads, 4),
    )(mine, theirs, ids.reshape(1, rows_all), ids.reshape(rows_all, 1))


def attend_pair_back(mine, theirs, g_mine, g_theirs, lse, ids, heads):
    wide, half = mine.shape
    rows_all, group = 2 * half, heads * HEAD
    chunk = 256

    def kernel(
        mine_ref, theirs_ref, gm_ref, gt_ref, lse_ref, idq_ref, idk_ref, dmine_ref, dtheirs_ref,
        x_ref, g_ref, dq_ref, dk_ref, dv_ref,
    ):
        x_ref[:, :half] = mine_ref[...]
        x_ref[:, half:] = theirs_ref[...]
        g_ref[:, :half] = gm_ref[...]
        g_ref[:, half:] = gt_ref[...]
        dk_ref[...] = jnp.zeros_like(dk_ref)
        dv_ref[...] = jnp.zeros_like(dv_ref)

        def one_chunk(step, carry):
            rows = pl.ds(pl.multiple_of(step * chunk, chunk), chunk)
            bias = jnp.where(idk_ref[...] == idq_ref[:, rows], 0.0, MASKED)
            for head in range(heads):
                at = slice(head * HEAD, (head + 1) * HEAD)
                base = 3 * head * HEAD
                q = scaled(x_ref[base : base + HEAD, rows])
                g = g_ref[at, rows]
                k = x_ref[base + HEAD : base + 2 * HEAD, :]
                v = x_ref[base + 2 * HEAD : base + 3 * HEAD, :]
                probs = jnp.exp(dot_tn(k, q) + bias - lse_ref[head : head + 1, rows])
                dv_ref[at, :] += dot_nt(g, probs.astype(BF))
                both = probs * dot_tn(v, g)
                delta = jnp.sum(both, axis=0, keepdims=True)
                dscores = (both - probs * delta).astype(BF)
                dk_ref[at, :] += dot_nt(q, dscores)
                dq_ref[at, rows] = (dot_nn(k, dscores) * HEAD**-0.5).astype(BF)
            return carry

        lax.fori_loop(0, rows_all // chunk, one_chunk, 0)
        for out_ref, cols in ((dmine_ref, slice(0, half)), (dtheirs_ref, slice(half, rows_all))):
            for head in range(heads):
                at = slice(head * HEAD, (head + 1) * HEAD)
                base = 3 * head * HEAD
                out_ref[base : base + HEAD, :] = dq_ref[at, cols]
                out_ref[base + HEAD : base + 2 * HEAD, :] = dk_ref[at, cols].astype(BF)
                out_ref[base + 2 * HEAD : base + 3 * HEAD, :] = dv_ref[at, cols].astype(BF)

    return pl.pallas_call(
        kernel,
        out_shape=(jax.ShapeDtypeStruct((wide, half), BF), jax.ShapeDtypeStruct((wide, half), BF)),
        scratch_shapes=[
            pltpu.VMEM((wide, rows_all), BF),
            pltpu.VMEM((group, rows_all), BF),
            pltpu.VMEM((group, rows_all), BF),
            pltpu.VMEM((group, rows_all), F32),
            pltpu.VMEM((group, rows_all), F32),
        ],
        compiler_params=VMEM_LIMIT,
        cost_estimate=attend_costs(rows_all, rows_all, heads, 10),
    )(mine, theirs, g_mine, g_theirs, lse, ids.reshape(1, rows_all), ids.reshape(rows_all, 1))


def after(x, *others):
    anywhere = pl.BlockSpec(memory_space=pl.ANY)

    def kernel(*refs):
        pass

    return pl.pallas_call(
        kernel,
        out_shape=jax.ShapeDtypeStruct(x.shape, x.dtype),
        in_specs=[anywhere] * (1 + len(others)),
        out_specs=anywhere,
        input_output_aliases={0: 0},
    )(x, *others)


def lanes(n):
    return -(-n // 128) * 128


def packed(sums, rest, groups_of, shares):
    rows, columns = sums.shape[1], sums.shape[2]
    seqs, share, extra = rows // groups_of, columns // shares, rest.shape[2]
    wide = lanes(max(share, extra))

    def kernel(sums_ref, rest_ref, out_ref):
        for group in range(groups_of):
            for j in range(2):
                out_ref[group, 0, j * seqs : (j + 1) * seqs, :share] = sums_ref[
                    j, group * seqs : (group + 1) * seqs, :
                ]
            out_ref[group, 0, 2 * seqs : 2 * seqs + 2, :extra] = rest_ref[group, 0]

    if share % 128 == 0:
        sums_in, sums_spec = sums, pl.BlockSpec((2, rows, share), lambda k: (0, 0, k))
    else:
        sums_in = sums.reshape(2, rows, shares, share).transpose(2, 0, 1, 3)
        sums_spec = pl.BlockSpec((None, 2, rows, share), lambda k: (k, 0, 0, 0))
    out = pl.pallas_call(
        kernel,
        grid=(shares,),
        in_specs=[sums_spec, pl.BlockSpec((groups_of, 1, 2, extra), lambda k: (0, k, 0, 0))],
        out_specs=pl.BlockSpec((groups_of, 1, 8, wide), lambda k: (0, k, 0, 0)),
        out_shape=jax.ShapeDtypeStruct((groups_of, shares, 8, wide), F32),
    )(sums_in, rest.reshape(groups_of, shares, 2, extra))
    return out.reshape(groups_of * shares, 8, wide)


def joined(*groups):
    sizes = [len(group) for group in groups]

    def kernel(*refs):
        taken = 0
        for out_ref, size in zip(refs[sum(sizes) :], sizes):
            at = 0
            for ref in refs[taken : taken + size]:
                out_ref[at : at + ref.shape[0], :] = ref[...]
                at += ref.shape[0]
            taken += size

    outs = [
        jax.ShapeDtypeStruct((sum(x.shape[0] for x in group), group[0].shape[1]), group[0].dtype)
        for group in groups
    ]
    return pl.pallas_call(kernel, out_shape=tuple(outs), compiler_params=VMEM_LIMIT)(
        *[x for group in groups for x in group]
    )


def text_packed(context, blocked, turned, stacked, part, count):
    rows = blocked[0].shape[0] if blocked else turned[0].shape[1]
    widths = [x.shape[1] // count for x in blocked] + [x.shape[0] for x in turned]
    widths += [x.shape[0] * part for x in stacked]
    nblocked, nturned = len(blocked), len(turned)
    ninputs = nblocked + nturned + len(stacked)

    def kernel(context_ref, *refs):
        ins, outs = refs[:ninputs], refs[ninputs:]
        at = 0
        for i, ref in enumerate(ins):
            wide = widths[i]
            if i < nblocked:
                for k in range(count):
                    lane = pl.multiple_of((context_ref[0] + k) % count * wide, 128)
                    outs[k][:, at : at + wide] = ref[:, pl.ds(lane, wide)]
            elif i < nblocked + nturned:
                value = ref[...].astype(F32).T.astype(BF)
                for k in range(count):
                    outs[k][:, at : at + wide] = value
            else:
                for t in range(ref.shape[0]):
                    for k in range(count):
                        outs[k][:, at + t * part : at + (t + 1) * part] = ref[t, :, :part]
            at += wide

    return pl.pallas_call(
        kernel,
        in_specs=[pl.BlockSpec(memory_space=pltpu.SMEM)] + [pl.BlockSpec(memory_space=pltpu.VMEM)] * ninputs,
        out_shape=tuple([jax.ShapeDtypeStruct((rows, sum(widths)), BF)] * count),
        compiler_params=VMEM_LIMIT,
    )(context, *blocked, *turned, *stacked)


def tensor_packed(places, hidden_rows, wide_rows, part, depth, count):
    tensors = places.shape[0] - 1
    rows = hidden_rows.shape[0]
    own = rows // count

    def kernel(places_ref, hidden_ref, wide_ref, out_ref):
        context = places_ref[tensors]
        lane = pl.multiple_of(context * depth, 128)
        for j in range(count):
            source = pl.ds(pl.multiple_of((context + count - j) % count * own, own), own)
            here = slice(j * own, (j + 1) * own)
            columns = wide_ref[source, pl.ds(lane, depth)]
            for k in range(tensors):
                at = pl.multiple_of(places_ref[k] * part, 128)
                out_ref[k, here, :part] = hidden_ref[source, pl.ds(at, part)]
                out_ref[k, here, part:] = columns

    return pl.pallas_call(
        kernel,
        in_specs=[pl.BlockSpec(memory_space=pltpu.SMEM)] + [pl.BlockSpec(memory_space=pltpu.VMEM)] * 2,
        out_shape=jax.ShapeDtypeStruct((tensors, rows, part + depth), BF),
    )(places, hidden_rows, wide_rows)


def tail_packed(micro, mod, rest, groups_of, shares):
    rows, mods = mod.shape
    share, seqs = mods // shares, rows // 2
    extra = (mods + rest.shape[1]) // (groups_of * shares)
    wide = lanes(max(share, extra))

    def kernel(micro_ref, mod_ref, rest_ref, out_ref, bias_ref, piece_ref):
        for j in range(2):
            bias_ref[j : j + 1, :mods] = jnp.sum(mod_ref[j * seqs : (j + 1) * seqs, :], axis=0, keepdims=True)
        bias_ref[:, mods:] = rest_ref[...]
        piece_ref[...] = jnp.zeros_like(piece_ref)
        for group in range(groups_of):
            mine = jnp.where(micro_ref[0] == group, 1.0, 0.0)
            for k in range(shares):
                device = group * shares + k
                piece_ref[device, :rows, :share] = mod_ref[:, k * share : (k + 1) * share] * mine
                piece_ref[device, rows : rows + 2, :extra] = bias_ref[:, device * extra : (device + 1) * extra]
        out_ref[...] = piece_ref[...].astype(BF)

    return pl.pallas_call(
        kernel,
        in_specs=[pl.BlockSpec(memory_space=pltpu.SMEM)] + [pl.BlockSpec(memory_space=pltpu.VMEM)] * 2,
        out_shape=jax.ShapeDtypeStruct((groups_of * shares, 8, wide), BF),
        scratch_shapes=[
            pltpu.VMEM((2, mods + rest.shape[1]), F32),
            pltpu.VMEM((groups_of * shares, 8, wide), F32),
        ],
    )(micro.reshape(1), mod, rest)


def finish_hidden(context, shard, got, at, cols, part, turned):
    depth, hidden = shard.shape
    count, tensors = len(got), cols.shape[0]
    shape = (2, hidden, depth) if turned else (2, depth, hidden)

    def kernel(context_ref, shard_ref, cols_ref, *refs):
        out_ref = refs[-1]
        image = shard_ref[...].astype(F32)
        out_ref[0] = image.T if turned else image
        for k in range(count):
            block = pl.ds(pl.multiple_of((context_ref[0] + count - k) % count * part, 128), part)
            total = 0.0
            for t in range(tensors):
                lane = at + t * part
                pair = (refs[k][:, lane : lane + part], cols_ref[t, :, part:])
                total += dot_tn(*pair) if turned else dot_tn(*pair[::-1])
            if turned:
                out_ref[1, block, :] = total
            else:
                out_ref[1, :, block] = total

    return pl.pallas_call(
        kernel,
        in_specs=[pl.BlockSpec(memory_space=pltpu.SMEM)]
        + [pl.BlockSpec(memory_space=pltpu.VMEM)] * (2 + count),
        out_shape=jax.ShapeDtypeStruct(shape, F32),
        compiler_params=VMEM_LIMIT,
    )(context, shard, cols, *got)


def finish_rows(shard, at, left_got, left, right_got, right, turned):
    m, n = left[1] - left[0], right[1] - right[0]
    count = len(left_got)

    def kernel(shard_ref, *refs):
        out_ref = refs[-1]
        image = shard_ref[:, at : at + (m if turned else n)].astype(F32)
        out_ref[0] = image.T if turned else image
        total = 0.0
        for k in range(count):
            total += dot_tn(refs[k][:, left[0] : left[1]], refs[count + k][:, right[0] : right[1]])
        out_ref[1] = total

    return pl.pallas_call(
        kernel, out_shape=jax.ShapeDtypeStruct((2, m, n), F32), compiler_params=VMEM_LIMIT
    )(shard, *left_got, *right_got)


def normalized(x):
    centred = x - jnp.mean(x, axis=-1, keepdims=True)
    inverse = lax.rsqrt(jnp.mean(centred * centred, axis=-1, keepdims=True) + NORM_EPS)
    return centred * inverse, inverse


def norm_back(n, inverse, w):
    return (w - jnp.mean(w, axis=-1, keepdims=True) - n * jnp.mean(w * n, axis=-1, keepdims=True)) * inverse


def row_call(kernel, row_mods, indices, arrays, outs):
    rows, width = row_mods.shape[0], row_mods.shape[1] // 6

    def whole(x):
        return pl.BlockSpec(x.shape, lambda i: (0,) * len(x.shape))

    return pl.pallas_call(
        kernel,
        grid=(1,),
        in_specs=[pl.BlockSpec((rows, width), lambda i, at=at: (0, at)) for at in indices]
        + [whole(x) for x in arrays],
        out_specs=tuple(whole(x) for x in outs),
        out_shape=tuple(outs),
        compiler_params=VMEM_LIMIT,
    )(*[row_mods] * len(indices), *arrays)


def enter_rows(row_mods, x, cut):
    rows, width = x.shape

    def kernel(shift_ref, scale_ref, x_ref, image_ref, text_ref):
        n = normalized(x_ref[...])[0]
        h = (n * (1.0 + scale_ref[...].astype(F32)) + shift_ref[...].astype(F32)).astype(BF)
        image_ref[...] = h[:cut]
        text_ref[...] = h[cut:]

    outs = [jax.ShapeDtypeStruct((cut, width), BF), jax.ShapeDtypeStruct((rows - cut, width), BF)]
    return row_call(kernel, row_mods, (0, 1), (x,), outs)


def middle_rows(row_mods, x, image_sum, text_sum, bias):
    rows, width = x.shape
    cut = image_sum.shape[0]

    def kernel(
        gate_ref, shift_ref, scale_ref, x_ref, image_ref, text_ref, bias_ref,
        branch_ref, middle_ref, himage_ref, htext_ref,
    ):
        branch_ref[:cut] = image_ref[...] + bias_ref[0:1, :]
        branch_ref[cut:] = text_ref[...] + bias_ref[1:2, :]
        middle = x_ref[...] + gate_ref[...].astype(F32) * branch_ref[...]
        middle_ref[...] = middle
        n = normalized(middle)[0]
        h = (n * (1.0 + scale_ref[...].astype(F32)) + shift_ref[...].astype(F32)).astype(BF)
        himage_ref[...] = h[:cut]
        htext_ref[...] = h[cut:]

    outs = [jax.ShapeDtypeStruct((rows, width), F32)] * 2
    outs += [jax.ShapeDtypeStruct((cut, width), BF), jax.ShapeDtypeStruct((rows - cut, width), BF)]
    return row_call(kernel, row_mods, (2, 3, 4), (x, image_sum, text_sum, bias), outs)


def halves_sum(rows, cut):
    return jnp.concatenate(
        (jnp.sum(rows[:cut], axis=0, keepdims=True), jnp.sum(rows[cut:], axis=0, keepdims=True)), 0
    )


def gated_rows(row_mods, g_out, cut):
    rows, width = g_out.shape

    def kernel(gate_ref, g_ref, image_ref, text_ref, sums_ref):
        g = (gate_ref[...].astype(F32) * g_ref[...]).astype(BF)
        image_ref[...] = g[:cut]
        text_ref[...] = g[cut:]
        sums_ref[...] = halves_sum(g.astype(F32), cut)

    outs = [jax.ShapeDtypeStruct((cut, width), BF), jax.ShapeDtypeStruct((rows - cut, width), BF)]
    outs += [jax.ShapeDtypeStruct((2, width), F32)]
    return row_call(kernel, row_mods, (5,), (g_out,), outs)


def middle_rows_back(row_mods, image_sum, text_sum, middle, g_out, branch, picks):
    rows, width = middle.shape
    cut = image_sum.shape[0]

    def kernel(
        gate_ref, scale_ref, image_ref, text_ref, middle_ref, g_ref, branch_ref, picks_ref,
        gmiddle_ref, gimage_ref, gtext_ref, sums_ref, mod_ref, gh_ref,
    ):
        gh_ref[:cut] = image_ref[...]
        gh_ref[cut:] = text_ref[...]
        gh = gh_ref[...]
        n, inverse = normalized(middle_ref[...])
        g_middle = g_ref[...] + norm_back(n, inverse, gh * (1.0 + scale_ref[...].astype(F32)))
        gmiddle_ref[...] = g_middle
        g_branch = (gate_ref[...].astype(F32) * g_middle).astype(BF)
        gimage_ref[...] = g_branch[:cut]
        gtext_ref[...] = g_branch[cut:]
        sums_ref[...] = halves_sum(g_branch.astype(F32), cut)
        for at, part in enumerate((g_middle * branch_ref[...], gh, gh * n)):
            mod_ref[:, at * width : (at + 1) * width] = dot_nn(picks_ref[...], part.astype(BF))

    outs = [jax.ShapeDtypeStruct((rows, width), F32), jax.ShapeDtypeStruct((cut, width), BF)]
    outs += [jax.ShapeDtypeStruct((rows - cut, width), BF), jax.ShapeDtypeStruct((2, width), F32)]
    outs += [jax.ShapeDtypeStruct((picks.shape[0], 3 * width), F32)]
    scratch = jax.ShapeDtypeStruct((rows, width), F32)
    return row_call(
        kernel, row_mods, (2, 4), (image_sum, text_sum, middle, g_out, branch, picks), outs + [scratch]
    )[:5]


def enter_rows_back(row_mods, image_sum, text_sum, x, g_middle, g_out, down, picks):
    rows, width = x.shape
    cut = image_sum.shape[0]

    def kernel(
        scale_ref, image_ref, text_ref, x_ref, gm_ref, g_ref, down_ref, picks_ref, gx_ref, mod_ref, gh_ref
    ):
        gh_ref[:cut] = image_ref[...]
        gh_ref[cut:] = text_ref[...]
        gh = gh_ref[...]
        n, inverse = normalized(x_ref[...])
        gx_ref[...] = gm_ref[...] + norm_back(n, inverse, gh * (1.0 + scale_ref[...].astype(F32)))
        for at, part in enumerate((gh, gh * n, g_ref[...] * down_ref[...])):
            mod_ref[:, at * width : (at + 1) * width] = dot_nn(picks_ref[...], part.astype(BF))

    outs = [jax.ShapeDtypeStruct((rows, width), F32), jax.ShapeDtypeStruct((picks.shape[0], 3 * width), F32)]
    scratch = jax.ShapeDtypeStruct((rows, width), F32)
    return row_call(
        kernel, row_mods, (1,), (image_sum, text_sum, x, g_middle, g_out, down, picks), outs + [scratch]
    )[:2]


def gelu_pair(u):
    c = 0.7978845608028654
    inner = jnp.tanh(c * (u + 0.044715 * u * u * u))
    value = 0.5 * u * (1.0 + inner)
    slope = 0.5 * (1.0 + inner) + 0.5 * u * (1.0 - inner * inner) * c * (1.0 + 3 * 0.044715 * u * u)
    return value.astype(BF), slope.astype(BF)


def shards(
    image_tokens,
    text_tokens,
    conditioning,
    image_seq_ids,
    text_seq_ids,
    ada_weight,
    qkv_weight,
    out_weight,
    up_weight,
    down_weight,
    biases,
    image_cotangent,
    text_cotangent,
):
    section = lax.axis_index("section")
    context = lax.axis_index("context")
    tensor = lax.axis_index("tensor")
    ncontext = lax.axis_size("context")
    ntensor = lax.axis_size("tensor")
    ndev = ncontext * ntensor
    first = section == 0
    micros, own_image, width = image_tokens.shape
    own_text = text_tokens.shape[1]
    seqs = conditioning.shape[1]
    rows_image, rows_text = micros * own_image, micros * own_text
    heads_here = HEADS // ntensor
    local = heads_here * HEAD
    hidden = up_weight.shape[3]
    bias_here = biases.shape[2]
    depth = qkv_weight.shape[2]
    mods = 6 * width
    table_rows = 2 * seqs
    per = ncontext // micros
    micro = context // per
    paired = per == 2 and heads_here % 2 == 0
    groups = 2 if paired else 1
    group_heads = heads_here // groups
    group = group_heads * HEAD
    side = context % per
    ctx_image, ctx_text = ntensor * rows_image, ntensor * rows_text
    ctx_rows = ctx_image + ctx_text

    order = (0, 2, 1, 3)

    def swapped(x, axis, bit):
        return lax.ppermute(x, axis, [(i, i ^ bit) for i in range(lax.axis_size(axis))])

    def sided(a, b):
        return jnp.where(side == 0, a, b), jnp.where(side == 0, b, a)

    def near(x):
        return swapped(x, "tensor", 1)

    def far(x):
        return swapped(x, "tensor", 2)

    def gather_tensor(x):
        beside = near(x)
        across = far(x)
        return x, across, beside, near(across)

    def reduce_tensor(x):
        n = x.shape[0] // 4
        got = near(x[2 * n :])
        mine = x[: 2 * n].astype(F32) + got.astype(F32)
        return mine[:n] + far(mine[n:].astype(BF)).astype(F32)

    def spread_both(image, text):
        return joined(gather_tensor(image), gather_tensor(text))

    def turned_by(x, by):
        return lax.ppermute(x, "context", [(i, (i + by) % ncontext) for i in range(ncontext)])

    def text_gather(rows):
        return [rows] + [turned_by(rows, k) for k in range(1, ncontext)]

    def text_scatter(partial_sums):
        sums = partial_sums.astype(BF).reshape(ncontext, rows_text, width)
        total = sums[0].astype(F32)
        for k in range(1, ncontext):
            total += turned_by(sums[k], -k).astype(F32)
        return total

    def spread_and_gather(image, text):
        return joined(gather_tensor(image)) + joined(text_gather(text))

    def by_tensor(x, axis):
        places = [jnp.array(order)[tensor ^ k] for k in range(ntensor)]
        return jnp.stack([lax.dynamic_index_in_dim(x, at, axis, keepdims=False) for at in places], axis)

    def in_group(x, axis):
        places = [tensor ^ bit for bit in order]
        return jnp.stack([lax.dynamic_index_in_dim(x, at, axis, keepdims=False) for at in places], axis)

    def gather_both(x):
        got = lax.all_gather(x, "tensor")
        got = lax.all_to_all(jnp.broadcast_to(got[None], (ncontext,) + got.shape), "context", 0, 0)
        return got.reshape((ndev,) + x.shape)

    def rounds(step, back):
        pairs = []
        for h in range(ncontext):
            m = (h + step) % micros
            pairs.append((h, m * per + h // micros))
        return [(b, a) for a, b in pairs] if back else pairs

    def to_work(image, text):
        pieces = []
        for step in range(micros):
            m = (context + step) % micros
            pieces.append(
                [
                    lax.ppermute(
                        lax.dynamic_index_in_dim(x, m, 0, keepdims=False), "context", rounds(step, False)
                    )
                    for x in (image, text)
                ]
            )
        return jnp.concatenate([p[0] for p in pieces] + [p[1] for p in pieces], 0).astype(F32)

    def to_home(rows):
        rows = rows.astype(BF)
        pieces = []
        for step in range(micros):
            at, below = step * own_image, rows_image + step * own_text
            both = jnp.concatenate((rows[at : at + own_image], rows[below : below + own_text]), 0)
            pieces.append(lax.ppermute(both, "context", rounds(step, True)))
        pieces = jnp.stack(pieces).astype(F32)
        image, text = pieces[:, :own_image], pieces[:, own_image:]
        turns = [(m - context) % micros for m in range(micros)]
        return tuple(
            jnp.stack([lax.dynamic_index_in_dim(x, turn, 0, keepdims=False) for turn in turns])[None]
            for x in (image, text)
        )

    def gathered(w):
        return lax.all_gather(w, "context", axis=0, tiled=True)

    qkv_full = [gathered(qkv_weight[0, 0])]
    out_full = [gathered(out_weight[0, 0].T)]
    up_full = [gathered(up_weight[0, 0])]
    down_full = [gathered(down_weight[0, 0].T)]

    def ring(w, send_after=None):
        pieces = [w if send_after is None else after(w, send_after)]
        for step in range(1, ncontext):
            pieces.append(lax.ppermute(pieces[-1], "context", [(i, (i + 1) % ncontext) for i in range(ncontext)]))
        return pieces

    def laid(pieces):
        full = jnp.zeros((width, pieces[0].shape[1]), BF)
        for step, piece in enumerate(pieces):
            full = lax.dynamic_update_slice_in_dim(full, piece, (context - step) % ncontext * depth, 0)
        return full

    ring_first = ring(jnp.concatenate((qkv_weight[0, 1], out_weight[0, 1].T), axis=1))
    stage = (ncontext + 2) // 3
    part = hidden // ncontext
    text_sent = jnp.concatenate(
        [w.reshape(ncontext, part, depth) for w in (up_weight[0, 1].T, down_weight[0, 1])], axis=1
    )
    text_moved = lax.all_to_all(after(text_sent, ring_first[-1]), "context", 0, 0)
    feed = []

    cond_float = conditioning.astype(F32)
    silu_cond = jax.nn.silu(cond_float).astype(BF).reshape(micros * seqs, -1)
    ada_part = jnp.einsum("rc,jck->jrk", silu_cond, ada_weight[0], preferred_element_type=F32)
    sharing = [[m * per + u for u in range(per)] for m in range(micros)]
    shares = per * ntensor
    share = mods // shares
    bias_placed = lax.dynamic_update_slice_in_dim(
        jnp.zeros((2, bias_here * ndev), F32),
        biases[0].astype(F32),
        (context * ntensor + tensor) * bias_here,
        1,
    )
    ada_sent = packed(
        ada_part + bias_placed[:, None, :mods],
        jnp.broadcast_to(biases[0].astype(F32)[None], (ndev, 2, bias_here)),
        micros,
        shares,
    )
    ada_got = lax.all_to_all(ada_sent.astype(BF), BOTH, 0, 0)
    bias_full = ada_got[:, table_rows : table_rows + 2, :bias_here].transpose(1, 0, 2).reshape(2, -1).astype(F32)
    ada_sum = jnp.sum(ada_got[:, :table_rows, :share].astype(F32), axis=0).astype(BF)
    table = lax.all_gather(ada_sum, "tensor")
    if paired:
        table = jnp.stack(sided(table, swapped(table, "context", 1)))
    else:
        table = lax.all_gather(table, "context", axis_index_groups=sharing)
    table = after(table, ring_first[stage - 1])
    table = table.reshape(shares, table_rows, share).transpose(1, 0, 2).reshape(table_rows, mods)
    query_bias = lax.dynamic_slice_in_dim(bias_full, mods + tensor * local, local, 1)
    value_bias = lax.dynamic_slice_in_dim(bias_full, mods + width + tensor * local, local, 1)
    qkv_bias = jnp.stack(
        (
            query_bias.reshape(2, heads_here, HEAD),
            jnp.zeros((2, heads_here, HEAD), F32),
            value_bias.reshape(2, heads_here, HEAD),
        ),
        axis=2,
    ).reshape(2, 3 * local)
    out_bias = bias_full[:, mods + 2 * width : mods + 3 * width]
    at_up = mods + 3 * width
    up_bias = lax.dynamic_slice_in_dim(bias_full[0], at_up + tensor * hidden, hidden, 0)
    up_bias_text = bias_full[1, at_up : at_up + ntensor * hidden].reshape(ntensor, ncontext, part)
    up_bias_text = in_group(lax.dynamic_index_in_dim(up_bias_text, context, 1, keepdims=False), 0).reshape(-1)
    down_bias = bias_full[:, mods + 3 * width + hidden * ntensor :]

    def by_modality(pair):
        return jnp.concatenate(
            (
                jnp.broadcast_to(pair[0][None], (rows_image, width)),
                jnp.broadcast_to(pair[1][None], (rows_text, width)),
            ),
            0,
        )

    def ids_of(work_context):
        m, u = work_context // per, work_context % per
        homes = jnp.stack([u * micros + (m - step) % micros for step in range(micros)])
        places = homes[None, :] * ntensor + (tensor ^ jnp.array(order))[:, None]
        found = []
        for ids, own in ((image_seq_ids, own_image), (text_seq_ids, own_text)):
            table_ids = lax.dynamic_index_in_dim(ids, m, 0, keepdims=False).reshape(ndev, own)
            found.append(jnp.take(table_ids, places.reshape(-1), axis=0).reshape(-1))
        return found

    own_found = ids_of(context)
    own_ids = jnp.concatenate((own_found[0][:rows_image], own_found[1][:rows_text] + seqs))
    onehot = (own_ids[:, None] == jnp.arange(table_rows)[None, :]).astype(BF)
    row_mods = dot_nn(onehot, table).astype(BF)
    picks = onehot.T
    joint_ids = jnp.concatenate(own_found)
    if paired:
        attn_ids = jnp.concatenate([joint_ids] + ids_of(context ^ 1))
    else:
        attn_ids = jnp.concatenate([x for u in range(per) for x in ids_of(micro * per + u)])

    def row_mod(index):
        return row_mods[:, index * width : (index + 1) * width].astype(F32)

    def attention(joint):
        if paired:
            mine, theirs = sided(joint[: 3 * group], joint[3 * group :])
            theirs = swapped(theirs, "context", 1)
            here, there, lse = attend_pair(mine, theirs, attn_ids, group_heads)
            return jnp.concatenate(sided(here, swapped(there, "context", 1)), axis=0), (mine, theirs, lse)
        by_kind = joint.reshape(heads_here, 3, HEAD, ctx_rows)
        q, k, v = (by_kind[:, i].reshape(local, ctx_rows).T for i in range(3))
        k, v = (
            lax.all_gather(x, "context", axis=0, tiled=True, axis_index_groups=sharing) for x in (k, v)
        )
        attended, lse = attend(q, k, v, joint_ids, attn_ids, group_heads)
        return attended.T, (q, k, v, lse)

    def attention_back(grad, kept):
        if paired:
            mine, theirs, lse = kept
            g_mine, g_theirs = sided(grad[:group], grad[group:])
            g_theirs = swapped(g_theirs, "context", 1)
            d_mine, d_theirs = attend_pair_back(mine, theirs, g_mine, g_theirs, lse, attn_ids, group_heads)
            return jnp.concatenate(sided(d_mine, swapped(d_theirs, "context", 1)), axis=0)
        q, k, v, lse = kept
        dq, dk, dv = attend_back(q, k, v, grad.T, lse, joint_ids, attn_ids, group_heads)
        dk, dv = (
            lax.psum_scatter(x, "context", scatter_dimension=0, tiled=True, axis_index_groups=sharing)
            for x in (dk, dv)
        )
        kinds = [x.T.reshape(heads_here, HEAD, ctx_rows) for x in (dq, dk, dv)]
        return jnp.stack(kinds, axis=1).reshape(3 * local, ctx_rows)

    def forward(x, late=False):
        h1_image, h1_text = enter_rows(row_mods, x, rows_image)
        fresh = len(qkv_full) == 1
        if fresh:
            h1_image = after(h1_image, ring_first[2 * stage - 2])
            full = laid(ring_first)
            qkv_full.append(full[:, : 3 * local])
            out_full.append(full[:, 3 * local :])
        h1 = spread_both(h1_image, h1_text)
        joint = jnp.concatenate(
            [(dot_tt(qkv_full[j], h1[j]) + qkv_bias[j][:, None]).astype(BF) for j in range(2)], axis=1
        )
        attended, kept = attention(joint)
        if fresh:
            attended = after(attended, text_moved)
            moved = gather_tensor(text_moved.transpose(1, 0, 2).reshape(2 * part, width))
            feed.append(jnp.concatenate([b[:part] for b in moved], 0))
            feed.append(jnp.concatenate([b[part:] for b in moved], 0))
        image_sum = reduce_tensor(dot_tt(attended, out_full[0])[:ctx_image].astype(BF))
        text_sum = reduce_tensor(dot_tt(attended[:, ctx_image:], out_full[1]).astype(BF))
        if fresh:
            image_sum = after(image_sum, *feed)
        branch, middle, h2_image, h2_text = middle_rows(row_mods, x, image_sum, text_sum, out_bias)
        up_text, down_text = feed
        h2 = spread_and_gather(h2_image, h2_text)
        pairs = [
            gelu_pair(dot_nn(h2[0], up_full[0]) + up_bias),
            gelu_pair(dot_nt(h2[1], up_text) + up_bias_text),
        ]
        acts, slopes = [p[0] for p in pairs], [p[1] for p in pairs]
        saved = dict(
            x=x, h1=h1, kept=kept, attn=attended, branch=branch, middle=middle, h2=h2, acts=acts,
            slopes=slopes,
        )

        def finish(gate):
            if gate is not None:
                saved["acts"] = [after(act, gate) for act in acts]
            down = jnp.concatenate(
                (
                    reduce_tensor(dot_nt(saved["acts"][0], down_full[0]).astype(BF)),
                    text_scatter(dot_nn(saved["acts"][1], down_text)),
                ),
                0,
            ) + by_modality(down_bias)
            saved["down"] = down
            saved["out"] = middle + row_mod(5) * down

        saved["finish"] = finish
        if not late:
            finish(None)
        return saved

    def chosen(a, b):
        return jax.tree.map(lambda x, y: jnp.where(first, x, y), a, b)

    def scattered(full):
        return lax.psum_scatter(full.astype(BF), "context", scatter_dimension=0, tiled=True)

    def backward(saved, g_out, last=None):
        gd_image, gd_text, gd_sums = gated_rows(row_mods, g_out, rows_image)
        up_text, down_text = feed
        gd = spread_and_gather(gd_image, gd_text)
        g_up = [
            (dot_nn(gd[0], down_full[0]) * saved["slopes"][0].astype(F32)).astype(BF),
            (dot_nt(gd[1], down_text) * saved["slopes"][1].astype(F32)).astype(BF),
        ]
        g_h2_image = reduce_tensor(dot_nt(g_up[0], up_full[0]).astype(BF))
        g_h2_text = text_scatter(dot_nn(g_up[1], up_text))
        early = []
        if last:
            use = chosen(
                dict(h2=saved["h2"][0], acts=saved["acts"][0], gd=gd[0], g_up=g_up[0]),
                {k: last[k][0] for k in ("h2", "acts", "gd", "g_up")},
            )
            early = [
                dot_tn(use["gd"], use["acts"]).astype(BF),
                dot_tn(use["h2"], use["g_up"]).astype(BF),
            ]
            g_h2_image = after(g_h2_image, *early)
            early = [scattered(part) for part in early]
        g_middle, gb_image, gb_text, gb_sums, mod_late = middle_rows_back(
            row_mods, g_h2_image, g_h2_text, saved["middle"], g_out, saved["branch"], picks
        )
        gb = spread_both(gb_image, gb_text)
        if "down" not in saved:
            saved["finish"](gb[0])
        g_attn = jnp.concatenate([dot_tt(out_full[j], gb[j]).astype(BF) for j in range(2)], axis=1)
        if last:
            use = chosen(dict(gb=gb[0], attn=saved["attn"]), dict(gb=last["gb"][0], attn=last["attn"]))
            early.append(dot_tt(use["gb"], use["attn"][:, :ctx_image]).astype(BF))
            g_attn = after(g_attn, early[2])
        g_joint = attention_back(g_attn, saved["kept"])
        g_h1_image = reduce_tensor(dot_tt(g_joint, qkv_full[0])[:ctx_image].astype(BF))
        g_h1_text = reduce_tensor(dot_tt(g_joint[:, ctx_image:], qkv_full[1]).astype(BF))
        if last:
            use = chosen(dict(h1=saved["h1"][0], g=g_joint), dict(h1=last["h1"][0], g=last["g_joint"]))
            early.append(dot_tt(use["h1"], use["g"][:, :ctx_image]).astype(BF))
            g_h1_image = after(g_h1_image, early[3])
        g_x, mod_early = enter_rows_back(
            row_mods, g_h1_image, g_h1_text, saved["x"], g_middle, g_out, saved["down"], picks
        )
        if last:
            g_x = after(g_x, *early[:2])
        mod_grad = jnp.concatenate((mod_early[:, : 2 * width], mod_late, mod_early[:, 2 * width :]), axis=1)
        tensors = dict(
            h1=saved["h1"], attn=saved["attn"], h2=saved["h2"], acts=saved["acts"], g_joint=g_joint,
            gb=gb, g_up=g_up, gd=gd, gd_sums=gd_sums, gb_sums=gb_sums, mod=mod_grad,
        )
        return g_x, tensors, early

    aligned = part % 128 == 0 and depth % 128 == 0 and local % 128 == 0 and ncontext == ntensor
    offsets = tensor ^ jnp.arange(ntensor, dtype=jnp.int32)
    places = jnp.concatenate(((offsets & 1) * 2 + offsets // 2, context.reshape(1).astype(jnp.int32)))

    own_context = context.reshape(1).astype(jnp.int32)

    def tensor_round(hidden_rows, wide_rows):
        if aligned:
            sent = tensor_packed(places, hidden_rows, wide_rows, part, depth, ncontext)
        else:
            back = (context - jnp.arange(ncontext)) % ncontext
            hidden_rows, wide_rows = (
                jnp.take(x.reshape(ncontext, rows_text, -1), back, axis=0).reshape(x.shape)
                for x in (hidden_rows, wide_rows)
            )
            pieces = by_tensor(hidden_rows.reshape(hidden_rows.shape[0], ntensor, part), 1).transpose(1, 0, 2)
            own = lax.dynamic_slice_in_dim(wide_rows, context * depth, depth, 1)
            sent = jnp.concatenate((pieces, jnp.broadcast_to(own[None], (ntensor,) + own.shape)), axis=2)
        return lax.all_to_all(sent, "tensor", 0, 0)

    def context_round(blocked, turned, stacked):
        if aligned:
            sent = text_packed(own_context, blocked, turned, stacked, part, ncontext)
            return [turned_by(x, k) if k else x for k, x in enumerate(sent)]
        parts = [x.reshape(x.shape[0], ncontext, -1).transpose(1, 0, 2) for x in blocked]
        parts += [jnp.broadcast_to(x.T[None], (ncontext,) + x.T.shape) for x in turned]
        stacks = [x[:, :, :part].transpose(1, 0, 2).reshape(x.shape[1], -1) for x in stacked]
        stacks = [jnp.broadcast_to(x[None], (ncontext,) + x.shape) for x in stacks]
        return [
            lax.all_to_all(jnp.concatenate(group, axis=2), "context", 0, 0) for group in (parts, stacks) if group
        ]

    def handed(rows, by):
        return lax.ppermute(rows.astype(BF), "section", [(0, 1)] if by > 0 else [(1, 0)]).astype(F32)

    saved_first = forward(to_work(image_tokens, text_tokens))
    saved_last = forward(handed(saved_first["out"], 1), late=True)
    grad_last, tensors_last, unused = backward(saved_last, to_work(image_cotangent, text_cotangent))
    kept = chosen(
        [saved_first[n][1] for n in ("acts", "h1", "h2")] + [saved_first["attn"][:, ctx_image:]],
        [saved_last[n][1] for n in ("acts", "h1", "h2")] + [saved_last["attn"][:, ctx_image:]],
    )
    kept[0] = after(kept[0], tensors_last["g_joint"])
    ours_before = tensor_round(kept[0], kept[2])
    got_before = context_round([kept[1]], [kept[3]], [ours_before])
    out = to_home(after(jnp.where(first, saved_first["out"], saved_last["out"]), tensors_last["g_joint"]))
    returned = after(handed(grad_last, -1), *got_before, *out)
    grad_first, tensors_first, early = backward(saved_first, returned, tensors_last)
    grad = to_home(jnp.where(first, grad_first, grad_last))
    use = chosen(tensors_first, tensors_last)

    down_shard, up_shard, out_part, qkv_part = early
    rows_shard = after(scattered(jnp.concatenate((out_part, qkv_part), axis=1)), grad_first)

    ours_after = tensor_round(use["g_up"][1], use["gd"][1])

    def column_sums(parts):
        return jnp.stack([dot_nn(jnp.ones((8, p.shape[0]), BF), p)[0] for p in parts])

    qkv_sums = jnp.stack(
        [
            dot_nt(jnp.ones((8, part.shape[1]), BF), part)[0]
            for part in (use["g_joint"][:, :ctx_image], use["g_joint"][:, ctx_image:])
        ]
    ).reshape(2, heads_here, 3, HEAD)
    up_sums_text = lax.dynamic_update_slice_in_dim(
        jnp.zeros((ntensor, ncontext, part), F32),
        by_tensor(column_sums((use["g_up"][1],)).reshape(ntensor, 1, part), 0),
        context,
        1,
    ).reshape(1, -1)
    up_sums_image = lax.dynamic_update_slice_in_dim(
        jnp.zeros((1, ntensor * hidden), F32), column_sums((use["g_up"][0],)), tensor * hidden, 1
    )
    rest = jnp.zeros((2, bias_here * ndev - mods), F32)
    for at, value in (
        (tensor * local, qkv_sums[:, :, 0].reshape(2, local)),
        (width + tensor * local, qkv_sums[:, :, 2].reshape(2, local)),
        (2 * width, use["gb_sums"]),
        (3 * width, jnp.concatenate((up_sums_image, up_sums_text), 0)),
        (3 * width + ntensor * hidden, use["gd_sums"]),
    ):
        rest = lax.dynamic_update_slice_in_dim(rest, value, at, 1)
    if aligned:
        sent = tail_packed(micro.astype(jnp.int32), use["mod"], rest, micros, shares)
    else:
        bias_part = jnp.concatenate((jnp.sum(use["mod"].reshape(2, seqs, mods), axis=1), rest), axis=1)
        mod_sent = use["mod"].reshape(2, 1, seqs, mods)
        mod_sent = jnp.where(jnp.arange(micros)[None, :, None, None] == micro, mod_sent, 0.0)
        bias_sent = bias_part.reshape(2, ndev, bias_here).transpose(1, 0, 2)
        sent = packed(mod_sent.reshape(2, micros * seqs, mods), bias_sent, micros, shares).astype(BF)
    sent = after(sent, ours_after)
    got = jnp.sum(lax.all_to_all(sent, BOTH, 0, 0).astype(F32), axis=0)
    bias_grad = got[table_rows:, :bias_here]
    mod_all = (
        gather_both(got[:table_rows, :share].astype(BF))
        .reshape(micros, shares, 2, seqs, share)
        .transpose(2, 0, 3, 1, 4)
        .reshape(2, micros * seqs, mods)
    )
    if aligned:
        down_grad = finish_hidden(own_context, down_shard, got_before, depth + local, ours_after, part, True)
        mod_all = after(mod_all, down_grad, *grad)
    ada_grad = jnp.einsum("rc,jrk->jck", silu_cond, mod_all, preferred_element_type=F32)
    cond_inner = jnp.einsum("jrk,jck->rc", mod_all, ada_weight[0], preferred_element_type=F32)
    got_after = context_round([after(use["gb"][1], mod_all)], [], [ours_after])
    got_qkv = context_round([], [after(use["g_joint"][:, ctx_image:], mod_all)], [])
    if aligned:
        up_grad = finish_hidden(own_context, up_shard, got_after, depth, ours_before, part, False)
        out_grad = finish_rows(rows_shard, 0, got_before, (depth, depth + local), got_after, (0, depth), True)
        qkv_grad = finish_rows(rows_shard, local, got_before, (0, depth), got_qkv, (0, 3 * local), False)
    else:
        acts_all = got_before[1].reshape(ncontext, -1, ntensor, part)
        g_up_all = got_after[1].reshape(ncontext, -1, ntensor, part)
        text_down = jnp.einsum("crtj,trd->cjd", acts_all, ours_after[:, :, part:], preferred_element_type=F32)
        text_up = jnp.einsum("trk,crtj->kcj", ours_before[:, :, part:], g_up_all, preferred_element_type=F32)
        text_out = jnp.einsum(
            "crh,crd->hd", got_before[0][:, :, depth:], got_after[0], preferred_element_type=F32
        )
        text_qkv = jnp.einsum("crk,crh->kh", got_before[0][:, :, :depth], got_qkv[0], preferred_element_type=F32)
        down_grad = jnp.stack((down_shard.astype(F32).T, text_down.reshape(hidden, depth)))
        up_grad = jnp.stack((up_shard.astype(F32), text_up.reshape(depth, hidden)))
        out_grad = jnp.stack((rows_shard[:, :local].astype(F32).T, text_out))
        qkv_grad = jnp.stack((rows_shard[:, local:].astype(F32), text_qkv))
    unused, silu_back = jax.vjp(jax.nn.silu, cond_float)
    cond_inner = cond_inner + lax.ppermute(cond_inner, "section", [(0, 1), (1, 0)])
    cond_grad = silu_back(cond_inner.reshape(cond_float.shape))[0]
    return (
        *out,
        *grad,
        cond_grad,
        ada_grad[None],
        qkv_grad[None],
        out_grad[None],
        up_grad[None],
        down_grad[None],
        bias_grad[None],
    )


def solution(mesh):
    tokens = P(None, BOTH, None)
    block_rows = P("section", None, BOTH, None)
    by_rows = P("section", None, "context", "tensor")
    by_cols = P("section", None, "tensor", "context")
    block_biases = P("section", None, BOTH)
    in_specs = (
        tokens,
        tokens,
        P(None, None, BOTH),
        P(),
        P(),
        block_rows,
        by_rows,
        by_cols,
        by_rows,
        by_cols,
        block_biases,
        tokens,
        tokens,
    )
    out_specs = (
        block_rows,
        block_rows,
        block_rows,
        block_rows,
        P(None, None, BOTH),
        block_rows,
        by_rows,
        by_cols,
        by_rows,
        by_cols,
        block_biases,
    )
    return jax.shard_map(shards, mesh=mesh, in_specs=in_specs, out_specs=out_specs, check_vma=False)
```

```python
from functools import partial

import jax
import jax.numpy as jnp
from jax import lax
from jax.experimental import pallas as pl
from jax.experimental.pallas import tpu as pltpu
from jax.sharding import PartitionSpec as P

HEADS = 24
HEAD = 64
NORM_EPS = 1e-06
MASKED = -1e30
BF = jnp.bfloat16
F32 = jnp.float32
BOTH = ("context", "tensor")


def dot_nn(a, b):
    return lax.dot_general(a, b, (((1,), (0,)), ((), ())), preferred_element_type=F32)


def dot_nt(a, b):
    return lax.dot_general(a, b, (((1,), (1,)), ((), ())), preferred_element_type=F32)


def dot_tn(a, b):
    return lax.dot_general(a, b, (((0,), (0,)), ((), ())), preferred_element_type=F32)


def dot_tt(a, b):
    return lax.dot_general(a, b, (((0,), (1,)), ((), ())), preferred_element_type=F32)


def scaled(q):
    return q * jnp.asarray(HEAD**-0.5, BF)


def attend_body(heads, chunk, places, q_ref, k_ref, v_ref, idq_ref, idk_ref, store, lse_ref):
    at_q, at_k, at_v = places

    def one_chunk(step, carry):
        rows = pl.ds(pl.multiple_of(step * chunk, chunk), chunk)
        bias = jnp.where(idk_ref[...] == idq_ref[:, rows], 0.0, MASKED)
        outs = []
        for head in range(heads):
            at = head * HEAD
            q = scaled(q_ref[rows, at_q + at : at_q + at + HEAD])
            scores = dot_nt(k_ref[:, at_k + at : at_k + at + HEAD], q) + bias
            top = jnp.max(scores, axis=0, keepdims=True)
            weights = jnp.exp(scores - top)
            total = jnp.sum(weights, axis=0, keepdims=True)
            summed = dot_tn(v_ref[:, at_v + at : at_v + at + HEAD], weights.astype(BF))
            outs.append((summed / total).T)
            lse_ref[head : head + 1, rows] = top + jnp.log(total)
        store(rows, jnp.concatenate(outs, axis=1).astype(BF))
        return carry

    lax.fori_loop(0, idq_ref.shape[1] // chunk, one_chunk, 0)


def attend_back_body(
    heads, chunk, places, q_ref, k_ref, v_ref, g_ref, lse_ref, idq_ref, idk_ref, store_dq, dk_acc, dv_acc
):
    at_q, at_k, at_v = places
    dk_acc[...] = jnp.zeros_like(dk_acc)
    dv_acc[...] = jnp.zeros_like(dv_acc)

    def one_chunk(step, carry):
        rows = pl.ds(pl.multiple_of(step * chunk, chunk), chunk)
        bias = jnp.where(idk_ref[...] == idq_ref[:, rows], 0.0, MASKED)
        grads = []
        for head in range(heads):
            at = head * HEAD
            q = scaled(q_ref[rows, at_q + at : at_q + at + HEAD])
            g = g_ref[rows, at : at + HEAD]
            k = k_ref[:, at_k + at : at_k + at + HEAD]
            probs = jnp.exp(dot_nt(k, q) + bias - lse_ref[head : head + 1, rows])
            dv_acc[head] += dot_nn(probs.astype(BF), g)
            both = probs * dot_nt(v_ref[:, at_v + at : at_v + at + HEAD], g)
            delta = jnp.sum(both, axis=0, keepdims=True)
            dscores = (both - probs * delta).astype(BF)
            dk_acc[head] += dot_nn(dscores, q)
            grads.append((dot_tn(k, dscores) * HEAD**-0.5).T)
        store_dq(rows, jnp.concatenate(grads, axis=1).astype(BF))
        return carry

    lax.fori_loop(0, idq_ref.shape[1] // chunk, one_chunk, 0)


def heads_of(acc):
    return jnp.concatenate([acc[head] for head in range(acc.shape[0])], axis=1).astype(BF)


def attend_costs(queries, keys, heads, factor):
    return pl.CostEstimate(
        flops=factor * queries * keys * heads * HEAD,
        bytes_accessed=2 * (queries + 2 * keys) * heads * HEAD * factor // 4,
        transcendentals=queries * keys * heads,
    )


def chunk_for(keys):
    return 256 if keys <= 1024 else 128


VMEM_LIMIT = pltpu.CompilerParams(vmem_limit_bytes=56 * 2**20)


def attend(q, k, v, ids_q, ids_k, heads):
    queries, keys = q.shape[0], k.shape[0]

    def kernel(q_ref, k_ref, v_ref, idq_ref, idk_ref, out_ref, lse_ref):
        def store(rows, value):
            out_ref[rows, :] = value

        attend_body(
            heads, chunk_for(keys), (0, 0, 0), q_ref, k_ref, v_ref, idq_ref, idk_ref, store, lse_ref
        )

    return pl.pallas_call(
        kernel,
        out_shape=(
            jax.ShapeDtypeStruct((queries, heads * HEAD), BF),
            jax.ShapeDtypeStruct((heads, queries), F32),
        ),
        compiler_params=VMEM_LIMIT,
        cost_estimate=attend_costs(queries, keys, heads, 4),
    )(q, k, v, ids_q.reshape(1, queries), ids_k.reshape(keys, 1))


def attend_back(q, k, v, g, lse, ids_q, ids_k, heads):
    queries, keys = q.shape[0], k.shape[0]

    def kernel(
        q_ref, k_ref, v_ref, g_ref, lse_ref, idq_ref, idk_ref, dq_ref, dk_ref, dv_ref, dk_acc, dv_acc
    ):
        def store(rows, value):
            dq_ref[rows, :] = value

        attend_back_body(
            heads, chunk_for(keys), (0, 0, 0), q_ref, k_ref, v_ref, g_ref, lse_ref, idq_ref, idk_ref,
            store, dk_acc, dv_acc,
        )
        dk_ref[...] = heads_of(dk_acc)
        dv_ref[...] = heads_of(dv_acc)

    return pl.pallas_call(
        kernel,
        out_shape=(
            jax.ShapeDtypeStruct((queries, heads * HEAD), BF),
            jax.ShapeDtypeStruct((keys, heads * HEAD), BF),
            jax.ShapeDtypeStruct((keys, heads * HEAD), BF),
        ),
        scratch_shapes=[pltpu.VMEM((heads, keys, HEAD), F32), pltpu.VMEM((heads, keys, HEAD), F32)],
        compiler_params=VMEM_LIMIT,
        cost_estimate=attend_costs(queries, keys, heads, 10),
    )(q, k, v, g, lse, ids_q.reshape(1, queries), ids_k.reshape(keys, 1))


def attend_pair(mine, theirs, ids, heads):
    wide, half = mine.shape
    rows_all, group = 2 * half, heads * HEAD
    chunk = 256

    def kernel(mine_ref, theirs_ref, idq_ref, idk_ref, here_ref, there_ref, lse_ref, x_ref, out_ref):
        x_ref[:, :half] = mine_ref[...]
        x_ref[:, half:] = theirs_ref[...]

        def one_chunk(step, carry):
            rows = pl.ds(pl.multiple_of(step * chunk, chunk), chunk)
            bias = jnp.where(idk_ref[...] == idq_ref[:, rows], 0.0, MASKED)
            for head in range(heads):
                at = slice(head * HEAD, (head + 1) * HEAD)
                base = 3 * head * HEAD
                q = scaled(x_ref[base : base + HEAD, rows])
                k = x_ref[base + HEAD : base + 2 * HEAD, :]
                v = x_ref[base + 2 * HEAD : base + 3 * HEAD, :]
                scores = dot_tn(k, q) + bias
                top = jnp.max(scores, axis=0, keepdims=True)
                weights = jnp.exp(scores - top)
                total = jnp.sum(weights, axis=0, keepdims=True)
                out_ref[at, rows] = (dot_nn(v, weights.astype(BF)) / total).astype(BF)
                lse_ref[head : head + 1, rows] = top + jnp.log(total)
            return carry

        lax.fori_loop(0, rows_all // chunk, one_chunk, 0)
        here_ref[...] = out_ref[:, :half]
        there_ref[...] = out_ref[:, half:]

    return pl.pallas_call(
        kernel,
        out_shape=(
            jax.ShapeDtypeStruct((group, half), BF),
            jax.ShapeDtypeStruct((group, half), BF),
            jax.ShapeDtypeStruct((heads, rows_all), F32),
        ),
        scratch_shapes=[pltpu.VMEM((wide, rows_all), BF), pltpu.VMEM((group, rows_all), BF)],
        compiler_params=VMEM_LIMIT,
        cost_estimate=attend_costs(rows_all, rows_all, heads, 4),
    )(mine, theirs, ids.reshape(1, rows_all), ids.reshape(rows_all, 1))


def attend_pair_back(mine, theirs, g_mine, g_theirs, lse, ids, heads):
    wide, half = mine.shape
    rows_all, group = 2 * half, heads * HEAD
    chunk = 256

    def kernel(
        mine_ref, theirs_ref, gm_ref, gt_ref, lse_ref, idq_ref, idk_ref, dmine_ref, dtheirs_ref,
        x_ref, g_ref, dq_ref, dk_ref, dv_ref,
    ):
        x_ref[:, :half] = mine_ref[...]
        x_ref[:, half:] = theirs_ref[...]
        g_ref[:, :half] = gm_ref[...]
        g_ref[:, half:] = gt_ref[...]
        dk_ref[...] = jnp.zeros_like(dk_ref)
        dv_ref[...] = jnp.zeros_like(dv_ref)

        def one_chunk(step, carry):
            rows = pl.ds(pl.multiple_of(step * chunk, chunk), chunk)
            bias = jnp.where(idk_ref[...] == idq_ref[:, rows], 0.0, MASKED)
            for head in range(heads):
                at = slice(head * HEAD, (head + 1) * HEAD)
                base = 3 * head * HEAD
                q = scaled(x_ref[base : base + HEAD, rows])
                g = g_ref[at, rows]
                k = x_ref[base + HEAD : base + 2 * HEAD, :]
                v = x_ref[base + 2 * HEAD : base + 3 * HEAD, :]
                probs = jnp.exp(dot_tn(k, q) + bias - lse_ref[head : head + 1, rows])
                dv_ref[at, :] += dot_nt(g, probs.astype(BF))
                both = probs * dot_tn(v, g)
                delta = jnp.sum(both, axis=0, keepdims=True)
                dscores = (both - probs * delta).astype(BF)
                dk_ref[at, :] += dot_nt(q, dscores)
                dq_ref[at, rows] = (dot_nn(k, dscores) * HEAD**-0.5).astype(BF)
            return carry

        lax.fori_loop(0, rows_all // chunk, one_chunk, 0)
        for out_ref, cols in ((dmine_ref, slice(0, half)), (dtheirs_ref, slice(half, rows_all))):
            for head in range(heads):
                at = slice(head * HEAD, (head + 1) * HEAD)
                base = 3 * head * HEAD
                out_ref[base : base + HEAD, :] = dq_ref[at, cols]
                out_ref[base + HEAD : base + 2 * HEAD, :] = dk_ref[at, cols].astype(BF)
                out_ref[base + 2 * HEAD : base + 3 * HEAD, :] = dv_ref[at, cols].astype(BF)

    return pl.pallas_call(
        kernel,
        out_shape=(jax.ShapeDtypeStruct((wide, half), BF), jax.ShapeDtypeStruct((wide, half), BF)),
        scratch_shapes=[
            pltpu.VMEM((wide, rows_all), BF),
            pltpu.VMEM((group, rows_all), BF),
            pltpu.VMEM((group, rows_all), BF),
            pltpu.VMEM((group, rows_all), F32),
            pltpu.VMEM((group, rows_all), F32),
        ],
        compiler_params=VMEM_LIMIT,
        cost_estimate=attend_costs(rows_all, rows_all, heads, 10),
    )(mine, theirs, g_mine, g_theirs, lse, ids.reshape(1, rows_all), ids.reshape(rows_all, 1))


def after(x, *others):
    anywhere = pl.BlockSpec(memory_space=pl.ANY)

    def kernel(*refs):
        pass

    return pl.pallas_call(
        kernel,
        out_shape=jax.ShapeDtypeStruct(x.shape, x.dtype),
        in_specs=[anywhere] * (1 + len(others)),
        out_specs=anywhere,
        input_output_aliases={0: 0},
    )(x, *others)


def lanes(n):
    return -(-n // 128) * 128


def packed(sums, rest, groups_of, shares):
    rows, columns = sums.shape[1], sums.shape[2]
    seqs, share, extra = rows // groups_of, columns // shares, rest.shape[2]
    wide = lanes(max(share, extra))

    def kernel(sums_ref, rest_ref, out_ref):
        for group in range(groups_of):
            for j in range(2):
                out_ref[group, 0, j * seqs : (j + 1) * seqs, :share] = sums_ref[
                    j, group * seqs : (group + 1) * seqs, :
                ]
            out_ref[group, 0, 2 * seqs : 2 * seqs + 2, :extra] = rest_ref[group, 0]

    if share % 128 == 0:
        sums_in, sums_spec = sums, pl.BlockSpec((2, rows, share), lambda k: (0, 0, k))
    else:
        sums_in = sums.reshape(2, rows, shares, share).transpose(2, 0, 1, 3)
        sums_spec = pl.BlockSpec((None, 2, rows, share), lambda k: (k, 0, 0, 0))
    out = pl.pallas_call(
        kernel,
        grid=(shares,),
        in_specs=[sums_spec, pl.BlockSpec((groups_of, 1, 2, extra), lambda k: (0, k, 0, 0))],
        out_specs=pl.BlockSpec((groups_of, 1, 8, wide), lambda k: (0, k, 0, 0)),
        out_shape=jax.ShapeDtypeStruct((groups_of, shares, 8, wide), F32),
    )(sums_in, rest.reshape(groups_of, shares, 2, extra))
    return out.reshape(groups_of * shares, 8, wide)


def joined(*groups):
    sizes = [len(group) for group in groups]

    def kernel(*refs):
        taken = 0
        for out_ref, size in zip(refs[sum(sizes) :], sizes):
            at = 0
            for ref in refs[taken : taken + size]:
                out_ref[at : at + ref.shape[0], :] = ref[...]
                at += ref.shape[0]
            taken += size

    outs = [
        jax.ShapeDtypeStruct((sum(x.shape[0] for x in group), group[0].shape[1]), group[0].dtype)
        for group in groups
    ]
    return pl.pallas_call(kernel, out_shape=tuple(outs), compiler_params=VMEM_LIMIT)(
        *[x for group in groups for x in group]
    )


def text_packed(context, blocked, turned, stacked, part, count):
    rows = blocked[0].shape[0] if blocked else turned[0].shape[1]
    widths = [x.shape[1] // count for x in blocked] + [x.shape[0] for x in turned]
    widths += [x.shape[0] * part for x in stacked]
    nblocked, nturned = len(blocked), len(turned)
    ninputs = nblocked + nturned + len(stacked)

    def kernel(context_ref, *refs):
        ins, outs = refs[:ninputs], refs[ninputs:]
        at = 0
        for i, ref in enumerate(ins):
            wide = widths[i]
            if i < nblocked:
                for k in range(count):
                    lane = pl.multiple_of((context_ref[0] + k) % count * wide, 128)
                    outs[k][:, at : at + wide] = ref[:, pl.ds(lane, wide)]
            elif i < nblocked + nturned:
                value = ref[...].astype(F32).T.astype(BF)
                for k in range(count):
                    outs[k][:, at : at + wide] = value
            else:
                for t in range(ref.shape[0]):
                    for k in range(count):
                        outs[k][:, at + t * part : at + (t + 1) * part] = ref[t, :, :part]
            at += wide

    return pl.pallas_call(
        kernel,
        in_specs=[pl.BlockSpec(memory_space=pltpu.SMEM)] + [pl.BlockSpec(memory_space=pltpu.VMEM)] * ninputs,
        out_shape=tuple([jax.ShapeDtypeStruct((rows, sum(widths)), BF)] * count),
        compiler_params=VMEM_LIMIT,
    )(context, *blocked, *turned, *stacked)


def tensor_packed(places, hidden_rows, wide_rows, part, depth, count):
    tensors = places.shape[0] - 1
    rows = hidden_rows.shape[0]
    own = rows // count

    def kernel(places_ref, hidden_ref, wide_ref, out_ref):
        context = places_ref[tensors]
        lane = pl.multiple_of(context * depth, 128)
        for j in range(count):
            source = pl.ds(pl.multiple_of((context + count - j) % count * own, own), own)
            here = slice(j * own, (j + 1) * own)
            columns = wide_ref[source, pl.ds(lane, depth)]
            for k in range(tensors):
                at = pl.multiple_of(places_ref[k] * part, 128)
                out_ref[k, here, :part] = hidden_ref[source, pl.ds(at, part)]
                out_ref[k, here, part:] = columns

    return pl.pallas_call(
        kernel,
        in_specs=[pl.BlockSpec(memory_space=pltpu.SMEM)] + [pl.BlockSpec(memory_space=pltpu.VMEM)] * 2,
        out_shape=jax.ShapeDtypeStruct((tensors, rows, part + depth), BF),
    )(places, hidden_rows, wide_rows)


def tail_packed(micro, mod, rest, groups_of, shares):
    rows, mods = mod.shape
    share, seqs = mods // shares, rows // 2
    extra = (mods + rest.shape[1]) // (groups_of * shares)
    wide = lanes(max(share, extra))

    def kernel(micro_ref, mod_ref, rest_ref, out_ref, bias_ref, piece_ref):
        for j in range(2):
            bias_ref[j : j + 1, :mods] = jnp.sum(mod_ref[j * seqs : (j + 1) * seqs, :], axis=0, keepdims=True)
        bias_ref[:, mods:] = rest_ref[...]
        piece_ref[...] = jnp.zeros_like(piece_ref)
        for group in range(groups_of):
            mine = jnp.where(micro_ref[0] == group, 1.0, 0.0)
            for k in range(shares):
                device = group * shares + k
                piece_ref[device, :rows, :share] = mod_ref[:, k * share : (k + 1) * share] * mine
                piece_ref[device, rows : rows + 2, :extra] = bias_ref[:, device * extra : (device + 1) * extra]
        out_ref[...] = piece_ref[...].astype(BF)

    return pl.pallas_call(
        kernel,
        in_specs=[pl.BlockSpec(memory_space=pltpu.SMEM)] + [pl.BlockSpec(memory_space=pltpu.VMEM)] * 2,
        out_shape=jax.ShapeDtypeStruct((groups_of * shares, 8, wide), BF),
        scratch_shapes=[
            pltpu.VMEM((2, mods + rest.shape[1]), F32),
            pltpu.VMEM((groups_of * shares, 8, wide), F32),
        ],
    )(micro.reshape(1), mod, rest)


def finish_hidden(context, shard, got, at, cols, part, turned):
    depth, hidden = shard.shape
    count, tensors = len(got), cols.shape[0]
    shape = (2, hidden, depth) if turned else (2, depth, hidden)

    def kernel(context_ref, shard_ref, cols_ref, *refs):
        out_ref = refs[-1]
        image = shard_ref[...].astype(F32)
        out_ref[0] = image.T if turned else image
        for k in range(count):
            block = pl.ds(pl.multiple_of((context_ref[0] + count - k) % count * part, 128), part)
            total = 0.0
            for t in range(tensors):
                lane = at + t * part
                pair = (refs[k][:, lane : lane + part], cols_ref[t, :, part:])
                total += dot_tn(*pair) if turned else dot_tn(*pair[::-1])
            if turned:
                out_ref[1, block, :] = total
            else:
                out_ref[1, :, block] = total

    return pl.pallas_call(
        kernel,
        in_specs=[pl.BlockSpec(memory_space=pltpu.SMEM)]
        + [pl.BlockSpec(memory_space=pltpu.VMEM)] * (2 + count),
        out_shape=jax.ShapeDtypeStruct(shape, F32),
        compiler_params=VMEM_LIMIT,
    )(context, shard, cols, *got)


def finish_rows(shard, at, left_got, left, right_got, right, turned):
    m, n = left[1] - left[0], right[1] - right[0]
    count = len(left_got)

    def kernel(shard_ref, *refs):
        out_ref = refs[-1]
        image = shard_ref[:, at : at + (m if turned else n)].astype(F32)
        out_ref[0] = image.T if turned else image
        total = 0.0
        for k in range(count):
            total += dot_tn(refs[k][:, left[0] : left[1]], refs[count + k][:, right[0] : right[1]])
        out_ref[1] = total

    return pl.pallas_call(
        kernel, out_shape=jax.ShapeDtypeStruct((2, m, n), F32), compiler_params=VMEM_LIMIT
    )(shard, *left_got, *right_got)


def normalized(x):
    centred = x - jnp.mean(x, axis=-1, keepdims=True)
    inverse = lax.rsqrt(jnp.mean(centred * centred, axis=-1, keepdims=True) + NORM_EPS)
    return centred * inverse, inverse


def norm_back(n, inverse, w):
    return (w - jnp.mean(w, axis=-1, keepdims=True) - n * jnp.mean(w * n, axis=-1, keepdims=True)) * inverse


def row_call(kernel, row_mods, indices, arrays, outs):
    rows, width = row_mods.shape[0], row_mods.shape[1] // 6

    def whole(x):
        return pl.BlockSpec(x.shape, lambda i: (0,) * len(x.shape))

    return pl.pallas_call(
        kernel,
        grid=(1,),
        in_specs=[pl.BlockSpec((rows, width), lambda i, at=at: (0, at)) for at in indices]
        + [whole(x) for x in arrays],
        out_specs=tuple(whole(x) for x in outs),
        out_shape=tuple(outs),
        compiler_params=VMEM_LIMIT,
    )(*[row_mods] * len(indices), *arrays)


def enter_rows(row_mods, x, cut):
    rows, width = x.shape

    def kernel(shift_ref, scale_ref, x_ref, image_ref, text_ref):
        n = normalized(x_ref[...])[0]
        h = (n * (1.0 + scale_ref[...].astype(F32)) + shift_ref[...].astype(F32)).astype(BF)
        image_ref[...] = h[:cut]
        text_ref[...] = h[cut:]

    outs = [jax.ShapeDtypeStruct((cut, width), BF), jax.ShapeDtypeStruct((rows - cut, width), BF)]
    return row_call(kernel, row_mods, (0, 1), (x,), outs)


def middle_rows(row_mods, x, image_sum, text_sum, bias):
    rows, width = x.shape
    cut = image_sum.shape[0]

    def kernel(
        gate_ref, shift_ref, scale_ref, x_ref, image_ref, text_ref, bias_ref,
        branch_ref, middle_ref, himage_ref, htext_ref,
    ):
        branch_ref[:cut] = image_ref[...] + bias_ref[0:1, :]
        branch_ref[cut:] = text_ref[...] + bias_ref[1:2, :]
        middle = x_ref[...] + gate_ref[...].astype(F32) * branch_ref[...]
        middle_ref[...] = middle
        n = normalized(middle)[0]
        h = (n * (1.0 + scale_ref[...].astype(F32)) + shift_ref[...].astype(F32)).astype(BF)
        himage_ref[...] = h[:cut]
        htext_ref[...] = h[cut:]

    outs = [jax.ShapeDtypeStruct((rows, width), F32)] * 2
    outs += [jax.ShapeDtypeStruct((cut, width), BF), jax.ShapeDtypeStruct((rows - cut, width), BF)]
    return row_call(kernel, row_mods, (2, 3, 4), (x, image_sum, text_sum, bias), outs)


def halves_sum(rows, cut):
    return jnp.concatenate(
        (jnp.sum(rows[:cut], axis=0, keepdims=True), jnp.sum(rows[cut:], axis=0, keepdims=True)), 0
    )


def gated_rows(row_mods, g_out, cut):
    rows, width = g_out.shape

    def kernel(gate_ref, g_ref, image_ref, text_ref, sums_ref):
        g = (gate_ref[...].astype(F32) * g_ref[...]).astype(BF)
        image_ref[...] = g[:cut]
        text_ref[...] = g[cut:]
        sums_ref[...] = halves_sum(g.astype(F32), cut)

    outs = [jax.ShapeDtypeStruct((cut, width), BF), jax.ShapeDtypeStruct((rows - cut, width), BF)]
    outs += [jax.ShapeDtypeStruct((2, width), F32)]
    return row_call(kernel, row_mods, (5,), (g_out,), outs)


def middle_rows_back(row_mods, image_sum, text_sum, middle, g_out, branch, picks):
    rows, width = middle.shape
    cut = image_sum.shape[0]

    def kernel(
        gate_ref, scale_ref, image_ref, text_ref, middle_ref, g_ref, branch_ref, picks_ref,
        gmiddle_ref, gimage_ref, gtext_ref, sums_ref, mod_ref, gh_ref,
    ):
        gh_ref[:cut] = image_ref[...]
        gh_ref[cut:] = text_ref[...]
        gh = gh_ref[...]
        n, inverse = normalized(middle_ref[...])
        g_middle = g_ref[...] + norm_back(n, inverse, gh * (1.0 + scale_ref[...].astype(F32)))
        gmiddle_ref[...] = g_middle
        g_branch = (gate_ref[...].astype(F32) * g_middle).astype(BF)
        gimage_ref[...] = g_branch[:cut]
        gtext_ref[...] = g_branch[cut:]
        sums_ref[...] = halves_sum(g_branch.astype(F32), cut)
        for at, part in enumerate((g_middle * branch_ref[...], gh, gh * n)):
            mod_ref[:, at * width : (at + 1) * width] = dot_nn(picks_ref[...], part.astype(BF))

    outs = [jax.ShapeDtypeStruct((rows, width), F32), jax.ShapeDtypeStruct((cut, width), BF)]
    outs += [jax.ShapeDtypeStruct((rows - cut, width), BF), jax.ShapeDtypeStruct((2, width), F32)]
    outs += [jax.ShapeDtypeStruct((picks.shape[0], 3 * width), F32)]
    scratch = jax.ShapeDtypeStruct((rows, width), F32)
    return row_call(
        kernel, row_mods, (2, 4), (image_sum, text_sum, middle, g_out, branch, picks), outs + [scratch]
    )[:5]


def enter_rows_back(row_mods, image_sum, text_sum, x, g_middle, g_out, down, picks):
    rows, width = x.shape
    cut = image_sum.shape[0]

    def kernel(
        scale_ref, image_ref, text_ref, x_ref, gm_ref, g_ref, down_ref, picks_ref, gx_ref, mod_ref, gh_ref
    ):
        gh_ref[:cut] = image_ref[...]
        gh_ref[cut:] = text_ref[...]
        gh = gh_ref[...]
        n, inverse = normalized(x_ref[...])
        gx_ref[...] = gm_ref[...] + norm_back(n, inverse, gh * (1.0 + scale_ref[...].astype(F32)))
        for at, part in enumerate((gh, gh * n, g_ref[...] * down_ref[...])):
            mod_ref[:, at * width : (at + 1) * width] = dot_nn(picks_ref[...], part.astype(BF))

    outs = [jax.ShapeDtypeStruct((rows, width), F32), jax.ShapeDtypeStruct((picks.shape[0], 3 * width), F32)]
    scratch = jax.ShapeDtypeStruct((rows, width), F32)
    return row_call(
        kernel, row_mods, (1,), (image_sum, text_sum, x, g_middle, g_out, down, picks), outs + [scratch]
    )[:2]


def gelu_pair(u):
    c = 0.7978845608028654
    inner = jnp.tanh(c * (u + 0.044715 * u * u * u))
    value = 0.5 * u * (1.0 + inner)
    slope = 0.5 * (1.0 + inner) + 0.5 * u * (1.0 - inner * inner) * c * (1.0 + 3 * 0.044715 * u * u)
    return value.astype(BF), slope.astype(BF)


def shards(
    image_tokens,
    text_tokens,
    conditioning,
    image_seq_ids,
    text_seq_ids,
    ada_weight,
    qkv_weight,
    out_weight,
    up_weight,
    down_weight,
    biases,
    image_cotangent,
    text_cotangent,
):
    section = lax.axis_index("section")
    context = lax.axis_index("context")
    tensor = lax.axis_index("tensor")
    ncontext = lax.axis_size("context")
    ntensor = lax.axis_size("tensor")
    ndev = ncontext * ntensor
    first = section == 0
    micros, own_image, width = image_tokens.shape
    own_text = text_tokens.shape[1]
    seqs = conditioning.shape[1]
    rows_image, rows_text = micros * own_image, micros * own_text
    heads_here = HEADS // ntensor
    local = heads_here * HEAD
    hidden = up_weight.shape[3]
    bias_here = biases.shape[2]
    depth = qkv_weight.shape[2]
    mods = 6 * width
    table_rows = 2 * seqs
    per = ncontext // micros
    micro = context // per
    paired = per == 2 and heads_here % 2 == 0
    groups = 2 if paired else 1
    group_heads = heads_here // groups
    group = group_heads * HEAD
    side = context % per
    ctx_image, ctx_text = ntensor * rows_image, ntensor * rows_text
    ctx_rows = ctx_image + ctx_text

    order = (0, 2, 1, 3)

    def swapped(x, axis, bit):
        return lax.ppermute(x, axis, [(i, i ^ bit) for i in range(lax.axis_size(axis))])

    def sided(a, b):
        return jnp.where(side == 0, a, b), jnp.where(side == 0, b, a)

    def near(x):
        return swapped(x, "tensor", 1)

    def far(x):
        return swapped(x, "tensor", 2)

    def gather_tensor(x):
        beside = near(x)
        across = far(x)
        return x, across, beside, near(across)

    def reduce_tensor(x):
        n = x.shape[0] // 4
        got = near(x[2 * n :])
        mine = x[: 2 * n].astype(F32) + got.astype(F32)
        return mine[:n] + far(mine[n:].astype(BF)).astype(F32)

    def spread_both(image, text):
        return joined(gather_tensor(image), gather_tensor(text))

    def turned_by(x, by):
        return lax.ppermute(x, "context", [(i, (i + by) % ncontext) for i in range(ncontext)])

    def text_gather(rows):
        return [rows] + [turned_by(rows, k) for k in range(1, ncontext)]

    def text_scatter(partial_sums):
        sums = partial_sums.astype(BF).reshape(ncontext, rows_text, width)
        total = sums[0].astype(F32)
        for k in range(1, ncontext):
            total += turned_by(sums[k], -k).astype(F32)
        return total

    def spread_and_gather(image, text):
        return joined(gather_tensor(image)) + joined(text_gather(text))

    def by_tensor(x, axis):
        places = [jnp.array(order)[tensor ^ k] for k in range(ntensor)]
        return jnp.stack([lax.dynamic_index_in_dim(x, at, axis, keepdims=False) for at in places], axis)

    def in_group(x, axis):
        places = [tensor ^ bit for bit in order]
        return jnp.stack([lax.dynamic_index_in_dim(x, at, axis, keepdims=False) for at in places], axis)

    def gather_both(x):
        got = lax.all_gather(x, "tensor")
        got = lax.all_to_all(jnp.broadcast_to(got[None], (ncontext,) + got.shape), "context", 0, 0)
        return got.reshape((ndev,) + x.shape)

    def rounds(step, back):
        pairs = []
        for h in range(ncontext):
            m = (h + step) % micros
            pairs.append((h, m * per + h // micros))
        return [(b, a) for a, b in pairs] if back else pairs

    def to_work(image, text):
        pieces = []
        for step in range(micros):
            m = (context + step) % micros
            pieces.append(
                [
                    lax.ppermute(
                        lax.dynamic_index_in_dim(x, m, 0, keepdims=False), "context", rounds(step, False)
                    )
                    for x in (image, text)
                ]
            )
        return jnp.concatenate([p[0] for p in pieces] + [p[1] for p in pieces], 0).astype(F32)

    def to_home(rows):
        rows = rows.astype(BF)
        pieces = []
        for step in range(micros):
            at, below = step * own_image, rows_image + step * own_text
            both = jnp.concatenate((rows[at : at + own_image], rows[below : below + own_text]), 0)
            pieces.append(lax.ppermute(both, "context", rounds(step, True)))
        pieces = jnp.stack(pieces).astype(F32)
        image, text = pieces[:, :own_image], pieces[:, own_image:]
        turns = [(m - context) % micros for m in range(micros)]
        return tuple(
            jnp.stack([lax.dynamic_index_in_dim(x, turn, 0, keepdims=False) for turn in turns])[None]
            for x in (image, text)
        )

    def gathered(w):
        return lax.all_gather(w, "context", axis=0, tiled=True)

    qkv_full = [gathered(qkv_weight[0, 0])]
    out_full = [gathered(out_weight[0, 0].T)]
    up_full = [gathered(up_weight[0, 0])]
    down_full = [gathered(down_weight[0, 0].T)]

    def ring(w, send_after=None):
        pieces = [w if send_after is None else after(w, send_after)]
        for step in range(1, ncontext):
            pieces.append(lax.ppermute(pieces[-1], "context", [(i, (i + 1) % ncontext) for i in range(ncontext)]))
        return pieces

    def laid(pieces):
        full = jnp.zeros((width, pieces[0].shape[1]), BF)
        for step, piece in enumerate(pieces):
            full = lax.dynamic_update_slice_in_dim(full, piece, (context - step) % ncontext * depth, 0)
        return full

    ring_first = ring(jnp.concatenate((qkv_weight[0, 1], out_weight[0, 1].T), axis=1))
    stage = (ncontext + 2) // 3
    part = hidden // ncontext
    text_sent = jnp.concatenate(
        [w.reshape(ncontext, part, depth) for w in (up_weight[0, 1].T, down_weight[0, 1])], axis=1
    )
    text_moved = lax.all_to_all(after(text_sent, ring_first[-1]), "context", 0, 0)
    feed = []

    cond_float = conditioning.astype(F32)
    silu_cond = jax.nn.silu(cond_float).astype(BF).reshape(micros * seqs, -1)
    ada_part = jnp.einsum("rc,jck->jrk", silu_cond, ada_weight[0], preferred_element_type=F32)
    sharing = [[m * per + u for u in range(per)] for m in range(micros)]
    shares = per * ntensor
    share = mods // shares
    bias_placed = lax.dynamic_update_slice_in_dim(
        jnp.zeros((2, bias_here * ndev), F32),
        biases[0].astype(F32),
        (context * ntensor + tensor) * bias_here,
        1,
    )
    ada_sent = packed(
        ada_part + bias_placed[:, None, :mods],
        jnp.broadcast_to(biases[0].astype(F32)[None], (ndev, 2, bias_here)),
        micros,
        shares,
    )
    ada_got = lax.all_to_all(ada_sent.astype(BF), BOTH, 0, 0)
    bias_full = ada_got[:, table_rows : table_rows + 2, :bias_here].transpose(1, 0, 2).reshape(2, -1).astype(F32)
    ada_sum = jnp.sum(ada_got[:, :table_rows, :share].astype(F32), axis=0).astype(BF)
    table = lax.all_gather(ada_sum, "tensor")
    if paired:
        table = jnp.stack(sided(table, swapped(table, "context", 1)))
    else:
        table = lax.all_gather(table, "context", axis_index_groups=sharing)
    table = after(table, ring_first[stage - 1])
    table = table.reshape(shares, table_rows, share).transpose(1, 0, 2).reshape(table_rows, mods)
    query_bias = lax.dynamic_slice_in_dim(bias_full, mods + tensor * local, local, 1)
    value_bias = lax.dynamic_slice_in_dim(bias_full, mods + width + tensor * local, local, 1)
    qkv_bias = jnp.stack(
        (
            query_bias.reshape(2, heads_here, HEAD),
            jnp.zeros((2, heads_here, HEAD), F32),
            value_bias.reshape(2, heads_here, HEAD),
        ),
        axis=2,
    ).reshape(2, 3 * local)
    out_bias = bias_full[:, mods + 2 * width : mods + 3 * width]
    at_up = mods + 3 * width
    up_bias = lax.dynamic_slice_in_dim(bias_full[0], at_up + tensor * hidden, hidden, 0)
    up_bias_text = bias_full[1, at_up : at_up + ntensor * hidden].reshape(ntensor, ncontext, part)
    up_bias_text = in_group(lax.dynamic_index_in_dim(up_bias_text, context, 1, keepdims=False), 0).reshape(-1)
    down_bias = bias_full[:, mods + 3 * width + hidden * ntensor :]

    def by_modality(pair):
        return jnp.concatenate(
            (
                jnp.broadcast_to(pair[0][None], (rows_image, width)),
                jnp.broadcast_to(pair[1][None], (rows_text, width)),
            ),
            0,
        )

    def ids_of(work_context):
        m, u = work_context // per, work_context % per
        homes = jnp.stack([u * micros + (m - step) % micros for step in range(micros)])
        places = homes[None, :] * ntensor + (tensor ^ jnp.array(order))[:, None]
        found = []
        for ids, own in ((image_seq_ids, own_image), (text_seq_ids, own_text)):
            table_ids = lax.dynamic_index_in_dim(ids, m, 0, keepdims=False).reshape(ndev, own)
            found.append(jnp.take(table_ids, places.reshape(-1), axis=0).reshape(-1))
        return found

    own_found = ids_of(context)
    own_ids = jnp.concatenate((own_found[0][:rows_image], own_found[1][:rows_text] + seqs))
    onehot = (own_ids[:, None] == jnp.arange(table_rows)[None, :]).astype(BF)
    row_mods = dot_nn(onehot, table).astype(BF)
    picks = onehot.T
    joint_ids = jnp.concatenate(own_found)
    if paired:
        attn_ids = jnp.concatenate([joint_ids] + ids_of(context ^ 1))
    else:
        attn_ids = jnp.concatenate([x for u in range(per) for x in ids_of(micro * per + u)])

    def row_mod(index):
        return row_mods[:, index * width : (index + 1) * width].astype(F32)

    def attention(joint):
        if paired:
            mine, theirs = sided(joint[: 3 * group], joint[3 * group :])
            theirs = swapped(theirs, "context", 1)
            here, there, lse = attend_pair(mine, theirs, attn_ids, group_heads)
            return jnp.concatenate(sided(here, swapped(there, "context", 1)), axis=0), (mine, theirs, lse)
        by_kind = joint.reshape(heads_here, 3, HEAD, ctx_rows)
        q, k, v = (by_kind[:, i].reshape(local, ctx_rows).T for i in range(3))
        k, v = (
            lax.all_gather(x, "context", axis=0, tiled=True, axis_index_groups=sharing) for x in (k, v)
        )
        attended, lse = attend(q, k, v, joint_ids, attn_ids, group_heads)
        return attended.T, (q, k, v, lse)

    def attention_back(grad, kept):
        if paired:
            mine, theirs, lse = kept
            g_mine, g_theirs = sided(grad[:group], grad[group:])
            g_theirs = swapped(g_theirs, "context", 1)
            d_mine, d_theirs = attend_pair_back(mine, theirs, g_mine, g_theirs, lse, attn_ids, group_heads)
            return jnp.concatenate(sided(d_mine, swapped(d_theirs, "context", 1)), axis=0)
        q, k, v, lse = kept
        dq, dk, dv = attend_back(q, k, v, grad.T, lse, joint_ids, attn_ids, group_heads)
        dk, dv = (
            lax.psum_scatter(x, "context", scatter_dimension=0, tiled=True, axis_index_groups=sharing)
            for x in (dk, dv)
        )
        kinds = [x.T.reshape(heads_here, HEAD, ctx_rows) for x in (dq, dk, dv)]
        return jnp.stack(kinds, axis=1).reshape(3 * local, ctx_rows)

    def forward(x, late=False):
        h1_image, h1_text = enter_rows(row_mods, x, rows_image)
        fresh = len(qkv_full) == 1
        if fresh:
            h1_image = after(h1_image, ring_first[2 * stage - 2])
            full = laid(ring_first)
            qkv_full.append(full[:, : 3 * local])
            out_full.append(full[:, 3 * local :])
        h1 = spread_both(h1_image, h1_text)
        joint = jnp.concatenate(
            [(dot_tt(qkv_full[j], h1[j]) + qkv_bias[j][:, None]).astype(BF) for j in range(2)], axis=1
        )
        attended, kept = attention(joint)
        if fresh:
            attended = after(attended, text_moved)
            moved = gather_tensor(text_moved.transpose(1, 0, 2).reshape(2 * part, width))
            feed.append(jnp.concatenate([b[:part] for b in moved], 0))
            feed.append(jnp.concatenate([b[part:] for b in moved], 0))
        image_sum = reduce_tensor(dot_tt(attended, out_full[0])[:ctx_image].astype(BF))
        text_sum = reduce_tensor(dot_tt(attended[:, ctx_image:], out_full[1]).astype(BF))
        if fresh:
            image_sum = after(image_sum, *feed)
        branch, middle, h2_image, h2_text = middle_rows(row_mods, x, image_sum, text_sum, out_bias)
        up_text, down_text = feed
        h2 = spread_and_gather(h2_image, h2_text)
        pairs = [
            gelu_pair(dot_nn(h2[0], up_full[0]) + up_bias),
            gelu_pair(dot_nt(h2[1], up_text) + up_bias_text),
        ]
        acts, slopes = [p[0] for p in pairs], [p[1] for p in pairs]
        saved = dict(
            x=x, h1=h1, kept=kept, attn=attended, branch=branch, middle=middle, h2=h2, acts=acts,
            slopes=slopes,
        )

        def finish(gate):
            if gate is not None:
                saved["acts"] = [after(act, gate) for act in acts]
            down = jnp.concatenate(
                (
                    reduce_tensor(dot_nt(saved["acts"][0], down_full[0]).astype(BF)),
                    text_scatter(dot_nn(saved["acts"][1], down_text)),
                ),
                0,
            ) + by_modality(down_bias)
            saved["down"] = down
            saved["out"] = middle + row_mod(5) * down

        saved["finish"] = finish
        if not late:
            finish(None)
        return saved

    def chosen(a, b):
        return jax.tree.map(lambda x, y: jnp.where(first, x, y), a, b)

    def scattered(full):
        return lax.psum_scatter(full.astype(BF), "context", scatter_dimension=0, tiled=True)

    def backward(saved, g_out, last=None):
        gd_image, gd_text, gd_sums = gated_rows(row_mods, g_out, rows_image)
        up_text, down_text = feed
        gd = spread_and_gather(gd_image, gd_text)
        g_up = [
            (dot_nn(gd[0], down_full[0]) * saved["slopes"][0].astype(F32)).astype(BF),
            (dot_nt(gd[1], down_text) * saved["slopes"][1].astype(F32)).astype(BF),
        ]
        g_h2_image = reduce_tensor(dot_nt(g_up[0], up_full[0]).astype(BF))
        g_h2_text = text_scatter(dot_nn(g_up[1], up_text))
        early = []
        if last:
            use = chosen(
                dict(h2=saved["h2"][0], acts=saved["acts"][0], gd=gd[0], g_up=g_up[0]),
                {k: last[k][0] for k in ("h2", "acts", "gd", "g_up")},
            )
            early = [
                dot_tn(use["gd"], use["acts"]).astype(BF),
                dot_tn(use["h2"], use["g_up"]).astype(BF),
            ]
            g_h2_image = after(g_h2_image, *early)
            early = [scattered(part) for part in early]
        g_middle, gb_image, gb_text, gb_sums, mod_late = middle_rows_back(
            row_mods, g_h2_image, g_h2_text, saved["middle"], g_out, saved["branch"], picks
        )
        gb = spread_both(gb_image, gb_text)
        if "down" not in saved:
            saved["finish"](gb[0])
        g_attn = jnp.concatenate([dot_tt(out_full[j], gb[j]).astype(BF) for j in range(2)], axis=1)
        if last:
            use = chosen(dict(gb=gb[0], attn=saved["attn"]), dict(gb=last["gb"][0], attn=last["attn"]))
            early.append(dot_tt(use["gb"], use["attn"][:, :ctx_image]).astype(BF))
            g_attn = after(g_attn, early[2])
        g_joint = attention_back(g_attn, saved["kept"])
        g_h1_image = reduce_tensor(dot_tt(g_joint, qkv_full[0])[:ctx_image].astype(BF))
        g_h1_text = reduce_tensor(dot_tt(g_joint[:, ctx_image:], qkv_full[1]).astype(BF))
        if last:
            use = chosen(dict(h1=saved["h1"][0], g=g_joint), dict(h1=last["h1"][0], g=last["g_joint"]))
            early.append(dot_tt(use["h1"], use["g"][:, :ctx_image]).astype(BF))
            g_h1_image = after(g_h1_image, early[3])
        g_x, mod_early = enter_rows_back(
            row_mods, g_h1_image, g_h1_text, saved["x"], g_middle, g_out, saved["down"], picks
        )
        if last:
            g_x = after(g_x, *early[:2])
        mod_grad = jnp.concatenate((mod_early[:, : 2 * width], mod_late, mod_early[:, 2 * width :]), axis=1)
        tensors = dict(
            h1=saved["h1"], attn=saved["attn"], h2=saved["h2"], acts=saved["acts"], g_joint=g_joint,
            gb=gb, g_up=g_up, gd=gd, gd_sums=gd_sums, gb_sums=gb_sums, mod=mod_grad,
        )
        return g_x, tensors, early

    aligned = part % 128 == 0 and depth % 128 == 0 and local % 128 == 0 and ncontext == ntensor
    offsets = tensor ^ jnp.arange(ntensor, dtype=jnp.int32)
    places = jnp.concatenate(((offsets & 1) * 2 + offsets // 2, context.reshape(1).astype(jnp.int32)))

    own_context = context.reshape(1).astype(jnp.int32)

    def tensor_round(hidden_rows, wide_rows):
        if aligned:
            sent = tensor_packed(places, hidden_rows, wide_rows, part, depth, ncontext)
        else:
            back = (context - jnp.arange(ncontext)) % ncontext
            hidden_rows, wide_rows = (
                jnp.take(x.reshape(ncontext, rows_text, -1), back, axis=0).reshape(x.shape)
                for x in (hidden_rows, wide_rows)
            )
            pieces = by_tensor(hidden_rows.reshape(hidden_rows.shape[0], ntensor, part), 1).transpose(1, 0, 2)
            own = lax.dynamic_slice_in_dim(wide_rows, context * depth, depth, 1)
            sent = jnp.concatenate((pieces, jnp.broadcast_to(own[None], (ntensor,) + own.shape)), axis=2)
        return lax.all_to_all(sent, "tensor", 0, 0)

    def context_round(blocked, turned, stacked):
        if aligned:
            sent = text_packed(own_context, blocked, turned, stacked, part, ncontext)
            return [turned_by(x, k) if k else x for k, x in enumerate(sent)]
        parts = [x.reshape(x.shape[0], ncontext, -1).transpose(1, 0, 2) for x in blocked]
        parts += [jnp.broadcast_to(x.T[None], (ncontext,) + x.T.shape) for x in turned]
        stacks = [x[:, :, :part].transpose(1, 0, 2).reshape(x.shape[1], -1) for x in stacked]
        stacks = [jnp.broadcast_to(x[None], (ncontext,) + x.shape) for x in stacks]
        return [
            lax.all_to_all(jnp.concatenate(group, axis=2), "context", 0, 0) for group in (parts, stacks) if group
        ]

    def handed(rows, by):
        return lax.ppermute(rows.astype(BF), "section", [(0, 1)] if by > 0 else [(1, 0)]).astype(F32)

    saved_first = forward(to_work(image_tokens, text_tokens))
    saved_last = forward(handed(saved_first["out"], 1), late=True)
    grad_last, tensors_last, unused = backward(saved_last, to_work(image_cotangent, text_cotangent))
    kept = chosen(
        [saved_first[n][1] for n in ("acts", "h1", "h2")] + [saved_first["attn"][:, ctx_image:]],
        [saved_last[n][1] for n in ("acts", "h1", "h2")] + [saved_last["attn"][:, ctx_image:]],
    )
    kept[0] = after(kept[0], tensors_last["g_joint"])
    ours_before = tensor_round(kept[0], kept[2])
    got_before = context_round([kept[1]], [kept[3]], [ours_before])
    out = to_home(after(jnp.where(first, saved_first["out"], saved_last["out"]), tensors_last["g_joint"]))
    returned = after(handed(grad_last, -1), *got_before, *out)
    grad_first, tensors_first, early = backward(saved_first, returned, tensors_last)
    grad = to_home(jnp.where(first, grad_first, grad_last))
    use = chosen(tensors_first, tensors_last)

    down_shard, up_shard, out_part, qkv_part = early
    rows_shard = after(scattered(jnp.concatenate((out_part, qkv_part), axis=1)), grad_first)

    ours_after = tensor_round(use["g_up"][1], use["gd"][1])

    def column_sums(parts):
        return jnp.stack([dot_nn(jnp.ones((8, p.shape[0]), BF), p)[0] for p in parts])

    qkv_sums = jnp.stack(
        [
            dot_nt(jnp.ones((8, part.shape[1]), BF), part)[0]
            for part in (use["g_joint"][:, :ctx_image], use["g_joint"][:, ctx_image:])
        ]
    ).reshape(2, heads_here, 3, HEAD)
    up_sums_text = lax.dynamic_update_slice_in_dim(
        jnp.zeros((ntensor, ncontext, part), F32),
        by_tensor(column_sums((use["g_up"][1],)).reshape(ntensor, 1, part), 0),
        context,
        1,
    ).reshape(1, -1)
    up_sums_image = lax.dynamic_update_slice_in_dim(
        jnp.zeros((1, ntensor * hidden), F32), column_sums((use["g_up"][0],)), tensor * hidden, 1
    )
    rest = jnp.zeros((2, bias_here * ndev - mods), F32)
    for at, value in (
        (tensor * local, qkv_sums[:, :, 0].reshape(2, local)),
        (width + tensor * local, qkv_sums[:, :, 2].reshape(2, local)),
        (2 * width, use["gb_sums"]),
        (3 * width, jnp.concatenate((up_sums_image, up_sums_text), 0)),
        (3 * width + ntensor * hidden, use["gd_sums"]),
    ):
        rest = lax.dynamic_update_slice_in_dim(rest, value, at, 1)
    if aligned:
        sent = tail_packed(micro.astype(jnp.int32), use["mod"], rest, micros, shares)
    else:
        bias_part = jnp.concatenate((jnp.sum(use["mod"].reshape(2, seqs, mods), axis=1), rest), axis=1)
        mod_sent = use["mod"].reshape(2, 1, seqs, mods)
        mod_sent = jnp.where(jnp.arange(micros)[None, :, None, None] == micro, mod_sent, 0.0)
        bias_sent = bias_part.reshape(2, ndev, bias_here).transpose(1, 0, 2)
        sent = packed(mod_sent.reshape(2, micros * seqs, mods), bias_sent, micros, shares).astype(BF)
    got = jnp.sum(lax.all_to_all(sent, BOTH, 0, 0).astype(F32), axis=0)
    bias_grad = got[table_rows:, :bias_here]
    mod_all = (
        gather_both(got[:table_rows, :share].astype(BF))
        .reshape(micros, shares, 2, seqs, share)
        .transpose(2, 0, 3, 1, 4)
        .reshape(2, micros * seqs, mods)
    )
    if aligned:
        down_grad = finish_hidden(own_context, down_shard, got_before, depth + local, ours_after, part, True)
        mod_all = after(mod_all, down_grad)
    ada_grad = jnp.einsum("rc,jrk->jck", silu_cond, mod_all, preferred_element_type=F32)
    cond_inner = jnp.einsum("jrk,jck->rc", mod_all, ada_weight[0], preferred_element_type=F32)
    got_after = context_round([after(use["gb"][1], mod_all)], [], [ours_after])
    got_qkv = context_round([], [after(use["g_joint"][:, ctx_image:], mod_all)], [])
    if aligned:
        up_grad = finish_hidden(own_context, up_shard, got_after, depth, ours_before, part, False)
        out_grad = finish_rows(rows_shard, 0, got_before, (depth, depth + local), got_after, (0, depth), True)
        qkv_grad = finish_rows(rows_shard, local, got_before, (0, depth), got_qkv, (0, 3 * local), False)
    else:
        acts_all = got_before[1].reshape(ncontext, -1, ntensor, part)
        g_up_all = got_after[1].reshape(ncontext, -1, ntensor, part)
        text_down = jnp.einsum("crtj,trd->cjd", acts_all, ours_after[:, :, part:], preferred_element_type=F32)
        text_up = jnp.einsum("trk,crtj->kcj", ours_before[:, :, part:], g_up_all, preferred_element_type=F32)
        text_out = jnp.einsum(
            "crh,crd->hd", got_before[0][:, :, depth:], got_after[0], preferred_element_type=F32
        )
        text_qkv = jnp.einsum("crk,crh->kh", got_before[0][:, :, :depth], got_qkv[0], preferred_element_type=F32)
        down_grad = jnp.stack((down_shard.astype(F32).T, text_down.reshape(hidden, depth)))
        up_grad = jnp.stack((up_shard.astype(F32), text_up.reshape(depth, hidden)))
        out_grad = jnp.stack((rows_shard[:, :local].astype(F32).T, text_out))
        qkv_grad = jnp.stack((rows_shard[:, local:].astype(F32), text_qkv))
    unused, silu_back = jax.vjp(jax.nn.silu, cond_float)
    cond_inner = cond_inner + lax.ppermute(cond_inner, "section", [(0, 1), (1, 0)])
    cond_grad = silu_back(cond_inner.reshape(cond_float.shape))[0]
    return (
        *out,
        *grad,
        cond_grad,
        ada_grad[None],
        qkv_grad[None],
        out_grad[None],
        up_grad[None],
        down_grad[None],
        bias_grad[None],
    )


def solution(mesh):
    tokens = P(None, BOTH, None)
    block_rows = P("section", None, BOTH, None)
    by_rows = P("section", None, "context", "tensor")
    by_cols = P("section", None, "tensor", "context")
    block_biases = P("section", None, BOTH)
    in_specs = (
        tokens,
        tokens,
        P(None, None, BOTH),
        P(),
        P(),
        block_rows,
        by_rows,
        by_cols,
        by_rows,
        by_cols,
        block_biases,
        tokens,
        tokens,
    )
    out_specs = (
        block_rows,
        block_rows,
        block_rows,
        block_rows,
        P(None, None, BOTH),
        block_rows,
        by_rows,
        by_cols,
        by_rows,
        by_cols,
        block_biases,
    )
    return jax.shard_map(shards, mesh=mesh, in_specs=in_specs, out_specs=out_specs, check_vma=False)
```
